32 devices in a mesh: dp: 8 (over y, x, core), tensor: 4 (over z).
Axes of the slice: x: 2, y: 2, z: 4, core: 2. Of those that a mesh axis runs over, the one named last changes fastest.
Arguments:
- hidden_in: bfloat16 [8704, 1024], P(('dp', 'tensor')), may hold values from -6 to 6
- cotangent: bfloat16 [8704, 1024], P(('dp', 'tensor')), may hold values from -6 to 6
- group_ids: int32 [8], P('dp'), may hold values from 0 to 7
- group_sizes: int32 [8], replicated, may hold values from 1 to 4
- w_qkv: bfloat16 [2, 3, 1024, 1024], P(None, None, None, 'tensor'), may hold values from -0.1875 to 0.1875
- w_out: bfloat16 [2, 1024, 1024], P(None, 'tensor'), may hold values from -0.75 to 0.75
- w_up: bfloat16 [2, 1024, 4096], P(None, None, 'tensor'), may hold values from -0.1875 to 0.1875
- w_down: bfloat16 [2, 4096, 1024], P(None, 'tensor'), may hold values from -0.09375 to 0.09375
- gains: float32 [2, 4, 1024], replicated, may hold values from 0.25 to 1.75
- shifts: float32 [2, 4, 1024], replicated, may hold values from -1.5 to 1.5
Outputs:
- mixed: float32 [8704, 1024], P(('dp', 'tensor'))
- grad_in: float32 [8704, 1024], P(('dp', 'tensor'))
- grad_qkv: float32 [2, 3, 1024, 1024], P(None, None, None, 'tensor')
- grad_out: float32 [2, 1024, 1024], P(None, 'tensor')
- grad_up: float32 [2, 1024, 4096], P(None, None, 'tensor')
- grad_down: float32 [2, 4096, 1024], P(None, 'tensor')
- grad_gains: float32 [2, 4, 1024], replicated
- grad_shifts: float32 [2, 4, 1024], replicated
The draws below stay inside these ranges and needn't reach their ends.
All inputs are finite; a program needn't handle non-finite values.
Results may differ from the reference program's by a relative error of at most 0.02.
Values may be sent and summed in bfloat16 or wider, within the bound.
A program may use at most 256 MiB of HBM per device.

```python
import jax
import jax.numpy as jnp
from jax import lax

D = 1024
HEADS = 16
HEAD_DIM = 64
FF = 4096
LAYERS = 2
GROUPS = 8
LENGTH = 1088
HD = 1024
SEQS = 8
TOKENS = 8704


def set_ends(drawn, key, least, largest):
    longest = drawn.shape.index(max(drawn.shape))
    spots = []
    for shift in (0, 1):
        where = [jax.random.randint(jax.random.fold_in(key, axis), (), 0, length) for axis, length in enumerate(drawn.shape)]
        where[longest] = (where[longest] + shift) % drawn.shape[longest]
        spots.append(tuple(where))
    return drawn.at[spots[0]].set(least).at[spots[1]].set(largest)


def raised(entries, own_key, source, target, parts, factor):
    owner, partner = [(jnp.arange(entries.shape[dim]) // (entries.shape[dim] // parts)).reshape([-1 if axis == dim else 1 for axis in range(entries.ndim)]) for dim in (source, target)]
    chosen = jax.random.permutation(own_key, parts)[partner]
    strong = (owner == chosen) | (owner == (partner + parts // 2) % parts)
    return jnp.where(strong, factor * entries, entries)


def level_of(rng, extent, cuts, low, high):
    factor_of, own = 1.0, jax.random.fold_in(rng, 6)
    for dim, blocks in cuts:
        draws = jnp.exp(jax.random.uniform(jax.random.fold_in(own, dim), (blocks,), jnp.float32, low / len(cuts), high / len(cuts)))
        factor_of = factor_of * jnp.repeat(draws, extent[dim] // blocks).reshape([-1 if axis == dim else 1 for axis in range(len(extent))])
    return factor_of


def normal_values(stream_key, extent, deviation, reach, shards=(), held_as=jnp.bfloat16):
    entries = deviation * jax.random.normal(stream_key, extent, jnp.float32)
    if shards:
        entries = entries * level_of(stream_key, extent, shards, -0.22, 0.18)
    return jnp.clip(entries, -reach, reach).astype(held_as)


def bell_draw_with(stream_key, shape, scale, bound, pieces, heavy, dtype=jnp.bfloat16):
    result = scale * jax.random.normal(stream_key, shape, jnp.float32)
    if pieces:
        result = result * level_of(stream_key, shape, pieces, -0.22, 0.18)
    return jnp.clip(raised(result, jax.random.fold_in(stream_key, 3), *heavy), -bound, bound).astype(dtype)


def setup_inputs(seed: int = 0) -> dict:
    streams_of = jax.random.split(jax.random.key(seed), 11)
    return {
        "hidden_in": normal_values(streams_of[0], (TOKENS, D), 1.0, 6.0, ((0, 32),)),
        "cotangent": bell_draw_with(streams_of[1], (TOKENS, D), 1.0, 6.0, ((0, 32),), (0, 1, 32, 2.75)),
        "group_ids": set_ends(jax.random.randint(streams_of[2], (SEQS,), 0, GROUPS), jax.random.fold_in(streams_of[2], 1), 0, GROUPS - 1).astype(jnp.int32),
        "group_sizes": set_ends(jax.random.randint(streams_of[3], (GROUPS,), 1, 5), jax.random.fold_in(streams_of[3], 1), 1, 4).astype(jnp.int32),
        "w_qkv": normal_values(streams_of[4], (LAYERS, 3, D, HD), D ** -0.5, 0.1875, ((3, 4),)),
        "w_out": normal_values(streams_of[5], (LAYERS, HD, D), HEAD_DIM ** -0.5, 0.75, ((1, 4),)),
        "w_up": normal_values(streams_of[6], (LAYERS, D, FF), D ** -0.5, 0.1875, ((2, 4),)),
        "w_down": normal_values(streams_of[7], (LAYERS, FF, D), FF ** -0.5, 0.09375, ((1, 4),)),
        "gains": jnp.clip(1.0 + 0.15 * jax.random.normal(streams_of[8], (LAYERS, 4, D), jnp.float32), 0.25, 1.75),
        "shifts": normal_values(streams_of[9], (LAYERS, 4, D), 0.3, 1.5, (), jnp.float32),
    }


@jax.custom_vjp
def low(v):
    return lax.optimization_barrier(v.astype(jnp.bfloat16)).astype(jnp.float32)

@jax.custom_vjp
def low_back(v):
    return v

def low_keep(v):
    return (low(v), None)

def low_pass(kept, grad):
    return (grad,)

def back_keep(v):
    return (v, None)

def back_low(kept, grad):
    return (low(grad),)
low.defvjp(low_keep, low_pass)
low_back.defvjp(back_keep, back_low)
eps_norm = 1e-05
highest = lax.Precision.HIGHEST

def layer_norm(values, gain, shift):
    mean = lax.optimization_barrier(jnp.mean(values, axis=-1, keepdims=True))
    centred = values - mean
    spread = lax.optimization_barrier(jnp.mean(centred * centred, axis=-1, keepdims=True))
    return centred * lax.rsqrt(spread + eps_norm) * gain + shift

def attend(query, key, value):
    scale = HEAD_DIM ** (-0.5)
    scores = low_back(jnp.einsum('qhd,khd->hqk', query, key, precision=highest) * scale)
    places = jnp.arange(LENGTH)
    causal = places[:, None] >= places[None, :]
    scores = jnp.where(causal[None], scores, -1e+30)
    top = lax.optimization_barrier(jnp.max(scores, axis=-1, keepdims=True))
    weights = jnp.exp(scores - top)
    probs = weights / lax.optimization_barrier(jnp.sum(weights, axis=-1, keepdims=True))
    return jnp.einsum('hqk,khd->qhd', low(probs), value, precision=highest)

def forward(stream, w_qkv, w_out, w_up, w_down, gains, shifts):
    attend_saved = jax.checkpoint(attend)
    for layer in range(LAYERS):
        normed = low(layer_norm(stream, gains[layer, 0], shifts[layer, 0]))
        qkv = jnp.einsum('td,cde->cte', normed, w_qkv[layer], precision=highest)
        qkv = low_back(low(qkv))
        split = qkv.reshape(3, SEQS, LENGTH, HEADS, HEAD_DIM)
        attended = lax.map(lambda item: attend_saved(item[0], item[1], item[2]), (split[0], split[1], split[2]))
        attended = low_back(low(attended.reshape(TOKENS, HD)))
        branch = low_back(jnp.dot(attended, w_out[layer], precision=highest))
        middle = stream + layer_norm(branch, gains[layer, 1], shifts[layer, 1])
        normed2 = low(layer_norm(middle, gains[layer, 2], shifts[layer, 2]))
        upper = low_back(jnp.dot(normed2, w_up[layer], precision=highest))
        active = low(jax.nn.gelu(upper, approximate=True))
        second = low_back(jnp.dot(active, w_down[layer], precision=highest))
        stream = middle + layer_norm(second, gains[layer, 3], shifts[layer, 3])
    return stream

def reference(hidden_in, cotangent, group_ids, group_sizes, w_qkv, w_out, w_up, w_down, gains, shifts):
    f32 = jnp.float32
    inputs = (hidden_in.astype(f32), w_qkv.astype(f32), w_out.astype(f32), w_up.astype(f32), w_down.astype(f32), gains.astype(f32), shifts.astype(f32))
    mixed, pull = jax.vjp(forward, *inputs)
    seq_weight = 1.0 / group_sizes[group_ids].astype(f32)
    row_weight = jnp.repeat(seq_weight, LENGTH)
    grads = pull(cotangent.astype(f32) * row_weight[:, None])
    return (mixed, grads[0], grads[1], grads[2], grads[3], grads[4], grads[5], grads[6])
```

```python
import jax
import jax.numpy as jnp
from jax import lax
from jax.sharding import PartitionSpec as P

HEAD_DIM = 64
LENGTH = 1088
AXES = ("gh", "gl", "p", "c", "zh", "zl")
TP = ("c", "zl")
SHARE = ("gl", "p")
BATCH = ("gh", "gl", "p")


def swap_rows(values):
    return lax.ppermute(values, ("c", "zh"), ((0, 0), (1, 2), (2, 1), (3, 3)))


def keeps():
    return lax.axis_index("c") == lax.axis_index("zh")


def fetch_weight(weight):
    shape = weight.shape
    flat = weight.reshape(4, -1, 1024)
    part = lax.dynamic_index_in_dim(flat, lax.axis_index(SHARE), 0, keepdims=False)
    part = lax.ppermute(part, ("c", "zh"), ((0, 1), (3, 2)))
    rest = lax.all_gather(part, SHARE, axis=0, tiled=True).reshape(shape)
    return jnp.where(keeps(), weight, rest)


def sum_weight(grad):
    shape = grad.shape
    flat = grad.astype(jnp.bfloat16).reshape(-1, 1024)
    part = lax.psum_scatter(flat, BATCH, scatter_dimension=0, tiled=True)
    other = lax.ppermute(part, ("c", "zh"), ((1, 0), (2, 3)))
    part = (part.astype(jnp.float32) + other.astype(jnp.float32)).astype(jnp.bfloat16)
    mate = lax.ppermute(part, "c", ((0, 1), (1, 0)))
    part = jnp.where(keeps(), part, mate)
    return lax.all_gather(part, BATCH, axis=0, tiled=True).reshape(shape).astype(jnp.float32)


eps_norm = 1e-05


def norm_rows(values, gain, shift):
    mean = jnp.mean(values, axis=-1, keepdims=True)
    centred = values - mean
    spread = jnp.mean(centred * centred, axis=-1, keepdims=True)
    return centred * lax.rsqrt(spread + eps_norm) * gain + shift


def gelu_tanh(values):
    return jax.nn.gelu(values, approximate=True)


def masked_scores(query, key):
    scale = query.shape[-1] ** (-0.5)
    scores = jnp.einsum("qhd,khd->hqk", query, key, preferred_element_type=jnp.float32) * scale
    places = jnp.arange(query.shape[0])
    causal = places[:, None] >= places[None, :]
    return jnp.where(causal[None], scores, -1e30)


def attend_forward(query, key, value):
    scores = masked_scores(query, key)
    top = jnp.max(scores, axis=-1, keepdims=True)
    weights = jnp.exp(scores - top)
    total = jnp.sum(weights, axis=-1, keepdims=True)
    probs = (weights / total).astype(jnp.bfloat16)
    result = jnp.einsum("hqk,khd->qhd", probs, value, preferred_element_type=jnp.float32)
    return (result.astype(jnp.bfloat16), (top + jnp.log(total))[..., 0])


def attend_backward(query, key, value, grad_result, logsum):
    scale = query.shape[-1] ** (-0.5)
    probs = jnp.exp(masked_scores(query, key) - logsum[..., None])
    grad_probs = jnp.einsum("qhd,khd->hqk", grad_result, value, preferred_element_type=jnp.float32)
    inner = jnp.sum(probs * grad_probs, axis=-1, keepdims=True)
    grad_scores = (probs * (grad_probs - inner)).astype(jnp.bfloat16) * scale
    grad_query = jnp.einsum("hqk,khd->qhd", grad_scores, key, preferred_element_type=jnp.float32)
    grad_key = jnp.einsum("hqk,qhd->khd", grad_scores, query, preferred_element_type=jnp.float32)
    grad_value = jnp.einsum(
        "hqk,qhd->khd", probs.astype(jnp.bfloat16), grad_result, preferred_element_type=jnp.float32
    )
    return jnp.stack([grad_query, grad_key, grad_value]).astype(jnp.bfloat16)


def per_device(
    hidden_in, cotangent, group_ids, group_sizes, w_qkv, w_out, w_up, w_down, gains, shifts
):
    f32 = jnp.float32
    bf16 = jnp.bfloat16
    rows = hidden_in.shape[0]
    hidden_in = swap_rows(hidden_in)
    cotangent = swap_rows(cotangent)
    layers = w_qkv.shape[0]
    w_qkv = [fetch_weight(w_qkv[layer]) for layer in range(layers)]
    w_out = [fetch_weight(w_out[layer]) for layer in range(layers)]
    w_up = [fetch_weight(w_up[layer]) for layer in range(layers)]
    w_down = [fetch_weight(w_down[layer]) for layer in range(layers)]
    local_width = w_qkv[0].shape[2]
    heads_here = local_width // HEAD_DIM
    stream = hidden_in.astype(f32)
    saved = []
    for layer in range(layers):
        normed = norm_rows(stream, gains[layer, 0], shifts[layer, 0]).astype(bf16)
        rows_all = lax.all_gather(normed, TP, axis=0, tiled=True)
        group_rows = rows_all.shape[0]
        seqs = group_rows // LENGTH
        qkv = jnp.einsum("td,cde->cte", rows_all, w_qkv[layer], preferred_element_type=f32).astype(
            bf16
        )
        split = qkv.reshape(3, seqs, LENGTH, heads_here, HEAD_DIM)
        attended, logsum = lax.map(
            lambda item: attend_forward(item[0], item[1], item[2]), (split[0], split[1], split[2])
        )
        attended = attended.reshape(group_rows, local_width)

        def project_out(start, count, attended=attended, layer=layer):
            return jnp.dot(attended, w_out[layer], preferred_element_type=f32)

        branch = lax.psum_scatter(
            project_out(jnp.int32(0), rows * lax.axis_size(TP)).astype(bf16),
            TP,
            scatter_dimension=0,
            tiled=True,
        ).astype(f32)
        middle = stream + norm_rows(branch, gains[layer, 1], shifts[layer, 1])
        normed2 = norm_rows(middle, gains[layer, 2], shifts[layer, 2]).astype(bf16)
        ffn_all = lax.all_gather(normed2, TP, axis=0, tiled=True)
        upper = jnp.dot(ffn_all, w_up[layer], preferred_element_type=f32)
        active = gelu_tanh(upper).astype(bf16)

        def project_down(start, count, active=active, layer=layer):
            return jnp.dot(active, w_down[layer], preferred_element_type=f32)

        second = lax.psum_scatter(
            project_down(jnp.int32(0), lax.axis_size(TP) * rows).astype(jnp.bfloat16),
            TP,
            scatter_dimension=0,
            tiled=True,
        ).astype(jnp.float32)
        saved.append(
            (
                stream,
                rows_all,
                qkv,
                attended,
                logsum,
                branch,
                middle,
                ffn_all,
                upper,
                active,
                second,
            )
        )
        stream = middle + norm_rows(second, gains[layer, 3], shifts[layer, 3])
    ids = lax.all_gather(group_ids, "c", axis=0, tiled=True)
    mine = lax.dynamic_index_in_dim(ids, lax.axis_index("zh"), 0, keepdims=False)
    count = jnp.sum(jnp.where(jnp.arange(group_sizes.shape[0]) == mine, group_sizes, 0)).astype(f32)
    grad_stream = cotangent.astype(f32) * (1.0 / count)
    weight_grads = [None] * layers
    gain_grads = [None] * layers
    shift_grads = [None] * layers
    for layer in reversed(range(layers)):
        (
            stream_in,
            rows_all,
            qkv,
            attended,
            logsum,
            branch,
            middle,
            ffn_all,
            upper,
            active,
            second,
        ) = saved[layer]
        group_rows = rows_all.shape[0]
        seqs = group_rows // LENGTH
        _, pull_three = jax.vjp(norm_rows, second, gains[layer, 3], shifts[layer, 3])
        grad_second, gain_three, shift_three = pull_three(grad_stream)
        second_all = lax.all_gather(grad_second.astype(bf16), TP, axis=0, tiled=True)
        grad_downw = jnp.einsum("tf,td->fd", active, second_all, preferred_element_type=f32)
        grad_active = jnp.einsum("td,fd->tf", second_all, w_down[layer], preferred_element_type=f32)
        _, gelu_pull = jax.vjp(gelu_tanh, upper)
        grad_upper = gelu_pull(grad_active)[0].astype(bf16)
        grad_upw = jnp.einsum("td,tf->df", ffn_all, grad_upper, preferred_element_type=f32)

        def back_up(start, count, grad_upper=grad_upper, layer=layer):
            return jnp.einsum("tf,df->td", grad_upper, w_up[layer], preferred_element_type=f32)

        grad_normed2 = lax.psum_scatter(
            back_up(jnp.int32(0), lax.axis_size(TP) * rows).astype(jnp.bfloat16),
            TP,
            scatter_dimension=0,
            tiled=True,
        ).astype(jnp.float32)
        _, pull_two = jax.vjp(norm_rows, middle, gains[layer, 2], shifts[layer, 2])
        grad_mid_part, gain_two, shift_two = pull_two(grad_normed2)
        grad_middle = grad_stream + grad_mid_part
        _, pull_one = jax.vjp(norm_rows, branch, gains[layer, 1], shifts[layer, 1])
        grad_branch, gain_one, shift_one = pull_one(grad_middle)
        branch_all = lax.all_gather(grad_branch.astype(bf16), TP, axis=0, tiled=True)
        grad_outw = jnp.einsum("te,td->ed", attended, branch_all, preferred_element_type=f32)
        grad_attended = jnp.einsum(
            "td,ed->te", branch_all, w_out[layer], preferred_element_type=f32
        ).astype(bf16)
        split = qkv.reshape(3, seqs, LENGTH, heads_here, HEAD_DIM)
        grad_split = grad_attended.reshape(seqs, LENGTH, heads_here, HEAD_DIM)
        grads_seq = lax.map(
            lambda item: attend_backward(item[0], item[1], item[2], item[3], item[4]),
            (split[0], split[1], split[2], grad_split, logsum),
        )
        grad_rows = jnp.moveaxis(grads_seq, 1, 0).reshape(3, group_rows, local_width)
        grad_qkvw = jnp.einsum("td,cte->cde", rows_all, grad_rows, preferred_element_type=f32)

        def back_qkv(start, count, grad_rows=grad_rows, layer=layer):
            return jnp.einsum("cte,cde->td", grad_rows, w_qkv[layer], preferred_element_type=f32)

        grad_normed = lax.psum_scatter(
            back_qkv(jnp.int32(0), lax.axis_size(TP) * rows).astype(jnp.bfloat16),
            TP,
            scatter_dimension=0,
            tiled=True,
        ).astype(jnp.float32)
        _, pull_zero = jax.vjp(norm_rows, stream_in, gains[layer, 0], shifts[layer, 0])
        grad_in_part, gain_zero, shift_zero = pull_zero(grad_normed)
        grad_stream = grad_middle + grad_in_part
        gain_grads[layer] = jnp.stack([gain_zero, gain_one, gain_two, gain_three])
        shift_grads[layer] = jnp.stack([shift_zero, shift_one, shift_two, shift_three])
        weight_grads[layer] = tuple(sum_weight(value) for value in (grad_qkvw, grad_outw, grad_upw, grad_downw))
    stacked = [
        jnp.stack([weight_grads[index][member] for index in range(layers)]) for member in range(4)
    ]
    norm_sums = lax.psum((jnp.stack(gain_grads), jnp.stack(shift_grads)), AXES)
    return (
        swap_rows(stream.astype(bf16)).astype(f32),
        swap_rows(grad_stream.astype(bf16)).astype(f32),
        stacked[0],
        stacked[1],
        stacked[2],
        stacked[3],
        norm_sums[0],
        norm_sums[1],
    )


def solution(mesh):
    fine = jax.sharding.Mesh(mesh.devices.reshape(-1, 2, 2, 2, 2, 2), AXES)
    dp = ("gh", "gl", "p", "c")
    tensor = ("zh", "zl")
    rows = P((*dp, *tensor), None)
    weights = (
        P(None, None, None, tensor),
        P(None, tensor, None),
        P(None, None, tensor),
        P(None, tensor, None),
    )
    return jax.shard_map(
        per_device,
        mesh=fine,
        in_specs=(rows, rows, P(dp), P(), *weights, P(), P()),
        out_specs=(rows, rows, *weights, P(), P()),
        check_vma=False,
    )
```

```python
import functools

import jax
import jax.numpy as jnp
from jax import lax
from jax.experimental import pallas as pl
from jax.experimental.pallas import tpu as pltpu
from jax.sharding import PartitionSpec as P

HEAD_DIM = 64
LENGTH = 1088
AXES = ("gh", "gl", "p", "c", "zh", "zl")
f32 = jnp.float32
bf16 = jnp.bfloat16
MESH = pl.DeviceIdType.MESH
eps_norm = 1e-05
TILE = 256


def centre(values):
    mean = jnp.mean(values, axis=-1, keepdims=True)
    centred = values - mean
    spread = jnp.mean(centred * centred, axis=-1, keepdims=True)
    rate = lax.rsqrt(spread + eps_norm)
    return centred * rate, rate


def norm_rows(values, gain, shift):
    return centre(values)[0] * gain + shift


def norm_pull(values, gain, grad):
    hat, rate = centre(values)
    scaled = grad * gain
    along = jnp.mean(scaled * hat, axis=-1, keepdims=True)
    level = jnp.mean(scaled, axis=-1, keepdims=True)
    return (
        rate * (scaled - level - hat * along),
        jnp.sum(grad * hat, axis=0, keepdims=True),
        jnp.sum(grad, axis=0, keepdims=True),
    )


def dot_nt(left, right):
    return lax.dot_general(left, right, (((1,), (1,)), ((), ())), preferred_element_type=f32)


def dot_tn(left, right):
    return lax.dot_general(left, right, (((0,), (0,)), ((), ())), preferred_element_type=f32)


def dot_nn(left, right):
    return jnp.dot(left, right, preferred_element_type=f32)


def cut_rows(rows):
    first = (rows // 2 + 15) // 16 * 16
    return ((0, first), (first, rows - first))


def greet():
    mate = {"c": 1 - lax.axis_index("c")}
    near = {"zl": 1 - lax.axis_index("zl")}
    barrier = pltpu.get_barrier_semaphore()
    for other in (mate, near):
        pl.semaphore_signal(barrier, inc=1, device_id=other, device_id_type=MESH)
    pl.semaphore_wait(barrier, 2)
    return mate, near


def remote(source, target, send, receive, device):
    return pltpu.make_async_remote_copy(
        src_ref=source,
        dst_ref=target,
        send_sem=send,
        recv_sem=receive,
        device_id=device,
        device_id_type=MESH,
    )


def tiles(width, body):
    def step(index, carry):
        body(pl.ds(pl.multiple_of(index * TILE, TILE), TILE))
        return carry

    lax.fori_loop(0, width // TILE, step, 0)


def exchange(rows, mate, near, held, work, first, sums, send, receive):
    own = pl.ds(0, rows)
    parts = cut_rows(rows)
    copies = [remote(held.at[own], held.at[pl.ds(rows, rows)], send.at[0], receive.at[0], mate)]
    copies[0].start()
    along = []
    for index, (start, size) in enumerate(parts):
        place = pl.ds(2 * rows + 2 * start, size)
        copy = remote(held.at[pl.ds(start, size)], held.at[place], send.at[1 + index], receive.at[1 + index], near)
        copy.start()
        along.append(copy)

    def keep(row, columns, value):
        first[pl.ds(row, value.shape[0]), columns] = value

    work(0, rows, keep)
    copies[0].wait_recv()

    def keep_mate(row, columns, value):
        sums[0, pl.ds(row - rows, value.shape[0]), columns] = value.astype(bf16)

    work(rows, rows, keep_mate)
    back = remote(sums.at[0], sums.at[1], send.at[3], receive.at[3], mate)
    back.start()
    copies.append(back)
    final = []
    for index, (start, size) in enumerate(parts):
        place = 2 * rows + 2 * start
        along[index].wait_recv()
        relay = remote(
            held.at[pl.ds(place, size)], held.at[pl.ds(place + size, size)], send.at[4 + index], receive.at[4 + index], mate
        )
        relay.start()
        relay.wait_recv()

        def keep_far(row, columns, value, place=place, start=start, size=size):
            first[pl.ds(rows + start, size), columns] = value[:size]
            sums[2, pl.ds(start, size), columns] = value[size:].astype(bf16)

        work(place, 2 * size, keep_far)
        part = pl.ds(start, size)
        cross = remote(sums.at[2, part], sums.at[3, part], send.at[6 + index], receive.at[6 + index], mate)
        cross.start()
        cross.wait_recv()
        sums[4, part, :] = (first[pl.ds(rows + start, size), :] + sums[3, part, :].astype(f32)).astype(bf16)
        last = remote(sums.at[4, part], sums.at[5, part], send.at[8 + index], receive.at[8 + index], near)
        last.start()
        final.append(last)
        copies += [relay, cross]

    def finish():
        back.wait_recv()
        for copy in final:
            copy.wait_recv()
        for copy in copies + along + final:
            copy.wait_send()

    return finish


def gelu_and_slope(values):
    rate, cubic = 0.7978845608028654, 0.044715
    square = values * values
    bend = jnp.tanh(rate * values * (1.0 + cubic * square))
    half = 0.5 * (1.0 + bend)
    slope = half + 0.5 * values * (1.0 - bend * bend) * (rate * (1.0 + 3.0 * cubic * square))
    return values * half, slope


def ffn_forward_kernel(
    layer, middle, gains, shifts, w_up, w_down, second, stream, held_out, active_out, slope_out,
    held, active, slope, up, down, first, sums, send, receive, local,
):
    rows = middle.shape[0]
    loads = [pltpu.make_async_copy(w_up, up, local.at[0]), pltpu.make_async_copy(w_down, down, local.at[1])]
    for copy in loads:
        copy.start()
    mate, near = greet()
    held[pl.ds(0, rows), :] = norm_rows(middle[...], gains[2:3, :], shifts[2:3, :]).astype(bf16)
    for copy in loads:
        copy.wait()

    def work(start, size, sink):
        here = pl.ds(start, size)

        def step(columns):
            upper = dot_nn(held[here, :], up[:, columns])
            value, bend = gelu_and_slope(upper)
            active[here, columns] = value.astype(bf16)
            slope[here, columns] = bend.astype(bf16)

        tiles(up.shape[1], step)

        def step_down(columns):
            sink(start, columns, dot_nn(active[here, :], down[:, columns]))

        tiles(down.shape[1], step_down)

    finish = exchange(rows, mate, near, held, work, first, sums, send, receive)
    stores = [
        pltpu.make_async_copy(held, held_out, local.at[2]),
        pltpu.make_async_copy(active, active_out, local.at[3]),
        pltpu.make_async_copy(slope, slope_out, local.at[4]),
    ]
    for copy in stores:
        copy.start()
    finish()
    total = first[pl.ds(0, rows), :] + sums[1].astype(f32) + sums[5].astype(f32)
    second[...] = total
    stream[...] = middle[...] + norm_rows(total, gains[3:4, :], shifts[3:4, :])
    for copy in stores:
        copy.wait()


def vmem(count):
    return [pl.BlockSpec(memory_space=pltpu.VMEM)] * count


def anywhere(count):
    return [pl.BlockSpec(memory_space=pl.ANY)] * count


def sums_scratch(rows, width):
    return [
        pltpu.VMEM((2 * rows, width), f32),
        pltpu.VMEM((6, rows, width), bf16),
        pltpu.SemaphoreType.DMA((10,)),
        pltpu.SemaphoreType.DMA((10,)),
    ]


def ffn_forward(middle, gains, shifts, w_up, w_down):
    rows, width = middle.shape
    hidden = w_up.shape[1]
    shape = jax.ShapeDtypeStruct
    return pl.pallas_call(
        functools.partial(ffn_forward_kernel, 0),
        out_shape=(
            shape((rows, width), f32),
            shape((rows, width), f32),
            shape((4 * rows, width), bf16),
            shape((4 * rows, hidden), bf16),
            shape((4 * rows, hidden), bf16),
        ),
        in_specs=vmem(3) + anywhere(2),
        out_specs=vmem(2) + anywhere(3),
        scratch_shapes=[
            pltpu.VMEM((4 * rows, width), bf16),
            pltpu.VMEM((4 * rows, hidden), bf16),
            pltpu.VMEM((4 * rows, hidden), bf16),
            pltpu.VMEM(w_up.shape, bf16),
            pltpu.VMEM(w_down.shape, bf16),
            *sums_scratch(rows, width),
            pltpu.SemaphoreType.DMA((5,)),
        ],
        compiler_params=pltpu.CompilerParams(collective_id=0, has_side_effects=True, vmem_limit_bytes=56 << 20),
        cost_estimate=pl.CostEstimate(flops=16 * rows * width * hidden, bytes_accessed=24 << 20, transcendentals=4 * rows * hidden),
    )(middle, gains, shifts, w_up, w_down)


def ffn_backward_kernel(
    layer, grad, second, middle, gains, shifts, held_in, active_in, slope_in, w_up, w_down,
    grad_middle, sums_out, grad_up, grad_down,
    held, past, active, slope, pushed, up, down, outcome, first, sums, send, receive, local,
):
    rows = middle.shape[0]
    loads = [
        pltpu.make_async_copy(w_down, down, local.at[0]),
        pltpu.make_async_copy(w_up, up, local.at[1]),
        pltpu.make_async_copy(slope_in, slope, local.at[2]),
        pltpu.make_async_copy(active_in, active, local.at[3]),
        pltpu.make_async_copy(held_in, past, local.at[4]),
    ]
    for copy in loads:
        copy.start()
    mate, near = greet()
    pulled, gain_three, shift_three = norm_pull(second[...], gains[3:4, :], grad[...])
    held[pl.ds(0, rows), :] = pulled.astype(bf16)
    for copy in loads:
        copy.wait()

    def work(start, size, sink):
        here = pl.ds(start, size)

        def step(columns):
            value = dot_nt(held[here, :], down[columns, :])
            pushed[here, columns] = (value * slope[here, columns].astype(f32)).astype(bf16)

        tiles(down.shape[0], step)

        def step_up(columns):
            sink(start, columns, dot_nt(pushed[here, :], up[columns, :]))

        tiles(up.shape[0], step_up)

    finish = exchange(rows, mate, near, held, work, first, sums, send, receive)

    def step_down(columns):
        outcome[0, columns, :] = dot_tn(active[:, columns], held[...]).astype(bf16)

    tiles(down.shape[0], step_down)
    out_down = pltpu.make_async_copy(outcome.at[0], grad_down, local.at[0])
    out_down.start()

    def step_up(columns):
        outcome[1, columns, :] = dot_tn(past[:, columns], pushed[...]).astype(bf16)

    tiles(up.shape[0], step_up)
    out_up = pltpu.make_async_copy(outcome.at[1], grad_up, local.at[1])
    out_up.start()
    finish()
    total = first[pl.ds(0, rows), :] + sums[1].astype(f32) + sums[5].astype(f32)
    pulled, gain_two, shift_two = norm_pull(middle[...], gains[2:3, :], total)
    grad_middle[...] = grad[...] + pulled
    sums_out[0:1, :] = gain_two
    sums_out[1:2, :] = shift_two
    sums_out[2:3, :] = gain_three
    sums_out[3:4, :] = shift_three
    out_down.wait()
    out_up.wait()


def ffn_backward(grad, second, middle, gains, shifts, held, active, slope, w_up, w_down):
    rows, width = middle.shape
    hidden = w_up.shape[1]
    shape = jax.ShapeDtypeStruct
    return pl.pallas_call(
        functools.partial(ffn_backward_kernel, 0),
        out_shape=(
            shape((rows, width), f32),
            shape((4, width), f32),
            shape(w_up.shape, bf16),
            shape(w_down.shape, bf16),
        ),
        in_specs=vmem(5) + anywhere(5),
        out_specs=vmem(2) + anywhere(2),
        scratch_shapes=[
            pltpu.VMEM((4 * rows, width), bf16),
            pltpu.VMEM((4 * rows, width), bf16),
            pltpu.VMEM((4 * rows, hidden), bf16),
            pltpu.VMEM((4 * rows, hidden), bf16),
            pltpu.VMEM((4 * rows, hidden), bf16),
            pltpu.VMEM(w_up.shape, bf16),
            pltpu.VMEM(w_down.shape, bf16),
            pltpu.VMEM((2, width, hidden), bf16),
            *sums_scratch(rows, width),
            pltpu.SemaphoreType.DMA((5,)),
        ],
        compiler_params=pltpu.CompilerParams(collective_id=1, has_side_effects=True, vmem_limit_bytes=56 << 20),
        cost_estimate=pl.CostEstimate(flops=32 * rows * width * hidden, bytes_accessed=32 << 20, transcendentals=0),
    )(grad, second, middle, gains, shifts, held, active, slope, w_up, w_down)


def places(rows):
    c, zl = lax.axis_index("c"), lax.axis_index("zl")

    def at(core, part):
        return pl.multiple_of((2 * core + part) * rows, 16)

    return at(c, zl), at(1 - c, zl), at(c, 1 - zl), at(1 - c, 1 - zl)


def gather(rows, mate, near, held, arrived, send, receive):
    own, others, along, across = places(rows)
    parts = cut_rows(rows)
    here = pl.ds(own, rows)
    copies = [remote(held.at[here], held.at[here], send.at[0], receive.at[0], mate)]
    copies[0].start()
    for index, (start, size) in enumerate(parts):
        part = pl.ds(pl.multiple_of(own + start, 16), size)
        copy = remote(held.at[part], held.at[part], send.at[1 + index], receive.at[1 + index], near)
        copy.start()
        copies.append(copy)
    arrived(own, rows)
    copies[0].wait_recv()
    arrived(others, rows)
    for index, (start, size) in enumerate(parts):
        copies[1 + index].wait_recv()
        first = pl.multiple_of(along + start, 16)
        part = pl.ds(first, size)
        relay = remote(held.at[part], held.at[part], send.at[4 + index], receive.at[4 + index], mate)
        relay.start()
        copies.append(relay)
        arrived(first, size)
        relay.wait_recv()
        arrived(pl.multiple_of(across + start, 16), size)

    def finish():
        for copy in copies:
            copy.wait_send()

    return finish


def scatter(rows, mate, near, project, first, sums, send, receive):
    own, others, along, across = places(rows)
    parts = cut_rows(rows)
    copies, crossing, final = [], [], []
    for index, (start, size) in enumerate(parts):
        part = pl.ds(start, size)

        def keep_far(columns, value, part=part):
            sums[2, part, columns] = value.astype(bf16)

        project(pl.multiple_of(across + start, 16), size, keep_far)
        cross = remote(sums.at[2, part], sums.at[3, part], send.at[6 + index], receive.at[6 + index], mate)
        cross.start()
        crossing.append(cross)
    for index, (start, size) in enumerate(parts):
        part = pl.ds(start, size)

        def keep_near(columns, value, start=start, size=size):
            first[pl.ds(rows + start, size), columns] = value

        project(pl.multiple_of(along + start, 16), size, keep_near)
        crossing[index].wait_recv()
        sums[4, part, :] = (first[pl.ds(rows + start, size), :] + sums[3, part, :].astype(f32)).astype(bf16)
        last = remote(sums.at[4, part], sums.at[5, part], send.at[8 + index], receive.at[8 + index], near)
        last.start()
        final.append(last)

    def keep_mate(columns, value):
        sums[0, :, columns] = value.astype(bf16)

    project(others, rows, keep_mate)
    back = remote(sums.at[0], sums.at[1], send.at[3], receive.at[3], mate)
    back.start()

    def keep(columns, value):
        first[pl.ds(0, rows), columns] = value

    project(own, rows, keep)

    def finish():
        back.wait_recv()
        for copy in final:
            copy.wait_recv()
        for copy in [back] + crossing + final:
            copy.wait_send()

    return finish


def head_lanes(shape, half):
    lane = lax.broadcasted_iota(jnp.int32, shape, len(shape) - 1)
    return (lane < HEAD_DIM) if half == 0 else (lane >= HEAD_DIM)


def masked(scores, start, first_key):
    query = lax.broadcasted_iota(jnp.int32, scores.shape, 0) + start
    key = lax.broadcasted_iota(jnp.int32, scores.shape, 1) + first_key
    return jnp.where(key <= query, scores, -1e30)


def spans(rows, high):
    if not high:
        return ((0, 2 * rows, True),)
    free = 2 * rows // 128 * 128
    return ((0, free, False), (free, 4 * rows - free, True))


def attend_block(rows, start, high, qkv, attended, lse):
    width = attended.shape[1]
    here = pl.ds(start, rows)
    lane = lax.broadcasted_iota(jnp.int32, (rows, 128), 1)
    tops = jnp.zeros((rows, 128), f32)
    for pair in range(width // 128):
        columns = slice(pair * 128, pair * 128 + 128)
        query = qkv[here, columns] * bf16(HEAD_DIM ** (-0.5))
        results = []
        for half in range(2):
            only = jnp.where(head_lanes(query.shape, half), query, 0)
            scores = []
            for begin, size, mask in spans(rows, high):
                part = dot_nt(only, qkv[pl.ds(begin, size), width + pair * 128 : width + pair * 128 + 128])
                scores.append(masked(part, start, begin) if mask else part)
            top = functools.reduce(jnp.maximum, [jnp.max(part, axis=-1, keepdims=True) for part in scores])
            total, result = 0.0, 0.0
            for (begin, size, _), part in zip(spans(rows, high), scores):
                weights = jnp.exp(part - top)
                total = total + jnp.sum(weights, axis=-1, keepdims=True)
                values = qkv[pl.ds(begin, size), 2 * width + pair * 128 : 2 * width + pair * 128 + 128]
                result = result + dot_nn(weights.astype(bf16), values)
            results.append(result / total)
            tops = jnp.where(lane == 2 * pair + half, top + jnp.log(total), tops)
        attended[here, columns] = jnp.where(head_lanes((rows, 128), 0), results[0], results[1]).astype(bf16)
    lse[here, :] = tops


def attention_forward_kernel(
    layer, stream, gains, shifts, w_qkv, w_out, branch, middle, held_out, qkv_out, attended_out, lse_out,
    held, qkv, attended, lse, weight, project, first, sums, send, receive, local,
):
    rows = stream.shape[0]
    width = attended.shape[1]
    loads = [
        pltpu.make_async_copy(w_qkv.at[index], weight.at[:, pl.ds(index * width, width)], local.at[index]) for index in range(3)
    ]
    loads.append(pltpu.make_async_copy(w_out, project, local.at[3]))
    for copy in loads:
        copy.start()
    mate, near = greet()
    own, others, along, across = places(rows)
    held[pl.ds(own, rows), :] = norm_rows(stream[...], gains[0:1, :], shifts[0:1, :]).astype(bf16)
    for copy in loads:
        copy.wait()

    def arrived(start, size):
        here = pl.ds(start, size)

        def step(columns):
            qkv[here, columns] = dot_nn(held[here, :], weight[:, columns]).astype(bf16)

        tiles(3 * width, step)

    sent = gather(rows, mate, near, held, arrived, send, receive)
    stores = [pltpu.make_async_copy(held, held_out, local.at[0]), pltpu.make_async_copy(qkv, qkv_out, local.at[1])]
    for copy in stores:
        copy.start()
    zl = lax.axis_index("zl")

    def at(quarter):
        return pl.multiple_of(quarter * rows, 16)

    attend_block(rows, at(3 - zl), True, qkv, attended, lse)
    attend_block(rows, at(1 - zl), False, qkv, attended, lse)
    done = []

    def term(start, size, sink):
        if size == rows and not done:
            done.append(True)
            attend_block(rows, at(2 + zl), True, qkv, attended, lse)
            attend_block(rows, at(zl), False, qkv, attended, lse)
        here = pl.ds(start, size)

        def step(columns):
            sink(columns, dot_nn(attended[here, :], project[:, columns]))

        tiles(project.shape[1], step)

    finish = scatter(rows, mate, near, term, first, sums, send, receive)
    late = [pltpu.make_async_copy(attended, attended_out, local.at[2]), pltpu.make_async_copy(lse, lse_out, local.at[3])]
    for copy in late:
        copy.start()
    finish()
    total = first[pl.ds(0, rows), :] + sums[1].astype(f32) + sums[5].astype(f32)
    branch[...] = total
    middle[...] = stream[...] + norm_rows(total, gains[1:2, :], shifts[1:2, :])
    sent()
    for copy in stores + late:
        copy.wait()


def attention_forward(stream, gains, shifts, w_qkv, w_out):
    rows, model = stream.shape
    width = w_out.shape[0]
    shape = jax.ShapeDtypeStruct
    return pl.pallas_call(
        functools.partial(attention_forward_kernel, 0),
        out_shape=(
            shape((rows, model), f32),
            shape((rows, model), f32),
            shape((4 * rows, model), bf16),
            shape((4 * rows, 3 * width), bf16),
            shape((4 * rows, width), bf16),
            shape((4 * rows, 128), f32),
        ),
        in_specs=vmem(3) + anywhere(2),
        out_specs=vmem(2) + anywhere(4),
        scratch_shapes=[
            pltpu.VMEM((4 * rows, model), bf16),
            pltpu.VMEM((4 * rows, 3 * width), bf16),
            pltpu.VMEM((4 * rows, width), bf16),
            pltpu.VMEM((4 * rows, 128), f32),
            pltpu.VMEM((model, 3 * width), bf16),
            pltpu.VMEM(w_out.shape, bf16),
            *sums_scratch(rows, model),
            pltpu.SemaphoreType.DMA((4,)),
        ],
        compiler_params=pltpu.CompilerParams(collective_id=2, has_side_effects=True, vmem_limit_bytes=56 << 20),
        cost_estimate=pl.CostEstimate(flops=24 * rows * model * width, bytes_accessed=16 << 20, transcendentals=16 * rows * rows * 4),
    )(stream, gains, shifts, w_qkv, w_out)


def attend_block_back(rows, start, high, qkv, attended_grad, lse, inner, grad_query, grad_key, grad_value):
    width = attended_grad.shape[1]
    here = pl.ds(start, rows)
    scale = HEAD_DIM ** (-0.5)
    for pair in range(width // 128):
        columns = slice(pair * 128, pair * 128 + 128)
        query = qkv[here, columns] * bf16(scale)
        above = attended_grad[here, columns]
        result = 0.0
        for half in range(2):
            head = 2 * pair + half
            only = jnp.where(head_lanes(query.shape, half), query, 0)
            grad = jnp.where(head_lanes(query.shape, half), above, 0)
            for begin, size, mask in spans(rows, high):
                keys = pl.ds(begin, size)
                key = qkv[keys, width + pair * 128 : width + pair * 128 + 128]
                value = qkv[keys, 2 * width + pair * 128 : 2 * width + pair * 128 + 128]
                scores = dot_nt(only, key)
                if mask:
                    scores = masked(scores, start, begin)
                probs = jnp.exp(scores - lse[here, head : head + 1])
                grad_probs = dot_nt(grad, value)
                grad_scores = (probs * (grad_probs - inner[here, head : head + 1])).astype(bf16)
                key_only = jnp.where(head_lanes(key.shape, half), key, 0)
                result = result + dot_nn(grad_scores, key_only)
                grad_key[keys, columns] += dot_tn(grad_scores, only)
                grad_value[keys, columns] += dot_tn(probs.astype(bf16), grad)
        grad_query[here, columns] = (result * scale).astype(bf16)


def attention_backward_kernel(
    layer, grad, branch, stream, gains, shifts, held_in, qkv_in, attended_in, lse_in, w_qkv, w_out,
    grad_stream, sums_out, grad_qkv, grad_out,
    held, past, qkv, attended, lse, inner, above, pushed, grad_key, grad_value, weight, project, outcome, outcome_out,
    first, sums, send, receive, local,
):
    rows = stream.shape[0]
    width = attended.shape[1]
    model = stream.shape[1]
    loads = [
        pltpu.make_async_copy(w_out, project, local.at[3]),
        pltpu.make_async_copy(attended_in, attended, local.at[4]),
        pltpu.make_async_copy(qkv_in, qkv, local.at[5]),
        pltpu.make_async_copy(lse_in, lse, local.at[6]),
        *[pltpu.make_async_copy(w_qkv.at[index], weight.at[:, pl.ds(index * width, width)], local.at[index]) for index in range(3)],
        pltpu.make_async_copy(held_in, past, local.at[7]),
    ]
    for copy in loads:
        copy.start()
    mate, near = greet()
    own, others, along, across = places(rows)
    pulled, gain_one, shift_one = norm_pull(branch[...], gains[1:2, :], grad[...])
    held[pl.ds(own, rows), :] = pulled.astype(bf16)
    grad_key[...] = jnp.zeros_like(grad_key)
    grad_value[...] = jnp.zeros_like(grad_value)
    for copy in loads:
        copy.wait()
    zl = lax.axis_index("zl")

    def at(quarter):
        return pl.multiple_of(quarter * rows, 16)

    blocks = []

    def arrived(start, size):
        here = pl.ds(start, size)
        value = dot_nt(held[here, :], project[...]).astype(bf16)
        above[here, :] = value
        product = value.astype(f32) * attended[here, :].astype(f32)
        lane = lax.broadcasted_iota(jnp.int32, (size, 128), 1)
        tile = jnp.zeros((size, 128), f32)
        for pair in range(width // 128):
            part = product[:, pair * 128 : pair * 128 + 128]
            for half in range(2):
                one = jnp.sum(jnp.where(head_lanes(part.shape, half), part, 0.0), axis=-1, keepdims=True)
                tile = jnp.where(lane == 2 * pair + half, one, tile)
        inner[here, :] = tile
        blocks.append(size)
        if len(blocks) == 2:
            back(2 + zl, True)
            back(zl, False)

    def back(quarter, high):
        attend_block_back(rows, at(quarter), high, qkv, above, lse, inner, pushed, grad_key, grad_value)

    sent = gather(rows, mate, near, held, arrived, send, receive)
    back(3 - zl, True)
    back(1 - zl, False)
    pushed[:, pl.ds(width, width)] = grad_key[...].astype(bf16)
    pushed[:, pl.ds(2 * width, width)] = grad_value[...].astype(bf16)

    def term(start, size, sink):
        here = pl.ds(start, size)

        def step(columns):
            sink(columns, dot_nt(pushed[here, :], weight[columns, :]))

        tiles(model, step)

    finish = scatter(rows, mate, near, term, first, sums, send, receive)

    def step_out(columns):
        outcome_out[:, columns] = dot_tn(attended[...], held[:, columns]).astype(bf16)

    tiles(model, step_out)
    out = pltpu.make_async_copy(outcome_out, grad_out, local.at[0])
    out.start()

    def step_qkv(columns):
        outcome[columns, :] = dot_tn(past[:, columns], pushed[...]).astype(bf16)

    tiles(model, step_qkv)
    outs = [out]
    for index in range(3):
        copy = pltpu.make_async_copy(outcome.at[:, pl.ds(index * width, width)], grad_qkv.at[index], local.at[1 + index])
        copy.start()
        outs.append(copy)
    finish()
    total = first[pl.ds(0, rows), :] + sums[1].astype(f32) + sums[5].astype(f32)
    pulled, gain_zero, shift_zero = norm_pull(stream[...], gains[0:1, :], total)
    grad_stream[...] = grad[...] + pulled
    sums_out[0:1, :] = gain_zero
    sums_out[1:2, :] = shift_zero
    sums_out[2:3, :] = gain_one
    sums_out[3:4, :] = shift_one
    sent()
    for copy in outs:
        copy.wait()


def attention_backward(grad, branch, stream, gains, shifts, held, qkv, attended, lse, w_qkv, w_out):
    rows, model = stream.shape
    width = w_out.shape[0]
    shape = jax.ShapeDtypeStruct
    return pl.pallas_call(
        functools.partial(attention_backward_kernel, 0),
        out_shape=(
            shape((rows, model), f32),
            shape((4, model), f32),
            shape(w_qkv.shape, bf16),
            shape(w_out.shape, bf16),
        ),
        in_specs=vmem(5) + anywhere(6),
        out_specs=vmem(2) + anywhere(2),
        scratch_shapes=[
            pltpu.VMEM((4 * rows, model), bf16),
            pltpu.VMEM((4 * rows, model), bf16),
            pltpu.VMEM((4 * rows, 3 * width), bf16),
            pltpu.VMEM((4 * rows, width), bf16),
            pltpu.VMEM((4 * rows, 128), f32),
            pltpu.VMEM((4 * rows, 128), f32),
            pltpu.VMEM((4 * rows, width), bf16),
            pltpu.VMEM((4 * rows, 3 * width), bf16),
            pltpu.VMEM((4 * rows, width), f32),
            pltpu.VMEM((4 * rows, width), f32),
            pltpu.VMEM((model, 3 * width), bf16),
            pltpu.VMEM(w_out.shape, bf16),
            pltpu.VMEM((model, 3 * width), bf16),
            pltpu.VMEM(w_out.shape, bf16),
            *sums_scratch(rows, model),
            pltpu.SemaphoreType.DMA((8,)),
        ],
        compiler_params=pltpu.CompilerParams(collective_id=3, has_side_effects=True, vmem_limit_bytes=56 << 20),
        cost_estimate=pl.CostEstimate(flops=60 * rows * model * width, bytes_accessed=24 << 20, transcendentals=16 * rows * rows * 4),
    )(grad, branch, stream, gains, shifts, held, qkv, attended, lse, w_qkv, w_out)


TP = ("c", "zl")
SHARE = ("gl", "p")
BATCH = ("gh", "gl", "p")


def swap_rows(values):
    return lax.ppermute(values, ("c", "zh"), ((0, 0), (1, 2), (2, 1), (3, 3)))


def keeps():
    return lax.axis_index("c") == lax.axis_index("zh")


def fetch_weight(weight):
    shape = weight.shape
    flat = weight.reshape(4, -1, 1024)
    part = lax.dynamic_index_in_dim(flat, lax.axis_index(SHARE), 0, keepdims=False)
    part = lax.ppermute(part, ("c", "zh"), ((0, 1), (3, 2)))
    rest = lax.all_gather(part, SHARE, axis=0, tiled=True).reshape(shape)
    return jnp.where(keeps(), weight, rest)


def sum_weight(grad):
    shape = grad.shape
    flat = grad.astype(jnp.bfloat16).reshape(-1, 1024)
    part = lax.psum_scatter(flat, BATCH, scatter_dimension=0, tiled=True)
    other = lax.ppermute(part, ("c", "zh"), ((1, 0), (2, 3)))
    part = (part.astype(jnp.float32) + other.astype(jnp.float32)).astype(jnp.bfloat16)
    mate = lax.ppermute(part, "c", ((0, 1), (1, 0)))
    part = jnp.where(keeps(), part, mate)
    return lax.all_gather(part, BATCH, axis=0, tiled=True).reshape(shape).astype(jnp.float32)


def per_device(hidden_in, cotangent, group_ids, group_sizes, w_qkv, w_out, w_up, w_down, gains, shifts):
    layers = w_qkv.shape[0]
    hidden_in = swap_rows(hidden_in)
    cotangent = swap_rows(cotangent)
    weights = [[fetch_weight(value[layer]) for value in (w_qkv, w_out, w_up, w_down)] for layer in range(layers)]
    stream = hidden_in.astype(f32)
    saved = []
    for layer in range(layers):
        qkv, out, up, down = weights[layer]
        branch, middle, *kept = attention_forward(stream, gains[layer], shifts[layer], qkv, out)
        second, later, *kept_ffn = ffn_forward(middle, gains[layer], shifts[layer], up, down)
        saved.append((stream, branch, kept, middle, second, kept_ffn))
        stream = later
    ids = lax.all_gather(group_ids, "c", axis=0, tiled=True)
    mine = lax.dynamic_index_in_dim(ids, lax.axis_index("zh"), 0, keepdims=False)
    count = jnp.sum(jnp.where(jnp.arange(group_sizes.shape[0]) == mine, group_sizes, 0)).astype(f32)
    grad = cotangent.astype(f32) * (1.0 / count)
    weight_grads, norm_grads = [None] * layers, [None] * layers
    for layer in reversed(range(layers)):
        qkv, out, up, down = weights[layer]
        before, branch, kept, middle, second, kept_ffn = saved[layer]
        grad, sums_ffn, grad_up, grad_down = ffn_backward(
            grad, second, middle, gains[layer], shifts[layer], *kept_ffn, up, down
        )
        grad, sums_att, grad_qkv, grad_out = attention_backward(
            grad, branch, before, gains[layer], shifts[layer], *kept, qkv, out
        )
        weight_grads[layer] = [sum_weight(value) for value in (grad_qkv, grad_out, grad_up, grad_down)]
        norm_grads[layer] = jnp.concatenate([sums_att, sums_ffn])
    norm_sums = lax.psum(jnp.stack(norm_grads), AXES).reshape(layers, 4, 2, -1)
    return (
        swap_rows(stream.astype(bf16)).astype(f32),
        swap_rows(grad.astype(bf16)).astype(f32),
        *[jnp.stack([weight_grads[layer][member] for layer in range(layers)]) for member in range(4)],
        norm_sums[:, :, 0],
        norm_sums[:, :, 1],
    )


def solution(mesh):
    fine = jax.sharding.Mesh(mesh.devices.reshape(-1, 2, 2, 2, 2, 2), AXES)
    dp = ("gh", "gl", "p", "c")
    tensor = ("zh", "zl")
    rows = P((*dp, *tensor), None)
    weights = (
        P(None, None, None, tensor),
        P(None, tensor, None),
        P(None, None, tensor),
        P(None, tensor, None),
    )
    return jax.shard_map(
        per_device,
        mesh=fine,
        in_specs=(rows, rows, P(dp), P(), *weights, P(), P()),
        out_specs=(rows, rows, *weights, P(), P()),
        check_vma=False,
    )
```

```python
import functools
import types

import jax
import jax.numpy as jnp
from jax import lax
from jax.experimental import pallas as pl
from jax.experimental.pallas import tpu as pltpu
from jax.sharding import PartitionSpec as P

HEAD_DIM = 64
AXES = ("gh", "gl", "p", "c", "zh", "zl")
f32 = jnp.float32
bf16 = jnp.bfloat16
MESH = pl.DeviceIdType.MESH
VMEM, ANY = pltpu.VMEM, pl.ANY
eps_norm = 1e-05
TILE = 256


def centre(values):
    mean = jnp.mean(values, axis=-1, keepdims=True)
    centred = values - mean
    spread = jnp.mean(centred * centred, axis=-1, keepdims=True)
    rate = lax.rsqrt(spread + eps_norm)
    return centred * rate, rate


def norm_rows(values, gain, shift):
    return centre(values)[0] * gain + shift


def norm_pull(values, gain, grad):
    hat, rate = centre(values)
    scaled = grad * gain
    along = jnp.mean(scaled * hat, axis=-1, keepdims=True)
    level = jnp.mean(scaled, axis=-1, keepdims=True)
    return (
        rate * (scaled - level - hat * along),
        jnp.sum(grad * hat, axis=0, keepdims=True),
        jnp.sum(grad, axis=0, keepdims=True),
    )


def dot_nt(left, right):
    return lax.dot_general(left, right, (((1,), (1,)), ((), ())), preferred_element_type=f32)


def dot_tn(left, right):
    return lax.dot_general(left, right, (((0,), (0,)), ((), ())), preferred_element_type=f32)


def dot_nn(left, right):
    return jnp.dot(left, right, preferred_element_type=f32)


def cut_rows(rows):
    first = (rows // 2 + 15) // 16 * 16
    return ((0, first), (first, rows - first))


def flipped(*names):
    return {name: 1 - lax.axis_index(name) for name in names}


def greet(*others):
    barrier = pltpu.get_barrier_semaphore()
    for names in others:
        pl.semaphore_signal(barrier, inc=1, device_id=flipped(*names), device_id_type=MESH)
    pl.semaphore_wait(barrier, len(others))


GROUP = (("c",), ("zl",))
ACROSS = (("p",), ("gl",), ("gl", "p"))
FETCH = (("zh",), *ACROSS)


def remote(source, target, send, receive, device):
    return pltpu.make_async_remote_copy(
        src_ref=source,
        dst_ref=target,
        send_sem=send,
        recv_sem=receive,
        device_id=device,
        device_id_type=MESH,
    )


def tiles(width, body):
    def step(index, carry):
        body(pl.ds(pl.multiple_of(index * TILE, TILE), TILE))
        return carry

    lax.fori_loop(0, width // TILE, step, 0)


def exchange(rows, held, work, first, sums, send, receive):
    mate, near = flipped("c"), flipped("zl")
    own = pl.ds(0, rows)
    parts = cut_rows(rows)
    copies = [remote(held.at[own], held.at[pl.ds(rows, rows)], send.at[0], receive.at[0], mate)]
    copies[0].start()
    along = []
    for index, (start, size) in enumerate(parts):
        place = pl.ds(2 * rows + 2 * start, size)
        copy = remote(held.at[pl.ds(start, size)], held.at[place], send.at[1 + index], receive.at[1 + index], near)
        copy.start()
        along.append(copy)

    def keep(row, columns, value):
        first[pl.ds(row, value.shape[0]), columns] = value

    work(0, rows, keep)
    copies[0].wait_recv()

    def keep_mate(row, columns, value):
        sums[0, pl.ds(row - rows, value.shape[0]), columns] = value.astype(bf16)

    work(rows, rows, keep_mate)
    back = remote(sums.at[0], sums.at[1], send.at[3], receive.at[3], mate)
    back.start()
    copies.append(back)
    final = []
    for index, (start, size) in enumerate(parts):
        place = 2 * rows + 2 * start
        along[index].wait_recv()
        relay = remote(
            held.at[pl.ds(place, size)], held.at[pl.ds(place + size, size)], send.at[4 + index], receive.at[4 + index], mate
        )
        relay.start()
        relay.wait_recv()

        def keep_far(row, columns, value, place=place, start=start, size=size):
            first[pl.ds(rows + start, size), columns] = value[:size]
            sums[2, pl.ds(start, size), columns] = value[size:].astype(bf16)

        work(place, 2 * size, keep_far)
        part = pl.ds(start, size)
        cross = remote(sums.at[2, part], sums.at[3, part], send.at[6 + index], receive.at[6 + index], mate)
        cross.start()
        cross.wait_recv()
        sums[4, part, :] = (first[pl.ds(rows + start, size), :] + sums[3, part, :].astype(f32)).astype(bf16)
        last = remote(sums.at[4, part], sums.at[5, part], send.at[8 + index], receive.at[8 + index], near)
        last.start()
        final.append(last)
        copies += [relay, cross]

    def finish():
        back.wait_recv()
        for copy in final:
            copy.wait_recv()
        for copy in copies + along + final:
            copy.wait_send()

    return finish


def run(body, number, inputs, outputs, scratch, flops, transcendentals=0):
    names = [*inputs, *outputs, *scratch]

    def kernel(*refs):
        body(types.SimpleNamespace(**dict(zip(names, refs))))

    moved = sum(value.size * value.dtype.itemsize for value, _ in inputs.values())
    results = pl.pallas_call(
        kernel,
        out_shape=tuple(jax.ShapeDtypeStruct(shape, kind) for shape, kind, _ in outputs.values()),
        in_specs=[pl.BlockSpec(memory_space=memory) for _, memory in inputs.values()],
        out_specs=tuple(pl.BlockSpec(memory_space=memory) for _, _, memory in outputs.values()),
        scratch_shapes=list(scratch.values()),
        compiler_params=pltpu.CompilerParams(collective_id=number, has_side_effects=True, vmem_limit_bytes=58 << 20),
        cost_estimate=pl.CostEstimate(flops=flops, bytes_accessed=moved, transcendentals=transcendentals),
    )(*[value for value, _ in inputs.values()])
    return types.SimpleNamespace(**dict(zip(outputs, results)))


def semaphores(count):
    return pltpu.SemaphoreType.DMA((count,))


def group_scratch(rows, width):
    return {
        "first": VMEM((2 * rows, width), f32),
        "sums": VMEM((6, rows, width), bf16),
        "send": semaphores(10),
        "receive": semaphores(10),
    }


def pick(ref, rows):
    return ref.at[:, rows, :] if len(ref.shape) == 3 else ref.at[rows, :]


def part_shape(shape, parts):
    return (*shape[:-2], shape[-2] // parts, shape[-1])


def holds():
    return lax.axis_index("c") == lax.axis_index("zh")


class Fetching:
    copies = 4

    def __init__(self, source, target, send, receive, local):
        self.source, self.target, self.send, self.receive, self.local = source, target, send, receive, local
        self.size = source.shape[-2] // 4

    def rows_of(self, names=()):
        gl, p = [(1 - lax.axis_index(name)) if name in names else lax.axis_index(name) for name in ("gl", "p")]
        return pl.ds(pl.multiple_of((2 * gl + p) * self.size, 16), self.size)

    def along(self):
        rows = self.rows_of()
        return remote(
            pick(self.source, rows), pick(self.target, rows), self.send.at[0], self.receive.at[0], flipped("zh")
        )

    def share(self):
        rows = pick(self.target, self.rows_of())
        return [
            remote(rows, rows, self.send.at[1 + slot], self.receive.at[1 + slot], flipped(*names))
            for slot, names in enumerate(ACROSS)
        ]

    def step_along(self):
        @pl.when(holds())
        def _():
            self.along().start()
            pltpu.make_async_copy(self.source, self.target, self.local.at[0]).start()

    def step_share(self):
        @pl.when(jnp.logical_not(holds()))
        def _():
            self.along().wait_recv()
            for copy in self.share():
                copy.start()

    def step_end(self):
        @pl.when(holds())
        def _():
            self.along().wait_send()
            pltpu.make_async_copy(self.source, self.target, self.local.at[0]).wait()

        @pl.when(jnp.logical_not(holds()))
        def _():
            for copy in self.share():
                copy.wait()


def fetch_jobs(refs, names, layer):
    return [
        Fetching(
            getattr(refs, name + "_from").at[layer], getattr(refs, name + "_to"), getattr(refs, name + "_send"),
            getattr(refs, name + "_receive"), getattr(refs, name + "_local"),
        )
        for name in names
    ]


def fetch_inputs(weights):
    return {name + "_from": (value, ANY) for name, value in weights.items()}


def fetch_outputs(weights):
    return {name + "_to": (value.shape[1:], bf16, ANY) for name, value in weights.items()}


def fetch_scratch(weights):
    result = {}
    for name in weights:
        result[name + "_send"] = semaphores(4)
        result[name + "_receive"] = semaphores(4)
        result[name + "_local"] = semaphores(1)
    return result


def every(jobs, step):
    for job in jobs:
        getattr(job, step)()


def head(hidden_in, weight, weights):
    def body(r):
        greet(("c",), ("c", "zh"), *FETCH)
        jobs = fetch_jobs(r, weights, 0)
        jobs[0].step_along()
        swap = remote(r.hidden, r.landed, r.send.at[0], r.receive.at[0], flipped("c", "zh"))
        scale = remote(r.weight, r.other, r.send.at[1], r.receive.at[1], flipped("c"))
        scale.start()

        @pl.when(jnp.logical_not(holds()))
        def _():
            swap.start()

        every(jobs[1:], "step_along")
        every(jobs, "step_share")

        @pl.when(holds())
        def _():
            r.stream[...] = r.hidden[...].astype(f32)

        scale.wait()
        r.scale[...] = jnp.where(holds(), r.weight[...], r.other[...])

        @pl.when(jnp.logical_not(holds()))
        def _():
            swap.wait()
            r.stream[...] = r.landed[...].astype(f32)

        every(jobs, "step_end")

    return run(
        body,
        0,
        {"hidden": (hidden_in, VMEM), "weight": (weight, VMEM), **fetch_inputs(weights)},
        {"stream": (hidden_in.shape, f32, VMEM), "scale": (weight.shape, f32, VMEM), **fetch_outputs(weights)},
        {
            "landed": VMEM(hidden_in.shape, bf16),
            "other": VMEM(weight.shape, f32),
            "send": semaphores(2),
            "receive": semaphores(2),
            **fetch_scratch(weights),
        },
        1 << 20,
    )


def gelu_and_slope(values):
    rate, cubic = 0.7978845608028654, 0.044715
    square = values * values
    bend = jnp.tanh(rate * values * (1.0 + cubic * square))
    half = 0.5 * (1.0 + bend)
    slope = half + 0.5 * values * (1.0 - bend * bend) * (rate * (1.0 + 3.0 * cubic * square))
    return values * half, slope


def ffn_forward(layer, middle, gains, shifts, w_up, w_down, weights):
    rows, width = middle.shape
    hidden = w_up.shape[1]

    def body(r):
        loads = [pltpu.make_async_copy(r.w_up, r.up, r.local.at[0]), pltpu.make_async_copy(r.w_down, r.down, r.local.at[1])]
        for copy in loads:
            copy.start()
        greet(*GROUP, *(FETCH if weights else ()))
        jobs = fetch_jobs(r, weights, layer + 1)
        held, active, slope = r.held, r.active, r.slope
        held[pl.ds(0, rows), :] = norm_rows(r.middle[...], r.gains[layer, 2:3, :], r.shifts[layer, 2:3, :]).astype(bf16)
        for copy in loads:
            copy.wait()
        calls = []

        def work(start, size, sink):
            calls.append(start)
            if len(calls) == 1:
                every(jobs, "step_along")
            here = pl.ds(start, size)

            def step(columns):
                upper = dot_nn(held[here, :], r.up[:, columns])
                value, bend = gelu_and_slope(upper)
                active[here, columns] = value.astype(bf16)
                slope[here, columns] = bend.astype(bf16)

            tiles(hidden, step)

            def step_down(columns):
                sink(start, columns, dot_nn(active[here, :], r.down[:, columns]))

            tiles(width, step_down)

        finish = exchange(rows, held, work, r.first, r.sums, r.send, r.receive)
        stores = [
            pltpu.make_async_copy(held, r.held_out, r.local.at[2]),
            pltpu.make_async_copy(active, r.active_out, r.local.at[3]),
            pltpu.make_async_copy(slope, r.slope_out, r.local.at[4]),
        ]
        for copy in stores:
            copy.start()
        every(jobs, "step_share")
        finish()
        total = r.first[pl.ds(0, rows), :] + r.sums[1].astype(f32) + r.sums[5].astype(f32)
        r.second[...] = total
        r.stream[...] = r.middle[...] + norm_rows(total, r.gains[layer, 3:4, :], r.shifts[layer, 3:4, :])
        every(jobs, "step_end")
        for copy in stores:
            copy.wait()

    return run(
        body,
        3 + layer,
        {
            "middle": (middle, VMEM), "gains": (gains, VMEM), "shifts": (shifts, VMEM), "w_up": (w_up, ANY), "w_down": (w_down, ANY),
            **fetch_inputs(weights),
        },
        {
            "second": ((rows, width), f32, VMEM), "stream": ((rows, width), f32, VMEM),
            "held_out": ((4 * rows, width), bf16, ANY), "active_out": ((4 * rows, hidden), bf16, ANY),
            "slope_out": ((4 * rows, hidden), bf16, ANY), **fetch_outputs(weights),
        },
        {
            "held": VMEM((4 * rows, width), bf16), "active": VMEM((4 * rows, hidden), bf16), "slope": VMEM((4 * rows, hidden), bf16),
            "up": VMEM(w_up.shape, bf16), "down": VMEM(w_down.shape, bf16), **group_scratch(rows, width), "local": semaphores(5),
            **fetch_scratch(weights),
        },
        16 * rows * width * hidden,
        4 * rows * hidden,
    )


def ffn_backward(layer, grad, saved, gains, shifts, w_up, w_down):
    middle = saved.middle
    rows, width = middle.shape
    hidden = w_up.shape[1]

    def body(r):
        held, active, slope, pushed, past = r.held, r.active, r.slope, r.pushed, r.past
        loads = [
            pltpu.make_async_copy(r.w_down, r.down, r.local.at[0]),
            pltpu.make_async_copy(r.w_up, r.up, r.local.at[1]),
            pltpu.make_async_copy(r.slope_in, slope, r.local.at[2]),
            pltpu.make_async_copy(r.active_in, active, r.local.at[3]),
            pltpu.make_async_copy(r.held_in, past, r.local.at[4]),
        ]
        for copy in loads:
            copy.start()
        greet(*GROUP)
        pulled, gain_three, shift_three = norm_pull(r.second[...], r.gains[layer, 3:4, :], r.grad[...])
        held[pl.ds(0, rows), :] = pulled.astype(bf16)
        for copy in loads:
            copy.wait()

        def work(start, size, sink):
            here = pl.ds(start, size)

            def step(columns):
                value = dot_nt(held[here, :], r.down[columns, :])
                pushed[here, columns] = (value * slope[here, columns].astype(f32)).astype(bf16)

            tiles(hidden, step)

            def step_up(columns):
                sink(start, columns, dot_nt(pushed[here, :], r.up[columns, :]))

            tiles(width, step_up)

        finish = exchange(rows, held, work, r.first, r.sums, r.send, r.receive)

        def step_down(columns):
            r.outcome[0, columns, :] = dot_tn(active[:, columns], held[...]).astype(bf16)

        tiles(hidden, step_down)
        out_down = pltpu.make_async_copy(r.outcome.at[0], r.grad_down, r.local.at[0])
        out_down.start()

        def step_up(columns):
            r.outcome[1, columns, :] = dot_tn(past[:, columns], pushed[...]).astype(bf16)

        tiles(width, step_up)
        out_up = pltpu.make_async_copy(r.outcome.at[1], r.grad_up, r.local.at[1])
        out_up.start()
        finish()
        total = r.first[pl.ds(0, rows), :] + r.sums[1].astype(f32) + r.sums[5].astype(f32)
        pulled, gain_two, shift_two = norm_pull(r.middle[...], r.gains[layer, 2:3, :], total)
        r.grad_middle[...] = r.grad[...] + pulled
        for index, value in enumerate((gain_two, shift_two, gain_three, shift_three)):
            r.norms[index : index + 1, :] = value
        out_down.wait()
        out_up.wait()

    return run(
        body,
        5 + layer,
        {
            "grad": (grad, VMEM), "second": (saved.second, VMEM), "middle": (middle, VMEM), "gains": (gains, VMEM),
            "shifts": (shifts, VMEM), "held_in": (saved.held_out, ANY), "active_in": (saved.active_out, ANY),
            "slope_in": (saved.slope_out, ANY), "w_up": (w_up, ANY), "w_down": (w_down, ANY),
        },
        {
            "grad_middle": ((rows, width), f32, VMEM), "norms": ((4, width), f32, VMEM),
            "grad_up": (w_up.shape, bf16, ANY), "grad_down": (w_down.shape, bf16, ANY),
        },
        {
            "held": VMEM((4 * rows, width), bf16), "past": VMEM((4 * rows, width), bf16),
            "active": VMEM((4 * rows, hidden), bf16), "slope": VMEM((4 * rows, hidden), bf16),
            "pushed": VMEM((4 * rows, hidden), bf16), "up": VMEM(w_up.shape, bf16), "down": VMEM(w_down.shape, bf16),
            "outcome": VMEM((2, width, hidden), bf16), **group_scratch(rows, width), "local": semaphores(5),
        },
        32 * rows * width * hidden,
    )


def places(rows):
    c, zl = lax.axis_index("c"), lax.axis_index("zl")

    def at(core, part):
        return pl.multiple_of((2 * core + part) * rows, 16)

    return at(c, zl), at(1 - c, zl), at(c, 1 - zl), at(1 - c, 1 - zl)


def gather(rows, held, arrived, send, receive):
    mate, near = flipped("c"), flipped("zl")
    own, others, along, across = places(rows)
    parts = cut_rows(rows)
    here = pl.ds(own, rows)
    copies = [remote(held.at[here], held.at[here], send.at[0], receive.at[0], mate)]
    copies[0].start()
    for index, (start, size) in enumerate(parts):
        part = pl.ds(pl.multiple_of(own + start, 16), size)
        copy = remote(held.at[part], held.at[part], send.at[1 + index], receive.at[1 + index], near)
        copy.start()
        copies.append(copy)
    arrived(own, rows)
    copies[0].wait_recv()
    arrived(others, rows)
    for index, (start, size) in enumerate(parts):
        copies[1 + index].wait_recv()
        first = pl.multiple_of(along + start, 16)
        part = pl.ds(first, size)
        relay = remote(held.at[part], held.at[part], send.at[4 + index], receive.at[4 + index], mate)
        relay.start()
        copies.append(relay)
        arrived(first, size)
        relay.wait_recv()
        arrived(pl.multiple_of(across + start, 16), size)

    def finish():
        for copy in copies:
            copy.wait_send()

    return finish


def scatter(rows, project, first, sums, send, receive):
    mate, near = flipped("c"), flipped("zl")
    own, others, along, across = places(rows)
    parts = cut_rows(rows)
    copies, crossing, final = [], [], []
    for index, (start, size) in enumerate(parts):
        part = pl.ds(start, size)

        def keep_far(columns, value, part=part):
            sums[2, part, columns] = value.astype(bf16)

        project(pl.multiple_of(across + start, 16), size, keep_far)
        cross = remote(sums.at[2, part], sums.at[3, part], send.at[6 + index], receive.at[6 + index], mate)
        cross.start()
        crossing.append(cross)
    for index, (start, size) in enumerate(parts):
        part = pl.ds(start, size)

        def keep_near(columns, value, start=start, size=size):
            first[pl.ds(rows + start, size), columns] = value

        project(pl.multiple_of(along + start, 16), size, keep_near)
        crossing[index].wait_recv()
        sums[4, part, :] = (first[pl.ds(rows + start, size), :] + sums[3, part, :].astype(f32)).astype(bf16)
        last = remote(sums.at[4, part], sums.at[5, part], send.at[8 + index], receive.at[8 + index], near)
        last.start()
        final.append(last)

    def keep_mate(columns, value):
        sums[0, :, columns] = value.astype(bf16)

    project(others, rows, keep_mate)
    back = remote(sums.at[0], sums.at[1], send.at[3], receive.at[3], mate)
    back.start()

    def keep(columns, value):
        first[pl.ds(0, rows), columns] = value

    project(own, rows, keep)

    def finish():
        back.wait_recv()
        for copy in final:
            copy.wait_recv()
        for copy in [back] + crossing + final:
            copy.wait_send()

    return finish


def head_lanes(shape, half):
    lane = lax.broadcasted_iota(jnp.int32, shape, len(shape) - 1)
    return (lane < HEAD_DIM) if half == 0 else (lane >= HEAD_DIM)


def masked(scores, start, first_key):
    query = lax.broadcasted_iota(jnp.int32, scores.shape, 0) + start
    key = lax.broadcasted_iota(jnp.int32, scores.shape, 1) + first_key
    return jnp.where(key <= query, scores, -1e30)


def spans(rows, high):
    if not high:
        return ((0, 2 * rows, True),)
    free = 2 * rows // 128 * 128
    return ((0, free, False), (free, 4 * rows - free, True))


def attend_block(rows, start, high, qkv, attended, lse):
    width = attended.shape[1]
    here = pl.ds(start, rows)
    lane = lax.broadcasted_iota(jnp.int32, (rows, 128), 1)
    tops = jnp.zeros((rows, 128), f32)
    for pair in range(width // 128):
        columns = slice(pair * 128, pair * 128 + 128)
        query = qkv[here, columns] * bf16(HEAD_DIM ** (-0.5))
        results = []
        for half in range(2):
            only = jnp.where(head_lanes(query.shape, half), query, 0)
            scores = []
            for begin, size, mask in spans(rows, high):
                part = dot_nt(only, qkv[pl.ds(begin, size), width + pair * 128 : width + pair * 128 + 128])
                scores.append(masked(part, start, begin) if mask else part)
            top = functools.reduce(jnp.maximum, [jnp.max(part, axis=-1, keepdims=True) for part in scores])
            total, result = 0.0, 0.0
            for (begin, size, _), part in zip(spans(rows, high), scores):
                weights = jnp.exp(part - top)
                total = total + jnp.sum(weights, axis=-1, keepdims=True)
                values = qkv[pl.ds(begin, size), 2 * width + pair * 128 : 2 * width + pair * 128 + 128]
                result = result + dot_nn(weights.astype(bf16), values)
            results.append(result / total)
            tops = jnp.where(lane == 2 * pair + half, top + jnp.log(total), tops)
        attended[here, columns] = jnp.where(head_lanes((rows, 128), 0), results[0], results[1]).astype(bf16)
    lse[here, :] = tops


def attention_forward(layer, stream, gains, shifts, w_qkv, w_out, weights):
    rows, model = stream.shape
    width = w_out.shape[0]

    def body(r):
        held, qkv, attended, lse, weight = r.held, r.qkv, r.attended, r.lse, r.weight
        loads = [
            pltpu.make_async_copy(r.w_qkv.at[index], weight.at[:, pl.ds(index * width, width)], r.local.at[index])
            for index in range(3)
        ]
        loads.append(pltpu.make_async_copy(r.w_out, r.out, r.local.at[3]))
        for copy in loads:
            copy.start()
        greet(*GROUP, *(FETCH if weights else ()))
        jobs = fetch_jobs(r, weights, layer)
        own = places(rows)[0]
        held[pl.ds(own, rows), :] = norm_rows(r.stream[...], r.gains[layer, 0:1, :], r.shifts[layer, 0:1, :]).astype(bf16)
        for copy in loads:
            copy.wait()
        calls = []

        def arrived(start, size):
            calls.append(start)
            if len(calls) == 1:
                every(jobs, "step_along")
            here = pl.ds(start, size)

            def step(columns):
                qkv[here, columns] = dot_nn(held[here, :], weight[:, columns]).astype(bf16)

            tiles(3 * width, step)

        sent = gather(rows, held, arrived, r.send, r.receive)
        stores = [pltpu.make_async_copy(held, r.held_out, r.local.at[0]), pltpu.make_async_copy(qkv, r.qkv_out, r.local.at[1])]
        for copy in stores:
            copy.start()
        zl = lax.axis_index("zl")

        def attend(quarter, high):
            attend_block(rows, pl.multiple_of(quarter * rows, 16), high, qkv, attended, lse)

        attend(3 - zl, True)
        attend(1 - zl, False)
        done = []

        def term(start, size, sink):
            if size == rows and not done:
                done.append(True)
                if jobs:
                    jobs[0].step_share()
                attend(2 + zl, True)
                every(jobs[1:], "step_share")
                attend(zl, False)
            here = pl.ds(start, size)

            def step(columns):
                sink(columns, dot_nn(attended[here, :], r.out[:, columns]))

            tiles(model, step)

        finish = scatter(rows, term, r.first, r.sums, r.send, r.receive)
        late = [pltpu.make_async_copy(attended, r.attended_out, r.local.at[2]), pltpu.make_async_copy(lse, r.lse_out, r.local.at[3])]
        for copy in late:
            copy.start()
        finish()
        total = r.first[pl.ds(0, rows), :] + r.sums[1].astype(f32) + r.sums[5].astype(f32)
        r.branch[...] = total
        r.middle[...] = r.stream[...] + norm_rows(total, r.gains[layer, 1:2, :], r.shifts[layer, 1:2, :])
        sent()
        every(jobs, "step_end")
        for copy in stores + late:
            copy.wait()

    return run(
        body,
        1 + layer,
        {
            "stream": (stream, VMEM), "gains": (gains, VMEM), "shifts": (shifts, VMEM), "w_qkv": (w_qkv, ANY), "w_out": (w_out, ANY),
            **fetch_inputs(weights),
        },
        {
            "branch": ((rows, model), f32, VMEM), "middle": ((rows, model), f32, VMEM),
            "held_out": ((4 * rows, model), bf16, ANY), "qkv_out": ((4 * rows, 3 * width), bf16, ANY),
            "attended_out": ((4 * rows, width), bf16, ANY), "lse_out": ((4 * rows, 128), f32, ANY), **fetch_outputs(weights),
        },
        {
            "held": VMEM((4 * rows, model), bf16), "qkv": VMEM((4 * rows, 3 * width), bf16), "attended": VMEM((4 * rows, width), bf16),
            "lse": VMEM((4 * rows, 128), f32), "weight": VMEM((model, 3 * width), bf16), "out": VMEM(w_out.shape, bf16),
            **group_scratch(rows, model), "local": semaphores(4), **fetch_scratch(weights),
        },
        24 * rows * model * width,
        64 * rows * rows,
    )


def attend_block_back(rows, start, high, qkv, attended_grad, lse, inner, grad_query, grad_key, grad_value):
    width = attended_grad.shape[1]
    here = pl.ds(start, rows)
    scale = HEAD_DIM ** (-0.5)
    for pair in range(width // 128):
        columns = slice(pair * 128, pair * 128 + 128)
        query = qkv[here, columns] * bf16(scale)
        above = attended_grad[here, columns]
        result = 0.0
        for half in range(2):
            head = 2 * pair + half
            only = jnp.where(head_lanes(query.shape, half), query, 0)
            grad = jnp.where(head_lanes(query.shape, half), above, 0)
            for begin, size, mask in spans(rows, high):
                keys = pl.ds(begin, size)
                key = qkv[keys, width + pair * 128 : width + pair * 128 + 128]
                value = qkv[keys, 2 * width + pair * 128 : 2 * width + pair * 128 + 128]
                scores = dot_nt(only, key)
                if mask:
                    scores = masked(scores, start, begin)
                probs = jnp.exp(scores - lse[here, head : head + 1])
                grad_probs = dot_nt(grad, value)
                grad_scores = (probs * (grad_probs - inner[here, head : head + 1])).astype(bf16)
                key_only = jnp.where(head_lanes(key.shape, half), key, 0)
                result = result + dot_nn(grad_scores, key_only)
                grad_key[keys, columns] += dot_tn(grad_scores, only)
                grad_value[keys, columns] += dot_tn(probs.astype(bf16), grad)
        grad_query[here, columns] = (result * scale).astype(bf16)


def attention_backward(layer, grad, stream, saved, gains, shifts, w_qkv, w_out):
    rows, model = stream.shape
    width = w_out.shape[0]

    def body(r):
        held, past, qkv, attended, lse, inner, above = r.held, r.past, r.qkv, r.attended, r.lse, r.inner, r.above
        pushed, grad_key, grad_value, weight = r.pushed, r.grad_key, r.grad_value, r.weight
        loads = [
            pltpu.make_async_copy(r.w_out, r.out, r.local.at[3]),
            pltpu.make_async_copy(r.attended_in, attended, r.local.at[4]),
            pltpu.make_async_copy(r.qkv_in, qkv, r.local.at[5]),
            pltpu.make_async_copy(r.lse_in, lse, r.local.at[6]),
            *[
                pltpu.make_async_copy(r.w_qkv.at[index], weight.at[:, pl.ds(index * width, width)], r.local.at[index])
                for index in range(3)
            ],
            pltpu.make_async_copy(r.held_in, past, r.local.at[7]),
        ]
        for copy in loads:
            copy.start()
        greet(*GROUP)
        own = places(rows)[0]
        pulled, gain_one, shift_one = norm_pull(r.branch[...], r.gains[layer, 1:2, :], r.grad[...])
        held[pl.ds(own, rows), :] = pulled.astype(bf16)
        grad_key[...] = jnp.zeros_like(grad_key)
        grad_value[...] = jnp.zeros_like(grad_value)
        for copy in loads:
            copy.wait()
        zl = lax.axis_index("zl")

        def back(quarter, high):
            attend_block_back(
                rows, pl.multiple_of(quarter * rows, 16), high, qkv, above, lse, inner, pushed, grad_key, grad_value
            )

        blocks = []

        def arrived(start, size):
            here = pl.ds(start, size)
            value = dot_nt(held[here, :], r.out[...]).astype(bf16)
            above[here, :] = value
            product = value.astype(f32) * attended[here, :].astype(f32)
            lane = lax.broadcasted_iota(jnp.int32, (size, 128), 1)
            tile = jnp.zeros((size, 128), f32)
            for pair in range(width // 128):
                part = product[:, pair * 128 : pair * 128 + 128]
                for half in range(2):
                    one = jnp.sum(jnp.where(head_lanes(part.shape, half), part, 0.0), axis=-1, keepdims=True)
                    tile = jnp.where(lane == 2 * pair + half, one, tile)
            inner[here, :] = tile
            blocks.append(size)
            if len(blocks) == 2:
                back(2 + zl, True)
                back(zl, False)

        sent = gather(rows, held, arrived, r.send, r.receive)
        back(3 - zl, True)
        back(1 - zl, False)
        pushed[:, pl.ds(width, width)] = grad_key[...].astype(bf16)
        pushed[:, pl.ds(2 * width, width)] = grad_value[...].astype(bf16)

        def term(start, size, sink):
            here = pl.ds(start, size)

            def step(columns):
                sink(columns, dot_nt(pushed[here, :], weight[columns, :]))

            tiles(model, step)

        finish = scatter(rows, term, r.first, r.sums, r.send, r.receive)

        def step_out(columns):
            r.outcome_out[:, columns] = dot_tn(attended[...], held[:, columns]).astype(bf16)

        tiles(model, step_out)
        outs = [pltpu.make_async_copy(r.outcome_out, r.grad_out, r.local.at[0])]
        outs[0].start()

        def step_qkv(columns):
            r.outcome[columns, :] = dot_tn(past[:, columns], pushed[...]).astype(bf16)

        tiles(model, step_qkv)
        for index in range(3):
            copy = pltpu.make_async_copy(r.outcome.at[:, pl.ds(index * width, width)], r.grad_qkv.at[index], r.local.at[1 + index])
            copy.start()
            outs.append(copy)
        finish()
        total = r.first[pl.ds(0, rows), :] + r.sums[1].astype(f32) + r.sums[5].astype(f32)
        pulled, gain_zero, shift_zero = norm_pull(r.stream[...], r.gains[layer, 0:1, :], total)
        r.grad_stream[...] = r.grad[...] + pulled
        for index, value in enumerate((gain_zero, shift_zero, gain_one, shift_one)):
            r.norms[index : index + 1, :] = value
        sent()
        for copy in outs:
            copy.wait()

    return run(
        body,
        7 + layer,
        {
            "grad": (grad, VMEM), "branch": (saved.branch, VMEM), "stream": (stream, VMEM), "gains": (gains, VMEM),
            "shifts": (shifts, VMEM), "held_in": (saved.held_out, ANY), "qkv_in": (saved.qkv_out, ANY),
            "attended_in": (saved.attended_out, ANY), "lse_in": (saved.lse_out, ANY), "w_qkv": (w_qkv, ANY), "w_out": (w_out, ANY),
        },
        {
            "grad_stream": ((rows, model), f32, VMEM), "norms": ((4, model), f32, VMEM),
            "grad_qkv": (w_qkv.shape, bf16, ANY), "grad_out": (w_out.shape, bf16, ANY),
        },
        {
            "held": VMEM((4 * rows, model), bf16), "past": VMEM((4 * rows, model), bf16), "qkv": VMEM((4 * rows, 3 * width), bf16),
            "attended": VMEM((4 * rows, width), bf16), "lse": VMEM((4 * rows, 128), f32), "inner": VMEM((4 * rows, 128), f32),
            "above": VMEM((4 * rows, width), bf16), "pushed": VMEM((4 * rows, 3 * width), bf16),
            "grad_key": VMEM((4 * rows, width), f32), "grad_value": VMEM((4 * rows, width), f32),
            "weight": VMEM((model, 3 * width), bf16), "out": VMEM(w_out.shape, bf16), "outcome": VMEM((model, 3 * width), bf16),
            "outcome_out": VMEM(w_out.shape, bf16), **group_scratch(rows, model), "local": semaphores(8),
        },
        60 * rows * model * width,
        64 * rows * rows,
    )


SUM_COPIES = 11


class Summing:
    def __init__(self, source, target, land, mine, part, cross, send, receive, local):
        self.source, self.target = source, target
        self.land, self.mine, self.part, self.cross = land, mine, part, cross
        self.send, self.receive, self.local = send, receive, local
        self.size = source.shape[-2] // 4

    def rows_of(self, names=()):
        gl, p = [(1 - lax.axis_index(name)) if name in names else lax.axis_index(name) for name in ("gl", "p")]
        return pl.ds(pl.multiple_of((2 * gl + p) * self.size, 16), self.size)

    def copy(self, slot, source, target, device):
        return remote(source, target, self.send.at[slot], self.receive.at[slot], device)

    def spread(self):
        return [
            self.copy(slot, pick(self.source, self.rows_of(names)), self.land.at[slot], flipped(*names))
            for slot, names in enumerate(ACROSS)
        ]

    def keep(self):
        return pltpu.make_async_copy(pick(self.source, self.rows_of()), self.mine, self.local.at[0])

    def along(self):
        return self.copy(3, self.part, self.cross, flipped("zh"))

    def place(self):
        return pltpu.make_async_copy(self.part, pick(self.target, self.rows_of()), self.local.at[1])

    def share(self):
        own = pick(self.target, self.rows_of())
        return [self.copy(4 + slot, self.part, own, flipped(*names)) for slot, names in enumerate((*ACROSS, ("c",)))]

    def relays(self):
        rows = [pick(self.target, self.rows_of(names)) for names in ACROSS]
        return [self.copy(8 + slot, part, part, flipped("c")) for slot, part in enumerate(rows)]

    def step_spread(self):
        every(self.spread(), "start")
        self.keep().start()

    def step_add(self):
        self.keep().wait()
        every(self.spread(), "wait_recv")
        total = self.mine[...].astype(f32)
        for slot in range(3):
            total = total + self.land[slot].astype(f32)
        self.part[...] = total.astype(bf16)

        @pl.when(jnp.logical_not(holds()))
        def _():
            self.along().start()

    def step_share(self):
        @pl.when(holds())
        def _():
            self.along().wait_recv()
            self.part[...] = (self.part[...].astype(f32) + self.cross[...].astype(f32)).astype(bf16)
            every(self.share(), "start")
            self.place().start()

    def step_relay(self):
        @pl.when(holds())
        def _():
            for copy, relay in zip(self.share()[:3], self.relays()):
                copy.wait_recv()
                relay.start()

    def step_end(self):
        every(self.spread(), "wait_send")

        @pl.when(holds())
        def _():
            every(self.share() + self.relays(), "wait_send")
            self.place().wait()

        @pl.when(jnp.logical_not(holds()))
        def _():
            self.along().wait_send()
            every([self.share()[3]] + self.relays(), "wait_recv")


def summing_scratch(name, shape):
    part = part_shape(shape, 4)
    return {
        name + "_land": VMEM((3, *part), bf16),
        name + "_mine": VMEM(part, bf16),
        name + "_part": VMEM(part, bf16),
        name + "_cross": VMEM(part, bf16),
        name + "_send": semaphores(SUM_COPIES),
        name + "_receive": semaphores(SUM_COPIES),
        name + "_local": semaphores(2),
    }


CUBE = ("c", "zl", "p", "gl", "zh")


def tail(grads, norms, mixed, grad_in):
    def body(r):
        jobs = [
            Summing(*[getattr(r, name + end) for end in ("_from", "_to", "_land", "_mine", "_part", "_cross", "_send", "_receive", "_local")])
            for name in grads
        ]
        greet(*GROUP, *FETCH, ("c", "zh"))
        swaps = []
        for index, (source, low, landed) in enumerate(((r.mixed, r.low_mixed, r.land_mixed), (r.grad_in, r.low_grad, r.land_grad))):
            low[...] = source[...].astype(bf16)
            swaps.append(remote(low, landed, r.send.at[index], r.receive.at[index], flipped("c", "zh")))

        @pl.when(jnp.logical_not(holds()))
        def _():
            every(swaps, "start")

        total = r.norms[...]
        for index, name in enumerate(CUBE):
            r.norms_out[...] = total
            copy = remote(r.norms_out, r.land.at[index], r.send.at[2 + index], r.receive.at[2 + index], flipped(name))
            copy.start()
            if index == 0:
                every(jobs[:2], "step_spread")
            copy.wait()
            total = total + r.land[index]
        r.norms_out[...] = total
        count = len(jobs)
        for index in range(count + 3):
            if index < count:
                jobs[index].step_add()
                every(jobs[index + 2 : index + 3], "step_spread")
            if 0 <= index - 1 < count:
                jobs[index - 1].step_share()
            if 0 <= index - 2 < count:
                jobs[index - 2].step_relay()
            if 0 <= index - 3 < count:
                jobs[index - 3].step_end()

        @pl.when(holds())
        def _():
            r.mixed_out[...] = r.mixed[...]
            r.grad_out[...] = r.grad_in[...]

        @pl.when(jnp.logical_not(holds()))
        def _():
            every(swaps, "wait")
            r.mixed_out[...] = r.land_mixed[...].astype(f32)
            r.grad_out[...] = r.land_grad[...].astype(f32)

    scratch = {
        "land": VMEM((len(CUBE), *norms.shape), f32),
        "send": semaphores(2 + len(CUBE)),
        "receive": semaphores(2 + len(CUBE)),
        **{name: VMEM(mixed.shape, bf16) for name in ("low_mixed", "land_mixed", "low_grad", "land_grad")},
    }
    for name, value in grads.items():
        scratch.update(summing_scratch(name, value.shape))
    return run(
        body,
        9,
        {
            **{name + "_from": (value, ANY) for name, value in grads.items()},
            "norms": (norms, VMEM), "mixed": (mixed, VMEM), "grad_in": (grad_in, VMEM),
        },
        {
            **{name + "_to": (value.shape, bf16, ANY) for name, value in grads.items()},
            "norms_out": (norms.shape, f32, VMEM), "mixed_out": (mixed.shape, f32, VMEM), "grad_out": (mixed.shape, f32, VMEM),
        },
        scratch,
        1 << 20,
    )


def per_device(hidden_in, cotangent, group_ids, group_sizes, w_qkv, w_out, w_up, w_down, gains, shifts):
    layers = w_qkv.shape[0]
    size = jnp.sum(jnp.where(jnp.arange(group_sizes.shape[0]) == group_ids[0], group_sizes, 0))
    weight = jnp.full((8, 128), 1.0 / size.astype(f32), f32)
    start = head(hidden_in, weight, {"qkv": w_qkv, "out": w_out})
    stream, qkv, out = start.stream, start.qkv_to, start.out_to
    attentions, ffns = [], []
    for layer in range(layers):
        last = layer + 1 == layers
        att = attention_forward(layer, stream, gains, shifts, qkv, out, {"up": w_up, "down": w_down})
        ffn = ffn_forward(layer, att.middle, gains, shifts, att.up_to, att.down_to, {} if last else {"qkv": w_qkv, "out": w_out})
        ffn.middle = att.middle
        attentions.append((stream, att, qkv, out))
        ffns.append((ffn, att.up_to, att.down_to))
        stream = ffn.stream
        if not last:
            qkv, out = ffn.qkv_to, ffn.out_to
    cotangent = lax.ppermute(cotangent, ("c", "zh"), ((0, 0), (1, 2), (2, 1), (3, 3)))
    grad = cotangent.astype(f32) * start.scale[0, 0]
    grads, norms = {}, [None] * layers
    for layer in reversed(range(layers)):
        back = ffn_backward(layer, grad, ffns[layer][0], gains, shifts, *ffns[layer][1:])
        before, att, qkv, out = attentions[layer]
        deep = attention_backward(layer, back.grad_middle, before, att, gains, shifts, qkv, out)
        grad = deep.grad_stream
        for name, value in (("up", back.grad_up), ("down", back.grad_down), ("qkv", deep.grad_qkv), ("out", deep.grad_out)):
            grads[f"{name}{layer}"] = value
        norms[layer] = jnp.concatenate([deep.norms, back.norms])
    total = tail(grads, jnp.concatenate(norms), stream, grad)

    def stacked(name):
        whole = jnp.stack([getattr(total, f"{name}{layer}_to") for layer in range(layers)]).astype(f32)
        return lax.psum(whole, "gh") if lax.axis_size("gh") > 1 else whole

    sums = total.norms_out.reshape(layers, 4, 2, -1)
    if lax.axis_size("gh") > 1:
        sums = lax.psum(sums, "gh")
    return (
        total.mixed_out, total.grad_out, stacked("qkv"), stacked("out"), stacked("up"), stacked("down"), sums[:, :, 0], sums[:, :, 1]
    )


def solution(mesh):
    fine = jax.sharding.Mesh(mesh.devices.reshape(-1, 2, 2, 2, 2, 2), AXES)
    dp = ("gh", "gl", "p", "c")
    tensor = ("zh", "zl")
    rows = P((*dp, *tensor), None)
    weights = (
        P(None, None, None, tensor),
        P(None, tensor, None),
        P(None, None, tensor),
        P(None, tensor, None),
    )
    return jax.shard_map(
        per_device,
        mesh=fine,
        in_specs=(rows, rows, P(dp), P(), *weights, P(), P()),
        out_specs=(rows, rows, *weights, P(), P()),
        check_vma=False,
    )
```

```python
import functools
import types

import jax
import jax.numpy as jnp
from jax import lax
from jax.experimental import pallas as pl
from jax.experimental.pallas import tpu as pltpu
from jax.sharding import PartitionSpec as P

HEAD_DIM = 64
AXES = ("gh", "gl", "p", "c", "zh", "zl")
f32 = jnp.float32
bf16 = jnp.bfloat16
MESH = pl.DeviceIdType.MESH
VMEM, ANY = pltpu.VMEM, pl.ANY
eps_norm = 1e-05
TILE = 256


def centre(values):
    mean = jnp.mean(values, axis=-1, keepdims=True)
    centred = values - mean
    spread = jnp.mean(centred * centred, axis=-1, keepdims=True)
    rate = lax.rsqrt(spread + eps_norm)
    return centred * rate, rate


def norm_rows(values, gain, shift):
    return centre(values)[0] * gain + shift


def norm_pull(values, gain, grad):
    hat, rate = centre(values)
    scaled = grad * gain
    along = jnp.mean(scaled * hat, axis=-1, keepdims=True)
    level = jnp.mean(scaled, axis=-1, keepdims=True)
    return (
        rate * (scaled - level - hat * along),
        jnp.sum(grad * hat, axis=0, keepdims=True),
        jnp.sum(grad, axis=0, keepdims=True),
    )


def dot_nt(left, right):
    return lax.dot_general(left, right, (((1,), (1,)), ((), ())), preferred_element_type=f32)


def dot_tn(left, right):
    return lax.dot_general(left, right, (((0,), (0,)), ((), ())), preferred_element_type=f32)


def dot_nn(left, right):
    return jnp.dot(left, right, preferred_element_type=f32)


def cut_rows(rows):
    first = (rows // 2 + 15) // 16 * 16
    return ((0, first), (first, rows - first))


def flipped(*names):
    return {name: 1 - lax.axis_index(name) for name in names}


def greet(*others):
    barrier = pltpu.get_barrier_semaphore()
    for names in others:
        pl.semaphore_signal(barrier, inc=1, device_id=flipped(*names), device_id_type=MESH)
    pl.semaphore_wait(barrier, len(others))


GROUP = (("c",), ("zl",))
ACROSS = (("p",), ("gl",), ("gl", "p"))
FETCH = (("zh",), *ACROSS)


def remote(source, target, send, receive, device):
    return pltpu.make_async_remote_copy(
        src_ref=source,
        dst_ref=target,
        send_sem=send,
        recv_sem=receive,
        device_id=device,
        device_id_type=MESH,
    )


def tiles(width, body):
    def step(index, carry):
        body(pl.ds(pl.multiple_of(index * TILE, TILE), TILE))
        return carry

    lax.fori_loop(0, width // TILE, step, 0)


def exchange(rows, held, work, first, sums, send, receive):
    mate, near = flipped("c"), flipped("zl")
    own = pl.ds(0, rows)
    parts = cut_rows(rows)
    copies = [remote(held.at[own], held.at[pl.ds(rows, rows)], send.at[0], receive.at[0], mate)]
    copies[0].start()
    along = []
    for index, (start, size) in enumerate(parts):
        place = pl.ds(2 * rows + 2 * start, size)
        copy = remote(held.at[pl.ds(start, size)], held.at[place], send.at[1 + index], receive.at[1 + index], near)
        copy.start()
        along.append(copy)

    def keep(row, columns, value):
        first[pl.ds(row, value.shape[0]), columns] = value

    work(0, rows, keep)
    copies[0].wait_recv()

    def keep_mate(row, columns, value):
        sums[0, pl.ds(row - rows, value.shape[0]), columns] = value.astype(bf16)

    work(rows, rows, keep_mate)
    back = remote(sums.at[0], sums.at[1], send.at[3], receive.at[3], mate)
    back.start()
    copies.append(back)
    final = []
    for index, (start, size) in enumerate(parts):
        place = 2 * rows + 2 * start
        along[index].wait_recv()
        relay = remote(
            held.at[pl.ds(place, size)], held.at[pl.ds(place + size, size)], send.at[4 + index], receive.at[4 + index], mate
        )
        relay.start()
        relay.wait_recv()

        def keep_far(row, columns, value, place=place, start=start, size=size):
            first[pl.ds(rows + start, size), columns] = value[:size]
            sums[2, pl.ds(start, size), columns] = value[size:].astype(bf16)

        work(place, 2 * size, keep_far)
        part = pl.ds(start, size)
        cross = remote(sums.at[2, part], sums.at[3, part], send.at[6 + index], receive.at[6 + index], mate)
        cross.start()
        cross.wait_recv()
        sums[4, part, :] = (first[pl.ds(rows + start, size), :] + sums[3, part, :].astype(f32)).astype(bf16)
        last = remote(sums.at[4, part], sums.at[5, part], send.at[8 + index], receive.at[8 + index], near)
        last.start()
        final.append(last)
        copies += [relay, cross]

    def finish():
        back.wait_recv()
        for copy in final:
            copy.wait_recv()
        for copy in copies + along + final:
            copy.wait_send()

    return finish


def run(body, number, inputs, outputs, scratch, flops, transcendentals=0):
    names = [*inputs, *outputs, *scratch]

    def kernel(*refs):
        body(types.SimpleNamespace(**dict(zip(names, refs))))

    moved = sum(value.size * value.dtype.itemsize for value, _ in inputs.values())
    results = pl.pallas_call(
        kernel,
        out_shape=tuple(jax.ShapeDtypeStruct(shape, kind) for shape, kind, _ in outputs.values()),
        in_specs=[pl.BlockSpec(memory_space=memory) for _, memory in inputs.values()],
        out_specs=tuple(pl.BlockSpec(memory_space=memory) for _, _, memory in outputs.values()),
        scratch_shapes=list(scratch.values()),
        compiler_params=pltpu.CompilerParams(collective_id=number, has_side_effects=True, vmem_limit_bytes=58 << 20),
        cost_estimate=pl.CostEstimate(flops=flops, bytes_accessed=moved, transcendentals=transcendentals),
    )(*[value for value, _ in inputs.values()])
    return types.SimpleNamespace(**dict(zip(outputs, results)))


def semaphores(count):
    return pltpu.SemaphoreType.DMA((count,))


def group_scratch(rows, width):
    return {
        "first": VMEM((2 * rows, width), f32),
        "sums": VMEM((6, rows, width), bf16),
        "send": semaphores(10),
        "receive": semaphores(10),
    }


def pick(ref, rows):
    return ref.at[:, rows, :] if len(ref.shape) == 3 else ref.at[rows, :]


def part_shape(shape, parts):
    return (*shape[:-2], int(shape[-2] / parts), shape[-1])


def holds():
    return lax.axis_index("c") == lax.axis_index("zh")


class Fetching:
    copies = 4

    def __init__(self, source, target, send, receive):
        self.source, self.target, self.send, self.receive = source, target, send, receive
        self.size = source.shape[-2] // 4

    def rows_of(self, names=()):
        gl, p = [(1 - lax.axis_index(name)) if name in names else lax.axis_index(name) for name in ("gl", "p")]
        return pl.ds(pl.multiple_of((2 * gl + p) * self.size, 16), self.size)

    def along(self):
        rows = self.rows_of()
        return remote(
            pick(self.source, rows), pick(self.target, rows), self.send.at[0], self.receive.at[0], flipped("zh")
        )

    def share(self):
        rows = pick(self.target, self.rows_of())
        return [
            remote(rows, rows, self.send.at[1 + slot], self.receive.at[1 + slot], flipped(*names))
            for slot, names in enumerate(ACROSS)
        ]

    def step_along(self):
        @pl.when(holds())
        def _():
            self.along().start()

    def step_share(self):
        @pl.when(jnp.logical_not(holds()))
        def _():
            self.along().wait_recv()
            for copy in self.share():
                copy.start()

    def step_end(self):
        @pl.when(holds())
        def _():
            self.along().wait_send()

        @pl.when(jnp.logical_not(holds()))
        def _():
            for copy in self.share():
                copy.wait()


def fetch_jobs(refs, names, layer):
    return [
        Fetching(
            getattr(refs, name + "_from").at[layer], getattr(refs, name + "_to"), getattr(refs, name + "_send"),
            getattr(refs, name + "_receive"),
        )
        for name in names
    ]


def fetch_inputs(weights):
    return {name + "_from": (value, ANY) for name, value in weights.items()}


def fetch_outputs(weights):
    return {name + "_to": (value.shape[1:], bf16, ANY) for name, value in weights.items()}


def fetch_scratch(weights):
    result = {}
    for name in weights:
        result[name + "_send"] = semaphores(4)
        result[name + "_receive"] = semaphores(4)
    return result


class Loading:
    def __init__(self, own, fetched, target, semaphore):
        self.ways = [pltpu.make_async_copy(source, target, semaphore) for source in (own, fetched)]

    def start(self):
        pl.when(holds())(self.ways[0].start)
        pl.when(jnp.logical_not(holds()))(self.ways[1].start)

    def wait(self):
        pl.when(holds())(self.ways[0].wait)
        pl.when(jnp.logical_not(holds()))(self.ways[1].wait)


def every(jobs, step):
    for job in jobs:
        getattr(job, step)()


ORDERS = (("p", "gl"), ("gl", "p"))


class Halves:
    def copy(self, slot, source, target, name):
        return remote(source, target, self.send.at[slot], self.receive.at[slot], flipped(name))

    def at(self, half, first, second=None):
        start = (4 * half + 2 * first) * self.size
        if second is None:
            return pl.ds(pl.multiple_of(start, 16), 2 * self.size)
        return pl.ds(pl.multiple_of(start + second * self.size, 16), self.size)


class Scattering(Halves):
    def __init__(self, source, out, land, mine, more, part, send, receive, local):
        self.source, self.out = source, out
        self.land, self.mine, self.more, self.part = land, mine, more, part
        self.send, self.receive, self.local = send, receive, local
        self.size = source.shape[-2] // 8

    def spread(self, half):
        name = ORDERS[half][0]
        return self.copy(half, pick(self.source, self.at(half, 1 - lax.axis_index(name))), self.land.at[half], name)

    def keep(self, half):
        rows = self.at(half, lax.axis_index(ORDERS[half][0]))
        return pltpu.make_async_copy(pick(self.source, rows), self.mine.at[half], self.local.at[half])

    def second(self, index):
        return pl.ds(pl.multiple_of(index * self.size, 16), self.size)

    def fold(self, half):
        name = ORDERS[half][1]
        return self.copy(2 + half, pick(self.mine.at[half], self.second(1 - lax.axis_index(name))), self.more.at[half], name)

    def store(self):
        return pltpu.make_async_copy(self.part, self.out, self.local.at[2])

    def step_spread(self):
        for half in range(2):
            self.spread(half).start()
            self.keep(half).start()

    def step_fold(self):
        for half in range(2):
            self.keep(half).wait()
            self.spread(half).wait_recv()
            self.mine[half] = (self.mine[half].astype(f32) + self.land[half].astype(f32)).astype(bf16)
            self.fold(half).start()

    def step_add(self):
        for half in range(2):
            self.fold(half).wait_recv()
            own = pick(self.mine.at[half], self.second(lax.axis_index(ORDERS[half][1])))
            total = own[...].astype(f32) + self.more[half].astype(f32)
            pick(self.part, pl.ds(half * self.size, self.size))[...] = total.astype(bf16)
        self.store().start()

    def step_end(self):
        for half in range(2):
            self.spread(half).wait_send()
            self.fold(half).wait_send()
        self.store().wait()


class Sharing(Halves):
    def __init__(self, part, target, mine, cross, send, receive, local):
        self.part, self.target, self.mine, self.cross = part, target, mine, cross
        self.send, self.receive, self.local = send, receive, local
        self.size = target.shape[-2] // 8

    def place_of(self, half):
        return [lax.axis_index(name) for name in ORDERS[half]]

    def along(self):
        return self.copy(0, self.part, self.cross, "zh")

    def load(self):
        return pltpu.make_async_copy(self.part, self.mine, self.local.at[0])

    def place(self, half):
        own = pick(self.target, self.at(half, *self.place_of(half)))
        return pltpu.make_async_copy(self.own(half), own, self.local.at[1 + half])

    def own(self, half):
        return pick(self.mine, pl.ds(half * self.size, self.size))

    def direct(self, half, axis):
        own = pick(self.target, self.at(half, *self.place_of(half)))
        return self.copy(1 + 2 * half + axis, self.own(half), own, ORDERS[half][axis])

    def relay(self, half):
        first, second = self.place_of(half)
        rows = pick(self.target, self.at(half, first, 1 - second))
        return self.copy(5 + half, rows, rows, ORDERS[half][0])

    def mate(self, half, index):
        first = self.place_of(half)[0]
        rows = pick(self.target, self.at(half, first if index == 0 else 1 - first))
        return self.copy(7 + 2 * half + index, rows, rows, "c")

    def step_along(self):
        pl.when(holds())(self.load().start)
        pl.when(jnp.logical_not(holds()))(self.along().start)

    def step_share(self):
        @pl.when(holds())
        def _():
            self.load().wait()
            self.along().wait_recv()
            self.mine[...] = (self.mine[...].astype(f32) + self.cross[...].astype(f32)).astype(bf16)
            for half in range(2):
                self.direct(half, 1).start()
                self.direct(half, 0).start()
                self.place(half).start()

    def step_relay(self):
        @pl.when(holds())
        def _():
            for half in range(2):
                self.direct(half, 1).wait_recv()
                self.relay(half).start()
                self.place(half).wait()
                self.mate(half, 0).start()

    def step_mate(self):
        @pl.when(holds())
        def _():
            for half in range(2):
                self.direct(half, 0).wait_recv()
                self.relay(half).wait_recv()
                self.mate(half, 1).start()

    def step_end(self):
        @pl.when(holds())
        def _():
            for half in range(2):
                self.direct(half, 0).wait_send()
                self.direct(half, 1).wait_send()
                self.relay(half).wait_send()
                self.mate(half, 0).wait_send()
                self.mate(half, 1).wait_send()

        @pl.when(jnp.logical_not(holds()))
        def _():
            self.along().wait_send()
            for half in range(2):
                self.mate(half, 0).wait_recv()
                self.mate(half, 1).wait_recv()


SPREAD = ("from", "part", "land", "mine", "more", "sum", "send", "receive", "local")
SHARE = ("part", "to", "own", "cross", "along_send", "along_receive", "along_local")


def scatter_jobs(refs, names):
    return [Scattering(*[getattr(refs, f"{name}_{end}") for end in SPREAD]) for name in names]


def scatter_inputs(grads):
    return {name + "_from": (value, ANY) for name, value in grads.items()}


def scatter_outputs(grads):
    return {name + "_part": (part_shape(value.shape, 4), bf16, ANY) for name, value in grads.items()}


def scatter_scratch(grads):
    result = {}
    for name, value in grads.items():
        result[name + "_land"] = VMEM((2, *part_shape(value.shape, 4)), bf16)
        result[name + "_mine"] = VMEM((2, *part_shape(value.shape, 4)), bf16)
        result[name + "_more"] = VMEM((2, *part_shape(value.shape, 8)), bf16)
        result[name + "_sum"] = VMEM(part_shape(value.shape, 4), bf16)
        result[name + "_send"] = semaphores(4)
        result[name + "_receive"] = semaphores(4)
        result[name + "_local"] = semaphores(3)
    return result


def share_jobs(refs, names):
    return [Sharing(*[getattr(refs, f"{name}_{end}") for end in SHARE]) for name in names]


def share_inputs(parts):
    return {name + "_part": (value, ANY) for name, value in parts.items()}


def share_outputs(parts):
    return {name + "_to": (part_shape(value.shape, 1 / 4), bf16, ANY) for name, value in parts.items()}


def share_scratch(parts):
    result = {}
    for name, value in parts.items():
        result[name + "_own"] = VMEM(value.shape, bf16)
        result[name + "_cross"] = VMEM(value.shape, bf16)
        result[name + "_along_send"] = semaphores(11)
        result[name + "_along_receive"] = semaphores(11)
        result[name + "_along_local"] = semaphores(3)
    return result


def head(hidden_in, weight, weights):
    def body(r):
        greet(("c",), ("c", "zh"), *FETCH)
        jobs = fetch_jobs(r, weights, 0)
        jobs[0].step_along()
        swap = remote(r.hidden, r.landed, r.send.at[0], r.receive.at[0], flipped("c", "zh"))
        scale = remote(r.weight, r.other, r.send.at[1], r.receive.at[1], flipped("c"))
        scale.start()

        @pl.when(jnp.logical_not(holds()))
        def _():
            swap.start()

        every(jobs[1:], "step_along")
        every(jobs, "step_share")

        @pl.when(holds())
        def _():
            r.stream[...] = r.hidden[...].astype(f32)

        scale.wait()
        r.scale[...] = jnp.where(holds(), r.weight[...], r.other[...])

        @pl.when(jnp.logical_not(holds()))
        def _():
            swap.wait()
            r.stream[...] = r.landed[...].astype(f32)

        every(jobs, "step_end")

    return run(
        body,
        0,
        {"hidden": (hidden_in, VMEM), "weight": (weight, VMEM), **fetch_inputs(weights)},
        {"stream": (hidden_in.shape, f32, VMEM), "scale": (weight.shape, f32, VMEM), **fetch_outputs(weights)},
        {
            "landed": VMEM(hidden_in.shape, bf16),
            "other": VMEM(weight.shape, f32),
            "send": semaphores(2),
            "receive": semaphores(2),
            **fetch_scratch(weights),
        },
        1 << 20,
    )


def gelu_and_slope(values):
    rate, cubic = 0.7978845608028654, 0.044715
    square = values * values
    bend = jnp.tanh(rate * values * (1.0 + cubic * square))
    half = 0.5 * (1.0 + bend)
    slope = half + 0.5 * values * (1.0 - bend * bend) * (rate * (1.0 + 3.0 * cubic * square))
    return values * half, slope


def ffn_forward(layer, middle, gains, shifts, w_up, w_down, own_up, own_down, weights):
    rows, width = middle.shape
    hidden = w_up.shape[1]

    def body(r):
        loads = [Loading(r.own_up.at[layer], r.w_up, r.up, r.local.at[0]), Loading(r.own_down.at[layer], r.w_down, r.down, r.local.at[1])]
        for copy in loads:
            copy.start()
        greet(*GROUP, *(FETCH if weights else ()))
        jobs = fetch_jobs(r, weights, layer + 1)
        held, active, slope = r.held, r.active, r.slope
        held[pl.ds(0, rows), :] = norm_rows(r.middle[...], r.gains[layer, 2:3, :], r.shifts[layer, 2:3, :]).astype(bf16)
        for copy in loads:
            copy.wait()
        calls = []

        def work(start, size, sink):
            calls.append(start)
            if len(calls) == 1:
                every(jobs, "step_along")
            here = pl.ds(start, size)

            def step(columns):
                upper = dot_nn(held[here, :], r.up[:, columns])
                value, bend = gelu_and_slope(upper)
                active[here, columns] = value.astype(bf16)
                slope[here, columns] = bend.astype(bf16)

            tiles(hidden, step)

            def step_down(columns):
                sink(start, columns, dot_nn(active[here, :], r.down[:, columns]))

            tiles(width, step_down)

        finish = exchange(rows, held, work, r.first, r.sums, r.send, r.receive)
        stores = [
            pltpu.make_async_copy(held, r.held_out, r.local.at[2]),
            pltpu.make_async_copy(active, r.active_out, r.local.at[3]),
            pltpu.make_async_copy(slope, r.slope_out, r.local.at[4]),
        ]
        for copy in stores:
            copy.start()
        every(jobs, "step_share")
        finish()
        total = r.first[pl.ds(0, rows), :] + r.sums[1].astype(f32) + r.sums[5].astype(f32)
        r.second[...] = total
        r.stream[...] = r.middle[...] + norm_rows(total, r.gains[layer, 3:4, :], r.shifts[layer, 3:4, :])
        every(jobs, "step_end")
        for copy in stores:
            copy.wait()

    return run(
        body,
        3 + layer,
        {
            "middle": (middle, VMEM), "gains": (gains, VMEM), "shifts": (shifts, VMEM), "w_up": (w_up, ANY), "w_down": (w_down, ANY), "own_up": (own_up, ANY), "own_down": (own_down, ANY),
            **fetch_inputs(weights),
        },
        {
            "second": ((rows, width), f32, VMEM), "stream": ((rows, width), f32, VMEM),
            "held_out": ((4 * rows, width), bf16, ANY), "active_out": ((4 * rows, hidden), bf16, ANY),
            "slope_out": ((4 * rows, hidden), bf16, ANY), **fetch_outputs(weights),
        },
        {
            "held": VMEM((4 * rows, width), bf16), "active": VMEM((4 * rows, hidden), bf16), "slope": VMEM((4 * rows, hidden), bf16),
            "up": VMEM(w_up.shape, bf16), "down": VMEM(w_down.shape, bf16), **group_scratch(rows, width), "local": semaphores(5),
            **fetch_scratch(weights),
        },
        16 * rows * width * hidden,
        4 * rows * hidden,
    )


def ffn_backward(layer, grad, saved, gains, shifts, w_up, w_down, own_up, own_down, grads, parts):
    middle = saved.middle
    rows, width = middle.shape
    hidden = w_up.shape[1]

    def body(r):
        held, active, slope, pushed, past = r.held, r.active, r.slope, r.pushed, r.past
        loads = [
            Loading(r.own_down.at[layer], r.w_down, r.down, r.local.at[0]),
            Loading(r.own_up.at[layer], r.w_up, r.up, r.local.at[1]),
            pltpu.make_async_copy(r.slope_in, slope, r.local.at[2]),
            pltpu.make_async_copy(r.active_in, active, r.local.at[3]),
            pltpu.make_async_copy(r.held_in, past, r.local.at[4]),
        ]
        for copy in loads:
            copy.start()
        greet(*GROUP, *(FETCH if grads or parts else ()))
        jobs, shares = scatter_jobs(r, grads), share_jobs(r, parts)
        every(jobs, "step_spread")
        pulled, gain_three, shift_three = norm_pull(r.second[...], r.gains[layer, 3:4, :], r.grad[...])
        held[pl.ds(0, rows), :] = pulled.astype(bf16)
        for copy in loads:
            copy.wait()

        calls = []

        def work(start, size, sink):
            calls.append(start)
            if len(calls) == 1:
                every(shares, "step_along")
            if len(calls) == 4:
                every(jobs, "step_fold")
            here = pl.ds(start, size)

            def step(columns):
                value = dot_nt(held[here, :], r.down[columns, :])
                pushed[here, columns] = (value * slope[here, columns].astype(f32)).astype(bf16)

            tiles(hidden, step)

            def step_up(columns):
                sink(start, columns, dot_nt(pushed[here, :], r.up[columns, :]))

            tiles(width, step_up)

        finish = exchange(rows, held, work, r.first, r.sums, r.send, r.receive)

        every(shares, "step_share")

        def step_down(columns):
            r.outcome[0, columns, :] = dot_tn(active[:, columns], held[...]).astype(bf16)

        tiles(hidden, step_down)
        out_down = pltpu.make_async_copy(r.outcome.at[0], r.grad_down, r.local.at[0])
        out_down.start()
        every(jobs, "step_add")
        every(shares, "step_relay")

        def step_up(columns):
            r.outcome[1, columns, :] = dot_tn(past[:, columns], pushed[...]).astype(bf16)

        tiles(width, step_up)
        out_up = pltpu.make_async_copy(r.outcome.at[1], r.grad_up, r.local.at[1])
        out_up.start()
        every(shares, "step_mate")
        finish()
        total = r.first[pl.ds(0, rows), :] + r.sums[1].astype(f32) + r.sums[5].astype(f32)
        pulled, gain_two, shift_two = norm_pull(r.middle[...], r.gains[layer, 2:3, :], total)
        r.grad_middle[...] = r.grad[...] + pulled
        for index, value in enumerate((gain_two, shift_two, gain_three, shift_three)):
            r.norms[index : index + 1, :] = value
        out_down.wait()
        out_up.wait()
        every(jobs + shares, "step_end")

    return run(
        body,
        5 + layer,
        {
            "grad": (grad, VMEM), "second": (saved.second, VMEM), "middle": (middle, VMEM), "gains": (gains, VMEM),
            "shifts": (shifts, VMEM), "held_in": (saved.held_out, ANY), "active_in": (saved.active_out, ANY),
            "slope_in": (saved.slope_out, ANY), "w_up": (w_up, ANY), "w_down": (w_down, ANY), "own_up": (own_up, ANY), "own_down": (own_down, ANY),
            **scatter_inputs(grads), **share_inputs(parts),
        },
        {
            **scatter_outputs(grads), **share_outputs(parts),
            "grad_middle": ((rows, width), f32, VMEM), "norms": ((4, width), f32, VMEM),
            "grad_up": (w_up.shape, bf16, ANY), "grad_down": (w_down.shape, bf16, ANY),
        },
        {
            "held": VMEM((4 * rows, width), bf16), "past": VMEM((4 * rows, width), bf16),
            "active": VMEM((4 * rows, hidden), bf16), "slope": VMEM((4 * rows, hidden), bf16),
            "pushed": VMEM((4 * rows, hidden), bf16), "up": VMEM(w_up.shape, bf16), "down": VMEM(w_down.shape, bf16),
            "outcome": VMEM((2, width, hidden), bf16), **group_scratch(rows, width), "local": semaphores(5),
            **scatter_scratch(grads), **share_scratch(parts),
        },
        32 * rows * width * hidden,
    )


def places(rows):
    c, zl = lax.axis_index("c"), lax.axis_index("zl")

    def at(core, part):
        return pl.multiple_of((2 * core + part) * rows, 16)

    return at(c, zl), at(1 - c, zl), at(c, 1 - zl), at(1 - c, 1 - zl)


def gather(rows, held, arrived, send, receive):
    mate, near = flipped("c"), flipped("zl")
    own, others, along, across = places(rows)
    parts = cut_rows(rows)
    here = pl.ds(own, rows)
    copies = [remote(held.at[here], held.at[here], send.at[0], receive.at[0], mate)]
    copies[0].start()
    for index, (start, size) in enumerate(parts):
        part = pl.ds(pl.multiple_of(own + start, 16), size)
        copy = remote(held.at[part], held.at[part], send.at[1 + index], receive.at[1 + index], near)
        copy.start()
        copies.append(copy)
    arrived(own, rows)
    copies[0].wait_recv()
    arrived(others, rows)
    for index, (start, size) in enumerate(parts):
        copies[1 + index].wait_recv()
        first = pl.multiple_of(along + start, 16)
        part = pl.ds(first, size)
        relay = remote(held.at[part], held.at[part], send.at[4 + index], receive.at[4 + index], mate)
        relay.start()
        copies.append(relay)
        arrived(first, size)
        relay.wait_recv()
        arrived(pl.multiple_of(across + start, 16), size)

    def finish():
        for copy in copies:
            copy.wait_send()

    return finish


def scatter(rows, project, first, sums, send, receive):
    mate, near = flipped("c"), flipped("zl")
    own, others, along, across = places(rows)
    parts = cut_rows(rows)
    copies, crossing, final = [], [], []
    for index, (start, size) in enumerate(parts):
        part = pl.ds(start, size)

        def keep_far(columns, value, part=part):
            sums[2, part, columns] = value.astype(bf16)

        project(pl.multiple_of(across + start, 16), size, keep_far)
        cross = remote(sums.at[2, part], sums.at[3, part], send.at[6 + index], receive.at[6 + index], mate)
        cross.start()
        crossing.append(cross)
    for index, (start, size) in enumerate(parts):
        part = pl.ds(start, size)

        def keep_near(columns, value, start=start, size=size):
            first[pl.ds(rows + start, size), columns] = value

        project(pl.multiple_of(along + start, 16), size, keep_near)
        crossing[index].wait_recv()
        sums[4, part, :] = (first[pl.ds(rows + start, size), :] + sums[3, part, :].astype(f32)).astype(bf16)
        last = remote(sums.at[4, part], sums.at[5, part], send.at[8 + index], receive.at[8 + index], near)
        last.start()
        final.append(last)

    def keep_mate(columns, value):
        sums[0, :, columns] = value.astype(bf16)

    project(others, rows, keep_mate)
    back = remote(sums.at[0], sums.at[1], send.at[3], receive.at[3], mate)
    back.start()

    def keep(columns, value):
        first[pl.ds(0, rows), columns] = value

    project(own, rows, keep)

    def finish():
        back.wait_recv()
        for copy in final:
            copy.wait_recv()
        for copy in [back] + crossing + final:
            copy.wait_send()

    return finish


def head_lanes(shape, half):
    lane = lax.broadcasted_iota(jnp.int32, shape, len(shape) - 1)
    return (lane < HEAD_DIM) if half == 0 else (lane >= HEAD_DIM)


def masked(scores, start, first_key):
    query = lax.broadcasted_iota(jnp.int32, scores.shape, 0) + start
    key = lax.broadcasted_iota(jnp.int32, scores.shape, 1) + first_key
    return jnp.where(key <= query, scores, -1e30)


def spans(rows, high):
    if not high:
        return ((0, 2 * rows, True),)
    free = 2 * rows // 128 * 128
    return ((0, free, False), (free, 4 * rows - free, True))


def attend_block(rows, start, high, qkv, attended, lse):
    width = attended.shape[1]
    here = pl.ds(start, rows)
    lane = lax.broadcasted_iota(jnp.int32, (rows, 128), 1)
    tops = jnp.zeros((rows, 128), f32)
    for pair in range(width // 128):
        columns = slice(pair * 128, pair * 128 + 128)
        query = qkv[here, columns] * bf16(HEAD_DIM ** (-0.5))
        results = []
        for half in range(2):
            only = jnp.where(head_lanes(query.shape, half), query, 0)
            scores = []
            for begin, size, mask in spans(rows, high):
                part = dot_nt(only, qkv[pl.ds(begin, size), width + pair * 128 : width + pair * 128 + 128])
                scores.append(masked(part, start, begin) if mask else part)
            top = functools.reduce(jnp.maximum, [jnp.max(part, axis=-1, keepdims=True) for part in scores])
            total, result = 0.0, 0.0
            for (begin, size, _), part in zip(spans(rows, high), scores):
                weights = jnp.exp(part - top)
                total = total + jnp.sum(weights, axis=-1, keepdims=True)
                values = qkv[pl.ds(begin, size), 2 * width + pair * 128 : 2 * width + pair * 128 + 128]
                result = result + dot_nn(weights.astype(bf16), values)
            results.append(result / total)
            tops = jnp.where(lane == 2 * pair + half, top + jnp.log(total), tops)
        attended[here, columns] = jnp.where(head_lanes((rows, 128), 0), results[0], results[1]).astype(bf16)
    lse[here, :] = tops


def attention_forward(layer, stream, gains, shifts, w_qkv, w_out, own_qkv, own_out, weights):
    rows, model = stream.shape
    width = w_out.shape[0]

    def body(r):
        held, qkv, attended, lse, weight = r.held, r.qkv, r.attended, r.lse, r.weight
        loads = [
            Loading(r.own_qkv.at[layer, index], r.w_qkv.at[index], weight.at[:, pl.ds(index * width, width)], r.local.at[index])
            for index in range(3)
        ]
        loads.append(Loading(r.own_out.at[layer], r.w_out, r.out, r.local.at[3]))
        for copy in loads:
            copy.start()
        greet(*GROUP, *(FETCH if weights else ()))
        jobs = fetch_jobs(r, weights, layer)
        own = places(rows)[0]
        held[pl.ds(own, rows), :] = norm_rows(r.stream[...], r.gains[layer, 0:1, :], r.shifts[layer, 0:1, :]).astype(bf16)
        for copy in loads:
            copy.wait()
        calls = []

        def arrived(start, size):
            calls.append(start)
            if len(calls) == 1:
                every(jobs, "step_along")
            here = pl.ds(start, size)

            def step(columns):
                qkv[here, columns] = dot_nn(held[here, :], weight[:, columns]).astype(bf16)

            tiles(3 * width, step)

        sent = gather(rows, held, arrived, r.send, r.receive)
        stores = [pltpu.make_async_copy(held, r.held_out, r.local.at[0]), pltpu.make_async_copy(qkv, r.qkv_out, r.local.at[1])]
        for copy in stores:
            copy.start()
        zl = lax.axis_index("zl")

        def attend(quarter, high):
            attend_block(rows, pl.multiple_of(quarter * rows, 16), high, qkv, attended, lse)

        attend(3 - zl, True)
        attend(1 - zl, False)
        done = []

        def term(start, size, sink):
            if size == rows and not done:
                done.append(True)
                if jobs:
                    jobs[0].step_share()
                attend(2 + zl, True)
                every(jobs[1:], "step_share")
                attend(zl, False)
            here = pl.ds(start, size)

            def step(columns):
                sink(columns, dot_nn(attended[here, :], r.out[:, columns]))

            tiles(model, step)

        finish = scatter(rows, term, r.first, r.sums, r.send, r.receive)
        late = [pltpu.make_async_copy(attended, r.attended_out, r.local.at[2]), pltpu.make_async_copy(lse, r.lse_out, r.local.at[3])]
        for copy in late:
            copy.start()
        finish()
        total = r.first[pl.ds(0, rows), :] + r.sums[1].astype(f32) + r.sums[5].astype(f32)
        r.branch[...] = total
        r.middle[...] = r.stream[...] + norm_rows(total, r.gains[layer, 1:2, :], r.shifts[layer, 1:2, :])
        sent()
        every(jobs, "step_end")
        for copy in stores + late:
            copy.wait()

    return run(
        body,
        1 + layer,
        {
            "stream": (stream, VMEM), "gains": (gains, VMEM), "shifts": (shifts, VMEM), "w_qkv": (w_qkv, ANY), "w_out": (w_out, ANY), "own_qkv": (own_qkv, ANY), "own_out": (own_out, ANY),
            **fetch_inputs(weights),
        },
        {
            "branch": ((rows, model), f32, VMEM), "middle": ((rows, model), f32, VMEM),
            "held_out": ((4 * rows, model), bf16, ANY), "qkv_out": ((4 * rows, 3 * width), bf16, ANY),
            "attended_out": ((4 * rows, width), bf16, ANY), "lse_out": ((4 * rows, 128), f32, ANY), **fetch_outputs(weights),
        },
        {
            "held": VMEM((4 * rows, model), bf16), "qkv": VMEM((4 * rows, 3 * width), bf16), "attended": VMEM((4 * rows, width), bf16),
            "lse": VMEM((4 * rows, 128), f32), "weight": VMEM((model, 3 * width), bf16), "out": VMEM(w_out.shape, bf16),
            **group_scratch(rows, model), "local": semaphores(4), **fetch_scratch(weights),
        },
        24 * rows * model * width,
        64 * rows * rows,
    )


def attend_block_back(rows, start, high, qkv, attended_grad, lse, inner, grad_query, grad_key, grad_value):
    width = attended_grad.shape[1]
    here = pl.ds(start, rows)
    scale = HEAD_DIM ** (-0.5)
    for pair in range(width // 128):
        columns = slice(pair * 128, pair * 128 + 128)
        query = qkv[here, columns] * bf16(scale)
        above = attended_grad[here, columns]
        result = 0.0
        for half in range(2):
            head = 2 * pair + half
            only = jnp.where(head_lanes(query.shape, half), query, 0)
            grad = jnp.where(head_lanes(query.shape, half), above, 0)
            for begin, size, mask in spans(rows, high):
                keys = pl.ds(begin, size)
                key = qkv[keys, width + pair * 128 : width + pair * 128 + 128]
                value = qkv[keys, 2 * width + pair * 128 : 2 * width + pair * 128 + 128]
                scores = dot_nt(only, key)
                if mask:
                    scores = masked(scores, start, begin)
                probs = jnp.exp(scores - lse[here, head : head + 1])
                grad_probs = dot_nt(grad, value)
                grad_scores = (probs * (grad_probs - inner[here, head : head + 1])).astype(bf16)
                key_only = jnp.where(head_lanes(key.shape, half), key, 0)
                result = result + dot_nn(grad_scores, key_only)
                grad_key[keys, columns] += dot_tn(grad_scores, only)
                grad_value[keys, columns] += dot_tn(probs.astype(bf16), grad)
        grad_query[here, columns] = (result * scale).astype(bf16)


def attention_backward(layer, grad, stream, saved, gains, shifts, w_qkv, w_out, own_qkv, own_out, grads, parts):
    rows, model = stream.shape
    width = w_out.shape[0]

    def body(r):
        held, past, qkv, attended, lse, inner, above = r.held, r.past, r.qkv, r.attended, r.lse, r.inner, r.above
        pushed, grad_key, grad_value, weight = r.pushed, r.grad_key, r.grad_value, r.weight
        loads = [
            Loading(r.own_out.at[layer], r.w_out, r.out, r.local.at[3]),
            pltpu.make_async_copy(r.attended_in, attended, r.local.at[4]),
            pltpu.make_async_copy(r.qkv_in, qkv, r.local.at[5]),
            pltpu.make_async_copy(r.lse_in, lse, r.local.at[6]),
            *[
                Loading(r.own_qkv.at[layer, index], r.w_qkv.at[index], weight.at[:, pl.ds(index * width, width)], r.local.at[index])
                for index in range(3)
            ],
            pltpu.make_async_copy(r.held_in, past, r.local.at[7]),
        ]
        for copy in loads:
            copy.start()
        greet(*GROUP, *(FETCH if grads or parts else ()))
        jobs, shares = scatter_jobs(r, grads), share_jobs(r, parts)
        every(jobs, "step_spread")
        own = places(rows)[0]
        pulled, gain_one, shift_one = norm_pull(r.branch[...], r.gains[layer, 1:2, :], r.grad[...])
        held[pl.ds(own, rows), :] = pulled.astype(bf16)
        grad_key[...] = jnp.zeros_like(grad_key)
        grad_value[...] = jnp.zeros_like(grad_value)
        for copy in loads:
            copy.wait()
        zl = lax.axis_index("zl")

        def back(quarter, high):
            attend_block_back(
                rows, pl.multiple_of(quarter * rows, 16), high, qkv, above, lse, inner, pushed, grad_key, grad_value
            )

        blocks = []

        def arrived(start, size):
            here = pl.ds(start, size)
            value = dot_nt(held[here, :], r.out[...]).astype(bf16)
            above[here, :] = value
            product = value.astype(f32) * attended[here, :].astype(f32)
            lane = lax.broadcasted_iota(jnp.int32, (size, 128), 1)
            tile = jnp.zeros((size, 128), f32)
            for pair in range(width // 128):
                part = product[:, pair * 128 : pair * 128 + 128]
                for half in range(2):
                    one = jnp.sum(jnp.where(head_lanes(part.shape, half), part, 0.0), axis=-1, keepdims=True)
                    tile = jnp.where(lane == 2 * pair + half, one, tile)
            inner[here, :] = tile
            blocks.append(size)
            if len(blocks) == 2:
                every(shares, "step_along")
                back(2 + zl, True)
                back(zl, False)

        sent = gather(rows, held, arrived, r.send, r.receive)
        every(jobs[:1], "step_fold")
        back(3 - zl, True)
        every(shares, "step_share")
        every(jobs[1:], "step_fold")
        back(1 - zl, False)
        every(jobs[:1], "step_add")
        every(shares, "step_relay")
        pushed[:, pl.ds(width, width)] = grad_key[...].astype(bf16)
        pushed[:, pl.ds(2 * width, width)] = grad_value[...].astype(bf16)

        def term(start, size, sink):
            here = pl.ds(start, size)

            def step(columns):
                sink(columns, dot_nt(pushed[here, :], weight[columns, :]))

            tiles(model, step)

        finish = scatter(rows, term, r.first, r.sums, r.send, r.receive)

        every(jobs[1:], "step_add")

        def step_out(columns):
            r.outcome_out[:, columns] = dot_tn(attended[...], held[:, columns]).astype(bf16)

        tiles(model, step_out)
        outs = [pltpu.make_async_copy(r.outcome_out, r.grad_out, r.local.at[0])]
        outs[0].start()

        def step_qkv(columns):
            r.outcome[columns, :] = dot_tn(past[:, columns], pushed[...]).astype(bf16)

        tiles(model, step_qkv)
        for index in range(3):
            copy = pltpu.make_async_copy(r.outcome.at[:, pl.ds(index * width, width)], r.grad_qkv.at[index], r.local.at[1 + index])
            copy.start()
            outs.append(copy)
        every(shares, "step_mate")
        finish()
        total = r.first[pl.ds(0, rows), :] + r.sums[1].astype(f32) + r.sums[5].astype(f32)
        pulled, gain_zero, shift_zero = norm_pull(r.stream[...], r.gains[layer, 0:1, :], total)
        r.grad_stream[...] = r.grad[...] + pulled
        for index, value in enumerate((gain_zero, shift_zero, gain_one, shift_one)):
            r.norms[index : index + 1, :] = value
        sent()
        for copy in outs:
            copy.wait()
        every(jobs + shares, "step_end")

    return run(
        body,
        7 + layer,
        {
            "grad": (grad, VMEM), "branch": (saved.branch, VMEM), "stream": (stream, VMEM), "gains": (gains, VMEM),
            "shifts": (shifts, VMEM), "held_in": (saved.held_out, ANY), "qkv_in": (saved.qkv_out, ANY),
            "attended_in": (saved.attended_out, ANY), "lse_in": (saved.lse_out, ANY), "w_qkv": (w_qkv, ANY), "w_out": (w_out, ANY), "own_qkv": (own_qkv, ANY), "own_out": (own_out, ANY),
            **scatter_inputs(grads), **share_inputs(parts),
        },
        {
            **scatter_outputs(grads), **share_outputs(parts),
            "grad_stream": ((rows, model), f32, VMEM), "norms": ((4, model), f32, VMEM),
            "grad_qkv": (w_qkv.shape, bf16, ANY), "grad_out": (w_out.shape, bf16, ANY),
        },
        {
            "held": VMEM((4 * rows, model), bf16), "past": VMEM((4 * rows, model), bf16), "qkv": VMEM((4 * rows, 3 * width), bf16),
            "attended": VMEM((4 * rows, width), bf16), "lse": VMEM((4 * rows, 128), f32), "inner": VMEM((4 * rows, 128), f32),
            "above": VMEM((4 * rows, width), bf16), "pushed": VMEM((4 * rows, 3 * width), bf16),
            "grad_key": VMEM((4 * rows, width), f32), "grad_value": VMEM((4 * rows, width), f32),
            "weight": VMEM((model, 3 * width), bf16), "out": VMEM(w_out.shape, bf16), "outcome": VMEM((model, 3 * width), bf16),
            "outcome_out": VMEM(w_out.shape, bf16), **group_scratch(rows, model), "local": semaphores(8),
            **scatter_scratch(grads), **share_scratch(parts),
        },
        60 * rows * model * width,
        64 * rows * rows,
    )


CUBE = ("c", "zl", "p", "gl", "zh")


def tail(grads, parts, norms, grad_in):
    def body(r):
        greet(*GROUP, *FETCH, ("c", "zh"))
        jobs = scatter_jobs(r, grads)
        every(jobs, "step_spread")
        shares = share_jobs(r, parts)
        every(shares, "step_along")
        swap = remote(r.low, r.landed, r.send.at[0], r.receive.at[0], flipped("c", "zh"))
        r.low[...] = r.grad_in[...].astype(bf16)
        pl.when(jnp.logical_not(holds()))(swap.start)
        total = r.norms[...]
        for index, name in enumerate(CUBE):
            r.norms_out[...] = total
            copy = remote(r.norms_out, r.land.at[index], r.send.at[1 + index], r.receive.at[1 + index], flipped(name))
            copy.start()
            copy.wait()
            total = total + r.land[index]
        r.norms_out[...] = total
        every(jobs, "step_fold")
        every(shares, "step_share")
        every(jobs, "step_add")
        every(shares, "step_relay")
        last = [
            Sharing(
                getattr(r, name + "_sum"), getattr(r, name + "_to"),
                *[getattr(r, f"{name}_{end}") for end in SHARE[2:]],
            )
            for name in grads
        ]
        every(last, "step_along")
        every(shares, "step_mate")
        every(last, "step_share")
        every(last, "step_relay")
        every(last, "step_mate")

        @pl.when(holds())
        def _():
            r.grad_out[...] = r.grad_in[...]

        @pl.when(jnp.logical_not(holds()))
        def _():
            swap.wait()
            r.grad_out[...] = r.landed[...].astype(f32)

        every(jobs + shares + last, "step_end")

    extra = {name: jax.ShapeDtypeStruct(part_shape(value.shape, 4), bf16) for name, value in grads.items()}
    return run(
        body,
        9,
        {**scatter_inputs(grads), **share_inputs(parts), "norms": (norms, VMEM), "grad_in": (grad_in, VMEM)},
        {
            **scatter_outputs(grads), **share_outputs(parts), **share_outputs(extra),
            "norms_out": (norms.shape, f32, VMEM), "grad_out": (grad_in.shape, f32, VMEM),
        },
        {
            "land": VMEM((len(CUBE), *norms.shape), f32),
            "send": semaphores(1 + len(CUBE)),
            "receive": semaphores(1 + len(CUBE)),
            "low": VMEM(grad_in.shape, bf16),
            "landed": VMEM(grad_in.shape, bf16),
            **scatter_scratch(grads), **share_scratch(parts), **share_scratch(extra),
        },
        1 << 20,
    )


def per_device(hidden_in, cotangent, group_ids, group_sizes, w_qkv, w_out, w_up, w_down, gains, shifts):
    layers = w_qkv.shape[0]
    size = jnp.sum(jnp.where(jnp.arange(group_sizes.shape[0]) == group_ids[0], group_sizes, 0))
    weight = jnp.full((8, 128), 1.0 / size.astype(f32), f32)
    start = head(hidden_in, weight, {"qkv": w_qkv, "out": w_out})
    stream, qkv, out = start.stream, start.qkv_to, start.out_to
    attentions, ffns = [], []
    for layer in range(layers):
        last = layer + 1 == layers
        att = attention_forward(layer, stream, gains, shifts, qkv, out, w_qkv, w_out, {"up": w_up, "down": w_down})
        ffn = ffn_forward(layer, att.middle, gains, shifts, att.up_to, att.down_to, w_up, w_down, {} if last else {"qkv": w_qkv, "out": w_out})
        ffn.middle = att.middle
        attentions.append((stream, att, qkv, out))
        ffns.append((ffn, att.up_to, att.down_to))
        stream = ffn.stream
        if not last:
            qkv, out = ffn.qkv_to, ffn.out_to
    swap = functools.partial(lax.ppermute, axis_name=("c", "zh"), perm=((0, 0), (1, 2), (2, 1), (3, 3)))
    grad = swap(cotangent).astype(f32) * start.scale[0, 0]
    mixed = swap(stream.astype(bf16))
    norms, done, grads, parts = [None] * layers, {}, {}, {}

    def carry(result, names):
        done.update({name: getattr(result, name + "_to") for name in parts})
        following = {name: getattr(result, name + "_part") for name in grads}
        return dict(names), following

    for layer in reversed(range(layers)):
        back = ffn_backward(layer, grad, ffns[layer][0], gains, shifts, *ffns[layer][1:], w_up, w_down, grads, parts)
        grads, parts = carry(back, {f"up{layer}": back.grad_up, f"down{layer}": back.grad_down})
        before, att, qkv, out = attentions[layer]
        deep = attention_backward(
            layer, back.grad_middle, before, att, gains, shifts, qkv, out, w_qkv, w_out, grads, parts
        )
        grads, parts = carry(deep, {f"qkv{layer}": deep.grad_qkv, f"out{layer}": deep.grad_out})
        grad = deep.grad_stream
        norms[layer] = jnp.concatenate([deep.norms, back.norms])
    total = tail(grads, parts, jnp.concatenate(norms), grad)
    done.update({name: getattr(total, name + "_to") for name in (*grads, *parts)})

    def stacked(name):
        whole = jnp.stack([done[f"{name}{layer}"] for layer in range(layers)]).astype(f32)
        return lax.psum(whole, "gh") if lax.axis_size("gh") > 1 else whole

    sums = total.norms_out.reshape(layers, 4, 2, -1)
    if lax.axis_size("gh") > 1:
        sums = lax.psum(sums, "gh")
    return (
        mixed.astype(f32), total.grad_out, stacked("qkv"), stacked("out"), stacked("up"), stacked("down"), sums[:, :, 0], sums[:, :, 1]
    )


def solution(mesh):
    fine = jax.sharding.Mesh(mesh.devices.reshape(-1, 2, 2, 2, 2, 2), AXES)
    dp = ("gh", "gl", "p", "c")
    tensor = ("zh", "zl")
    rows = P((*dp, *tensor), None)
    weights = (
        P(None, None, None, tensor),
        P(None, tensor, None),
        P(None, None, tensor),
        P(None, tensor, None),
    )
    return jax.shard_map(
        per_device,
        mesh=fine,
        in_specs=(rows, rows, P(dp), P(), *weights, P(), P()),
        out_specs=(rows, rows, *weights, P(), P()),
        check_vma=False,
    )
```

```python
import functools
import types

import jax
import jax.numpy as jnp
from jax import lax
from jax.experimental import pallas as pl
from jax.experimental.pallas import tpu as pltpu
from jax.sharding import PartitionSpec as P

HEAD_DIM = 64
AXES = ("gh", "gl", "p", "c", "zh", "zl")
f32 = jnp.float32
bf16 = jnp.bfloat16
MESH = pl.DeviceIdType.MESH
VMEM, ANY = pltpu.VMEM, pl.ANY
eps_norm = 1e-05
TILE = 256


def centre(values):
    mean = jnp.mean(values, axis=-1, keepdims=True)
    centred = values - mean
    spread = jnp.mean(centred * centred, axis=-1, keepdims=True)
    rate = lax.rsqrt(spread + eps_norm)
    return centred * rate, rate


def norm_rows(values, gain, shift):
    return centre(values)[0] * gain + shift


def norm_pull(values, gain, grad):
    hat, rate = centre(values)
    scaled = grad * gain
    along = jnp.mean(scaled * hat, axis=-1, keepdims=True)
    level = jnp.mean(scaled, axis=-1, keepdims=True)
    return (
        rate * (scaled - level - hat * along),
        jnp.sum(grad * hat, axis=0, keepdims=True),
        jnp.sum(grad, axis=0, keepdims=True),
    )


def dot_nt(left, right):
    return lax.dot_general(left, right, (((1,), (1,)), ((), ())), preferred_element_type=f32)


def dot_tn(left, right):
    return lax.dot_general(left, right, (((0,), (0,)), ((), ())), preferred_element_type=f32)


def dot_nn(left, right):
    return jnp.dot(left, right, preferred_element_type=f32)


def cut_rows(rows):
    first = (rows // 2 + 15) // 16 * 16
    return ((0, first), (first, rows - first))


def flipped(*names):
    return {name: 1 - lax.axis_index(name) for name in names}


def greet(*others):
    barrier = pltpu.get_barrier_semaphore()
    for names in others:
        pl.semaphore_signal(barrier, inc=1, device_id=flipped(*names), device_id_type=MESH)
    pl.semaphore_wait(barrier, len(others))


GROUP = (("c",), ("zl",))
FETCH = (("zh",), ("p",), ("gl",))


def remote(source, target, send, receive, device):
    return pltpu.make_async_remote_copy(
        src_ref=source,
        dst_ref=target,
        send_sem=send,
        recv_sem=receive,
        device_id=device,
        device_id_type=MESH,
    )


def tiles(width, body):
    def step(index, carry):
        body(pl.ds(pl.multiple_of(index * TILE, TILE), TILE))
        return carry

    lax.fori_loop(0, width // TILE, step, 0)


def exchange(rows, held, work, first, sums, send, receive):
    mate, near = flipped("c"), flipped("zl")
    own = pl.ds(0, rows)
    parts = cut_rows(rows)
    copies = [remote(held.at[own], held.at[pl.ds(rows, rows)], send.at[0], receive.at[0], mate)]
    copies[0].start()
    along = []
    for index, (start, size) in enumerate(parts):
        place = pl.ds(2 * rows + 2 * start, size)
        copy = remote(held.at[pl.ds(start, size)], held.at[place], send.at[1 + index], receive.at[1 + index], near)
        copy.start()
        along.append(copy)

    def keep(row, columns, value):
        first[pl.ds(row, value.shape[0]), columns] = value

    work(0, rows, keep)
    copies[0].wait_recv()

    def keep_mate(row, columns, value):
        sums[0, pl.ds(row - rows, value.shape[0]), columns] = value.astype(bf16)

    work(rows, rows, keep_mate)
    back = remote(sums.at[0], sums.at[1], send.at[3], receive.at[3], mate)
    back.start()
    copies.append(back)
    final = []
    for index, (start, size) in enumerate(parts):
        place = 2 * rows + 2 * start
        along[index].wait_recv()
        relay = remote(
            held.at[pl.ds(place, size)], held.at[pl.ds(place + size, size)], send.at[4 + index], receive.at[4 + index], mate
        )
        relay.start()
        relay.wait_recv()

        def keep_far(row, columns, value, place=place, start=start, size=size):
            first[pl.ds(rows + start, size), columns] = value[:size]
            sums[2, pl.ds(start, size), columns] = value[size:].astype(bf16)

        work(place, 2 * size, keep_far)
        part = pl.ds(start, size)
        cross = remote(sums.at[2, part], sums.at[3, part], send.at[6 + index], receive.at[6 + index], mate)
        cross.start()
        cross.wait_recv()
        sums[4, part, :] = (first[pl.ds(rows + start, size), :] + sums[3, part, :].astype(f32)).astype(bf16)
        last = remote(sums.at[4, part], sums.at[5, part], send.at[8 + index], receive.at[8 + index], near)
        last.start()
        final.append(last)
        copies += [relay, cross]

    def finish():
        back.wait_recv()
        for copy in final:
            copy.wait_recv()
        for copy in copies + along + final:
            copy.wait_send()

    return finish


def run(body, number, inputs, outputs, scratch, flops, transcendentals=0):
    names = [*inputs, *outputs, *scratch]

    def kernel(*refs):
        body(types.SimpleNamespace(**dict(zip(names, refs))))

    moved = sum(value.size * value.dtype.itemsize for value, _ in inputs.values())
    results = pl.pallas_call(
        kernel,
        out_shape=tuple(jax.ShapeDtypeStruct(shape, kind) for shape, kind, _ in outputs.values()),
        in_specs=[pl.BlockSpec(memory_space=memory) for _, memory in inputs.values()],
        out_specs=tuple(pl.BlockSpec(memory_space=memory) for _, _, memory in outputs.values()),
        scratch_shapes=list(scratch.values()),
        compiler_params=pltpu.CompilerParams(collective_id=number, has_side_effects=True, vmem_limit_bytes=58 << 20),
        cost_estimate=pl.CostEstimate(flops=flops, bytes_accessed=moved, transcendentals=transcendentals),
    )(*[value for value, _ in inputs.values()])
    return types.SimpleNamespace(**dict(zip(outputs, results)))


def semaphores(count):
    return pltpu.SemaphoreType.DMA((count,))


def group_scratch(rows, width):
    return {
        "first": VMEM((2 * rows, width), f32),
        "sums": VMEM((6, rows, width), bf16),
        "send": semaphores(10),
        "receive": semaphores(10),
    }


def pick(ref, rows):
    return ref.at[:, rows, :] if len(ref.shape) == 3 else ref.at[rows, :]


def part_shape(shape, parts):
    return (*shape[:-2], int(shape[-2] / parts), shape[-1])


def inner():
    return lax.axis_index("zl") != lax.axis_index("zh")


def holds():
    return lax.axis_index("c") == lax.axis_index("zh")


def fetch_jobs(refs, names, layer):
    return [
        Fetching(
            getattr(refs, name + "_from").at[layer], getattr(refs, name + "_to"), getattr(refs, name + "_send"),
            getattr(refs, name + "_receive"),
        )
        for name in names
    ]


def fetch_inputs(weights):
    return {name + "_from": (value, ANY) for name, value in weights.items()}


def fetch_outputs(weights):
    return {name + "_to": (value.shape[1:], bf16, ANY) for name, value in weights.items()}


def fetch_scratch(weights):
    result = {}
    for name in weights:
        result[name + "_send"] = semaphores(8)
        result[name + "_receive"] = semaphores(8)
    return result


class Loading:
    def __init__(self, own, fetched, target, semaphore):
        self.ways = [pltpu.make_async_copy(source, target, semaphore) for source in (own, fetched)]

    def start(self):
        pl.when(holds())(self.ways[0].start)
        pl.when(jnp.logical_not(holds()))(self.ways[1].start)

    def wait(self):
        pl.when(holds())(self.ways[0].wait)
        pl.when(jnp.logical_not(holds()))(self.ways[1].wait)


def every(jobs, step):
    for job in jobs:
        getattr(job, step)()


CUBE = ("c", "zl", "p", "gl", "zh")
ORDERS = (("p", "gl"), ("gl", "p"))


class Halves:
    def copy(self, slot, source, target, name):
        return remote(source, target, self.send.at[slot], self.receive.at[slot], flipped(name))

    def at(self, half, first, second=None):
        start = (4 * half + 2 * first) * self.size
        if second is None:
            return pl.ds(pl.multiple_of(start, 16), 2 * self.size)
        return pl.ds(pl.multiple_of(start + second * self.size, 16), self.size)


class Fetching(Halves):
    def __init__(self, source, target, send, receive):
        self.source, self.target, self.send, self.receive = source, target, send, receive
        self.size = source.shape[-2] // 8

    def own(self, half):
        return self.at(half, *[lax.axis_index(name) for name in ORDERS[half]])

    def along(self, half):
        return self.copy(half, pick(self.source, self.own(half)), pick(self.target, self.own(half)), "zh")

    def direct(self, half, axis):
        rows = pick(self.target, self.own(half))
        return self.copy(2 + 2 * half + axis, rows, rows, ORDERS[half][axis])

    def relay(self, half):
        first, second = ORDERS[half]
        rows = pick(self.target, self.at(half, lax.axis_index(first), 1 - lax.axis_index(second)))
        return self.copy(6 + half, rows, rows, first)

    def start_along(self, here):
        @pl.when(jnp.logical_and(holds(), here))
        def _():
            for half in range(2):
                self.along(half).start()

    def step_inner(self):
        self.start_along(inner())

    def step_outer(self):
        self.start_along(jnp.logical_not(inner()))

    def step_share(self):
        @pl.when(jnp.logical_not(holds()))
        def _():
            for half in range(2):
                self.along(half).wait_recv()
                self.direct(half, 1).start()
                self.direct(half, 0).start()

    def step_relay(self):
        @pl.when(jnp.logical_not(holds()))
        def _():
            for half in range(2):
                self.direct(half, 1).wait_recv()
                self.relay(half).start()

    def step_end(self):
        @pl.when(holds())
        def _():
            for half in range(2):
                self.along(half).wait_send()

        @pl.when(jnp.logical_not(holds()))
        def _():
            for half in range(2):
                self.direct(half, 0).wait()
                self.direct(half, 1).wait_send()
                self.relay(half).wait()


class Passing(Halves):
    def __init__(self, refs, name, first, last, source=None):
        self.first, self.last = first, last
        for field in ("in", "out", "land", "mine", "more", "sum", "cross", "send", "receive", "local"):
            setattr(self, field, getattr(refs, f"{name}_{field}", None))
        self.source = source if source is not None else getattr(refs, f"{name}_in", None)
        self.size = self.sum.shape[-2] // 2

    def place_of(self, half):
        return [lax.axis_index(name) for name in ORDERS[half]]

    def spread(self, half):
        name = ORDERS[half][0]
        return self.copy(half, pick(self.source, self.at(half, 1 - lax.axis_index(name))), self.land.at[half], name)

    def keep(self, half):
        rows = self.at(half, lax.axis_index(ORDERS[half][0]))
        return pltpu.make_async_copy(pick(self.source, rows), self.mine.at[half], self.local.at[half])

    def second(self, index):
        return pl.ds(pl.multiple_of(index * self.size, 16), self.size)

    def fold(self, half):
        name = ORDERS[half][1]
        return self.copy(2 + half, pick(self.mine.at[half], self.second(1 - lax.axis_index(name))), self.more.at[half], name)

    def load(self):
        return pltpu.make_async_copy(self.source, self.sum, self.local.at[2])

    def store(self):
        return pltpu.make_async_copy(self.sum, self.out, self.local.at[2])

    def along(self):
        return self.copy(4, self.sum, self.cross, "zh")

    def own(self, half):
        return pick(self.sum, pl.ds(half * self.size, self.size))

    def place(self, half):
        return pltpu.make_async_copy(self.own(half), pick(self.out, self.at(half, *self.place_of(half))), self.local.at[half])

    def direct(self, half, axis):
        own = pick(self.out, self.at(half, *self.place_of(half)))
        return self.copy(5 + 2 * half + axis, self.own(half), own, ORDERS[half][axis])

    def relay(self, half):
        first, second = self.place_of(half)
        rows = pick(self.out, self.at(half, first, 1 - second))
        return self.copy(9 + half, rows, rows, ORDERS[half][0])

    def mate(self, half, index):
        first = self.place_of(half)[0]
        rows = pick(self.out, self.at(half, first if index == 0 else 1 - first))
        return self.copy(11 + 2 * half + index, rows, rows, "c")

    def step_spread(self):
        for half in range(2):
            self.spread(half).start()
            self.keep(half).start()

    def step_fold(self):
        for half in range(2):
            self.keep(half).wait()
            self.spread(half).wait_recv()
            self.mine[half] = (self.mine[half].astype(f32) + self.land[half].astype(f32)).astype(bf16)
            self.fold(half).start()

    def step_add(self):
        for half in range(2):
            self.fold(half).wait_recv()
            own = pick(self.mine.at[half], self.second(lax.axis_index(ORDERS[half][1])))
            self.own(half)[...] = (own[...].astype(f32) + self.more[half].astype(f32)).astype(bf16)

    def step_load(self):
        self.load().start()

    def step_loaded(self):
        self.load().wait()

    def step_inner(self):
        pl.when(jnp.logical_and(jnp.logical_not(holds()), inner()))(self.along().start)

    def step_outer(self):
        pl.when(jnp.logical_not(jnp.logical_or(holds(), inner())))(self.along().start)

    def step_join(self):
        @pl.when(holds())
        def _():
            self.along().wait_recv()
            self.sum[...] = (self.sum[...].astype(f32) + self.cross[...].astype(f32)).astype(bf16)

    def step_share(self):
        @pl.when(holds())
        def _():
            for half in range(2):
                self.direct(half, 1).start()
                self.direct(half, 0).start()
                self.place(half).start()

    def step_relay(self):
        @pl.when(holds())
        def _():
            for half in range(2):
                self.direct(half, 1).wait_recv()
                self.relay(half).start()
                self.place(half).wait()
                self.mate(half, 0).start()

    def step_mate(self):
        @pl.when(holds())
        def _():
            for half in range(2):
                self.direct(half, 0).wait_recv()
                self.relay(half).wait_recv()
                self.mate(half, 1).start()

    def step_store(self):
        self.store().start()

    def step_end(self):
        if self.first == 0:
            for half in range(2):
                self.spread(half).wait_send()
                self.fold(half).wait_send()
        if self.last < 2:
            self.store().wait()

        @pl.when(holds())
        def _():
            if self.last == 2:
                for half in range(2):
                    self.direct(half, 0).wait_send()
                    self.direct(half, 1).wait_send()
                    self.relay(half).wait_send()
                    self.mate(half, 0).wait_send()
                    self.mate(half, 1).wait_send()

        @pl.when(jnp.logical_not(holds()))
        def _():
            if self.first <= 1 <= self.last:
                self.along().wait_send()
            if self.last == 2:
                for half in range(2):
                    self.mate(half, 0).wait_recv()
                    self.mate(half, 1).wait_recv()


def pass_shapes(grads):
    for name, (value, first, last) in grads.items():
        whole = value.shape if first == 0 else part_shape(value.shape, 1 / 4)
        yield name, whole, part_shape(whole, 4), first, last


def pass_jobs(refs, grads, sources=None):
    return {name: Passing(refs, name, first, last, (sources or {}).get(name)) for name, (_, first, last) in grads.items()}


def pass_inputs(grads):
    return {name + "_in": (value, ANY) for name, (value, *_) in grads.items() if isinstance(value, jax.Array)}


def pass_outputs(grads):
    return {name + "_out": (whole if last == 2 else part, bf16, ANY) for name, whole, part, first, last in pass_shapes(grads)}


def pass_scratch(grads):
    result = {}
    for name, whole, part, first, last in pass_shapes(grads):
        if first == 0:
            result[name + "_land"] = VMEM((2, *part), bf16)
            result[name + "_mine"] = VMEM((2, *part), bf16)
            result[name + "_more"] = VMEM((2, *part_shape(whole, 8)), bf16)
        result[name + "_sum"] = VMEM(part, bf16)
        if first <= 1 <= last:
            result[name + "_cross"] = VMEM(part, bf16)
        result[name + "_send"] = semaphores(15)
        result[name + "_receive"] = semaphores(15)
        result[name + "_local"] = semaphores(3)
    return result


def every_of(jobs, names, *steps):
    for step in steps:
        for name in names:
            getattr(jobs[name], step)()


class Swapping:
    def __init__(self, source, landed, send, receive):
        self.landed = landed
        self.copy = remote(source, landed, send, receive, flipped("c", "zh"))

    def start(self):
        pl.when(jnp.logical_not(holds()))(self.copy.start)

    def step_inner(self):
        pl.when(jnp.logical_and(jnp.logical_not(holds()), inner()))(self.copy.start)

    def step_outer(self):
        pl.when(jnp.logical_not(jnp.logical_or(holds(), inner())))(self.copy.start)

    def wait(self):
        pl.when(jnp.logical_not(holds()))(self.copy.wait)

    def give(self, target, own, scale=None):
        factor = 1.0 if scale is None else scale

        @pl.when(holds())
        def _():
            target[...] = own[...].astype(f32) * factor

        @pl.when(jnp.logical_not(holds()))
        def _():
            target[...] = self.landed[...].astype(f32) * factor


def gelu_and_slope(values):
    rate, cubic = 0.7978845608028654, 0.044715
    square = values * values
    bend = jnp.tanh(rate * values * (1.0 + cubic * square))
    half = 0.5 * (1.0 + bend)
    slope = half + 0.5 * values * (1.0 - bend * bend) * (rate * (1.0 + 3.0 * cubic * square))
    return values * half, slope


def ffn_forward(layer, middle, gains, shifts, w_up, w_down, own_up, own_down, weights, cotangent=None, scale=None):
    rows, width = middle.shape
    hidden = w_up.shape[1]

    def body(r):
        loads = [Loading(r.own_up.at[layer], r.w_up, r.up, r.local.at[0]), Loading(r.own_down.at[layer], r.w_down, r.down, r.local.at[1])]
        for copy in loads:
            copy.start()
        greet(*GROUP, *(FETCH if weights else ()), *(() if cotangent is None else (("c", "zh"),)))
        jobs = fetch_jobs(r, weights, layer + 1)
        swaps = [] if cotangent is None else [Swapping(r.cotangent, r.landed, r.swap.at[0], r.swap.at[1])]
        every(jobs + swaps, "step_inner")
        held, active, slope = r.held, r.active, r.slope
        held[pl.ds(0, rows), :] = norm_rows(r.middle[...], r.gains[layer, 2:3, :], r.shifts[layer, 2:3, :]).astype(bf16)
        for copy in loads:
            copy.wait()
        calls = []

        def work(start, size, sink):
            calls.append(start)
            if len(calls) == 1:
                every(jobs + swaps, "step_outer")
            if len(calls) == 4:
                every(jobs, "step_share")
            here = pl.ds(start, size)

            def step(columns):
                upper = dot_nn(held[here, :], r.up[:, columns])
                value, bend = gelu_and_slope(upper)
                active[here, columns] = value.astype(bf16)
                slope[here, columns] = bend.astype(bf16)

            tiles(hidden, step)

            def step_down(columns):
                sink(start, columns, dot_nn(active[here, :], r.down[:, columns]))

            tiles(width, step_down)

        finish = exchange(rows, held, work, r.first, r.sums, r.send, r.receive)
        stores = [
            pltpu.make_async_copy(held, r.held_out, r.local.at[2]),
            pltpu.make_async_copy(active, r.active_out, r.local.at[3]),
            pltpu.make_async_copy(slope, r.slope_out, r.local.at[4]),
        ]
        for copy in stores:
            copy.start()
        every(jobs, "step_relay")
        finish()
        total = r.first[pl.ds(0, rows), :] + r.sums[1].astype(f32) + r.sums[5].astype(f32)
        r.second[...] = total
        r.stream[...] = r.middle[...] + norm_rows(total, r.gains[layer, 3:4, :], r.shifts[layer, 3:4, :])
        every(jobs, "step_end")
        for swap in swaps:
            swap.wait()
            swap.give(r.grad, r.cotangent, r.scale[0:1, 0:1])
        for copy in stores:
            copy.wait()

    return run(
        body,
        3 + layer,
        {
            "middle": (middle, VMEM), "gains": (gains, VMEM), "shifts": (shifts, VMEM), "w_up": (w_up, ANY), "w_down": (w_down, ANY), "own_up": (own_up, ANY), "own_down": (own_down, ANY),
            **fetch_inputs(weights), **({} if cotangent is None else {"cotangent": (cotangent, VMEM), "scale": (scale, VMEM)}),
        },
        {
            "second": ((rows, width), f32, VMEM), "stream": ((rows, width), f32, VMEM),
            "held_out": ((4 * rows, width), bf16, ANY), "active_out": ((4 * rows, hidden), bf16, ANY),
            "slope_out": ((4 * rows, hidden), bf16, ANY), **fetch_outputs(weights),
            **({} if cotangent is None else {"grad": ((rows, width), f32, VMEM)}),
        },
        {
            "held": VMEM((4 * rows, width), bf16), "active": VMEM((4 * rows, hidden), bf16), "slope": VMEM((4 * rows, hidden), bf16),
            "up": VMEM(w_up.shape, bf16), "down": VMEM(w_down.shape, bf16), **group_scratch(rows, width), "local": semaphores(5),
            **fetch_scratch(weights),
            **({} if cotangent is None else {"landed": VMEM(cotangent.shape, bf16), "swap": semaphores(2)}),
        },
        16 * rows * width * hidden,
        4 * rows * hidden,
    )


def ffn_backward(layer, grad, saved, gains, shifts, w_up, w_down, own_up, own_down, grads, mixed=None):
    middle = saved.middle
    rows, width = middle.shape
    hidden = w_up.shape[1]

    def body(r):
        held, active, slope, pushed, past = r.held, r.active, r.slope, r.pushed, r.past
        loads = [
            Loading(r.own_down.at[layer], r.w_down, r.down, r.local.at[0]),
            Loading(r.own_up.at[layer], r.w_up, r.up, r.local.at[1]),
            pltpu.make_async_copy(r.slope_in, slope, r.local.at[2]),
            pltpu.make_async_copy(r.active_in, active, r.local.at[3]),
            pltpu.make_async_copy(r.held_in, past, r.local.at[4]),
        ]
        for copy in loads:
            copy.start()
        greet(*GROUP, *(FETCH if grads else ()), *(() if mixed is None else (("c", "zh"),)))
        jobs = pass_jobs(r, grads)
        new = [name for name in grads if grads[name][1] == 0]
        late = [name for name in grads if grads[name][1] == 2]
        swaps = [] if mixed is None else [Swapping(r.low, r.landed, r.swap.at[0], r.swap.at[1])]
        if mixed is not None:
            r.low[...] = r.mixed[...].astype(bf16)
        crossing = [name for name in grads if grads[name][1] == 1]
        every(swaps, "step_inner")
        every_of(jobs, crossing, "step_load", "step_loaded", "step_inner")
        every_of(jobs, late, "step_load")
        every_of(jobs, new, "step_spread")
        pulled, gain_three, shift_three = norm_pull(r.second[...], r.gains[layer, 3:4, :], r.grad[...])
        held[pl.ds(0, rows), :] = pulled.astype(bf16)
        for copy in loads:
            copy.wait()

        calls = []

        def work(start, size, sink):
            calls.append(start)
            if len(calls) == 1:
                every(swaps, "step_outer")
                every_of(jobs, crossing, "step_outer")
                every_of(jobs, late, "step_loaded", "step_share")
            if len(calls) == 3:
                every_of(jobs, late, "step_relay")
            if len(calls) == 4:
                every_of(jobs, new, "step_fold")
            here = pl.ds(start, size)

            def step(columns):
                value = dot_nt(held[here, :], r.down[columns, :])
                pushed[here, columns] = (value * slope[here, columns].astype(f32)).astype(bf16)

            tiles(hidden, step)

            def step_up(columns):
                sink(start, columns, dot_nt(pushed[here, :], r.up[columns, :]))

            tiles(width, step_up)

        finish = exchange(rows, held, work, r.first, r.sums, r.send, r.receive)

        every_of(jobs, late, "step_mate")
        every_of(jobs, crossing, "step_join", "step_share")

        def step_down(columns):
            r.outcome[0, columns, :] = dot_tn(active[:, columns], held[...]).astype(bf16)

        tiles(hidden, step_down)
        out_down = pltpu.make_async_copy(r.outcome.at[0], r.grad_down, r.local.at[0])
        out_down.start()
        every_of(jobs, new, "step_add", "step_store")
        every_of(jobs, crossing, "step_relay")

        def step_up(columns):
            r.outcome[1, columns, :] = dot_tn(past[:, columns], pushed[...]).astype(bf16)

        tiles(width, step_up)
        out_up = pltpu.make_async_copy(r.outcome.at[1], r.grad_up, r.local.at[1])
        out_up.start()
        finish()
        total = r.first[pl.ds(0, rows), :] + r.sums[1].astype(f32) + r.sums[5].astype(f32)
        pulled, gain_two, shift_two = norm_pull(r.middle[...], r.gains[layer, 2:3, :], total)
        r.grad_middle[...] = r.grad[...] + pulled
        for index, value in enumerate((gain_two, shift_two, gain_three, shift_three)):
            r.norms[index : index + 1, :] = value
        out_down.wait()
        out_up.wait()
        every_of(jobs, crossing, "step_mate")
        every_of(jobs, grads, "step_end")
        for swap in swaps:
            swap.wait()
            swap.give(r.mixed_out, r.mixed)

    return run(
        body,
        5 + layer,
        {
            "grad": (grad, VMEM), "second": (saved.second, VMEM), "middle": (middle, VMEM), "gains": (gains, VMEM),
            "shifts": (shifts, VMEM), "held_in": (saved.held_out, ANY), "active_in": (saved.active_out, ANY),
            "slope_in": (saved.slope_out, ANY), "w_up": (w_up, ANY), "w_down": (w_down, ANY), "own_up": (own_up, ANY), "own_down": (own_down, ANY),
            **pass_inputs(grads), **({} if mixed is None else {"mixed": (mixed, VMEM)}),
        },
        {
            **pass_outputs(grads), **({} if mixed is None else {"mixed_out": (mixed.shape, f32, VMEM)}),
            "grad_middle": ((rows, width), f32, VMEM), "norms": ((4, width), f32, VMEM),
            "grad_up": (w_up.shape, bf16, ANY), "grad_down": (w_down.shape, bf16, ANY),
        },
        {
            "held": VMEM((4 * rows, width), bf16), "past": VMEM((4 * rows, width), bf16),
            "active": VMEM((4 * rows, hidden), bf16), "slope": VMEM((4 * rows, hidden), bf16),
            "pushed": VMEM((4 * rows, hidden), bf16), "up": VMEM(w_up.shape, bf16), "down": VMEM(w_down.shape, bf16),
            "outcome": VMEM((2, width, hidden), bf16), **group_scratch(rows, width), "local": semaphores(5),
            **pass_scratch(grads),
            **(
                {}
                if mixed is None
                else {"low": VMEM(mixed.shape, bf16), "landed": VMEM(mixed.shape, bf16), "swap": semaphores(2)}
            ),
        },
        32 * rows * width * hidden,
    )


def places(rows):
    c, zl = lax.axis_index("c"), lax.axis_index("zl")

    def at(core, part):
        return pl.multiple_of((2 * core + part) * rows, 16)

    return at(c, zl), at(1 - c, zl), at(c, 1 - zl), at(1 - c, 1 - zl)


def gather(rows, held, arrived, send, receive):
    mate, near = flipped("c"), flipped("zl")
    own, others, along, across = places(rows)
    parts = cut_rows(rows)
    here = pl.ds(own, rows)
    copies = [remote(held.at[here], held.at[here], send.at[0], receive.at[0], mate)]
    copies[0].start()
    for index, (start, size) in enumerate(parts):
        part = pl.ds(pl.multiple_of(own + start, 16), size)
        copy = remote(held.at[part], held.at[part], send.at[1 + index], receive.at[1 + index], near)
        copy.start()
        copies.append(copy)
    arrived(own, rows)
    copies[0].wait_recv()
    arrived(others, rows)
    for index, (start, size) in enumerate(parts):
        copies[1 + index].wait_recv()
        first = pl.multiple_of(along + start, 16)
        part = pl.ds(first, size)
        relay = remote(held.at[part], held.at[part], send.at[4 + index], receive.at[4 + index], mate)
        relay.start()
        copies.append(relay)
        arrived(first, size)
        relay.wait_recv()
        arrived(pl.multiple_of(across + start, 16), size)

    def finish():
        for copy in copies:
            copy.wait_send()

    return finish


def scatter(rows, project, first, sums, send, receive):
    mate, near = flipped("c"), flipped("zl")
    own, others, along, across = places(rows)
    parts = cut_rows(rows)
    copies, crossing, final = [], [], []
    for index, (start, size) in enumerate(parts):
        part = pl.ds(start, size)

        def keep_far(columns, value, part=part):
            sums[2, part, columns] = value.astype(bf16)

        project(pl.multiple_of(across + start, 16), size, keep_far)
        cross = remote(sums.at[2, part], sums.at[3, part], send.at[6 + index], receive.at[6 + index], mate)
        cross.start()
        crossing.append(cross)
    for index, (start, size) in enumerate(parts):
        part = pl.ds(start, size)

        def keep_near(columns, value, start=start, size=size):
            first[pl.ds(rows + start, size), columns] = value

        project(pl.multiple_of(along + start, 16), size, keep_near)
        crossing[index].wait_recv()
        sums[4, part, :] = (first[pl.ds(rows + start, size), :] + sums[3, part, :].astype(f32)).astype(bf16)
        last = remote(sums.at[4, part], sums.at[5, part], send.at[8 + index], receive.at[8 + index], near)
        last.start()
        final.append(last)

    def keep_mate(columns, value):
        sums[0, :, columns] = value.astype(bf16)

    project(others, rows, keep_mate)
    back = remote(sums.at[0], sums.at[1], send.at[3], receive.at[3], mate)
    back.start()

    def keep(columns, value):
        first[pl.ds(0, rows), columns] = value

    project(own, rows, keep)

    def finish():
        back.wait_recv()
        for copy in final:
            copy.wait_recv()
        for copy in [back] + crossing + final:
            copy.wait_send()

    return finish


def head_lanes(shape, half):
    lane = lax.broadcasted_iota(jnp.int32, shape, len(shape) - 1)
    return (lane < HEAD_DIM) if half == 0 else (lane >= HEAD_DIM)


def masked(scores, start, first_key):
    query = lax.broadcasted_iota(jnp.int32, scores.shape, 0) + start
    key = lax.broadcasted_iota(jnp.int32, scores.shape, 1) + first_key
    return jnp.where(key <= query, scores, -1e30)


def spans(rows, high):
    if not high:
        return ((0, 2 * rows, True),)
    free = 2 * rows // 128 * 128
    return ((0, free, False), (free, 4 * rows - free, True))


def attend_block(rows, start, high, qkv, attended, lse):
    width = attended.shape[1]
    here = pl.ds(start, rows)
    lane = lax.broadcasted_iota(jnp.int32, (rows, 128), 1)
    tops = jnp.zeros((rows, 128), f32)
    for pair in range(width // 128):
        columns = slice(pair * 128, pair * 128 + 128)
        query = qkv[here, columns] * bf16(HEAD_DIM ** (-0.5))
        results = []
        for half in range(2):
            only = jnp.where(head_lanes(query.shape, half), query, 0)
            scores = []
            for begin, size, mask in spans(rows, high):
                part = dot_nt(only, qkv[pl.ds(begin, size), width + pair * 128 : width + pair * 128 + 128])
                scores.append(masked(part, start, begin) if mask else part)
            top = functools.reduce(jnp.maximum, [jnp.max(part, axis=-1, keepdims=True) for part in scores])
            total, result = 0.0, 0.0
            for (begin, size, _), part in zip(spans(rows, high), scores):
                weights = jnp.exp(part - top)
                total = total + jnp.sum(weights, axis=-1, keepdims=True)
                values = qkv[pl.ds(begin, size), 2 * width + pair * 128 : 2 * width + pair * 128 + 128]
                result = result + dot_nn(weights.astype(bf16), values)
            results.append(result / total)
            tops = jnp.where(lane == 2 * pair + half, top + jnp.log(total), tops)
        attended[here, columns] = jnp.where(head_lanes((rows, 128), 0), results[0], results[1]).astype(bf16)
    lse[here, :] = tops


def attention_forward(layer, stream, gains, shifts, w_qkv, w_out, own_qkv, own_out, weights, scale=None):
    rows, model = stream.shape
    width = own_out.shape[1]
    first = scale is not None
    early = {"qkv": own_qkv, "out": own_out} if first else {}

    def body(r):
        held, qkv, attended, lse, weight = r.held, r.qkv, r.attended, r.lse, r.weight
        w_qkv, w_out = (r.qkv_to, r.out_to) if first else (r.w_qkv, r.w_out)
        loads = [
            Loading(r.own_qkv.at[layer, index], w_qkv.at[index], weight.at[:, pl.ds(index * width, width)], r.local.at[index])
            for index in range(3)
        ]
        loads.append(Loading(r.own_out.at[layer], w_out, r.out, r.local.at[3]))
        if not first:
            every(loads, "start")
        greet(*GROUP, *(FETCH if weights else ()), *((("c", "zh"),) if first else ()))
        jobs = fetch_jobs(r, weights, layer)
        stream = r.stream
        if first:
            swap = Swapping(r.stream, r.landed, r.swap.at[0], r.swap.at[1])
            exchanged = remote(r.weight_in, r.other, r.swap.at[2], r.swap.at[3], flipped("c"))
            exchanged.start()
            before = [
                Fetching(source.at[layer], target, send, receive)
                for source, target, send, receive in (
                    (r.own_qkv, r.qkv_to, r.qkv_send, r.qkv_receive), (r.own_out, r.out_to, r.out_send, r.out_receive)
                )
            ]
            every(before, "step_inner")
            every(before, "step_outer")
            before[0].step_share()
            swap.start()
            before[0].step_relay()
            before[1].step_share()
            exchanged.wait()
            r.scale[...] = jnp.where(holds(), r.weight_in[...], r.other[...])
            swap.wait()
            swap.give(r.stream_out, r.stream)
            stream = r.stream_out
        own = places(rows)[0]
        held[pl.ds(own, rows), :] = norm_rows(stream[...], r.gains[layer, 0:1, :], r.shifts[layer, 0:1, :]).astype(bf16)
        if not first:
            every(loads, "wait")
        calls = []

        def arrived(start, size):
            calls.append(start)
            if len(calls) == 1:
                if first:
                    before[1].step_relay()
                    before[0].step_end()
                    every(loads[:3], "start")
                    every(loads[:3], "wait")
                else:
                    every(jobs[:1], "step_outer")
            if len(calls) == 2 and first:
                every(jobs, "step_outer")
            here = pl.ds(start, size)

            def step(columns):
                qkv[here, columns] = dot_nn(held[here, :], weight[:, columns]).astype(bf16)

            tiles(3 * width, step)

        sent = gather(rows, held, arrived, r.send, r.receive)
        stores = [pltpu.make_async_copy(held, r.held_out, r.local.at[0]), pltpu.make_async_copy(qkv, r.qkv_out, r.local.at[1])]
        for copy in stores:
            copy.start()
        zl = lax.axis_index("zl")

        def attend(quarter, high):
            attend_block(rows, pl.multiple_of(quarter * rows, 16), high, qkv, attended, lse)

        every(jobs if first else jobs[:1], "step_inner")
        if not first:
            every(jobs[1:], "step_outer")
        attend(3 - zl, True)
        if not first:
            every(jobs[1:], "step_inner")
        if first:
            before[1].step_end()
            loads[3].start()
        attend(1 - zl, False)
        if first:
            loads[3].wait()
        done = []

        def term(start, size, sink):
            if size == rows and not done:
                done.append(True)
                attend(2 + zl, True)
                every(jobs[:1], "step_share")
                attend(zl, False)
                every(jobs[:1], "step_relay")
            here = pl.ds(start, size)

            def step(columns):
                sink(columns, dot_nn(attended[here, :], r.out[:, columns]))

            tiles(model, step)

        finish = scatter(rows, term, r.first, r.sums, r.send, r.receive)
        late = [pltpu.make_async_copy(attended, r.attended_out, r.local.at[2]), pltpu.make_async_copy(lse, r.lse_out, r.local.at[3])]
        for copy in late:
            copy.start()
        every(jobs[1:], "step_share")
        finish()
        every(jobs[1:], "step_relay")
        total = r.first[pl.ds(0, rows), :] + r.sums[1].astype(f32) + r.sums[5].astype(f32)
        r.branch[...] = total
        r.middle[...] = stream[...] + norm_rows(total, r.gains[layer, 1:2, :], r.shifts[layer, 1:2, :])
        sent()
        every(jobs, "step_end")
        for copy in stores + late:
            copy.wait()

    return run(
        body,
        1 + layer,
        {
            "stream": (stream, VMEM), "gains": (gains, VMEM), "shifts": (shifts, VMEM), "own_qkv": (own_qkv, ANY), "own_out": (own_out, ANY),
            **fetch_inputs(weights), **({"weight_in": (scale, VMEM)} if first else {"w_qkv": (w_qkv, ANY), "w_out": (w_out, ANY)}),
        },
        {
            "branch": ((rows, model), f32, VMEM), "middle": ((rows, model), f32, VMEM),
            "held_out": ((4 * rows, model), bf16, ANY), "qkv_out": ((4 * rows, 3 * width), bf16, ANY),
            "attended_out": ((4 * rows, width), bf16, ANY), "lse_out": ((4 * rows, 128), f32, ANY), **fetch_outputs(weights),
            **fetch_outputs(early),
            **({"stream_out": (stream.shape, f32, VMEM), "scale": (scale.shape, f32, VMEM)} if first else {}),
        },
        {
            "held": VMEM((4 * rows, model), bf16), "qkv": VMEM((4 * rows, 3 * width), bf16), "attended": VMEM((4 * rows, width), bf16),
            "lse": VMEM((4 * rows, 128), f32), "weight": VMEM((model, 3 * width), bf16), "out": VMEM((width, model), bf16),
            **group_scratch(rows, model), "local": semaphores(4), **fetch_scratch(weights),
            **fetch_scratch(early),
            **({"landed": VMEM(stream.shape, bf16), "other": VMEM(scale.shape, f32), "swap": semaphores(4)} if first else {}),
        },
        24 * rows * model * width,
        64 * rows * rows,
    )


def attend_block_back(rows, start, high, qkv, attended_grad, lse, inner, grad_query, grad_key, grad_value):
    width = attended_grad.shape[1]
    here = pl.ds(start, rows)
    scale = HEAD_DIM ** (-0.5)
    for pair in range(width // 128):
        columns = slice(pair * 128, pair * 128 + 128)
        query = qkv[here, columns] * bf16(scale)
        above = attended_grad[here, columns]
        result = 0.0
        for half in range(2):
            head = 2 * pair + half
            only = jnp.where(head_lanes(query.shape, half), query, 0)
            grad = jnp.where(head_lanes(query.shape, half), above, 0)
            for begin, size, mask in spans(rows, high):
                keys = pl.ds(begin, size)
                key = qkv[keys, width + pair * 128 : width + pair * 128 + 128]
                value = qkv[keys, 2 * width + pair * 128 : 2 * width + pair * 128 + 128]
                scores = dot_nt(only, key)
                if mask:
                    scores = masked(scores, start, begin)
                probs = jnp.exp(scores - lse[here, head : head + 1])
                grad_probs = dot_nt(grad, value)
                grad_scores = (probs * (grad_probs - inner[here, head : head + 1])).astype(bf16)
                key_only = jnp.where(head_lanes(key.shape, half), key, 0)
                result = result + dot_nn(grad_scores, key_only)
                grad_key[keys, columns] += dot_tn(grad_scores, only)
                grad_value[keys, columns] += dot_tn(probs.astype(bf16), grad)
        grad_query[here, columns] = (result * scale).astype(bf16)


def attention_backward(layer, grad, stream, saved, gains, shifts, w_qkv, w_out, own_qkv, own_out, grads, norms=None):
    rows, model = stream.shape
    width = w_out.shape[0]
    final = norms is not None
    shape = jax.ShapeDtypeStruct
    mine = {"qkv_last": (shape(w_qkv.shape, bf16), 0, 2), "out_last": (shape(w_out.shape, bf16), 0, 2)} if final else {}

    def body(r):
        held, past, qkv, attended, lse, inner, above = r.held, r.past, r.qkv, r.attended, r.lse, r.inner, r.above
        pushed, grad_key, grad_value, weight = r.pushed, r.grad_key, r.grad_value, r.weight
        loads = [
            Loading(r.own_out.at[layer], r.w_out, r.out, r.local.at[3]),
            pltpu.make_async_copy(r.attended_in, attended, r.local.at[4]),
            pltpu.make_async_copy(r.qkv_in, qkv, r.local.at[5]),
            pltpu.make_async_copy(r.lse_in, lse, r.local.at[6]),
            *[
                Loading(r.own_qkv.at[layer, index], r.w_qkv.at[index], weight.at[:, pl.ds(index * width, width)], r.local.at[index])
                for index in range(3)
            ],
            pltpu.make_async_copy(r.held_in, past, r.local.at[7]),
        ]
        for copy in loads:
            copy.start()
        greet(*GROUP, *(FETCH if grads else ()), *((("c", "zh"),) if final else ()))
        jobs = pass_jobs(r, {**grads, **mine}, {"qkv_last": r.outcome, "out_last": r.outcome_out})
        new = [name for name in grads if grads[name][1] == 0]
        crossing = [name for name in grads if grads[name][1] == 1]
        every_of(jobs, crossing, "step_load")
        every_of(jobs, new[:1], "step_spread")
        own = places(rows)[0]
        pulled, gain_one, shift_one = norm_pull(r.branch[...], r.gains[layer, 1:2, :], r.grad[...])
        held[pl.ds(own, rows), :] = pulled.astype(bf16)
        grad_key[...] = jnp.zeros_like(grad_key)
        grad_value[...] = jnp.zeros_like(grad_value)
        for copy in loads:
            copy.wait()
        zl = lax.axis_index("zl")

        def back(quarter, high):
            attend_block_back(
                rows, pl.multiple_of(quarter * rows, 16), high, qkv, above, lse, inner, pushed, grad_key, grad_value
            )

        blocks = []

        def arrived(start, size):
            here = pl.ds(start, size)
            value = dot_nt(held[here, :], r.out[...]).astype(bf16)
            above[here, :] = value
            product = value.astype(f32) * attended[here, :].astype(f32)
            lane = lax.broadcasted_iota(jnp.int32, (size, 128), 1)
            tile = jnp.zeros((size, 128), f32)
            for pair in range(width // 128):
                part = product[:, pair * 128 : pair * 128 + 128]
                for half in range(2):
                    one = jnp.sum(jnp.where(head_lanes(part.shape, half), part, 0.0), axis=-1, keepdims=True)
                    tile = jnp.where(lane == 2 * pair + half, one, tile)
            inner[here, :] = tile
            blocks.append(size)
            if len(blocks) == 2:
                back(2 + zl, True)
                back(zl, False)

        sent = gather(rows, held, arrived, r.send, r.receive)
        every_of(jobs, crossing, "step_loaded", "step_outer")
        every_of(jobs, new[:1], "step_fold")
        every_of(jobs, new[1:], "step_spread")
        back(3 - zl, True)
        every_of(jobs, new[:1], "step_add")
        if not final:
            every_of(jobs, new[:1], "step_outer")
        every_of(jobs, crossing, "step_inner")
        back(1 - zl, False)
        if not final:
            every_of(jobs, new[:1], "step_inner")
        pushed[:, pl.ds(width, width)] = grad_key[...].astype(bf16)
        pushed[:, pl.ds(2 * width, width)] = grad_value[...].astype(bf16)

        def term(start, size, sink):
            here = pl.ds(start, size)

            def step(columns):
                sink(columns, dot_nt(pushed[here, :], weight[columns, :]))

            tiles(model, step)

        finish = scatter(rows, term, r.first, r.sums, r.send, r.receive)

        every_of(jobs, new[1:], "step_fold")
        if final:
            every_of(jobs, new[:1], "step_outer", "step_inner")

        def step_out(columns):
            r.outcome_out[:, columns] = dot_tn(attended[...], held[:, columns]).astype(bf16)

        tiles(model, step_out)
        outs = [] if final else [pltpu.make_async_copy(r.outcome_out, r.grad_out, r.local.at[0])]
        every(outs, "start")
        every_of(jobs, [name for name in mine if name == "out_last"], "step_spread")

        def step_qkv(columns):
            value = dot_tn(past[:, columns], pushed[...]).astype(bf16)
            for index in range(3):
                r.outcome[index, columns, :] = value[:, index * width : (index + 1) * width]

        tiles(model, step_qkv)
        if final:
            jobs["qkv_last"].step_spread()
            every_of(jobs, new[1:], "step_add", "step_outer", "step_inner")
            for name in crossing:
                every_of(jobs, [name], "step_join", "step_share")
        else:
            out = pltpu.make_async_copy(r.outcome, r.grad_qkv, r.local.at[1])
            out.start()
            outs.append(out)
            every_of(jobs, new[:1], "step_join")
            every_of(jobs, new[1:], "step_add")
            every_of(jobs, new, "step_store")
        finish()
        total = r.first[pl.ds(0, rows), :] + r.sums[1].astype(f32) + r.sums[5].astype(f32)
        pulled, gain_zero, shift_zero = norm_pull(r.stream[...], r.gains[layer, 0:1, :], total)
        rows_norms = (gain_zero, shift_zero, gain_one, shift_one)
        if final:
            r.home[...] = r.grad[...] + pulled
            r.low[...] = r.home[...].astype(bf16)
            swap = Swapping(r.low, r.landed, r.swap.at[0], r.swap.at[1])
            for index, value in enumerate(rows_norms):
                r.norms[index : index + 1, :] = value
            for index in range(len(norms)):
                r.norms[pl.ds(4 + 4 * index, 4), :] = getattr(r, f"norms{index}")[...]

            def cube(index, wait):
                copy = remote(
                    r.norms, r.norms_land.at[index], r.swap.at[2 + index], r.swap.at[7 + index], flipped(CUBE[index])
                )
                if not wait:
                    copy.start()
                    return
                copy.wait()
                r.norms[...] = r.norms[...] + r.norms_land[index]

            cube(0, False)
            every_of(jobs, mine, "step_fold")
            cube(0, True)
            cube(1, False)
            every_of(jobs, crossing, "step_relay")
            cube(1, True)
            cube(2, False)
            every_of(jobs, mine, "step_add", "step_outer", "step_inner")
            swap.start()
            every_of(jobs, crossing, "step_mate")
            cube(2, True)
            cube(3, False)
            every_of(jobs, new[:1], "step_join", "step_share")
            cube(3, True)
            cube(4, False)
            every_of(jobs, new[1:], "step_join", "step_share")
            every_of(jobs, new, "step_relay")
            every_of(jobs, new[:1], "step_mate")
            every_of(jobs, mine, "step_join", "step_share")
            every_of(jobs, new[1:], "step_mate")
            every_of(jobs, mine, "step_relay")
            every_of(jobs, mine, "step_mate")
            cube(4, True)
            swap.wait()
            swap.give(r.grad_stream, r.home)
        else:
            r.grad_stream[...] = r.grad[...] + pulled
            for index, value in enumerate(rows_norms):
                r.norms[index : index + 1, :] = value
        sent()
        every(outs, "wait")
        every_of(jobs, jobs, "step_end")

    return run(
        body,
        7 + layer,
        {
            "grad": (grad, VMEM), "branch": (saved.branch, VMEM), "stream": (stream, VMEM), "gains": (gains, VMEM),
            "shifts": (shifts, VMEM), "held_in": (saved.held_out, ANY), "qkv_in": (saved.qkv_out, ANY),
            "attended_in": (saved.attended_out, ANY), "lse_in": (saved.lse_out, ANY), "w_qkv": (w_qkv, ANY), "w_out": (w_out, ANY), "own_qkv": (own_qkv, ANY), "own_out": (own_out, ANY),
            **pass_inputs(grads), **({f"norms{index}": (value, VMEM) for index, value in enumerate(norms)} if final else {}),
        },
        {
            **pass_outputs({**grads, **mine}),
            "grad_stream": ((rows, model), f32, VMEM), "norms": ((16 if final else 4, model), f32, VMEM),
            **({} if final else {"grad_qkv": (w_qkv.shape, bf16, ANY), "grad_out": (w_out.shape, bf16, ANY)}),
        },
        {
            "held": VMEM((4 * rows, model), bf16), "past": VMEM((4 * rows, model), bf16), "qkv": VMEM((4 * rows, 3 * width), bf16),
            "attended": VMEM((4 * rows, width), bf16), "lse": VMEM((4 * rows, 128), f32), "inner": VMEM((4 * rows, 128), f32),
            "above": VMEM((4 * rows, width), bf16), "pushed": VMEM((4 * rows, 3 * width), bf16),
            "grad_key": VMEM((4 * rows, width), f32), "grad_value": VMEM((4 * rows, width), f32),
            "weight": VMEM((model, 3 * width), bf16), "out": VMEM(w_out.shape, bf16), "outcome": VMEM((3, model, width), bf16),
            "outcome_out": VMEM(w_out.shape, bf16), **group_scratch(rows, model), "local": semaphores(8),
            **pass_scratch({**grads, **mine}),
            **(
                {
                    "home": VMEM((rows, model), f32), "low": VMEM((rows, model), bf16), "landed": VMEM((rows, model), bf16),
                    "norms_land": VMEM((len(CUBE), 16, model), f32), "swap": semaphores(12),
                }
                if final
                else {}
            ),
        },
        60 * rows * model * width,
        64 * rows * rows,
    )


def per_device(hidden_in, cotangent, group_ids, group_sizes, w_qkv, w_out, w_up, w_down, gains, shifts):
    size = jnp.sum(jnp.where(jnp.arange(group_sizes.shape[0]) == group_ids[0], group_sizes, 0))
    weight = jnp.full((8, 128), 1.0 / size.astype(f32), f32)
    own_att, own_ffn = (w_qkv, w_out), (w_up, w_down)
    att_zero = attention_forward(
        0, hidden_in, gains, shifts, None, None, *own_att, {"up": w_up, "down": w_down}, weight
    )
    att_weights = [(att_zero.qkv_to, att_zero.out_to)]
    ffn_weights = [(att_zero.up_to, att_zero.down_to)]
    ffn_zero = ffn_forward(
        0, att_zero.middle, gains, shifts, *ffn_weights[0], *own_ffn, {"qkv": w_qkv, "out": w_out}
    )
    att_weights.append((ffn_zero.qkv_to, ffn_zero.out_to))
    att_one = attention_forward(1, ffn_zero.stream, gains, shifts, *att_weights[1], *own_att, {"up": w_up, "down": w_down})
    ffn_weights.append((att_one.up_to, att_one.down_to))
    ffn_one = ffn_forward(
        1, att_one.middle, gains, shifts, *ffn_weights[1], *own_ffn, {}, cotangent, att_zero.scale
    )
    ffn_zero.middle, ffn_one.middle = att_zero.middle, att_one.middle
    back_one = ffn_backward(1, ffn_one.grad, ffn_one, gains, shifts, *ffn_weights[1], *own_ffn, {}, ffn_one.stream)
    deep_one = attention_backward(
        1, back_one.grad_middle, ffn_zero.stream, att_one, gains, shifts, *att_weights[1], *own_att,
        {"up1": (back_one.grad_up, 0, 1), "down1": (back_one.grad_down, 0, 0)},
    )
    back_zero = ffn_backward(
        0, deep_one.grad_stream, ffn_zero, gains, shifts, *ffn_weights[0], *own_ffn,
        {"up1": (deep_one.up1_out, 2, 2), "down1": (deep_one.down1_out, 1, 2), "qkv1": (deep_one.grad_qkv, 0, 0), "out1": (deep_one.grad_out, 0, 0)},
    )
    last = attention_backward(
        0, back_zero.grad_middle, att_zero.stream_out, att_zero, gains, shifts, *att_weights[0], *own_att,
        {
            "qkv1": (back_zero.qkv1_out, 1, 2), "out1": (back_zero.out1_out, 1, 2),
            "up0": (back_zero.grad_up, 0, 2), "down0": (back_zero.grad_down, 0, 2),
        },
        (back_zero.norms, deep_one.norms, back_one.norms),
    )
    grads = [
        jnp.stack(pair).astype(f32)
        for pair in (
            (last.qkv_last_out, last.qkv1_out),
            (last.out_last_out, last.out1_out),
            (last.up0_out, back_zero.up1_out),
            (last.down0_out, back_zero.down1_out),
        )
    ]
    sums = last.norms.reshape(2, 4, 2, -1)
    if lax.axis_size("gh") > 1:
        grads, sums = lax.psum((grads, sums), "gh")
    return (back_one.mixed_out, last.grad_stream, *grads, sums[:, :, 0], sums[:, :, 1])


def solution(mesh):
    fine = jax.sharding.Mesh(mesh.devices.reshape(-1, 2, 2, 2, 2, 2), AXES)
    dp = ("gh", "gl", "p", "c")
    tensor = ("zh", "zl")
    rows = P((*dp, *tensor), None)
    weights = (
        P(None, None, None, tensor),
        P(None, tensor, None),
        P(None, None, tensor),
        P(None, tensor, None),
    )
    return jax.shard_map(
        per_device,
        mesh=fine,
        in_specs=(rows, rows, P(dp), P(), *weights, P(), P()),
        out_specs=(rows, rows, *weights, P(), P()),
        check_vma=False,
    )
```

```python
import functools
import types

import jax
import jax.numpy as jnp
from jax import lax
from jax.experimental import pallas as pl
from jax.experimental.pallas import tpu as pltpu
from jax.sharding import PartitionSpec as P

HEAD_DIM = 64
AXES = ("gh", "gl", "p", "c", "zh", "zl")
f32 = jnp.float32
bf16 = jnp.bfloat16
MESH = pl.DeviceIdType.MESH
VMEM, ANY = pltpu.VMEM, pl.ANY
eps_norm = 1e-05
TILE = 256


def centre(values):
    mean = jnp.mean(values, axis=-1, keepdims=True)
    centred = values - mean
    spread = jnp.mean(centred * centred, axis=-1, keepdims=True)
    rate = lax.rsqrt(spread + eps_norm)
    return centred * rate, rate


def norm_rows(values, gain, shift):
    return centre(values)[0] * gain + shift


def norm_pull(values, gain, grad):
    hat, rate = centre(values)
    scaled = grad * gain
    along = jnp.mean(scaled * hat, axis=-1, keepdims=True)
    level = jnp.mean(scaled, axis=-1, keepdims=True)
    return (
        rate * (scaled - level - hat * along),
        jnp.sum(grad * hat, axis=0, keepdims=True),
        jnp.sum(grad, axis=0, keepdims=True),
    )


def dot_nt(left, right):
    return lax.dot_general(left, right, (((1,), (1,)), ((), ())), preferred_element_type=f32)


def dot_tn(left, right):
    return lax.dot_general(left, right, (((0,), (0,)), ((), ())), preferred_element_type=f32)


def dot_nn(left, right):
    return jnp.dot(left, right, preferred_element_type=f32)


def cut_rows(rows):
    first = (rows // 2 + 15) // 16 * 16
    return ((0, first), (first, rows - first))


def flipped(*names):
    return {name: 1 - lax.axis_index(name) for name in names}


def greet(*others):
    barrier = pltpu.get_barrier_semaphore()
    for names in others:
        pl.semaphore_signal(barrier, inc=1, device_id=flipped(*names), device_id_type=MESH)
    pl.semaphore_wait(barrier, len(others))


GROUP = (("c",), ("zl",))
FETCH = (("zh",), ("p",), ("gl",))


def remote(source, target, send, receive, device):
    return pltpu.make_async_remote_copy(
        src_ref=source,
        dst_ref=target,
        send_sem=send,
        recv_sem=receive,
        device_id=device,
        device_id_type=MESH,
    )


def tiles(width, body):
    def step(index, carry):
        body(pl.ds(pl.multiple_of(index * TILE, TILE), TILE))
        return carry

    lax.fori_loop(0, width // TILE, step, 0)


def exchange(rows, held, prepare, work, first, sums, send, receive):
    mate, near = flipped("c"), flipped("zl")
    own = pl.ds(0, rows)
    parts = cut_rows(rows)
    along = []
    for index, (start, size) in enumerate(parts):
        prepare(start, size)
        place = pl.ds(2 * rows + 2 * start, size)
        copy = remote(held.at[pl.ds(start, size)], held.at[place], send.at[1 + index], receive.at[1 + index], near)
        copy.start()
        along.append(copy)
    copies = [remote(held.at[own], held.at[pl.ds(rows, rows)], send.at[0], receive.at[0], mate)]
    copies[0].start()

    def keep(row, columns, value):
        first[pl.ds(row, value.shape[0]), columns] = value

    work(0, rows, keep)
    copies[0].wait_recv()

    def keep_mate(row, columns, value):
        sums[0, pl.ds(row - rows, value.shape[0]), columns] = value.astype(bf16)

    work(rows, rows, keep_mate)
    back = remote(sums.at[0], sums.at[1], send.at[3], receive.at[3], mate)
    back.start()
    copies.append(back)
    final = []
    for index, (start, size) in enumerate(parts):
        place = 2 * rows + 2 * start
        along[index].wait_recv()
        relay = remote(
            held.at[pl.ds(place, size)], held.at[pl.ds(place + size, size)], send.at[4 + index], receive.at[4 + index], mate
        )
        relay.start()
        relay.wait_recv()

        def keep_far(row, columns, value, place=place, start=start, size=size):
            first[pl.ds(rows + start, size), columns] = value[:size]
            sums[2, pl.ds(start, size), columns] = value[size:].astype(bf16)

        work(place, 2 * size, keep_far)
        part = pl.ds(start, size)
        cross = remote(sums.at[2, part], sums.at[3, part], send.at[6 + index], receive.at[6 + index], mate)
        cross.start()
        cross.wait_recv()
        sums[4, part, :] = (first[pl.ds(rows + start, size), :] + sums[3, part, :].astype(f32)).astype(bf16)
        last = remote(sums.at[4, part], sums.at[5, part], send.at[8 + index], receive.at[8 + index], near)
        last.start()
        final.append(last)
        copies += [relay, cross]

    def finish(done):
        back.wait_recv()
        for copy, (start, size) in zip(final, parts):
            copy.wait_recv()
            done(start, size, summed(first, sums, start, size))
        every(copies + along + final, "wait_send")

    return finish


def summed(first, sums, start, size):
    part = pl.ds(start, size)
    return first[part, :] + sums[1, part, :].astype(f32) + sums[5, part, :].astype(f32)


def run(body, number, inputs, outputs, scratch, flops, transcendentals=0):
    copied = [name for name, (_, memory) in inputs.items() if memory is VMEM]
    own = {name: VMEM(inputs[name][0].shape, inputs[name][0].dtype) for name in copied}
    names = [*inputs, *outputs, *scratch, *(name + "_copy" for name in copied), "arrivals"]

    def kernel(*refs):
        found = dict(zip(names, refs))
        copies = [
            pltpu.make_async_copy(found[name], found[name + "_copy"], found["arrivals"].at[index])
            for index, name in enumerate(copied)
        ]
        every(copies, "start")
        found.update({name: found[name + "_copy"] for name in copied})
        body(types.SimpleNamespace(**found, ready=lambda: every(copies, "wait")))

    moved = sum(value.size * value.dtype.itemsize for value, _ in inputs.values())
    results = pl.pallas_call(
        kernel,
        out_shape=tuple(jax.ShapeDtypeStruct(shape, kind) for shape, kind, _ in outputs.values()),
        in_specs=[pl.BlockSpec(memory_space=ANY) for _ in inputs],
        out_specs=tuple(pl.BlockSpec(memory_space=memory) for _, _, memory in outputs.values()),
        scratch_shapes=[*scratch.values(), *own.values(), semaphores(len(copied))],
        compiler_params=pltpu.CompilerParams(collective_id=number, has_side_effects=True, vmem_limit_bytes=58 << 20),
        cost_estimate=pl.CostEstimate(flops=flops, bytes_accessed=moved, transcendentals=transcendentals),
    )(*[value for value, _ in inputs.values()])
    return types.SimpleNamespace(**dict(zip(outputs, results)))


def semaphores(count):
    return pltpu.SemaphoreType.DMA((count,))


def group_scratch(rows, width):
    return {
        "first": VMEM((2 * rows, width), f32),
        "sums": VMEM((6, rows, width), bf16),
        "send": semaphores(10),
        "receive": semaphores(10),
    }


def pick(ref, rows):
    return ref.at[:, rows, :] if len(ref.shape) == 3 else ref.at[rows, :]


def part_shape(shape, parts):
    return (*shape[:-2], int(shape[-2] / parts), shape[-1])


def inner():
    return lax.axis_index("zl") != lax.axis_index("zh")


def holds():
    return lax.axis_index("c") == lax.axis_index("zh")


def fetch_jobs(refs, names, layer):
    return [
        Fetching(
            getattr(refs, name + "_from").at[layer], getattr(refs, name + "_to"), getattr(refs, name + "_send"),
            getattr(refs, name + "_receive"),
        )
        for name in names
    ]


def fetch_inputs(weights):
    return {name + "_from": (value, ANY) for name, value in weights.items()}


def fetch_outputs(weights):
    return {name + "_to": (value.shape[1:], bf16, ANY) for name, value in weights.items()}


def fetch_scratch(weights):
    result = {}
    for name in weights:
        result[name + "_send"] = semaphores(8)
        result[name + "_receive"] = semaphores(8)
    return result


class Loading:
    def __init__(self, own, fetched, target, semaphore):
        self.ways = [pltpu.make_async_copy(source, target, semaphore) for source in (own, fetched)]

    def start(self):
        pl.when(holds())(self.ways[0].start)
        pl.when(jnp.logical_not(holds()))(self.ways[1].start)

    def wait(self):
        pl.when(holds())(self.ways[0].wait)
        pl.when(jnp.logical_not(holds()))(self.ways[1].wait)


def every(jobs, step):
    for job in jobs:
        getattr(job, step)()


CUBE = ("c", "zl", "p", "gl", "zh")
ORDERS = (("p", "gl"), ("gl", "p"))


class Halves:
    def copy(self, slot, source, target, name):
        return remote(source, target, self.send.at[slot], self.receive.at[slot], flipped(name))

    def at(self, half, first, second=None):
        start = (4 * half + 2 * first) * self.size
        if second is None:
            return pl.ds(pl.multiple_of(start, 16), 2 * self.size)
        return pl.ds(pl.multiple_of(start + second * self.size, 16), self.size)


class Fetching(Halves):
    def __init__(self, source, target, send, receive):
        self.source, self.target, self.send, self.receive = source, target, send, receive
        self.size = source.shape[-2] // 8

    def own(self, half):
        return self.at(half, *[lax.axis_index(name) for name in ORDERS[half]])

    def quarter(self, half):
        return pick(self.target, self.own(half))

    def along(self, half):
        return self.copy(half, pick(self.source, self.own(half)), self.quarter(half), "zh")

    def direct(self, half, axis):
        rows = self.quarter(half)
        return self.copy(2 + 2 * half + axis, rows, rows, ORDERS[half][axis])

    def relay(self, half):
        first, second = ORDERS[half]
        rows = pick(self.target, self.at(half, lax.axis_index(first), 1 - lax.axis_index(second)))
        return self.copy(6 + half, rows, rows, first)

    def start_along(self, here):
        @pl.when(jnp.logical_and(holds(), here))
        def _():
            for half in range(2):
                self.along(half).start()

    def step_inner(self):
        self.start_along(inner())

    def step_outer(self):
        self.start_along(jnp.logical_not(inner()))

    def step_sent(self):
        @pl.when(holds())
        def _():
            for half in range(2):
                self.along(half).wait_send()

    def share_if(self, here):
        @pl.when(jnp.logical_and(jnp.logical_not(holds()), here))
        def _():
            for half in range(2):
                self.along(half).wait_recv()
                self.direct(half, 1).start()
                self.direct(half, 0).start()

    def step_share(self):
        self.share_if(True)

    def step_share_outer(self):
        self.share_if(jnp.logical_not(inner()))

    def step_share_inner(self):
        self.share_if(inner())

    def step_relay(self):
        @pl.when(jnp.logical_not(holds()))
        def _():
            for half in range(2):
                self.direct(half, 1).wait_recv()
                self.relay(half).start()

    def step_got(self):
        @pl.when(jnp.logical_not(holds()))
        def _():
            for half in range(2):
                self.direct(half, 0).wait()
                self.direct(half, 1).wait_send()
                self.relay(half).wait()

    def step_end(self):
        self.step_sent()
        self.step_got()


class Passing(Halves):
    def __init__(self, refs, name, first, last, source=None, out=None):
        self.first, self.last = first, last
        for field in ("in", "out", "land", "mine", "more", "sum", "cross", "send", "receive", "local"):
            setattr(self, field, getattr(refs, f"{name}_{field}", None))
        self.source = source if source is not None else getattr(refs, f"{name}_in", None)
        if out is not None:
            self.out = out
        self.size = self.sum.shape[-2] // 2

    def place_of(self, half):
        return [lax.axis_index(name) for name in ORDERS[half]]

    def spread(self, half):
        name = ORDERS[half][0]
        return self.copy(half, pick(self.source, self.at(half, 1 - lax.axis_index(name))), self.land.at[half], name)

    def keep(self, half):
        rows = self.at(half, lax.axis_index(ORDERS[half][0]))
        return pltpu.make_async_copy(pick(self.source, rows), self.mine.at[half], self.local.at[half])

    def second(self, index):
        return pl.ds(pl.multiple_of(index * self.size, 16), self.size)

    def fold(self, half):
        name = ORDERS[half][1]
        return self.copy(2 + half, pick(self.mine.at[half], self.second(1 - lax.axis_index(name))), self.more.at[half], name)

    def load(self):
        return pltpu.make_async_copy(self.source, self.sum, self.local.at[2])

    def store(self):
        return pltpu.make_async_copy(self.sum, self.out, self.local.at[2])

    def along(self):
        return self.copy(4, self.sum, self.cross, "zh")

    def own(self, half):
        return pick(self.sum, pl.ds(half * self.size, self.size))

    def place(self, half):
        return pltpu.make_async_copy(self.own(half), pick(self.out, self.at(half, *self.place_of(half))), self.local.at[half])

    def direct(self, half, axis):
        own = pick(self.out, self.at(half, *self.place_of(half)))
        return self.copy(5 + 2 * half + axis, self.own(half), own, ORDERS[half][axis])

    def relay(self, half):
        first, second = self.place_of(half)
        rows = pick(self.out, self.at(half, first, 1 - second))
        return self.copy(9 + half, rows, rows, ORDERS[half][0])

    def mate(self, half, index):
        first = self.place_of(half)[0]
        rows = pick(self.out, self.at(half, first if index == 0 else 1 - first))
        return self.copy(11 + 2 * half + index, rows, rows, "c")

    def step_spread(self):
        for half in range(2):
            self.spread(half).start()
            self.keep(half).start()

    def step_fold(self):
        for half in range(2):
            self.keep(half).wait()
            self.spread(half).wait_recv()
            self.mine[half] = (self.mine[half].astype(f32) + self.land[half].astype(f32)).astype(bf16)
            self.fold(half).start()

    def step_add(self):
        for half in range(2):
            self.fold(half).wait_recv()
            own = pick(self.mine.at[half], self.second(lax.axis_index(ORDERS[half][1])))
            self.own(half)[...] = (own[...].astype(f32) + self.more[half].astype(f32)).astype(bf16)

    def step_load(self):
        self.load().start()

    def step_loaded(self):
        self.load().wait()

    def step_inner(self):
        pl.when(jnp.logical_and(jnp.logical_not(holds()), inner()))(self.along().start)

    def step_outer(self):
        pl.when(jnp.logical_not(jnp.logical_or(holds(), inner())))(self.along().start)

    def join_if(self, here):
        @pl.when(jnp.logical_and(holds(), here))
        def _():
            self.along().wait_recv()
            self.sum[...] = (self.sum[...].astype(f32) + self.cross[...].astype(f32)).astype(bf16)
            if self.last == 2:
                for half in range(2):
                    self.direct(half, 1).start()
                    self.direct(half, 0).start()
                    self.place(half).start()

    def step_join_outer(self):
        self.join_if(jnp.logical_not(inner()))

    def step_join_inner(self):
        self.join_if(inner())

    def step_join(self):
        self.join_if(True)

    def step_share(self):
        @pl.when(holds())
        def _():
            for half in range(2):
                self.direct(half, 1).start()
                self.direct(half, 0).start()
                self.place(half).start()

    def step_relay(self):
        @pl.when(holds())
        def _():
            for half in range(2):
                self.direct(half, 1).wait_recv()
                self.relay(half).start()
                self.place(half).wait()
                self.mate(half, 0).start()

    def step_mate(self):
        @pl.when(holds())
        def _():
            for half in range(2):
                self.direct(half, 0).wait_recv()
                self.relay(half).wait_recv()
                self.mate(half, 1).start()

    def step_store(self):
        self.store().start()

    def step_end(self):
        if self.first == 0:
            for half in range(2):
                self.spread(half).wait_send()
                self.fold(half).wait_send()
        if self.last < 2:
            self.store().wait()

        @pl.when(holds())
        def _():
            if self.last == 2:
                for half in range(2):
                    self.direct(half, 0).wait_send()
                    self.direct(half, 1).wait_send()
                    self.relay(half).wait_send()
                    self.mate(half, 0).wait_send()
                    self.mate(half, 1).wait_send()

        @pl.when(jnp.logical_not(holds()))
        def _():
            if self.first <= 1 <= self.last:
                self.along().wait_send()
            if self.last == 2:
                for half in range(2):
                    self.mate(half, 0).wait_recv()
                    self.mate(half, 1).wait_recv()


def pass_shapes(grads):
    for name, (value, first, last) in grads.items():
        whole = value.shape if first == 0 else part_shape(value.shape, 1 / 4)
        yield name, whole, part_shape(whole, 4), first, last


def pass_jobs(refs, grads, ends=None):
    return {name: Passing(refs, name, first, last, *(ends or {}).get(name, ())) for name, (_, first, last) in grads.items()}


def pass_inputs(grads):
    return {name + "_in": (value, ANY) for name, (value, *_) in grads.items() if isinstance(value, jax.Array)}


def pass_outputs(grads):
    return {name + "_out": (whole if last == 2 else part, bf16, ANY) for name, whole, part, first, last in pass_shapes(grads)}


def pass_scratch(grads):
    result = {}
    for name, whole, part, first, last in pass_shapes(grads):
        if first == 0:
            result[name + "_land"] = VMEM((2, *part), bf16)
            result[name + "_mine"] = VMEM((2, *part), bf16)
            result[name + "_more"] = VMEM((2, *part_shape(whole, 8)), bf16)
        result[name + "_sum"] = VMEM(part, bf16)
        if first <= 1 <= last:
            result[name + "_cross"] = VMEM(part, bf16)
        result[name + "_send"] = semaphores(15)
        result[name + "_receive"] = semaphores(15)
        result[name + "_local"] = semaphores(3)
    return result


def every_of(jobs, names, *steps):
    for step in steps:
        for name in names:
            getattr(jobs[name], step)()


class Swapping:
    def __init__(self, source, landed, semaphores):
        self.source, self.landed = source, landed
        self.parts = cut_rows(source.shape[0])
        self.copies = [
            remote(
                source.at[pl.ds(start, size)], landed.at[pl.ds(start, size)], semaphores.at[index], semaphores.at[2 + index],
                flipped("c", "zh"),
            )
            for index, (start, size) in enumerate(self.parts)
        ]

    def start_if(self, here):
        @pl.when(here)
        def _():
            every(self.copies, "start")

    def start(self):
        self.start_if(jnp.logical_not(holds()))

    def step_inner(self):
        self.start_if(jnp.logical_and(jnp.logical_not(holds()), inner()))

    def step_outer(self):
        self.start_if(jnp.logical_not(jnp.logical_or(holds(), inner())))

    def give(self, target, own, scale=None, only=(0, 1)):
        factor = 1.0 if scale is None else scale
        for index in only:
            rows = pl.ds(*self.parts[index])

            @pl.when(holds())
            def _(rows=rows):
                target[rows, :] = own[rows, :].astype(f32) * factor

            @pl.when(jnp.logical_not(holds()))
            def _(index=index, rows=rows):
                self.copies[index].wait_recv()
                target[rows, :] = self.landed[rows, :].astype(f32) * factor

    def end(self):
        @pl.when(jnp.logical_not(holds()))
        def _():
            every(self.copies, "wait_send")


def gelu_and_slope(values):
    rate, cubic = 0.7978845608028654, 0.044715
    square = values * values
    bend = jnp.tanh(rate * values * (1.0 + cubic * square))
    half = 0.5 * (1.0 + bend)
    slope = half + 0.5 * values * (1.0 - bend * bend) * (rate * (1.0 + 3.0 * cubic * square))
    return values * half, slope


def ffn_forward(layer, middle, gains, shifts, w_up, w_down, own_up, own_down, weights, cotangent=None, scale=None):
    rows, width = middle.shape
    hidden = w_up.shape[1]

    def body(r):
        loads = [Loading(r.own_up.at[layer], r.w_up, r.up, r.local.at[0]), Loading(r.own_down.at[layer], r.w_down, r.down, r.local.at[1])]
        for copy in loads:
            copy.start()
        greet(*GROUP, *(FETCH if weights else ()), *(() if cotangent is None else (("c", "zh"),)))
        r.ready()
        jobs = fetch_jobs(r, weights, layer + 1)
        swaps = [] if cotangent is None else [Swapping(r.cotangent, r.landed, r.swap)]
        every(jobs + swaps, "step_inner")
        held, active, slope = r.held, r.active, r.slope

        def prepare(start, size):
            part = pl.ds(start, size)
            held[part, :] = norm_rows(r.middle[part, :], r.gains[layer, 2:3, :], r.shifts[layer, 2:3, :]).astype(bf16)

        calls = []

        def work(start, size, sink):
            calls.append(start)
            if len(calls) == 1:
                every(jobs + swaps, "step_outer")
                every(loads, "wait")
            if len(calls) == 3:
                every(jobs, "step_share_outer")
            if len(calls) == 4:
                every(jobs, "step_share_inner")
            here = pl.ds(start, size)

            def step(columns):
                upper = dot_nn(held[here, :], r.up[:, columns])
                value, bend = gelu_and_slope(upper)
                active[here, columns] = value.astype(bf16)
                slope[here, columns] = bend.astype(bf16)

            tiles(hidden, step)

            def step_down(columns):
                sink(start, columns, dot_nn(active[here, :], r.down[:, columns]))

            tiles(width, step_down)

        finish = exchange(rows, held, prepare, work, r.first, r.sums, r.send, r.receive)
        stores = [
            pltpu.make_async_copy(held, r.held_out, r.local.at[2]),
            pltpu.make_async_copy(active, r.active_out, r.local.at[3]),
            pltpu.make_async_copy(slope, r.slope_out, r.local.at[4]),
        ]
        for copy in stores:
            copy.start()
        every(jobs, "step_relay")

        def done(start, size, total):
            part = pl.ds(start, size)
            r.second[part, :] = total
            r.stream[part, :] = r.middle[part, :] + norm_rows(total, r.gains[layer, 3:4, :], r.shifts[layer, 3:4, :])

        finish(done)
        every(jobs, "step_end")
        for swap in swaps:
            swap.give(r.grad, r.cotangent, r.scale[0:1, 0:1])
            swap.end()
        for copy in stores:
            copy.wait()

    return run(
        body,
        3 + layer,
        {
            "middle": (middle, VMEM), "gains": (gains, VMEM), "shifts": (shifts, VMEM), "w_up": (w_up, ANY), "w_down": (w_down, ANY), "own_up": (own_up, ANY), "own_down": (own_down, ANY),
            **fetch_inputs(weights), **({} if cotangent is None else {"cotangent": (cotangent, VMEM), "scale": (scale, VMEM)}),
        },
        {
            "second": ((rows, width), f32, VMEM), "stream": ((rows, width), f32, VMEM),
            "held_out": ((4 * rows, width), bf16, ANY), "active_out": ((4 * rows, hidden), bf16, ANY),
            "slope_out": ((4 * rows, hidden), bf16, ANY), **fetch_outputs(weights),
            **({} if cotangent is None else {"grad": ((rows, width), f32, VMEM)}),
        },
        {
            "held": VMEM((4 * rows, width), bf16), "active": VMEM((4 * rows, hidden), bf16), "slope": VMEM((4 * rows, hidden), bf16),
            "up": VMEM(w_up.shape, bf16), "down": VMEM(w_down.shape, bf16), **group_scratch(rows, width), "local": semaphores(5),
            **fetch_scratch(weights),
            **({} if cotangent is None else {"landed": VMEM(cotangent.shape, bf16), "swap": semaphores(4)}),
        },
        16 * rows * width * hidden,
        4 * rows * hidden,
    )


def ffn_backward(layer, grad, saved, gains, shifts, w_up, w_down, own_up, own_down, grads):
    middle = saved.middle
    rows, width = middle.shape
    hidden = w_up.shape[1]

    def body(r):
        held, active, slope, pushed, past = r.held, r.active, r.slope, r.pushed, r.past
        loads = [
            Loading(r.own_down.at[layer], r.w_down, r.down, r.local.at[0]),
            Loading(r.own_up.at[layer], r.w_up, r.up, r.local.at[1]),
            pltpu.make_async_copy(r.slope_in, slope, r.local.at[2]),
            pltpu.make_async_copy(r.active_in, active, r.local.at[3]),
            pltpu.make_async_copy(r.held_in, past, r.local.at[4]),
        ]
        for copy in loads:
            copy.start()
        greet(*GROUP, *(FETCH if grads else ()))
        jobs = pass_jobs(r, grads)
        new = [name for name in grads if grads[name][1] == 0]
        late = [name for name in grads if grads[name][1] == 2]
        r.ready()
        crossing = [name for name in grads if grads[name][1] == 1]
        every_of(jobs, crossing, "step_load", "step_loaded", "step_inner")
        every_of(jobs, late, "step_load")
        every_of(jobs, new, "step_spread")
        norms = {}

        def pull(row, values, part, grad):
            pulled, *sums = norm_pull(values[part, :], r.gains[layer, row : row + 1, :], grad)
            norms[row] = [old + new for old, new in zip(norms.get(row, (0.0, 0.0)), sums)]
            return pulled

        def prepare(start, size):
            part = pl.ds(start, size)
            held[part, :] = pull(3, r.second, part, r.grad[part, :]).astype(bf16)

        calls = []

        def work(start, size, sink):
            calls.append(start)
            if len(calls) == 1:
                every_of(jobs, crossing, "step_outer")
                every_of(jobs, late, "step_loaded", "step_share")
                every(loads, "wait")
            if len(calls) == 4:
                every_of(jobs, new, "step_fold")
                every_of(jobs, crossing, "step_join_outer")
            here = pl.ds(start, size)

            def step(columns):
                value = dot_nt(held[here, :], r.down[columns, :])
                pushed[here, columns] = (value * slope[here, columns].astype(f32)).astype(bf16)

            tiles(hidden, step)

            def step_up(columns):
                sink(start, columns, dot_nt(pushed[here, :], r.up[columns, :]))

            tiles(width, step_up)

        finish = exchange(rows, held, prepare, work, r.first, r.sums, r.send, r.receive)

        every_of(jobs, late, "step_relay")
        every_of(jobs, crossing, "step_join_inner")

        def step_down(columns):
            r.outcome[0, columns, :] = dot_tn(active[:, columns], held[...]).astype(bf16)

        tiles(hidden, step_down)
        out_down = pltpu.make_async_copy(r.outcome.at[0], r.grad_down, r.local.at[0])
        out_down.start()
        def step_up(columns):
            r.outcome[1, columns, :] = dot_tn(past[:, columns], pushed[...]).astype(bf16)

        tiles(width, step_up)
        out_up = pltpu.make_async_copy(r.outcome.at[1], r.grad_up, r.local.at[1])
        out_up.start()
        every_of(jobs, new, "step_add", "step_store")
        every_of(jobs, crossing, "step_relay")
        every_of(jobs, late, "step_mate")

        def done(start, size, total):
            part = pl.ds(start, size)
            r.grad_middle[part, :] = r.grad[part, :] + pull(2, r.middle, part, total)

        finish(done)
        every_of(jobs, crossing, "step_mate")
        for index, value in enumerate((*norms[2], *norms[3])):
            r.norms[index : index + 1, :] = value
        out_down.wait()
        out_up.wait()
        every_of(jobs, grads, "step_end")

    return run(
        body,
        5 + layer,
        {
            "grad": (grad, VMEM), "second": (saved.second, VMEM), "middle": (middle, VMEM), "gains": (gains, VMEM),
            "shifts": (shifts, VMEM), "held_in": (saved.held_out, ANY), "active_in": (saved.active_out, ANY),
            "slope_in": (saved.slope_out, ANY), "w_up": (w_up, ANY), "w_down": (w_down, ANY), "own_up": (own_up, ANY), "own_down": (own_down, ANY),
            **pass_inputs(grads),
        },
        {
            **pass_outputs(grads),
            "grad_middle": ((rows, width), f32, VMEM), "norms": ((4, width), f32, VMEM),
            "grad_up": (w_up.shape, bf16, ANY), "grad_down": (w_down.shape, bf16, ANY),
        },
        {
            "held": VMEM((4 * rows, width), bf16), "past": VMEM((4 * rows, width), bf16),
            "active": VMEM((4 * rows, hidden), bf16), "slope": VMEM((4 * rows, hidden), bf16),
            "pushed": VMEM((4 * rows, hidden), bf16), "up": VMEM(w_up.shape, bf16), "down": VMEM(w_down.shape, bf16),
            "outcome": VMEM((2, width, hidden), bf16), **group_scratch(rows, width), "local": semaphores(5),
            **pass_scratch(grads),
        },
        32 * rows * width * hidden,
    )


def places(rows):
    c, zl = lax.axis_index("c"), lax.axis_index("zl")

    def at(core, part):
        return pl.multiple_of((2 * core + part) * rows, 16)

    return at(c, zl), at(1 - c, zl), at(c, 1 - zl), at(1 - c, 1 - zl)


def gather(rows, held, prepare, arrived, send, receive):
    mate, near = flipped("c"), flipped("zl")
    own, others, along, across = places(rows)
    parts = cut_rows(rows)
    copies = []
    for index, (start, size) in enumerate(parts):
        prepare(start, size)
        part = pl.ds(pl.multiple_of(own + start, 16), size)
        copy = remote(held.at[part], held.at[part], send.at[1 + index], receive.at[1 + index], near)
        copy.start()
        copies.append(copy)
    here = pl.ds(own, rows)
    copies.append(remote(held.at[here], held.at[here], send.at[0], receive.at[0], mate))
    copies[-1].start()
    arrived(own, rows)
    copies[-1].wait_recv()
    arrived(others, rows)
    for index, (start, size) in enumerate(parts):
        copies[index].wait_recv()
        first = pl.multiple_of(along + start, 16)
        part = pl.ds(first, size)
        relay = remote(held.at[part], held.at[part], send.at[4 + index], receive.at[4 + index], mate)
        relay.start()
        copies.append(relay)
        arrived(first, size)
        relay.wait_recv()
        arrived(pl.multiple_of(across + start, 16), size)

    def finish():
        every(copies, "wait_send")

    return finish


def scatter(rows, before, project, first, sums, send, receive):
    mate, near = flipped("c"), flipped("zl")
    own, others, _, _ = places(rows)
    parts = cut_rows(rows)
    crossing = [
        remote(sums.at[2, pl.ds(start, size)], sums.at[3, pl.ds(start, size)], send.at[6 + index], receive.at[6 + index], mate)
        for index, (start, size) in enumerate(parts)
    ]
    final = [
        remote(sums.at[4, pl.ds(start, size)], sums.at[5, pl.ds(start, size)], send.at[8 + index], receive.at[8 + index], near)
        for index, (start, size) in enumerate(parts)
    ]
    for half, name in ((1, "high"), (0, "low")):
        before(name)
        base = pl.multiple_of((2 * half + 1 - lax.axis_index("zl")) * rows, 16)
        far = lax.axis_index("c") != half
        for index, (start, size) in enumerate(parts):

            def keep(columns, value, start=start, size=size):
                first[pl.ds(rows + start, size), columns] = value

            project(pl.multiple_of(base + start, 16), size, keep)

            @pl.when(far)
            def _(index=index, start=start, size=size):
                sums[2, pl.ds(start, size), :] = first[pl.ds(rows + start, size), :].astype(bf16)
                crossing[index].start()

        @pl.when(jnp.logical_not(far))
        def _():
            for index, (start, size) in enumerate(parts):
                crossing[index].wait_recv()
                part = pl.ds(start, size)
                sums[4, part, :] = (first[pl.ds(rows + start, size), :] + sums[3, part, :].astype(f32)).astype(bf16)
                final[index].start()

    before("rest")

    def keep_mate(columns, value):
        sums[0, :, columns] = value.astype(bf16)

    project(others, rows, keep_mate)
    back = remote(sums.at[0], sums.at[1], send.at[3], receive.at[3], mate)
    back.start()

    def keep_own(columns, value):
        first[pl.ds(0, rows), columns] = value

    project(own, rows, keep_own)

    def finish(done):
        back.wait_recv()
        for copy, (start, size) in zip(final, parts):
            copy.wait_recv()
            done(start, size, summed(first, sums, start, size))
        every([back] + crossing + final, "wait_send")

    return finish


def head_lanes(shape, half):
    lane = lax.broadcasted_iota(jnp.int32, shape, len(shape) - 1)
    return (lane < HEAD_DIM) if half == 0 else (lane >= HEAD_DIM)


def masked(scores, start, first_key):
    query = lax.broadcasted_iota(jnp.int32, scores.shape, 0) + start
    key = lax.broadcasted_iota(jnp.int32, scores.shape, 1) + first_key
    return jnp.where(key <= query, scores, -1e30)


def spans(rows, high):
    if not high:
        return ((0, 2 * rows, True),)
    free = 2 * rows // 128 * 128
    return ((0, free, False), (free, 4 * rows - free, True))


def attend_block(rows, start, high, qkv, attended, lse):
    width = attended.shape[1]
    here = pl.ds(start, rows)
    lane = lax.broadcasted_iota(jnp.int32, (rows, 128), 1)
    tops = jnp.zeros((rows, 128), f32)
    for pair in range(width // 128):
        columns = slice(pair * 128, pair * 128 + 128)
        query = qkv[here, columns] * bf16(HEAD_DIM ** (-0.5))
        results = []
        for half in range(2):
            only = jnp.where(head_lanes(query.shape, half), query, 0)
            scores = []
            for begin, size, mask in spans(rows, high):
                part = dot_nt(only, qkv[pl.ds(begin, size), width + pair * 128 : width + pair * 128 + 128])
                scores.append(masked(part, start, begin) if mask else part)
            top = functools.reduce(jnp.maximum, [jnp.max(part, axis=-1, keepdims=True) for part in scores])
            total, result = 0.0, 0.0
            for (begin, size, _), part in zip(spans(rows, high), scores):
                weights = jnp.exp(part - top)
                total = total + jnp.sum(weights, axis=-1, keepdims=True)
                values = qkv[pl.ds(begin, size), 2 * width + pair * 128 : 2 * width + pair * 128 + 128]
                result = result + dot_nn(weights.astype(bf16), values)
            results.append(result / total)
            tops = jnp.where(lane == 2 * pair + half, top + jnp.log(total), tops)
        attended[here, columns] = jnp.where(head_lanes((rows, 128), 0), results[0], results[1]).astype(bf16)
    lse[here, :] = tops


def attention_forward(layer, stream, gains, shifts, w_qkv, w_out, own_qkv, own_out, weights, scale=None):
    rows, model = stream.shape
    width = own_out.shape[1]
    first = scale is not None
    early = {"qkv": own_qkv, "out": own_out} if first else {}

    def body(r):
        held, qkv, attended, lse, weight = r.held, r.qkv, r.attended, r.lse, r.weight
        w_qkv, w_out = (r.qkv_to, r.out_to) if first else (r.w_qkv, r.w_out)
        loads = [
            Loading(r.own_qkv.at[layer, index], w_qkv.at[index], weight.at[:, pl.ds(index * width, width)], r.local.at[index])
            for index in range(3)
        ]
        loads.append(Loading(r.own_out.at[layer], w_out, r.out, r.local.at[3]))
        if not first:
            every(loads, "start")
        greet(*GROUP, *(FETCH if weights else ()), *((("c", "zh"),) if first else ()))
        jobs = fetch_jobs(r, weights, layer)
        stream = r.stream
        r.ready()
        if first:
            swap = Swapping(r.stream, r.landed, r.swap)
            exchanged = remote(r.weight_in, r.other, r.swap.at[4], r.swap.at[5], flipped("c"))
            before = [
                Fetching(source.at[layer], target, send, receive)
                for source, target, send, receive in (
                    (r.own_qkv, r.qkv_to, r.qkv_send, r.qkv_receive), (r.own_out, r.out_to, r.out_send, r.out_receive)
                )
            ]
            before[0].step_inner()
            before[0].step_outer()
            before[0].step_sent()
            exchanged.start()
            before[0].step_share()
            exchanged.wait()
            r.scale[...] = jnp.where(holds(), r.weight_in[...], r.other[...])
            swap.start()
            before[1].step_inner()
            before[1].step_outer()
            before[0].step_relay()
            stream = r.stream_out
        own = places(rows)[0]

        def prepare(start, size):
            part = pl.ds(start, size)
            if first:
                swap.give(r.stream_out, r.stream, None, (0 if start == 0 else 1,))
            value = norm_rows(stream[part, :], r.gains[layer, 0:1, :], r.shifts[layer, 0:1, :])
            held[pl.ds(pl.multiple_of(own + start, 16), size), :] = value.astype(bf16)

        calls = []

        def arrived(start, size):
            calls.append(start)
            if len(calls) == 1:
                if first:
                    before[1].step_share()
                    before[0].step_got()
                    every(loads[:3], "start")
                    every(loads[:3], "wait")
                else:
                    every(jobs, "step_outer")
                    every(loads, "wait")
            if len(calls) == 2 and first:
                every(jobs, "step_outer")
                before[1].step_relay()
            here = pl.ds(start, size)

            def step(columns):
                qkv[here, columns] = dot_nn(held[here, :], weight[:, columns]).astype(bf16)

            tiles(3 * width, step)

        sent = gather(rows, held, prepare, arrived, r.send, r.receive)
        stores = [pltpu.make_async_copy(held, r.held_out, r.local.at[0]), pltpu.make_async_copy(qkv, r.qkv_out, r.local.at[1])]
        for copy in stores:
            copy.start()
        zl = lax.axis_index("zl")

        def attend(quarter, high):
            attend_block(rows, pl.multiple_of(quarter * rows, 16), high, qkv, attended, lse)

        every(jobs, "step_inner")

        def before_part(name):
            if name == "high":
                attend(3 - zl, True)
                if first:
                    before[1].step_end()
                    loads[3].start()
                    loads[3].wait()
            elif name == "low":
                attend(1 - zl, False)
                if first:
                    every(jobs[:1], "step_share")
            else:
                attend(2 + zl, True)
                every(jobs[1:] if first else jobs, "step_share")
                attend(zl, False)

        def term(start, size, sink):
            here = pl.ds(start, size)

            def step(columns):
                sink(columns, dot_nn(attended[here, :], r.out[:, columns]))

            tiles(model, step)

        finish = scatter(rows, before_part, term, r.first, r.sums, r.send, r.receive)
        late = [pltpu.make_async_copy(attended, r.attended_out, r.local.at[2]), pltpu.make_async_copy(lse, r.lse_out, r.local.at[3])]
        for copy in late:
            copy.start()
        every(jobs, "step_relay")

        def done(start, size, total):
            part = pl.ds(start, size)
            r.branch[part, :] = total
            r.middle[part, :] = stream[part, :] + norm_rows(total, r.gains[layer, 1:2, :], r.shifts[layer, 1:2, :])

        finish(done)
        sent()
        every(jobs, "step_end")
        if first:
            swap.end()
        for copy in stores + late:
            copy.wait()

    return run(
        body,
        1 + layer,
        {
            "stream": (stream, VMEM), "gains": (gains, VMEM), "shifts": (shifts, VMEM), "own_qkv": (own_qkv, ANY), "own_out": (own_out, ANY),
            **fetch_inputs(weights), **({"weight_in": (scale, VMEM)} if first else {"w_qkv": (w_qkv, ANY), "w_out": (w_out, ANY)}),
        },
        {
            "branch": ((rows, model), f32, VMEM), "middle": ((rows, model), f32, VMEM),
            "held_out": ((4 * rows, model), bf16, ANY), "qkv_out": ((4 * rows, 3 * width), bf16, ANY),
            "attended_out": ((4 * rows, width), bf16, ANY), "lse_out": ((4 * rows, 128), f32, ANY), **fetch_outputs(weights),
            **fetch_outputs(early),
            **({"stream_out": (stream.shape, f32, VMEM), "scale": (scale.shape, f32, VMEM)} if first else {}),
        },
        {
            "held": VMEM((4 * rows, model), bf16), "qkv": VMEM((4 * rows, 3 * width), bf16), "attended": VMEM((4 * rows, width), bf16),
            "lse": VMEM((4 * rows, 128), f32), "weight": VMEM((model, 3 * width), bf16), "out": VMEM((width, model), bf16),
            **group_scratch(rows, model), "local": semaphores(4), **fetch_scratch(weights),
            **fetch_scratch(early),
            **({"landed": VMEM(stream.shape, bf16), "other": VMEM(scale.shape, f32), "swap": semaphores(6)} if first else {}),
        },
        24 * rows * model * width,
        64 * rows * rows,
    )


def attend_block_back(rows, start, high, qkv, attended_grad, lse, inner, grad_query, grad_key, grad_value):
    width = attended_grad.shape[1]
    here = pl.ds(start, rows)
    scale = HEAD_DIM ** (-0.5)
    for pair in range(width // 128):
        columns = slice(pair * 128, pair * 128 + 128)
        query = qkv[here, columns] * bf16(scale)
        above = attended_grad[here, columns]
        result = 0.0
        for half in range(2):
            head = 2 * pair + half
            only = jnp.where(head_lanes(query.shape, half), query, 0)
            grad = jnp.where(head_lanes(query.shape, half), above, 0)
            for begin, size, mask in spans(rows, high):
                keys = pl.ds(begin, size)
                key = qkv[keys, width + pair * 128 : width + pair * 128 + 128]
                value = qkv[keys, 2 * width + pair * 128 : 2 * width + pair * 128 + 128]
                scores = dot_nt(only, key)
                if mask:
                    scores = masked(scores, start, begin)
                probs = jnp.exp(scores - lse[here, head : head + 1])
                grad_probs = dot_nt(grad, value)
                grad_scores = (probs * (grad_probs - inner[here, head : head + 1])).astype(bf16)
                key_only = jnp.where(head_lanes(key.shape, half), key, 0)
                result = result + dot_nn(grad_scores, key_only)
                grad_key[keys, columns] += dot_tn(grad_scores, only)
                grad_value[keys, columns] += dot_tn(probs.astype(bf16), grad)
        grad_query[here, columns] = (result * scale).astype(bf16)


def attention_backward(layer, grad, stream, saved, gains, shifts, w_qkv, w_out, own_qkv, own_out, grads, norms=None, mixed=None):
    rows, model = stream.shape
    width = w_out.shape[0]
    final = norms is not None
    shape = jax.ShapeDtypeStruct
    thirds = ("query_last", "key_last", "value_last")
    mine = {name: (shape(w_qkv.shape[1:], bf16), 0, 2) for name in thirds} if final else {}
    mine_out = {"out_last": (shape(w_out.shape, bf16), 0, 2)} if final else {}

    def body(r):
        held, past, qkv, attended, lse, inner, above = r.held, r.past, r.qkv, r.attended, r.lse, r.inner, r.above
        pushed, grad_key, grad_value, weight = r.pushed, r.grad_key, r.grad_value, r.weight
        loads = [
            Loading(r.own_out.at[layer], r.w_out, r.out, r.local.at[3]),
            pltpu.make_async_copy(r.attended_in, attended, r.local.at[4]),
            pltpu.make_async_copy(r.qkv_in, qkv, r.local.at[5]),
            pltpu.make_async_copy(r.lse_in, lse, r.local.at[6]),
            *[
                Loading(r.own_qkv.at[layer, index], r.w_qkv.at[index], weight.at[:, pl.ds(index * width, width)], r.local.at[index])
                for index in range(3)
            ],
            pltpu.make_async_copy(r.held_in, past, r.local.at[7]),
        ]
        for copy in loads:
            copy.start()
        greet(*GROUP, *(FETCH if grads else ()), *((("c", "zh"),) if final or mixed is not None else ()))
        ends = {"out_last": (r.outcome_out,)}
        if final:
            ends.update({name: (r.outcome.at[index], r.qkv_last_out.at[index]) for index, name in enumerate(thirds)})
        jobs = pass_jobs(r, {**grads, **mine, **mine_out}, ends)
        new = [name for name in grads if grads[name][1] == 0]
        crossing = [name for name in grads if grads[name][1] == 1]
        r.ready()
        swaps = []
        if mixed is not None:
            r.low[...] = r.mixed[...].astype(bf16)
            swaps.append(Swapping(r.low, r.landed, r.swap))
        every_of(jobs, crossing, "step_load")
        every_of(jobs, new[:1], "step_spread")
        older = crossing
        own = places(rows)[0]
        norms_of = {}

        def pull(row, values, part, grad):
            pulled, *sums = norm_pull(values[part, :], r.gains[layer, row : row + 1, :], grad)
            norms_of[row] = [old + new for old, new in zip(norms_of.get(row, (0.0, 0.0)), sums)]
            return pulled

        def prepare(start, size):
            part = pl.ds(start, size)
            value = pull(1, r.branch, part, r.grad[part, :])
            held[pl.ds(pl.multiple_of(own + start, 16), size), :] = value.astype(bf16)

        zl = lax.axis_index("zl")

        def back(quarter, high):
            attend_block_back(
                rows, pl.multiple_of(quarter * rows, 16), high, qkv, above, lse, inner, pushed, grad_key, grad_value
            )

        blocks = []

        def arrived(start, size):
            if not blocks:
                grad_key[...] = jnp.zeros_like(grad_key)
                grad_value[...] = jnp.zeros_like(grad_value)
                every(loads, "wait")
            here = pl.ds(start, size)
            value = dot_nt(held[here, :], r.out[...]).astype(bf16)
            above[here, :] = value
            product = value.astype(f32) * attended[here, :].astype(f32)
            lane = lax.broadcasted_iota(jnp.int32, (size, 128), 1)
            tile = jnp.zeros((size, 128), f32)
            for pair in range(width // 128):
                part = product[:, pair * 128 : pair * 128 + 128]
                for half in range(2):
                    one = jnp.sum(jnp.where(head_lanes(part.shape, half), part, 0.0), axis=-1, keepdims=True)
                    tile = jnp.where(lane == 2 * pair + half, one, tile)
            inner[here, :] = tile
            blocks.append(size)
            if len(blocks) == 2:
                back(2 + zl, True)
                back(zl, False)

        sent = gather(rows, held, prepare, arrived, r.send, r.receive)
        every(swaps, "start")
        every_of(jobs, crossing, "step_loaded", "step_outer", "step_inner")

        def step_out(columns):
            r.outcome_out[:, columns] = dot_tn(attended[...], held[:, columns]).astype(bf16)

        outs = []
        if final:
            tiles(model, step_out)
            every_of(jobs, mine_out, "step_spread")
        every_of(jobs, new[:1], "step_fold")
        every_of(jobs, new[1:], "step_spread")

        def step_qkv(columns):
            value = dot_tn(past[:, columns], pushed[...]).astype(bf16)
            for index in range(3):
                r.outcome[index, columns, :] = value[:, index * width : (index + 1) * width]

        def cast(quarter):
            part = pl.ds(pl.multiple_of(quarter * rows, 16), rows)
            pushed[part, pl.ds(width, width)] = grad_key[part, :].astype(bf16)
            pushed[part, pl.ds(2 * width, width)] = grad_value[part, :].astype(bf16)

        def before_part(name):
            if name == "high":
                back(3 - zl, True)
                cast(3 - zl)
            elif name == "low":
                every_of(jobs, new[:1], "step_add", "step_outer", "step_inner")
                every_of(jobs, mine_out, "step_fold")
                back(1 - zl, False)
                cast(1 - zl)
            else:
                cast(2 + zl)
                cast(zl)
                every_of(jobs, new[1:], "step_fold")
                if final:
                    tiles(model, step_qkv)
                    every_of(jobs, mine, "step_spread")
                    every_of(jobs, mine_out, "step_add")

        def term(start, size, sink):
            here = pl.ds(start, size)

            def step(columns):
                sink(columns, dot_nt(pushed[here, :], weight[columns, :]))

            tiles(model, step)

        finish = scatter(rows, before_part, term, r.first, r.sums, r.send, r.receive)
        if final:
            every_of(jobs, new[1:], "step_add", "step_outer", "step_inner")
            every_of(jobs, mine_out, "step_outer", "step_inner")
        else:
            tiles(model, step_out)
            outs.append(pltpu.make_async_copy(r.outcome_out, r.grad_out, r.local.at[0]))
            outs[0].start()
            tiles(model, step_qkv)
            outs.append(pltpu.make_async_copy(r.outcome, r.grad_qkv, r.local.at[1]))
            outs[1].start()

        def done(start, size, total):
            part = pl.ds(start, size)
            target = r.home if final else r.grad_stream
            target[part, :] = r.grad[part, :] + pull(0, r.stream, part, total)

        finish(done)
        if not final:
            every_of(jobs, new[1:], "step_add")
            every_of(jobs, new[:1], "step_join")
            every_of(jobs, new, "step_store")
        for swap in swaps:
            swap.give(r.mixed_out, r.mixed)
            swap.end()
        rows_norms = (*norms_of[0], *norms_of[1])
        if final:
            r.low[...] = r.home[...].astype(bf16)
            swap = Swapping(r.low, r.landed, r.swap)
            for index, value in enumerate(rows_norms):
                r.norms[index : index + 1, :] = value
            for index in range(len(norms)):
                r.norms[pl.ds(4 + 4 * index, 4), :] = getattr(r, f"norms{index}")[...]

            def cube(index, wait):
                copy = remote(
                    r.norms, r.norms_land.at[index], r.swap.at[4 + index], r.swap.at[9 + index], flipped(CUBE[index])
                )
                if not wait:
                    copy.start()
                    return
                copy.wait()
                r.norms[...] = r.norms[...] + r.norms_land[index]

            query, key, value = [[name] for name in thirds]
            cube(0, False)
            every_of(jobs, query, "step_fold")
            cube(0, True)
            cube(1, False)
            every_of(jobs, key, "step_fold")
            cube(1, True)
            every_of(jobs, value, "step_fold")
            cube(2, False)
            every_of(jobs, older, "step_join")
            every_of(jobs, query, "step_add", "step_outer", "step_inner")
            cube(2, True)
            cube(3, False)
            every_of(jobs, key, "step_add", "step_outer", "step_inner")
            every_of(jobs, value, "step_add", "step_outer", "step_inner")
            cube(3, True)
            cube(4, False)
            swap.start()
            every_of(jobs, new[:1], "step_join")
            every_of(jobs, older, "step_relay")
            every_of(jobs, new[1:], "step_join")
            every_of(jobs, mine_out, "step_join")
            every_of(jobs, older, "step_mate")
            every_of(jobs, new[:1], "step_relay")
            every_of(jobs, query, "step_join")
            every_of(jobs, key, "step_join")
            every_of(jobs, value, "step_join")
            every_of(jobs, new[1:], "step_relay")
            every_of(jobs, mine_out, "step_relay")
            every_of(jobs, new[:1], "step_mate")
            every_of(jobs, mine, "step_relay")
            every_of(jobs, new[1:], "step_mate")
            every_of(jobs, mine_out, "step_mate")
            every_of(jobs, mine, "step_mate")
            cube(4, True)
            swap.give(r.grad_stream, r.home)
            swap.end()
        else:
            for index, value in enumerate(rows_norms):
                r.norms[index : index + 1, :] = value
        sent()
        every(outs, "wait")
        every_of(jobs, jobs, "step_end")

    return run(
        body,
        7 + layer,
        {
            "grad": (grad, VMEM), "branch": (saved.branch, VMEM), "stream": (stream, VMEM), "gains": (gains, VMEM),
            "shifts": (shifts, VMEM), "held_in": (saved.held_out, ANY), "qkv_in": (saved.qkv_out, ANY),
            "attended_in": (saved.attended_out, ANY), "lse_in": (saved.lse_out, ANY), "w_qkv": (w_qkv, ANY), "w_out": (w_out, ANY), "own_qkv": (own_qkv, ANY), "own_out": (own_out, ANY),
            **pass_inputs(grads), **({} if mixed is None else {"mixed": (mixed, VMEM)}), **({f"norms{index}": (value, VMEM) for index, value in enumerate(norms)} if final else {}),
        },
        {
            **pass_outputs({**grads, **mine_out}),
            **({"qkv_last_out": (w_qkv.shape, bf16, ANY)} if final else {}),
            **({} if mixed is None else {"mixed_out": (mixed.shape, f32, VMEM)}),
            "grad_stream": ((rows, model), f32, VMEM), "norms": ((16 if final else 4, model), f32, VMEM),
            **({} if final else {"grad_qkv": (w_qkv.shape, bf16, ANY), "grad_out": (w_out.shape, bf16, ANY)}),
        },
        {
            "held": VMEM((4 * rows, model), bf16), "past": VMEM((4 * rows, model), bf16), "qkv": VMEM((4 * rows, 3 * width), bf16),
            "attended": VMEM((4 * rows, width), bf16), "lse": VMEM((4 * rows, 128), f32), "inner": VMEM((4 * rows, 128), f32),
            "above": VMEM((4 * rows, width), bf16), "pushed": VMEM((4 * rows, 3 * width), bf16),
            "grad_key": VMEM((4 * rows, width), f32), "grad_value": VMEM((4 * rows, width), f32),
            "weight": VMEM((model, 3 * width), bf16), "out": VMEM(w_out.shape, bf16), "outcome": VMEM((3, model, width), bf16),
            "outcome_out": VMEM(w_out.shape, bf16), **group_scratch(rows, model), "local": semaphores(8),
            **pass_scratch({**grads, **mine, **mine_out}),
            **(
                {}
                if mixed is None
                else {"low": VMEM(mixed.shape, bf16), "landed": VMEM(mixed.shape, bf16), "swap": semaphores(4)}
            ),
            **(
                {
                    "home": VMEM((rows, model), f32), "low": VMEM((rows, model), bf16), "landed": VMEM((rows, model), bf16),
                    "norms_land": VMEM((len(CUBE), 16, model), f32), "swap": semaphores(14),
                }
                if final
                else {}
            ),
        },
        60 * rows * model * width,
        64 * rows * rows,
    )


def per_device(hidden_in, cotangent, group_ids, group_sizes, w_qkv, w_out, w_up, w_down, gains, shifts):
    size = jnp.sum(jnp.where(jnp.arange(group_sizes.shape[0]) == group_ids[0], group_sizes, 0))
    weight = jnp.full((8, 128), 1.0 / size.astype(f32), f32)
    own_att, own_ffn = (w_qkv, w_out), (w_up, w_down)
    att_zero = attention_forward(
        0, hidden_in, gains, shifts, None, None, *own_att, {"up": w_up, "down": w_down}, weight
    )
    att_weights = [(att_zero.qkv_to, att_zero.out_to)]
    ffn_weights = [(att_zero.up_to, att_zero.down_to)]
    ffn_zero = ffn_forward(
        0, att_zero.middle, gains, shifts, *ffn_weights[0], *own_ffn, {"qkv": w_qkv, "out": w_out, "down": w_down}
    )
    att_weights.append((ffn_zero.qkv_to, ffn_zero.out_to))
    att_one = attention_forward(1, ffn_zero.stream, gains, shifts, *att_weights[1], *own_att, {"up": w_up})
    ffn_weights.append((att_one.up_to, ffn_zero.down_to))
    ffn_one = ffn_forward(
        1, att_one.middle, gains, shifts, *ffn_weights[1], *own_ffn, {}, cotangent, att_zero.scale
    )
    ffn_zero.middle, ffn_one.middle = att_zero.middle, att_one.middle
    back_one = ffn_backward(1, ffn_one.grad, ffn_one, gains, shifts, *ffn_weights[1], *own_ffn, {})
    deep_one = attention_backward(
        1, back_one.grad_middle, ffn_zero.stream, att_one, gains, shifts, *att_weights[1], *own_att,
        {"up1": (back_one.grad_up, 0, 1), "down1": (back_one.grad_down, 0, 0)},
        mixed=ffn_one.stream,
    )
    back_zero = ffn_backward(
        0, deep_one.grad_stream, ffn_zero, gains, shifts, *ffn_weights[0], *own_ffn,
        {"up1": (deep_one.up1_out, 2, 2), "down1": (deep_one.down1_out, 1, 2), "qkv1": (deep_one.grad_qkv, 0, 0), "out1": (deep_one.grad_out, 0, 0)},
    )
    last = attention_backward(
        0, back_zero.grad_middle, att_zero.stream_out, att_zero, gains, shifts, *att_weights[0], *own_att,
        {
            "qkv1": (back_zero.qkv1_out, 1, 2), "out1": (back_zero.out1_out, 1, 2),
            "up0": (back_zero.grad_up, 0, 2), "down0": (back_zero.grad_down, 0, 2),
        },
        (back_zero.norms, deep_one.norms, back_one.norms),
    )
    grads = [
        jnp.stack(pair).astype(f32)
        for pair in (
            (last.qkv_last_out, last.qkv1_out),
            (last.out_last_out, last.out1_out),
            (last.up0_out, back_zero.up1_out),
            (last.down0_out, back_zero.down1_out),
        )
    ]
    sums = last.norms.reshape(2, 4, 2, -1)
    if lax.axis_size("gh") > 1:
        grads, sums = lax.psum((grads, sums), "gh")
    return (deep_one.mixed_out, last.grad_stream, *grads, sums[:, :, 0], sums[:, :, 1])


def solution(mesh):
    fine = jax.sharding.Mesh(mesh.devices.reshape(-1, 2, 2, 2, 2, 2), AXES)
    dp = ("gh", "gl", "p", "c")
    tensor = ("zh", "zl")
    rows = P((*dp, *tensor), None)
    weights = (
        P(None, None, None, tensor),
        P(None, tensor, None),
        P(None, None, tensor),
        P(None, tensor, None),
    )
    return jax.shard_map(
        per_device,
        mesh=fine,
        in_specs=(rows, rows, P(dp), P(), *weights, P(), P()),
        out_specs=(rows, rows, *weights, P(), P()),
        check_vma=False,
    )
```

```python
import functools
import types

import jax
import jax.numpy as jnp
from jax import lax
from jax.experimental import pallas as pl
from jax.experimental.pallas import tpu as pltpu
from jax.sharding import PartitionSpec as P

HEAD_DIM = 64
AXES = ("gh", "gl", "p", "c", "zh", "zl")
f32 = jnp.float32
bf16 = jnp.bfloat16
MESH = pl.DeviceIdType.MESH
VMEM, ANY = pltpu.VMEM, pl.ANY
eps_norm = 1e-05
TILE = 256


def centre(values):
    mean = jnp.mean(values, axis=-1, keepdims=True)
    centred = values - mean
    spread = jnp.mean(centred * centred, axis=-1, keepdims=True)
    rate = lax.rsqrt(spread + eps_norm)
    return centred * rate, rate


def norm_rows(values, gain, shift):
    return centre(values)[0] * gain + shift


def norm_pull(values, gain, grad):
    hat, rate = centre(values)
    scaled = grad * gain
    along = jnp.mean(scaled * hat, axis=-1, keepdims=True)
    level = jnp.mean(scaled, axis=-1, keepdims=True)
    return (
        rate * (scaled - level - hat * along),
        jnp.sum(grad * hat, axis=0, keepdims=True),
        jnp.sum(grad, axis=0, keepdims=True),
    )


def dot_nt(left, right):
    return lax.dot_general(left, right, (((1,), (1,)), ((), ())), preferred_element_type=f32)


def dot_tn(left, right):
    return lax.dot_general(left, right, (((0,), (0,)), ((), ())), preferred_element_type=f32)


def dot_nn(left, right):
    return jnp.dot(left, right, preferred_element_type=f32)


def cut_rows(rows):
    first = (rows // 2 + 15) // 16 * 16
    return ((0, first), (first, rows - first))


def flipped(*names):
    return {name: 1 - lax.axis_index(name) for name in names}


def greet(*others):
    barrier = pltpu.get_barrier_semaphore()
    for names in others:
        pl.semaphore_signal(barrier, inc=1, device_id=flipped(*names), device_id_type=MESH)
    pl.semaphore_wait(barrier, len(others))


GROUP = (("c",), ("zl",))
FETCH = (("zh",), ("p",), ("gl",))


def remote(source, target, send, receive, device):
    return pltpu.make_async_remote_copy(
        src_ref=source,
        dst_ref=target,
        send_sem=send,
        recv_sem=receive,
        device_id=device,
        device_id_type=MESH,
    )


def tiles(width, body):
    def step(index, carry):
        body(pl.ds(pl.multiple_of(index * TILE, TILE), TILE))
        return carry

    lax.fori_loop(0, width // TILE, step, 0)


def exchange(rows, held, prepare, work, first, sums, send, receive):
    mate, near = flipped("c"), flipped("zl")
    own = pl.ds(0, rows)
    parts = cut_rows(rows)
    along = []
    for index, (start, size) in enumerate(parts):
        prepare(start, size)
        place = pl.ds(2 * rows + 2 * start, size)
        copy = remote(held.at[pl.ds(start, size)], held.at[place], send.at[1 + index], receive.at[1 + index], near)
        copy.start()
        along.append(copy)
    copies = [remote(held.at[own], held.at[pl.ds(rows, rows)], send.at[0], receive.at[0], mate)]
    copies[0].start()

    def keep(row, columns, value):
        first[pl.ds(row, value.shape[0]), columns] = value

    work(0, rows, keep)
    copies[0].wait_recv()

    def keep_mate(row, columns, value):
        sums[0, pl.ds(row - rows, value.shape[0]), columns] = value.astype(bf16)

    work(rows, rows, keep_mate)
    back = remote(sums.at[0], sums.at[1], send.at[3], receive.at[3], mate)
    back.start()
    copies.append(back)
    final = []
    for index, (start, size) in enumerate(parts):
        place = 2 * rows + 2 * start
        along[index].wait_recv()
        relay = remote(
            held.at[pl.ds(place, size)], held.at[pl.ds(place + size, size)], send.at[4 + index], receive.at[4 + index], mate
        )
        relay.start()
        relay.wait_recv()

        def keep_far(row, columns, value, place=place, start=start, size=size):
            first[pl.ds(rows + start, size), columns] = value[:size]
            sums[2, pl.ds(start, size), columns] = value[size:].astype(bf16)

        work(place, 2 * size, keep_far)
        part = pl.ds(start, size)
        cross = remote(sums.at[2, part], sums.at[3, part], send.at[6 + index], receive.at[6 + index], mate)
        cross.start()
        cross.wait_recv()
        sums[4, part, :] = (first[pl.ds(rows + start, size), :] + sums[3, part, :].astype(f32)).astype(bf16)
        last = remote(sums.at[4, part], sums.at[5, part], send.at[8 + index], receive.at[8 + index], near)
        last.start()
        final.append(last)
        copies += [relay, cross]

    def finish(done):
        back.wait_recv()
        for copy, (start, size) in zip(final, parts):
            copy.wait_recv()
            done(start, size, summed(first, sums, start, size))
        every(copies + along + final, "wait_send")

    return finish


def summed(first, sums, start, size):
    part = pl.ds(start, size)
    return first[part, :] + sums[1, part, :].astype(f32) + sums[5, part, :].astype(f32)


def run(body, number, inputs, outputs, scratch, flops, transcendentals=0):
    copied = [name for name, (_, memory) in inputs.items() if memory is VMEM]
    own = {name: VMEM(inputs[name][0].shape, inputs[name][0].dtype) for name in copied}
    names = [*inputs, *outputs, *scratch, *(name + "_copy" for name in copied), "arrivals"]

    def kernel(*refs):
        found = dict(zip(names, refs))
        copies = [
            pltpu.make_async_copy(found[name], found[name + "_copy"], found["arrivals"].at[index])
            for index, name in enumerate(copied)
        ]
        every(copies, "start")
        found.update({name: found[name + "_copy"] for name in copied})
        body(types.SimpleNamespace(**found, ready=lambda: every(copies, "wait")))

    moved = sum(value.size * value.dtype.itemsize for value, _ in inputs.values())
    results = pl.pallas_call(
        kernel,
        out_shape=tuple(jax.ShapeDtypeStruct(shape, kind) for shape, kind, _ in outputs.values()),
        in_specs=[pl.BlockSpec(memory_space=ANY) for _ in inputs],
        out_specs=tuple(pl.BlockSpec(memory_space=memory) for _, _, memory in outputs.values()),
        scratch_shapes=[*scratch.values(), *own.values(), semaphores(len(copied))],
        compiler_params=pltpu.CompilerParams(collective_id=number, has_side_effects=True, vmem_limit_bytes=58 << 20),
        cost_estimate=pl.CostEstimate(flops=flops, bytes_accessed=moved, transcendentals=transcendentals),
    )(*[value for value, _ in inputs.values()])
    return types.SimpleNamespace(**dict(zip(outputs, results)))


def semaphores(count):
    return pltpu.SemaphoreType.DMA((count,))


def group_scratch(rows, width):
    return {
        "first": VMEM((2 * rows, width), f32),
        "sums": VMEM((6, rows, width), bf16),
        "send": semaphores(10),
        "receive": semaphores(10),
    }


def pick(ref, rows):
    return ref.at[:, rows, :] if len(ref.shape) == 3 else ref.at[rows, :]


def part_shape(shape, parts):
    return (*shape[:-2], int(shape[-2] / parts), shape[-1])


def inner():
    return lax.axis_index("zl") != lax.axis_index("zh")


def holds():
    return lax.axis_index("c") == lax.axis_index("zh")


def fetch_jobs(refs, names, layer):
    return [
        Fetching(
            getattr(refs, name + "_from").at[layer], getattr(refs, name + "_to"), getattr(refs, name + "_send"),
            getattr(refs, name + "_receive"),
        )
        for name in names
    ]


def fetch_inputs(weights):
    return {name + "_from": (value, ANY) for name, value in weights.items()}


def fetch_outputs(weights):
    return {name + "_to": (value.shape[1:], bf16, ANY) for name, value in weights.items()}


def fetch_scratch(weights):
    result = {}
    for name in weights:
        result[name + "_send"] = semaphores(8)
        result[name + "_receive"] = semaphores(8)
    return result


class Loading:
    def __init__(self, own, fetched, target, semaphore):
        self.ways = [pltpu.make_async_copy(source, target, semaphore) for source in (own, fetched)]

    def start(self):
        pl.when(holds())(self.ways[0].start)
        pl.when(jnp.logical_not(holds()))(self.ways[1].start)

    def wait(self):
        pl.when(holds())(self.ways[0].wait)
        pl.when(jnp.logical_not(holds()))(self.ways[1].wait)


def every(jobs, step):
    for job in jobs:
        getattr(job, step)()


CUBE = ("c", "zl", "p", "gl", "zh")
ORDERS = (("p", "gl"), ("gl", "p"))


class Halves:
    def copy(self, slot, source, target, name):
        return remote(source, target, self.send.at[slot], self.receive.at[slot], flipped(name))

    def at(self, half, first, second=None):
        start = (4 * half + 2 * first) * self.size
        if second is None:
            return pl.ds(pl.multiple_of(start, 16), 2 * self.size)
        return pl.ds(pl.multiple_of(start + second * self.size, 16), self.size)


class Fetching(Halves):
    def __init__(self, source, target, send, receive):
        self.source, self.target, self.send, self.receive = source, target, send, receive
        self.size = source.shape[-2] // 8

    def own(self, half):
        return self.at(half, *[lax.axis_index(name) for name in ORDERS[half]])

    def quarter(self, half):
        return pick(self.target, self.own(half))

    def along(self, half):
        return self.copy(half, pick(self.source, self.own(half)), self.quarter(half), "zh")

    def direct(self, half, axis):
        rows = self.quarter(half)
        return self.copy(2 + 2 * half + axis, rows, rows, ORDERS[half][axis])

    def relay(self, half):
        first, second = ORDERS[half]
        rows = pick(self.target, self.at(half, lax.axis_index(first), 1 - lax.axis_index(second)))
        return self.copy(6 + half, rows, rows, first)

    def start_along(self, here):
        @pl.when(jnp.logical_and(holds(), here))
        def _():
            for half in range(2):
                self.along(half).start()

    def step_inner(self):
        self.start_along(inner())

    def step_outer(self):
        self.start_along(jnp.logical_not(inner()))

    def step_sent(self):
        @pl.when(holds())
        def _():
            for half in range(2):
                self.along(half).wait_send()

    def share_if(self, here):
        @pl.when(jnp.logical_and(jnp.logical_not(holds()), here))
        def _():
            for half in range(2):
                self.along(half).wait_recv()
                self.direct(half, 1).start()
                self.direct(half, 0).start()

    def step_share(self):
        self.share_if(True)

    def step_share_outer(self):
        self.share_if(jnp.logical_not(inner()))

    def step_share_inner(self):
        self.share_if(inner())

    def step_relay(self):
        @pl.when(jnp.logical_not(holds()))
        def _():
            for half in range(2):
                self.direct(half, 1).wait_recv()
                self.relay(half).start()

    def step_got(self):
        @pl.when(jnp.logical_not(holds()))
        def _():
            for half in range(2):
                self.direct(half, 0).wait()
                self.direct(half, 1).wait_send()
                self.relay(half).wait()

    def step_end(self):
        self.step_sent()
        self.step_got()


class Passing(Halves):
    def __init__(self, refs, name, first, last, source=None, out=None):
        self.first, self.last = first, last
        for field in ("in", "out", "land", "mine", "more", "sum", "cross", "send", "receive", "local"):
            setattr(self, field, getattr(refs, f"{name}_{field}", None))
        self.source = source if source is not None else getattr(refs, f"{name}_in", None)
        if out is not None:
            self.out = out
        self.size = self.sum.shape[-2] // 2

    def place_of(self, half):
        return [lax.axis_index(name) for name in ORDERS[half]]

    def spread(self, half):
        name = ORDERS[half][0]
        return self.copy(half, pick(self.source, self.at(half, 1 - lax.axis_index(name))), self.land.at[half], name)

    def keep(self, half):
        rows = self.at(half, lax.axis_index(ORDERS[half][0]))
        return pltpu.make_async_copy(pick(self.source, rows), self.mine.at[half], self.local.at[half])

    def second(self, index):
        return pl.ds(pl.multiple_of(index * self.size, 16), self.size)

    def fold(self, half):
        name = ORDERS[half][1]
        return self.copy(2 + half, pick(self.mine.at[half], self.second(1 - lax.axis_index(name))), self.more.at[half], name)

    def load(self):
        return pltpu.make_async_copy(self.source, self.sum, self.local.at[2])

    def store(self):
        return pltpu.make_async_copy(self.sum, self.out, self.local.at[2])

    def along(self):
        return self.copy(4, self.sum, self.cross, "zh")

    def own(self, half):
        return pick(self.sum, pl.ds(half * self.size, self.size))

    def place(self, half):
        return pltpu.make_async_copy(self.own(half), pick(self.out, self.at(half, *self.place_of(half))), self.local.at[half])

    def direct(self, half, axis):
        own = pick(self.out, self.at(half, *self.place_of(half)))
        return self.copy(5 + 2 * half + axis, self.own(half), own, ORDERS[half][axis])

    def relay(self, half):
        first, second = self.place_of(half)
        rows = pick(self.out, self.at(half, first, 1 - second))
        return self.copy(9 + half, rows, rows, ORDERS[half][0])

    def mate(self, half, index):
        first = self.place_of(half)[0]
        rows = pick(self.out, self.at(half, first if index == 0 else 1 - first))
        return self.copy(11 + 2 * half + index, rows, rows, "c")

    def step_spread(self):
        for half in range(2):
            self.spread(half).start()
            self.keep(half).start()

    def step_fold(self):
        for half in range(2):
            self.keep(half).wait()
            self.spread(half).wait_recv()
            self.mine[half] = (self.mine[half].astype(f32) + self.land[half].astype(f32)).astype(bf16)
            self.fold(half).start()

    def step_add(self):
        for half in range(2):
            self.fold(half).wait_recv()
            own = pick(self.mine.at[half], self.second(lax.axis_index(ORDERS[half][1])))
            self.own(half)[...] = (own[...].astype(f32) + self.more[half].astype(f32)).astype(bf16)

    def step_load(self):
        self.load().start()

    def step_loaded(self):
        self.load().wait()

    def step_inner(self):
        pl.when(jnp.logical_and(jnp.logical_not(holds()), inner()))(self.along().start)

    def step_outer(self):
        pl.when(jnp.logical_not(jnp.logical_or(holds(), inner())))(self.along().start)

    def join_if(self, here):
        @pl.when(jnp.logical_and(holds(), here))
        def _():
            self.along().wait_recv()
            self.sum[...] = (self.sum[...].astype(f32) + self.cross[...].astype(f32)).astype(bf16)
            if self.last == 2:
                for half in range(2):
                    self.direct(half, 1).start()
                    self.direct(half, 0).start()
                    self.place(half).start()

    def step_join_outer(self):
        self.join_if(jnp.logical_not(inner()))

    def step_join_inner(self):
        self.join_if(inner())

    def step_join(self):
        self.join_if(True)

    def step_share(self):
        @pl.when(holds())
        def _():
            for half in range(2):
                self.direct(half, 1).start()
                self.direct(half, 0).start()
                self.place(half).start()

    def step_relay(self):
        @pl.when(holds())
        def _():
            for half in range(2):
                self.direct(half, 1).wait_recv()
                self.relay(half).start()
                self.place(half).wait()
                self.mate(half, 0).start()

    def step_mate(self):
        @pl.when(holds())
        def _():
            for half in range(2):
                self.direct(half, 0).wait_recv()
                self.relay(half).wait_recv()
                self.mate(half, 1).start()

    def step_store(self):
        self.store().start()

    def step_end(self):
        if self.first == 0:
            for half in range(2):
                self.spread(half).wait_send()
                self.fold(half).wait_send()
        if self.last < 2:
            self.store().wait()

        @pl.when(holds())
        def _():
            if self.last == 2:
                for half in range(2):
                    self.direct(half, 0).wait_send()
                    self.direct(half, 1).wait_send()
                    self.relay(half).wait_send()
                    self.mate(half, 0).wait_send()
                    self.mate(half, 1).wait_send()

        @pl.when(jnp.logical_not(holds()))
        def _():
            if self.first <= 1 <= self.last:
                self.along().wait_send()
            if self.last == 2:
                for half in range(2):
                    self.mate(half, 0).wait_recv()
                    self.mate(half, 1).wait_recv()


def pass_shapes(grads):
    for name, (value, first, last) in grads.items():
        whole = value.shape if first == 0 else part_shape(value.shape, 1 / 4)
        yield name, whole, part_shape(whole, 4), first, last


def pass_jobs(refs, grads, ends=None):
    return {name: Passing(refs, name, first, last, *(ends or {}).get(name, ())) for name, (_, first, last) in grads.items()}


def pass_inputs(grads):
    return {name + "_in": (value, ANY) for name, (value, *_) in grads.items() if isinstance(value, jax.Array)}


def pass_outputs(grads):
    return {name + "_out": (whole if last == 2 else part, bf16, ANY) for name, whole, part, first, last in pass_shapes(grads)}


def pass_scratch(grads):
    result = {}
    for name, whole, part, first, last in pass_shapes(grads):
        if first == 0:
            result[name + "_land"] = VMEM((2, *part), bf16)
            result[name + "_mine"] = VMEM((2, *part), bf16)
            result[name + "_more"] = VMEM((2, *part_shape(whole, 8)), bf16)
        result[name + "_sum"] = VMEM(part, bf16)
        if first <= 1 <= last:
            result[name + "_cross"] = VMEM(part, bf16)
        result[name + "_send"] = semaphores(15)
        result[name + "_receive"] = semaphores(15)
        result[name + "_local"] = semaphores(3)
    return result


def every_of(jobs, names, *steps):
    for step in steps:
        for name in names:
            getattr(jobs[name], step)()


class Swapping:
    def __init__(self, source, landed, semaphores):
        self.source, self.landed = source, landed
        self.parts = cut_rows(source.shape[0])
        self.copies = [
            remote(
                source.at[pl.ds(start, size)], landed.at[pl.ds(start, size)], semaphores.at[index], semaphores.at[2 + index],
                flipped("c", "zh"),
            )
            for index, (start, size) in enumerate(self.parts)
        ]

    def start_if(self, here):
        @pl.when(here)
        def _():
            every(self.copies, "start")

    def start(self):
        self.start_if(jnp.logical_not(holds()))

    def step_inner(self):
        self.start_if(jnp.logical_and(jnp.logical_not(holds()), inner()))

    def step_outer(self):
        self.start_if(jnp.logical_not(jnp.logical_or(holds(), inner())))

    def give(self, target, own, scale=None, only=(0, 1)):
        factor = 1.0 if scale is None else scale
        for index in only:
            rows = pl.ds(*self.parts[index])

            @pl.when(holds())
            def _(rows=rows):
                target[rows, :] = own[rows, :].astype(f32) * factor

            @pl.when(jnp.logical_not(holds()))
            def _(index=index, rows=rows):
                self.copies[index].wait_recv()
                target[rows, :] = self.landed[rows, :].astype(f32) * factor

    def end(self):
        @pl.when(jnp.logical_not(holds()))
        def _():
            every(self.copies, "wait_send")


def gelu_and_slope(values):
    rate, cubic = 0.7978845608028654, 0.044715
    square = values * values
    bend = jnp.tanh(rate * values * (1.0 + cubic * square))
    half = 0.5 * (1.0 + bend)
    slope = half + 0.5 * values * (1.0 - bend * bend) * (rate * (1.0 + 3.0 * cubic * square))
    return values * half, slope


def ffn_forward(layer, middle, gains, shifts, w_up, w_down, own_up, own_down, weights, cotangent=None, scale=None):
    rows, width = middle.shape
    hidden = w_up.shape[1]

    def body(r):
        loads = [Loading(r.own_up.at[layer], r.w_up, r.up, r.local.at[0]), Loading(r.own_down.at[layer], r.w_down, r.down, r.local.at[1])]
        for copy in loads:
            copy.start()
        greet(*GROUP, *(FETCH if weights else ()), *(() if cotangent is None else (("c", "zh"),)))
        r.ready()
        jobs = fetch_jobs(r, weights, layer + 1)
        swaps = [] if cotangent is None else [Swapping(r.cotangent, r.landed, r.swap)]
        every(jobs + swaps, "step_inner")
        held, active, slope = r.held, r.active, r.slope

        def prepare(start, size):
            part = pl.ds(start, size)
            held[part, :] = norm_rows(r.middle[part, :], r.gains[layer, 2:3, :], r.shifts[layer, 2:3, :]).astype(bf16)

        calls = []

        def work(start, size, sink):
            calls.append(start)
            if len(calls) == 1:
                every(jobs + swaps, "step_outer")
                every(loads, "wait")
            if len(calls) == 3:
                every(jobs, "step_share_outer")
            if len(calls) == 4:
                every(jobs, "step_share_inner")
            here = pl.ds(start, size)

            def step(columns):
                upper = dot_nn(held[here, :], r.up[:, columns])
                value, bend = gelu_and_slope(upper)
                active[here, columns] = value.astype(bf16)
                slope[here, columns] = bend.astype(bf16)

            tiles(hidden, step)

            def step_down(columns):
                sink(start, columns, dot_nn(active[here, :], r.down[:, columns]))

            tiles(width, step_down)

        finish = exchange(rows, held, prepare, work, r.first, r.sums, r.send, r.receive)
        stores = [
            pltpu.make_async_copy(held, r.held_out, r.local.at[2]),
            pltpu.make_async_copy(active, r.active_out, r.local.at[3]),
            pltpu.make_async_copy(slope, r.slope_out, r.local.at[4]),
        ]
        for copy in stores:
            copy.start()
        every(jobs, "step_relay")

        def done(start, size, total):
            part = pl.ds(start, size)
            r.second[part, :] = total
            r.stream[part, :] = r.middle[part, :] + norm_rows(total, r.gains[layer, 3:4, :], r.shifts[layer, 3:4, :])

        finish(done)
        every(jobs, "step_end")
        for swap in swaps:
            swap.give(r.grad, r.cotangent, r.scale[0:1, 0:1])
            swap.end()
        for copy in stores:
            copy.wait()

    return run(
        body,
        3 + layer,
        {
            "middle": (middle, VMEM), "gains": (gains, VMEM), "shifts": (shifts, VMEM), "w_up": (w_up, ANY), "w_down": (w_down, ANY), "own_up": (own_up, ANY), "own_down": (own_down, ANY),
            **fetch_inputs(weights), **({} if cotangent is None else {"cotangent": (cotangent, VMEM), "scale": (scale, VMEM)}),
        },
        {
            "second": ((rows, width), f32, VMEM), "stream": ((rows, width), f32, VMEM),
            "held_out": ((4 * rows, width), bf16, ANY), "active_out": ((4 * rows, hidden), bf16, ANY),
            "slope_out": ((4 * rows, hidden), bf16, ANY), **fetch_outputs(weights),
            **({} if cotangent is None else {"grad": ((rows, width), f32, VMEM)}),
        },
        {
            "held": VMEM((4 * rows, width), bf16), "active": VMEM((4 * rows, hidden), bf16), "slope": VMEM((4 * rows, hidden), bf16),
            "up": VMEM(w_up.shape, bf16), "down": VMEM(w_down.shape, bf16), **group_scratch(rows, width), "local": semaphores(5),
            **fetch_scratch(weights),
            **({} if cotangent is None else {"landed": VMEM(cotangent.shape, bf16), "swap": semaphores(4)}),
        },
        16 * rows * width * hidden,
        4 * rows * hidden,
    )


def ffn_backward(layer, grad, saved, gains, shifts, w_up, w_down, own_up, own_down, grads):
    middle = saved.middle
    rows, width = middle.shape
    hidden = w_up.shape[1]

    def body(r):
        held, active, slope, pushed, past = r.held, r.active, r.slope, r.pushed, r.past
        loads = [
            Loading(r.own_down.at[layer], r.w_down, r.down, r.local.at[0]),
            Loading(r.own_up.at[layer], r.w_up, r.up, r.local.at[1]),
            pltpu.make_async_copy(r.slope_in, slope, r.local.at[2]),
            pltpu.make_async_copy(r.active_in, active, r.local.at[3]),
            pltpu.make_async_copy(r.held_in, past, r.local.at[4]),
        ]
        for copy in loads:
            copy.start()
        greet(*GROUP, *(FETCH if grads else ()))
        jobs = pass_jobs(r, grads)
        new = [name for name in grads if grads[name][1] == 0]
        late = [name for name in grads if grads[name][1] == 2]
        r.ready()
        crossing = [name for name in grads if grads[name][1] == 1]
        every_of(jobs, crossing, "step_load", "step_loaded", "step_inner")
        every_of(jobs, late, "step_load")
        every_of(jobs, new, "step_spread")
        norms = {}

        def pull(row, values, part, grad):
            pulled, *sums = norm_pull(values[part, :], r.gains[layer, row : row + 1, :], grad)
            norms[row] = [old + new for old, new in zip(norms.get(row, (0.0, 0.0)), sums)]
            return pulled

        def prepare(start, size):
            part = pl.ds(start, size)
            held[part, :] = pull(3, r.second, part, r.grad[part, :]).astype(bf16)

        calls = []

        def work(start, size, sink):
            calls.append(start)
            if len(calls) == 1:
                every_of(jobs, crossing, "step_outer")
                every_of(jobs, late, "step_loaded", "step_share")
                every(loads, "wait")
            if len(calls) == 4:
                every_of(jobs, new, "step_fold")
                every_of(jobs, crossing, "step_join_outer")
            here = pl.ds(start, size)

            def step(columns):
                value = dot_nt(held[here, :], r.down[columns, :])
                pushed[here, columns] = (value * slope[here, columns].astype(f32)).astype(bf16)

            tiles(hidden, step)

            def step_up(columns):
                sink(start, columns, dot_nt(pushed[here, :], r.up[columns, :]))

            tiles(width, step_up)

        finish = exchange(rows, held, prepare, work, r.first, r.sums, r.send, r.receive)

        every_of(jobs, late, "step_relay")
        every_of(jobs, crossing, "step_join_inner")

        def step_down(columns):
            r.outcome[0, columns, :] = dot_tn(active[:, columns], held[...]).astype(bf16)

        tiles(hidden, step_down)
        out_down = pltpu.make_async_copy(r.outcome.at[0], r.grad_down, r.local.at[0])
        out_down.start()
        def step_up(columns):
            r.outcome[1, columns, :] = dot_tn(past[:, columns], pushed[...]).astype(bf16)

        tiles(width, step_up)
        out_up = pltpu.make_async_copy(r.outcome.at[1], r.grad_up, r.local.at[1])
        out_up.start()
        every_of(jobs, new, "step_add", "step_store")
        every_of(jobs, crossing, "step_relay")
        every_of(jobs, late, "step_mate")

        def done(start, size, total):
            part = pl.ds(start, size)
            r.grad_middle[part, :] = r.grad[part, :] + pull(2, r.middle, part, total)

        finish(done)
        every_of(jobs, crossing, "step_mate")
        for index, value in enumerate((*norms[2], *norms[3])):
            r.norms[index : index + 1, :] = value
        out_down.wait()
        out_up.wait()
        every_of(jobs, grads, "step_end")

    return run(
        body,
        5 + layer,
        {
            "grad": (grad, VMEM), "second": (saved.second, VMEM), "middle": (middle, VMEM), "gains": (gains, VMEM),
            "shifts": (shifts, VMEM), "held_in": (saved.held_out, ANY), "active_in": (saved.active_out, ANY),
            "slope_in": (saved.slope_out, ANY), "w_up": (w_up, ANY), "w_down": (w_down, ANY), "own_up": (own_up, ANY), "own_down": (own_down, ANY),
            **pass_inputs(grads),
        },
        {
            **pass_outputs(grads),
            "grad_middle": ((rows, width), f32, VMEM), "norms": ((4, width), f32, VMEM),
            "grad_up": (w_up.shape, bf16, ANY), "grad_down": (w_down.shape, bf16, ANY),
        },
        {
            "held": VMEM((4 * rows, width), bf16), "past": VMEM((4 * rows, width), bf16),
            "active": VMEM((4 * rows, hidden), bf16), "slope": VMEM((4 * rows, hidden), bf16),
            "pushed": VMEM((4 * rows, hidden), bf16), "up": VMEM(w_up.shape, bf16), "down": VMEM(w_down.shape, bf16),
            "outcome": VMEM((2, width, hidden), bf16), **group_scratch(rows, width), "local": semaphores(5),
            **pass_scratch(grads),
        },
        32 * rows * width * hidden,
    )


def places(rows):
    c, zl = lax.axis_index("c"), lax.axis_index("zl")

    def at(core, part):
        return pl.multiple_of((2 * core + part) * rows, 16)

    return at(c, zl), at(1 - c, zl), at(c, 1 - zl), at(1 - c, 1 - zl)


def gather(rows, held, prepare, arrived, send, receive):
    mate, near = flipped("c"), flipped("zl")
    own, others, along, across = places(rows)
    parts = cut_rows(rows)
    copies = []
    for index, (start, size) in enumerate(parts):
        prepare(start, size)
        part = pl.ds(pl.multiple_of(own + start, 16), size)
        copy = remote(held.at[part], held.at[part], send.at[1 + index], receive.at[1 + index], near)
        copy.start()
        copies.append(copy)
    here = pl.ds(own, rows)
    copies.append(remote(held.at[here], held.at[here], send.at[0], receive.at[0], mate))
    copies[-1].start()
    arrived(own, rows)
    copies[-1].wait_recv()
    arrived(others, rows)
    for index, (start, size) in enumerate(parts):
        copies[index].wait_recv()
        first = pl.multiple_of(along + start, 16)
        part = pl.ds(first, size)
        relay = remote(held.at[part], held.at[part], send.at[4 + index], receive.at[4 + index], mate)
        relay.start()
        copies.append(relay)
        arrived(first, size)
        relay.wait_recv()
        arrived(pl.multiple_of(across + start, 16), size)

    def finish():
        every(copies, "wait_send")

    return finish


def scatter(rows, before, project, first, sums, send, receive):
    mate, near = flipped("c"), flipped("zl")
    own, others, _, _ = places(rows)
    parts = cut_rows(rows)
    crossing = [
        remote(sums.at[2, pl.ds(start, size)], sums.at[3, pl.ds(start, size)], send.at[6 + index], receive.at[6 + index], mate)
        for index, (start, size) in enumerate(parts)
    ]
    final = [
        remote(sums.at[4, pl.ds(start, size)], sums.at[5, pl.ds(start, size)], send.at[8 + index], receive.at[8 + index], near)
        for index, (start, size) in enumerate(parts)
    ]
    for half, name in ((1, "high"), (0, "low")):
        before(name)
        base = pl.multiple_of((2 * half + 1 - lax.axis_index("zl")) * rows, 16)
        far = lax.axis_index("c") != half
        for index, (start, size) in enumerate(parts):

            def keep(columns, value, start=start, size=size):
                first[pl.ds(rows + start, size), columns] = value

            project(pl.multiple_of(base + start, 16), size, keep)

            @pl.when(far)
            def _(index=index, start=start, size=size):
                sums[2, pl.ds(start, size), :] = first[pl.ds(rows + start, size), :].astype(bf16)
                crossing[index].start()

        @pl.when(jnp.logical_not(far))
        def _():
            for index, (start, size) in enumerate(parts):
                crossing[index].wait_recv()
                part = pl.ds(start, size)
                sums[4, part, :] = (first[pl.ds(rows + start, size), :] + sums[3, part, :].astype(f32)).astype(bf16)
                final[index].start()

    before("rest")

    def keep_mate(columns, value):
        sums[0, :, columns] = value.astype(bf16)

    project(others, rows, keep_mate)
    back = remote(sums.at[0], sums.at[1], send.at[3], receive.at[3], mate)
    back.start()

    def keep_own(columns, value):
        first[pl.ds(0, rows), columns] = value

    project(own, rows, keep_own)

    def finish(done):
        back.wait_recv()
        for copy, (start, size) in zip(final, parts):
            copy.wait_recv()
            done(start, size, summed(first, sums, start, size))
        every([back] + crossing + final, "wait_send")

    return finish


def head_lanes(shape, half):
    lane = lax.broadcasted_iota(jnp.int32, shape, len(shape) - 1)
    return (lane < HEAD_DIM) if half == 0 else (lane >= HEAD_DIM)


def masked(scores, start, first_key):
    query = lax.broadcasted_iota(jnp.int32, scores.shape, 0) + start
    key = lax.broadcasted_iota(jnp.int32, scores.shape, 1) + first_key
    return jnp.where(key <= query, scores, -1e30)


def spans(rows, high):
    if not high:
        return ((0, 2 * rows, True),)
    free = 2 * rows // 128 * 128
    return ((0, free, False), (free, 4 * rows - free, True))


def attend_block(rows, start, high, qkv, attended, lse):
    width = attended.shape[1]
    here = pl.ds(start, rows)
    lane = lax.broadcasted_iota(jnp.int32, (rows, 128), 1)
    tops = jnp.zeros((rows, 128), f32)
    for pair in range(width // 128):
        columns = slice(pair * 128, pair * 128 + 128)
        query = qkv[here, columns] * bf16(HEAD_DIM ** (-0.5))
        results = []
        for half in range(2):
            only = jnp.where(head_lanes(query.shape, half), query, 0)
            scores = []
            for begin, size, mask in spans(rows, high):
                part = dot_nt(only, qkv[pl.ds(begin, size), width + pair * 128 : width + pair * 128 + 128])
                scores.append(masked(part, start, begin) if mask else part)
            top = functools.reduce(jnp.maximum, [jnp.max(part, axis=-1, keepdims=True) for part in scores])
            total, result = 0.0, 0.0
            for (begin, size, _), part in zip(spans(rows, high), scores):
                weights = jnp.exp(part - top)
                total = total + jnp.sum(weights, axis=-1, keepdims=True)
                values = qkv[pl.ds(begin, size), 2 * width + pair * 128 : 2 * width + pair * 128 + 128]
                result = result + dot_nn(weights.astype(bf16), values)
            results.append(result / total)
            tops = jnp.where(lane == 2 * pair + half, top + jnp.log(total), tops)
        attended[here, columns] = jnp.where(head_lanes((rows, 128), 0), results[0], results[1]).astype(bf16)
    lse[here, :] = tops


def attention_forward(layer, stream, gains, shifts, w_qkv, w_out, own_qkv, own_out, weights, groups=None):
    rows, model = stream.shape
    width = own_out.shape[1]
    first = groups is not None
    early = {"qkv": own_qkv, "out": own_out} if first else {}

    def body(r):
        held, qkv, attended, lse, weight = r.held, r.qkv, r.attended, r.lse, r.matrix
        w_qkv, w_out = (r.qkv_to, r.out_to) if first else (r.w_qkv, r.w_out)
        loads = [
            Loading(r.own_qkv.at[layer, index], w_qkv.at[index], weight.at[:, pl.ds(index * width, width)], r.local.at[index])
            for index in range(3)
        ]
        loads.append(Loading(r.own_out.at[layer], w_out, r.out, r.local.at[3]))
        if not first:
            every(loads, "start")
        greet(*GROUP, *(FETCH if weights else ()), *((("c", "zh"),) if first else ()))
        jobs = fetch_jobs(r, weights, layer)
        stream = r.stream
        r.ready()
        if first:
            swap = Swapping(r.stream, r.landed, r.swap)
            index = lax.broadcasted_iota(jnp.int32, r.sizes.shape, 1)
            size = jnp.sum(jnp.where(index == r.ids[...], r.sizes[...], 0), axis=1, keepdims=True)
            r.weight[...] = jnp.broadcast_to(1.0 / size.astype(f32), r.weight.shape)
            exchanged = remote(r.weight, r.other, r.swap.at[4], r.swap.at[5], flipped("c"))
            before = [
                Fetching(source.at[layer], target, send, receive)
                for source, target, send, receive in (
                    (r.own_qkv, r.qkv_to, r.qkv_send, r.qkv_receive), (r.own_out, r.out_to, r.out_send, r.out_receive)
                )
            ]
            before[0].step_inner()
            before[0].step_outer()
            before[0].step_sent()
            exchanged.start()
            before[0].step_share()
            exchanged.wait()
            r.scale[...] = jnp.where(holds(), r.weight[...], r.other[...])
            swap.start()
            before[1].step_inner()
            before[1].step_outer()
            before[0].step_relay()
            stream = r.stream_out
        own = places(rows)[0]

        def prepare(start, size):
            part = pl.ds(start, size)
            if first:
                swap.give(r.stream_out, r.stream, None, (0 if start == 0 else 1,))
            value = norm_rows(stream[part, :], r.gains[layer, 0:1, :], r.shifts[layer, 0:1, :])
            held[pl.ds(pl.multiple_of(own + start, 16), size), :] = value.astype(bf16)

        calls = []

        def arrived(start, size):
            calls.append(start)
            if len(calls) == 1:
                if first:
                    before[1].step_share()
                    before[0].step_got()
                    every(loads[:3], "start")
                    every(loads[:3], "wait")
                else:
                    every(jobs, "step_outer")
                    every(loads, "wait")
            if len(calls) == 2 and first:
                every(jobs, "step_outer")
                before[1].step_relay()
            here = pl.ds(start, size)

            def step(columns):
                qkv[here, columns] = dot_nn(held[here, :], weight[:, columns]).astype(bf16)

            tiles(3 * width, step)

        sent = gather(rows, held, prepare, arrived, r.send, r.receive)
        stores = [pltpu.make_async_copy(held, r.held_out, r.local.at[0]), pltpu.make_async_copy(qkv, r.qkv_out, r.local.at[1])]
        for copy in stores:
            copy.start()
        zl = lax.axis_index("zl")

        def attend(quarter, high):
            attend_block(rows, pl.multiple_of(quarter * rows, 16), high, qkv, attended, lse)

        every(jobs, "step_inner")

        def before_part(name):
            if name == "high":
                attend(3 - zl, True)
                if first:
                    before[1].step_end()
                    loads[3].start()
                    loads[3].wait()
            elif name == "low":
                attend(1 - zl, False)
                if first:
                    every(jobs[:1], "step_share")
            else:
                attend(2 + zl, True)
                every(jobs[1:] if first else jobs, "step_share")
                attend(zl, False)

        def term(start, size, sink):
            here = pl.ds(start, size)

            def step(columns):
                sink(columns, dot_nn(attended[here, :], r.out[:, columns]))

            tiles(model, step)

        finish = scatter(rows, before_part, term, r.first, r.sums, r.send, r.receive)
        late = [pltpu.make_async_copy(attended, r.attended_out, r.local.at[2]), pltpu.make_async_copy(lse, r.lse_out, r.local.at[3])]
        for copy in late:
            copy.start()
        every(jobs, "step_relay")

        def done(start, size, total):
            part = pl.ds(start, size)
            r.branch[part, :] = total
            r.middle[part, :] = stream[part, :] + norm_rows(total, r.gains[layer, 1:2, :], r.shifts[layer, 1:2, :])

        finish(done)
        sent()
        every(jobs, "step_end")
        if first:
            swap.end()
        for copy in stores + late:
            copy.wait()

    return run(
        body,
        1 + layer,
        {
            "stream": (stream, VMEM), "gains": (gains, VMEM), "shifts": (shifts, VMEM), "own_qkv": (own_qkv, ANY), "own_out": (own_out, ANY),
            **fetch_inputs(weights), **({"ids": (groups[0], VMEM), "sizes": (groups[1], VMEM)} if first else {"w_qkv": (w_qkv, ANY), "w_out": (w_out, ANY)}),
        },
        {
            "branch": ((rows, model), f32, VMEM), "middle": ((rows, model), f32, VMEM),
            "held_out": ((4 * rows, model), bf16, ANY), "qkv_out": ((4 * rows, 3 * width), bf16, ANY),
            "attended_out": ((4 * rows, width), bf16, ANY), "lse_out": ((4 * rows, 128), f32, ANY), **fetch_outputs(weights),
            **fetch_outputs(early),
            **({"stream_out": (stream.shape, f32, VMEM), "scale": ((8, 128), f32, VMEM)} if first else {}),
        },
        {
            "held": VMEM((4 * rows, model), bf16), "qkv": VMEM((4 * rows, 3 * width), bf16), "attended": VMEM((4 * rows, width), bf16),
            "lse": VMEM((4 * rows, 128), f32), "matrix": VMEM((model, 3 * width), bf16), "out": VMEM((width, model), bf16),
            **group_scratch(rows, model), "local": semaphores(4), **fetch_scratch(weights),
            **fetch_scratch(early),
            **({"landed": VMEM(stream.shape, bf16), "weight": VMEM((8, 128), f32), "other": VMEM((8, 128), f32), "swap": semaphores(6)} if first else {}),
        },
        24 * rows * model * width,
        64 * rows * rows,
    )


def attend_block_back(rows, start, high, qkv, attended_grad, lse, inner, grad_query, grad_key, grad_value):
    width = attended_grad.shape[1]
    here = pl.ds(start, rows)
    scale = HEAD_DIM ** (-0.5)
    for pair in range(width // 128):
        columns = slice(pair * 128, pair * 128 + 128)
        query = qkv[here, columns] * bf16(scale)
        above = attended_grad[here, columns]
        queries = [jnp.where(head_lanes(query.shape, half), query, 0) for half in range(2)]
        grads = [jnp.where(head_lanes(query.shape, half), above, 0) for half in range(2)]
        result = 0.0
        for begin, size, mask in spans(rows, high):
            keys = pl.ds(begin, size)
            key = qkv[keys, width + pair * 128 : width + pair * 128 + 128]
            value = qkv[keys, 2 * width + pair * 128 : 2 * width + pair * 128 + 128]
            both_probs, both_scores = [], []
            for half in range(2):
                head = 2 * pair + half
                scores = dot_nt(queries[half], key)
                if mask:
                    scores = masked(scores, start, begin)
                probs = jnp.exp(scores - lse[here, head : head + 1])
                grad_probs = dot_nt(grads[half], value)
                grad_scores = (probs * (grad_probs - inner[here, head : head + 1])).astype(bf16)
                key_only = jnp.where(head_lanes(key.shape, half), key, 0)
                result = result + dot_nn(grad_scores, key_only)
                both_probs.append(probs.astype(bf16))
                both_scores.append(grad_scores)
            grad_key[keys, columns] += dot_tn(jnp.concatenate(both_scores), jnp.concatenate(queries))
            grad_value[keys, columns] += dot_tn(jnp.concatenate(both_probs), jnp.concatenate(grads))
        grad_query[here, columns] = (result * scale).astype(bf16)


def attention_backward(layer, grad, stream, saved, gains, shifts, w_qkv, w_out, own_qkv, own_out, grads, norms=None, mixed=None):
    rows, model = stream.shape
    width = w_out.shape[0]
    final = norms is not None
    shape = jax.ShapeDtypeStruct
    thirds = ("query_last", "key_last", "value_last")
    mine = {name: (shape(w_qkv.shape[1:], bf16), 0, 2) for name in thirds} if final else {}
    mine_out = {"out_last": (shape(w_out.shape, bf16), 0, 2)} if final else {}

    def body(r):
        held, past, qkv, attended, lse, inner, above = r.held, r.past, r.qkv, r.attended, r.lse, r.inner, r.above
        pushed, grad_key, grad_value, weight = r.pushed, r.grad_key, r.grad_value, r.weight
        loads = [
            Loading(r.own_out.at[layer], r.w_out, r.out, r.local.at[3]),
            pltpu.make_async_copy(r.attended_in, attended, r.local.at[4]),
            pltpu.make_async_copy(r.qkv_in, qkv, r.local.at[5]),
            pltpu.make_async_copy(r.lse_in, lse, r.local.at[6]),
            *[
                Loading(r.own_qkv.at[layer, index], r.w_qkv.at[index], weight.at[:, pl.ds(index * width, width)], r.local.at[index])
                for index in range(3)
            ],
            pltpu.make_async_copy(r.held_in, past, r.local.at[7]),
        ]
        for copy in loads:
            copy.start()
        greet(*GROUP, *(FETCH if grads else ()), *((("c", "zh"),) if final or mixed is not None else ()))
        ends = {"out_last": (r.outcome_out,)}
        if final:
            ends.update({name: (r.outcome.at[index], r.qkv_last_out.at[index]) for index, name in enumerate(thirds)})
        jobs = pass_jobs(r, {**grads, **mine, **mine_out}, ends)
        new = [name for name in grads if grads[name][1] == 0]
        crossing = [name for name in grads if grads[name][1] == 1]
        r.ready()
        swaps = []
        if mixed is not None:
            r.low[...] = r.mixed[...].astype(bf16)
            swaps.append(Swapping(r.low, r.landed, r.swap))
        every_of(jobs, crossing, "step_load")
        every_of(jobs, new[:1], "step_spread")
        older = crossing
        own = places(rows)[0]
        norms_of = {}

        def pull(row, values, part, grad):
            pulled, *sums = norm_pull(values[part, :], r.gains[layer, row : row + 1, :], grad)
            norms_of[row] = [old + new for old, new in zip(norms_of.get(row, (0.0, 0.0)), sums)]
            return pulled

        def prepare(start, size):
            part = pl.ds(start, size)
            value = pull(1, r.branch, part, r.grad[part, :])
            held[pl.ds(pl.multiple_of(own + start, 16), size), :] = value.astype(bf16)

        zl = lax.axis_index("zl")

        def back(quarter, high):
            attend_block_back(
                rows, pl.multiple_of(quarter * rows, 16), high, qkv, above, lse, inner, pushed, grad_key, grad_value
            )

        blocks = []

        def arrived(start, size):
            if not blocks:
                grad_key[...] = jnp.zeros_like(grad_key)
                grad_value[...] = jnp.zeros_like(grad_value)
                every(loads, "wait")
            here = pl.ds(start, size)
            value = dot_nt(held[here, :], r.out[...]).astype(bf16)
            above[here, :] = value
            product = value.astype(f32) * attended[here, :].astype(f32)
            lane = lax.broadcasted_iota(jnp.int32, (size, 128), 1)
            tile = jnp.zeros((size, 128), f32)
            for pair in range(width // 128):
                part = product[:, pair * 128 : pair * 128 + 128]
                for half in range(2):
                    one = jnp.sum(jnp.where(head_lanes(part.shape, half), part, 0.0), axis=-1, keepdims=True)
                    tile = jnp.where(lane == 2 * pair + half, one, tile)
            inner[here, :] = tile
            blocks.append(size)
            if len(blocks) == 2:
                back(2 + zl, True)
                every_of(jobs, new[1:], "step_spread")
                back(zl, False)

        sent = gather(rows, held, prepare, arrived, r.send, r.receive)
        every(swaps, "start")
        every_of(jobs, crossing, "step_loaded", "step_outer", "step_inner")

        def step_out(columns):
            r.outcome_out[:, columns] = dot_tn(attended[...], held[:, columns]).astype(bf16)

        outs = []
        if final:
            tiles(model, step_out)
            every_of(jobs, mine_out, "step_spread")
        every_of(jobs, new[:1], "step_fold")

        def step_qkv(columns):
            value = dot_tn(past[:, columns], pushed[...]).astype(bf16)
            for index in range(3):
                r.outcome[index, columns, :] = value[:, index * width : (index + 1) * width]

        def cast(quarter):
            part = pl.ds(pl.multiple_of(quarter * rows, 16), rows)
            pushed[part, pl.ds(width, width)] = grad_key[part, :].astype(bf16)
            pushed[part, pl.ds(2 * width, width)] = grad_value[part, :].astype(bf16)

        def before_part(name):
            if name == "high":
                back(3 - zl, True)
                cast(3 - zl)
            elif name == "low":
                every_of(jobs, new[1:], "step_fold")
                every_of(jobs, new[:1], "step_add", "step_outer", "step_inner")
                every_of(jobs, mine_out, "step_fold")
                back(1 - zl, False)
                cast(1 - zl)
            else:
                cast(2 + zl)
                cast(zl)
                if final:
                    every_of(jobs, older, "step_join")
                    tiles(model, step_qkv)
                    every_of(jobs, mine, "step_spread")
                    every_of(jobs, mine_out, "step_add")
                    every_of(jobs, new[1:], "step_add", "step_outer", "step_inner")
                    every_of(jobs, mine_out, "step_outer", "step_inner")

        def term(start, size, sink):
            here = pl.ds(start, size)

            def step(columns):
                sink(columns, dot_nt(pushed[here, :], weight[columns, :]))

            tiles(model, step)

        finish = scatter(rows, before_part, term, r.first, r.sums, r.send, r.receive)
        if final:
            every_of(jobs, mine, "step_fold")
            every_of(jobs, older, "step_relay")
            every_of(jobs, new[:1], "step_join")
        else:
            every_of(jobs, new[1:], "step_add")
            tiles(model, step_out)
            outs.append(pltpu.make_async_copy(r.outcome_out, r.grad_out, r.local.at[0]))
            outs[0].start()
            tiles(model, step_qkv)
            outs.append(pltpu.make_async_copy(r.outcome, r.grad_qkv, r.local.at[1]))
            outs[1].start()

        def done(start, size, total):
            part = pl.ds(start, size)
            target = r.home if final else r.grad_stream
            target[part, :] = r.grad[part, :] + pull(0, r.stream, part, total)

        finish(done)
        if not final:
            every_of(jobs, new[:1], "step_join")
            every_of(jobs, new, "step_store")
        for swap in swaps:
            swap.give(r.mixed_out, r.mixed)
            swap.end()
        rows_norms = (*norms_of[0], *norms_of[1])
        if final:
            r.low[...] = r.home[...].astype(bf16)
            swap = Swapping(r.low, r.landed, r.swap)
            for index, value in enumerate(rows_norms):
                r.norms[index : index + 1, :] = value
            for index in range(len(norms)):
                r.norms[pl.ds(4 + 4 * index, 4), :] = getattr(r, f"norms{index}")[...]

            def cube(index, wait):
                copy = remote(
                    r.norms, r.norms_land.at[index], r.swap.at[4 + index], r.swap.at[9 + index], flipped(CUBE[index])
                )
                if not wait:
                    copy.start()
                    return
                copy.wait()
                r.norms[...] = r.norms[...] + r.norms_land[index]

            cube(0, False)
            cube(0, True)
            cube(1, False)
            for name in mine:
                every_of(jobs, [name], "step_add", "step_outer", "step_inner")
            cube(1, True)
            cube(2, False)
            every_of(jobs, older, "step_mate")
            cube(2, True)
            cube(3, False)
            every_of(jobs, new[1:], "step_join")
            every_of(jobs, mine_out, "step_join")
            cube(3, True)
            cube(4, False)
            swap.start()
            every_of(jobs, new[:1], "step_relay")
            every_of(jobs, new[:1], "step_mate")
            for name in mine:
                every_of(jobs, [name], "step_join")
            every_of(jobs, new[1:], "step_relay")
            every_of(jobs, mine_out, "step_relay")
            every_of(jobs, mine, "step_relay")
            every_of(jobs, new[1:], "step_mate")
            every_of(jobs, mine_out, "step_mate")
            every_of(jobs, mine, "step_mate")
            cube(4, True)
            swap.give(r.grad_stream, r.home)
            swap.end()
        else:
            for index, value in enumerate(rows_norms):
                r.norms[index : index + 1, :] = value
        sent()
        every(outs, "wait")
        every_of(jobs, jobs, "step_end")

    return run(
        body,
        7 + layer,
        {
            "grad": (grad, VMEM), "branch": (saved.branch, VMEM), "stream": (stream, VMEM), "gains": (gains, VMEM),
            "shifts": (shifts, VMEM), "held_in": (saved.held_out, ANY), "qkv_in": (saved.qkv_out, ANY),
            "attended_in": (saved.attended_out, ANY), "lse_in": (saved.lse_out, ANY), "w_qkv": (w_qkv, ANY), "w_out": (w_out, ANY), "own_qkv": (own_qkv, ANY), "own_out": (own_out, ANY),
            **pass_inputs(grads), **({} if mixed is None else {"mixed": (mixed, VMEM)}), **({f"norms{index}": (value, VMEM) for index, value in enumerate(norms)} if final else {}),
        },
        {
            **pass_outputs({**grads, **mine_out}),
            **({"qkv_last_out": (w_qkv.shape, bf16, ANY)} if final else {}),
            **({} if mixed is None else {"mixed_out": (mixed.shape, f32, VMEM)}),
            "grad_stream": ((rows, model), f32, VMEM), "norms": ((16 if final else 4, model), f32, VMEM),
            **({} if final else {"grad_qkv": (w_qkv.shape, bf16, ANY), "grad_out": (w_out.shape, bf16, ANY)}),
        },
        {
            "held": VMEM((4 * rows, model), bf16), "past": VMEM((4 * rows, model), bf16), "qkv": VMEM((4 * rows, 3 * width), bf16),
            "attended": VMEM((4 * rows, width), bf16), "lse": VMEM((4 * rows, 128), f32), "inner": VMEM((4 * rows, 128), f32),
            "above": VMEM((4 * rows, width), bf16), "pushed": VMEM((4 * rows, 3 * width), bf16),
            "grad_key": VMEM((4 * rows, width), f32), "grad_value": VMEM((4 * rows, width), f32),
            "weight": VMEM((model, 3 * width), bf16), "out": VMEM(w_out.shape, bf16), "outcome": VMEM((3, model, width), bf16),
            "outcome_out": VMEM(w_out.shape, bf16), **group_scratch(rows, model), "local": semaphores(8),
            **pass_scratch({**grads, **mine, **mine_out}),
            **(
                {}
                if mixed is None
                else {"low": VMEM(mixed.shape, bf16), "landed": VMEM(mixed.shape, bf16), "swap": semaphores(4)}
            ),
            **(
                {
                    "home": VMEM((rows, model), f32), "low": VMEM((rows, model), bf16), "landed": VMEM((rows, model), bf16),
                    "norms_land": VMEM((len(CUBE), 16, model), f32), "swap": semaphores(14),
                }
                if final
                else {}
            ),
        },
        60 * rows * model * width,
        64 * rows * rows,
    )


def per_device(hidden_in, cotangent, group_ids, group_sizes, w_qkv, w_out, w_up, w_down, gains, shifts):
    groups = (group_ids.reshape(1, 1), group_sizes.reshape(1, -1))
    own_att, own_ffn = (w_qkv, w_out), (w_up, w_down)
    att_zero = attention_forward(
        0, hidden_in, gains, shifts, None, None, *own_att, {"up": w_up, "down": w_down}, groups
    )
    att_weights = [(att_zero.qkv_to, att_zero.out_to)]
    ffn_weights = [(att_zero.up_to, att_zero.down_to)]
    ffn_zero = ffn_forward(
        0, att_zero.middle, gains, shifts, *ffn_weights[0], *own_ffn, {"qkv": w_qkv, "out": w_out, "down": w_down}
    )
    att_weights.append((ffn_zero.qkv_to, ffn_zero.out_to))
    att_one = attention_forward(1, ffn_zero.stream, gains, shifts, *att_weights[1], *own_att, {"up": w_up})
    ffn_weights.append((att_one.up_to, ffn_zero.down_to))
    ffn_one = ffn_forward(
        1, att_one.middle, gains, shifts, *ffn_weights[1], *own_ffn, {}, cotangent, att_zero.scale
    )
    ffn_zero.middle, ffn_one.middle = att_zero.middle, att_one.middle
    back_one = ffn_backward(1, ffn_one.grad, ffn_one, gains, shifts, *ffn_weights[1], *own_ffn, {})
    deep_one = attention_backward(
        1, back_one.grad_middle, ffn_zero.stream, att_one, gains, shifts, *att_weights[1], *own_att,
        {"up1": (back_one.grad_up, 0, 1), "down1": (back_one.grad_down, 0, 0)},
        mixed=ffn_one.stream,
    )
    back_zero = ffn_backward(
        0, deep_one.grad_stream, ffn_zero, gains, shifts, *ffn_weights[0], *own_ffn,
        {"up1": (deep_one.up1_out, 2, 2), "down1": (deep_one.down1_out, 1, 2), "qkv1": (deep_one.grad_qkv, 0, 0), "out1": (deep_one.grad_out, 0, 0)},
    )
    last = attention_backward(
        0, back_zero.grad_middle, att_zero.stream_out, att_zero, gains, shifts, *att_weights[0], *own_att,
        {
            "qkv1": (back_zero.qkv1_out, 1, 2), "out1": (back_zero.out1_out, 1, 2),
            "up0": (back_zero.grad_up, 0, 2), "down0": (back_zero.grad_down, 0, 2),
        },
        (back_zero.norms, deep_one.norms, back_one.norms),
    )
    grads = [
        jnp.stack(pair).astype(f32)
        for pair in (
            (last.qkv_last_out, last.qkv1_out),
            (last.out_last_out, last.out1_out),
            (last.up0_out, back_zero.up1_out),
            (last.down0_out, back_zero.down1_out),
        )
    ]
    sums = last.norms.reshape(2, 4, 2, -1)
    if lax.axis_size("gh") > 1:
        grads, sums = lax.psum((grads, sums), "gh")
    return (deep_one.mixed_out, last.grad_stream, *grads, sums[:, :, 0], sums[:, :, 1])


def solution(mesh):
    fine = jax.sharding.Mesh(mesh.devices.reshape(-1, 2, 2, 2, 2, 2), AXES)
    dp = ("gh", "gl", "p", "c")
    tensor = ("zh", "zl")
    rows = P((*dp, *tensor), None)
    weights = (
        P(None, None, None, tensor),
        P(None, tensor, None),
        P(None, None, tensor),
        P(None, tensor, None),
    )
    return jax.shard_map(
        per_device,
        mesh=fine,
        in_specs=(rows, rows, P(dp), P(), *weights, P(), P()),
        out_specs=(rows, rows, *weights, P(), P()),
        check_vma=False,
    )
```

```python
import functools
import types

import jax
import jax.numpy as jnp
from jax import lax
from jax.experimental import pallas as pl
from jax.experimental.pallas import tpu as pltpu
from jax.sharding import PartitionSpec as P

HEAD_DIM = 64
AXES = ("gh", "gl", "p", "c", "zh", "zl")
f32 = jnp.float32
bf16 = jnp.bfloat16
MESH = pl.DeviceIdType.MESH
VMEM, ANY = pltpu.VMEM, pl.ANY
eps_norm = 1e-05
TILE = 256


def centre(values):
    mean = jnp.mean(values, axis=-1, keepdims=True)
    centred = values - mean
    spread = jnp.mean(centred * centred, axis=-1, keepdims=True)
    rate = lax.rsqrt(spread + eps_norm)
    return centred * rate, rate


def norm_rows(values, gain, shift):
    return centre(values)[0] * gain + shift


def norm_pull(values, gain, grad):
    hat, rate = centre(values)
    scaled = grad * gain
    along = jnp.mean(scaled * hat, axis=-1, keepdims=True)
    level = jnp.mean(scaled, axis=-1, keepdims=True)
    return (
        rate * (scaled - level - hat * along),
        jnp.sum(grad * hat, axis=0, keepdims=True),
        jnp.sum(grad, axis=0, keepdims=True),
    )


def dot_nt(left, right):
    return lax.dot_general(left, right, (((1,), (1,)), ((), ())), preferred_element_type=f32)


def dot_tn(left, right):
    return lax.dot_general(left, right, (((0,), (0,)), ((), ())), preferred_element_type=f32)


def dot_nn(left, right):
    return jnp.dot(left, right, preferred_element_type=f32)


def cut_rows(rows):
    first = (rows // 2 + 15) // 16 * 16
    return ((0, first), (first, rows - first))


def flipped(*names):
    return {name: 1 - lax.axis_index(name) for name in names}


def greet(*others):
    barrier = pltpu.get_barrier_semaphore()
    for names in others:
        pl.semaphore_signal(barrier, inc=1, device_id=flipped(*names), device_id_type=MESH)
    pl.semaphore_wait(barrier, len(others))


GROUP = (("c",), ("zl",))
FETCH = (("zh",), ("p",), ("gl",))


def remote(source, target, send, receive, device):
    return pltpu.make_async_remote_copy(
        src_ref=source,
        dst_ref=target,
        send_sem=send,
        recv_sem=receive,
        device_id=device,
        device_id_type=MESH,
    )


def tiles(width, body):
    def step(index, carry):
        body(pl.ds(pl.multiple_of(index * TILE, TILE), TILE))
        return carry

    lax.fori_loop(0, width // TILE, step, 0)


def exchange(rows, held, prepare, work, first, sums, send, receive):
    mate, near = flipped("c"), flipped("zl")
    own = pl.ds(0, rows)
    parts = cut_rows(rows)
    along = []
    for index, (start, size) in enumerate(parts):
        prepare(start, size)
        place = pl.ds(2 * rows + 2 * start, size)
        copy = remote(held.at[pl.ds(start, size)], held.at[place], send.at[1 + index], receive.at[1 + index], near)
        copy.start()
        along.append(copy)
    copies = [remote(held.at[own], held.at[pl.ds(rows, rows)], send.at[0], receive.at[0], mate)]
    copies[0].start()

    def keep(row, columns, value):
        first[pl.ds(row, value.shape[0]), columns] = value

    work(0, rows, keep)
    copies[0].wait_recv()

    def keep_mate(row, columns, value):
        sums[0, pl.ds(row - rows, value.shape[0]), columns] = value.astype(bf16)

    work(rows, rows, keep_mate)
    back = remote(sums.at[0], sums.at[1], send.at[3], receive.at[3], mate)
    back.start()
    copies.append(back)
    final = []
    for index, (start, size) in enumerate(parts):
        place = 2 * rows + 2 * start
        along[index].wait_recv()
        relay = remote(
            held.at[pl.ds(place, size)], held.at[pl.ds(place + size, size)], send.at[4 + index], receive.at[4 + index], mate
        )
        relay.start()
        relay.wait_recv()

        def keep_far(row, columns, value, place=place, start=start, size=size):
            first[pl.ds(rows + start, size), columns] = value[:size]
            sums[2, pl.ds(start, size), columns] = value[size:].astype(bf16)

        work(place, 2 * size, keep_far)
        part = pl.ds(start, size)
        cross = remote(sums.at[2, part], sums.at[3, part], send.at[6 + index], receive.at[6 + index], mate)
        cross.start()
        cross.wait_recv()
        sums[4, part, :] = (first[pl.ds(rows + start, size), :] + sums[3, part, :].astype(f32)).astype(bf16)
        last = remote(sums.at[4, part], sums.at[5, part], send.at[8 + index], receive.at[8 + index], near)
        last.start()
        final.append(last)
        copies += [relay, cross]

    def finish(done):
        back.wait_recv()
        for copy, (start, size) in zip(final, parts):
            copy.wait_recv()
            done(start, size, summed(first, sums, start, size))
        every(copies + along + final, "wait_send")

    return finish


def summed(first, sums, start, size):
    part = pl.ds(start, size)
    return first[part, :] + sums[1, part, :].astype(f32) + sums[5, part, :].astype(f32)


def run(body, number, inputs, outputs, scratch, flops, transcendentals=0):
    copied = [name for name, (_, memory) in inputs.items() if memory is VMEM]
    own = {name: VMEM(inputs[name][0].shape, inputs[name][0].dtype) for name in copied}
    names = [*inputs, *outputs, *scratch, *(name + "_copy" for name in copied), "arrivals"]

    def kernel(*refs):
        found = dict(zip(names, refs))
        copies = [
            pltpu.make_async_copy(found[name], found[name + "_copy"], found["arrivals"].at[index])
            for index, name in enumerate(copied)
        ]
        every(copies, "start")
        found.update({name: found[name + "_copy"] for name in copied})
        body(types.SimpleNamespace(**found, ready=lambda: every(copies, "wait"), greet=greet))

    moved = sum(value.size * value.dtype.itemsize for value, _ in inputs.values())
    results = pl.pallas_call(
        kernel,
        out_shape=tuple(jax.ShapeDtypeStruct(shape, kind) for shape, kind, _ in outputs.values()),
        in_specs=[pl.BlockSpec(memory_space=ANY) for _ in inputs],
        out_specs=tuple(pl.BlockSpec(memory_space=memory) for _, _, memory in outputs.values()),
        scratch_shapes=[*scratch.values(), *own.values(), semaphores(len(copied))],
        compiler_params=pltpu.CompilerParams(collective_id=number, has_side_effects=True, vmem_limit_bytes=58 << 20),
        cost_estimate=pl.CostEstimate(flops=flops, bytes_accessed=moved, transcendentals=transcendentals),
    )(*[value for value, _ in inputs.values()])
    return types.SimpleNamespace(**dict(zip(outputs, results)))


def plan(body, inputs, outputs, scratch, flops, transcendentals=0):
    return types.SimpleNamespace(
        body=body, inputs=inputs, outputs=outputs, scratch=scratch, flops=flops, transcendentals=transcendentals
    )


def run_both(number, first, second, links, extra=()):
    def both(one, two):
        return {**{"a_" + name: value for name, value in one.items()}, **{"b_" + name: value for name, value in two.items()}}

    def parts(found):
        return [{name[2:]: value for name, value in found.items() if name[:2] == mark} for mark in ("a_", "b_")]

    def body(r):
        one, two = parts(vars(r))
        two.update({name: one[source] for name, source in links.items()})
        first.body(types.SimpleNamespace(**one, ready=r.ready, greet=lambda *others: greet(*others, *extra)))
        second.body(types.SimpleNamespace(**two, ready=lambda: None, greet=lambda *others: None))

    result = run(
        body,
        number,
        both(first.inputs, {name: value for name, value in second.inputs.items() if name not in links}),
        both(first.outputs, second.outputs),
        both(first.scratch, second.scratch),
        first.flops + second.flops,
        first.transcendentals + second.transcendentals,
    )
    return [types.SimpleNamespace(**part) for part in parts(vars(result))]


def semaphores(count):
    return pltpu.SemaphoreType.DMA((count,))


def group_scratch(rows, width):
    return {
        "first": VMEM((2 * rows, width), f32),
        "sums": VMEM((6, rows, width), bf16),
        "send": semaphores(10),
        "receive": semaphores(10),
    }


def pick(ref, rows):
    return ref.at[:, rows, :] if len(ref.shape) == 3 else ref.at[rows, :]


def part_shape(shape, parts):
    return (*shape[:-2], int(shape[-2] / parts), shape[-1])


def inner():
    return lax.axis_index("zl") != lax.axis_index("zh")


def holds():
    return lax.axis_index("c") == lax.axis_index("zh")


def fetch_jobs(refs, names, layer):
    return [
        Fetching(
            getattr(refs, name + "_from").at[layer], getattr(refs, name + "_to"), getattr(refs, name + "_send"),
            getattr(refs, name + "_receive"),
        )
        for name in names
    ]


def fetch_inputs(weights):
    return {name + "_from": (value, ANY) for name, value in weights.items()}


def fetch_outputs(weights):
    return {name + "_to": (value.shape[1:], bf16, ANY) for name, value in weights.items()}


def fetch_scratch(weights):
    result = {}
    for name in weights:
        result[name + "_send"] = semaphores(8)
        result[name + "_receive"] = semaphores(8)
    return result


class Loading:
    def __init__(self, own, fetched, target, semaphore):
        self.ways = [pltpu.make_async_copy(source, target, semaphore) for source in (own, fetched)]

    def start(self):
        pl.when(holds())(self.ways[0].start)
        pl.when(jnp.logical_not(holds()))(self.ways[1].start)

    def wait(self):
        pl.when(holds())(self.ways[0].wait)
        pl.when(jnp.logical_not(holds()))(self.ways[1].wait)


def every(jobs, step):
    for job in jobs:
        getattr(job, step)()


CUBE = ("c", "zl", "p", "gl", "zh")
ORDERS = (("p", "gl"), ("gl", "p"))


class Halves:
    def copy(self, slot, source, target, name):
        return remote(source, target, self.send.at[slot], self.receive.at[slot], flipped(name))

    def at(self, half, first, second=None):
        start = (4 * half + 2 * first) * self.size
        if second is None:
            return pl.ds(pl.multiple_of(start, 16), 2 * self.size)
        return pl.ds(pl.multiple_of(start + second * self.size, 16), self.size)


class Fetching(Halves):
    def __init__(self, source, target, send, receive):
        self.source, self.target, self.send, self.receive = source, target, send, receive
        self.size = source.shape[-2] // 8

    def own(self, half):
        return self.at(half, *[lax.axis_index(name) for name in ORDERS[half]])

    def quarter(self, half):
        return pick(self.target, self.own(half))

    def along(self, half):
        return self.copy(half, pick(self.source, self.own(half)), self.quarter(half), "zh")

    def direct(self, half, axis):
        rows = self.quarter(half)
        return self.copy(2 + 2 * half + axis, rows, rows, ORDERS[half][axis])

    def relay(self, half):
        first, second = ORDERS[half]
        rows = pick(self.target, self.at(half, lax.axis_index(first), 1 - lax.axis_index(second)))
        return self.copy(6 + half, rows, rows, first)

    def start_along(self, here):
        @pl.when(jnp.logical_and(holds(), here))
        def _():
            for half in range(2):
                self.along(half).start()

    def step_inner(self):
        self.start_along(inner())

    def step_outer(self):
        self.start_along(jnp.logical_not(inner()))

    def step_sent(self):
        @pl.when(holds())
        def _():
            for half in range(2):
                self.along(half).wait_send()

    def share_if(self, here):
        @pl.when(jnp.logical_and(jnp.logical_not(holds()), here))
        def _():
            for half in range(2):
                self.along(half).wait_recv()
                self.direct(half, 1).start()
                self.direct(half, 0).start()

    def step_share(self):
        self.share_if(True)

    def step_share_outer(self):
        self.share_if(jnp.logical_not(inner()))

    def step_share_inner(self):
        self.share_if(inner())

    def step_relay(self):
        @pl.when(jnp.logical_not(holds()))
        def _():
            for half in range(2):
                self.direct(half, 1).wait_recv()
                self.relay(half).start()

    def step_got(self):
        @pl.when(jnp.logical_not(holds()))
        def _():
            for half in range(2):
                self.direct(half, 0).wait()
                self.direct(half, 1).wait_send()
                self.relay(half).wait()

    def step_end(self):
        self.step_sent()
        self.step_got()


class Passing(Halves):
    def __init__(self, refs, name, first, last, source=None, out=None):
        self.first, self.last = first, last
        for field in ("in", "out", "land", "mine", "more", "sum", "cross", "send", "receive", "local"):
            setattr(self, field, getattr(refs, f"{name}_{field}", None))
        self.source = source if source is not None else getattr(refs, f"{name}_in", None)
        if out is not None:
            self.out = out
        self.size = self.sum.shape[-2] // 2

    def place_of(self, half):
        return [lax.axis_index(name) for name in ORDERS[half]]

    def spread(self, half):
        name = ORDERS[half][0]
        return self.copy(half, pick(self.source, self.at(half, 1 - lax.axis_index(name))), self.land.at[half], name)

    def keep(self, half):
        rows = self.at(half, lax.axis_index(ORDERS[half][0]))
        return pltpu.make_async_copy(pick(self.source, rows), self.mine.at[half], self.local.at[half])

    def second(self, index):
        return pl.ds(pl.multiple_of(index * self.size, 16), self.size)

    def fold(self, half):
        name = ORDERS[half][1]
        return self.copy(2 + half, pick(self.mine.at[half], self.second(1 - lax.axis_index(name))), self.more.at[half], name)

    def load(self):
        return pltpu.make_async_copy(self.source, self.sum, self.local.at[2])

    def store(self):
        return pltpu.make_async_copy(self.sum, self.out, self.local.at[2])

    def along(self):
        return self.copy(4, self.sum, self.cross, "zh")

    def own(self, half):
        return pick(self.sum, pl.ds(half * self.size, self.size))

    def place(self, half):
        return pltpu.make_async_copy(self.own(half), pick(self.out, self.at(half, *self.place_of(half))), self.local.at[half])

    def direct(self, half, axis):
        own = pick(self.out, self.at(half, *self.place_of(half)))
        return self.copy(5 + 2 * half + axis, self.own(half), own, ORDERS[half][axis])

    def relay(self, half):
        first, second = self.place_of(half)
        rows = pick(self.out, self.at(half, first, 1 - second))
        return self.copy(9 + half, rows, rows, ORDERS[half][0])

    def mate(self, half, index):
        first = self.place_of(half)[0]
        rows = pick(self.out, self.at(half, first if index == 0 else 1 - first))
        return self.copy(11 + 2 * half + index, rows, rows, "c")

    def step_spread(self):
        for half in range(2):
            self.spread(half).start()
            self.keep(half).start()

    def step_fold(self):
        for half in range(2):
            self.keep(half).wait()
            self.spread(half).wait_recv()
            self.mine[half] = (self.mine[half].astype(f32) + self.land[half].astype(f32)).astype(bf16)
            self.fold(half).start()

    def step_add(self):
        for half in range(2):
            self.fold(half).wait_recv()
            own = pick(self.mine.at[half], self.second(lax.axis_index(ORDERS[half][1])))
            self.own(half)[...] = (own[...].astype(f32) + self.more[half].astype(f32)).astype(bf16)

    def step_load(self):
        self.load().start()

    def step_loaded(self):
        self.load().wait()

    def step_inner(self):
        pl.when(jnp.logical_and(jnp.logical_not(holds()), inner()))(self.along().start)

    def step_outer(self):
        pl.when(jnp.logical_not(jnp.logical_or(holds(), inner())))(self.along().start)

    def join_if(self, here):
        @pl.when(jnp.logical_and(holds(), here))
        def _():
            self.along().wait_recv()
            self.sum[...] = (self.sum[...].astype(f32) + self.cross[...].astype(f32)).astype(bf16)
            if self.last == 2:
                for half in range(2):
                    self.direct(half, 1).start()
                    self.direct(half, 0).start()
                    self.place(half).start()

    def step_join_outer(self):
        self.join_if(jnp.logical_not(inner()))

    def step_join_inner(self):
        self.join_if(inner())

    def step_join(self):
        self.join_if(True)

    def step_share(self):
        @pl.when(holds())
        def _():
            for half in range(2):
                self.direct(half, 1).start()
                self.direct(half, 0).start()
                self.place(half).start()

    def step_relay(self):
        @pl.when(holds())
        def _():
            for half in range(2):
                self.direct(half, 1).wait_recv()
                self.relay(half).start()
                self.place(half).wait()
                self.mate(half, 0).start()

    def step_mate(self):
        @pl.when(holds())
        def _():
            for half in range(2):
                self.direct(half, 0).wait_recv()
                self.relay(half).wait_recv()
                self.mate(half, 1).start()

    def step_store(self):
        self.store().start()

    def step_end(self):
        if self.first == 0:
            for half in range(2):
                self.spread(half).wait_send()
                self.fold(half).wait_send()
        if self.last < 2:
            self.store().wait()

        @pl.when(holds())
        def _():
            if self.last == 2:
                for half in range(2):
                    self.direct(half, 0).wait_send()
                    self.direct(half, 1).wait_send()
                    self.relay(half).wait_send()
                    self.mate(half, 0).wait_send()
                    self.mate(half, 1).wait_send()

        @pl.when(jnp.logical_not(holds()))
        def _():
            if self.first <= 1 <= self.last:
                self.along().wait_send()
            if self.last == 2:
                for half in range(2):
                    self.mate(half, 0).wait_recv()
                    self.mate(half, 1).wait_recv()


def pass_shapes(grads):
    for name, (value, first, last) in grads.items():
        whole = value.shape if first == 0 else part_shape(value.shape, 1 / 4)
        yield name, whole, part_shape(whole, 4), first, last


def pass_jobs(refs, grads, ends=None):
    return {name: Passing(refs, name, first, last, *(ends or {}).get(name, ())) for name, (_, first, last) in grads.items()}


def pass_inputs(grads):
    return {name + "_in": (value, ANY) for name, (value, *_) in grads.items() if isinstance(value, jax.Array)}


def pass_outputs(grads):
    return {name + "_out": (whole if last == 2 else part, bf16, ANY) for name, whole, part, first, last in pass_shapes(grads)}


def pass_scratch(grads):
    result = {}
    for name, whole, part, first, last in pass_shapes(grads):
        if first == 0:
            result[name + "_land"] = VMEM((2, *part), bf16)
            result[name + "_mine"] = VMEM((2, *part), bf16)
            result[name + "_more"] = VMEM((2, *part_shape(whole, 8)), bf16)
        result[name + "_sum"] = VMEM(part, bf16)
        if first <= 1 <= last:
            result[name + "_cross"] = VMEM(part, bf16)
        result[name + "_send"] = semaphores(15)
        result[name + "_receive"] = semaphores(15)
        result[name + "_local"] = semaphores(3)
    return result


def every_of(jobs, names, *steps):
    for step in steps:
        for name in names:
            getattr(jobs[name], step)()


class Swapping:
    def __init__(self, source, landed, semaphores):
        self.source, self.landed = source, landed
        self.parts = cut_rows(source.shape[0])
        self.copies = [
            remote(
                source.at[pl.ds(start, size)], landed.at[pl.ds(start, size)], semaphores.at[index], semaphores.at[2 + index],
                flipped("c", "zh"),
            )
            for index, (start, size) in enumerate(self.parts)
        ]

    def start_if(self, here):
        @pl.when(here)
        def _():
            every(self.copies, "start")

    def start(self):
        self.start_if(jnp.logical_not(holds()))

    def step_inner(self):
        self.start_if(jnp.logical_and(jnp.logical_not(holds()), inner()))

    def step_outer(self):
        self.start_if(jnp.logical_not(jnp.logical_or(holds(), inner())))

    def give(self, target, own, scale=None, only=(0, 1)):
        factor = 1.0 if scale is None else scale
        for index in only:
            rows = pl.ds(*self.parts[index])

            @pl.when(holds())
            def _(rows=rows):
                target[rows, :] = own[rows, :].astype(f32) * factor

            @pl.when(jnp.logical_not(holds()))
            def _(index=index, rows=rows):
                self.copies[index].wait_recv()
                target[rows, :] = self.landed[rows, :].astype(f32) * factor

    def end(self):
        @pl.when(jnp.logical_not(holds()))
        def _():
            every(self.copies, "wait_send")


def gelu_and_slope(values):
    rate, cubic = 0.7978845608028654, 0.044715
    square = values * values
    bend = jnp.tanh(rate * values * (1.0 + cubic * square))
    half = 0.5 * (1.0 + bend)
    slope = half + 0.5 * values * (1.0 - bend * bend) * (rate * (1.0 + 3.0 * cubic * square))
    return values * half, slope


def ffn_forward(layer, middle, gains, shifts, w_up, w_down, own_up, own_down, weights, cotangent=None, scale=None):
    rows, width = middle.shape
    hidden = w_up.shape[1]

    def body(r):
        loads = [Loading(r.own_up.at[layer], r.w_up, r.up, r.local.at[0]), Loading(r.own_down.at[layer], r.w_down, r.down, r.local.at[1])]
        for copy in loads:
            copy.start()
        r.greet(*GROUP, *(FETCH if weights else ()), *(() if cotangent is None else (("c", "zh"),)))
        r.ready()
        jobs = fetch_jobs(r, weights, layer + 1)
        swaps = [] if cotangent is None else [Swapping(r.cotangent, r.landed, r.swap)]
        every(jobs + swaps, "step_inner")
        held, active, slope = r.held, r.active, r.slope

        def prepare(start, size):
            part = pl.ds(start, size)
            held[part, :] = norm_rows(r.middle[part, :], r.gains[layer, 2:3, :], r.shifts[layer, 2:3, :]).astype(bf16)

        calls = []

        def work(start, size, sink):
            calls.append(start)
            if len(calls) == 1:
                every(jobs + swaps, "step_outer")
                every(loads, "wait")
            if len(calls) == 3:
                every(jobs, "step_share_outer")
            if len(calls) == 4:
                every(jobs, "step_share_inner")
            here = pl.ds(start, size)

            def step(columns):
                upper = dot_nn(held[here, :], r.up[:, columns])
                value, bend = gelu_and_slope(upper)
                active[here, columns] = value.astype(bf16)
                slope[here, columns] = bend.astype(bf16)

            tiles(hidden, step)

            def step_down(columns):
                sink(start, columns, dot_nn(active[here, :], r.down[:, columns]))

            tiles(width, step_down)

        finish = exchange(rows, held, prepare, work, r.first, r.sums, r.send, r.receive)
        stores = [
            pltpu.make_async_copy(held, r.held_out, r.local.at[2]),
            pltpu.make_async_copy(active, r.active_out, r.local.at[3]),
            pltpu.make_async_copy(slope, r.slope_out, r.local.at[4]),
        ]
        for copy in stores:
            copy.start()
        every(jobs, "step_relay")

        def done(start, size, total):
            part = pl.ds(start, size)
            r.second[part, :] = total
            r.stream[part, :] = r.middle[part, :] + norm_rows(total, r.gains[layer, 3:4, :], r.shifts[layer, 3:4, :])

        finish(done)
        every(jobs, "step_end")
        for swap in swaps:
            swap.give(r.grad, r.cotangent, r.scale[0:1, 0:1])
            swap.end()
        for copy in stores:
            copy.wait()

    return plan(
        body,
        {
            "middle": (middle, VMEM), "gains": (gains, VMEM), "shifts": (shifts, VMEM), "w_up": (w_up, ANY), "w_down": (w_down, ANY), "own_up": (own_up, ANY), "own_down": (own_down, ANY),
            **fetch_inputs(weights), **({} if cotangent is None else {"cotangent": (cotangent, VMEM), "scale": (scale, VMEM)}),
        },
        {
            "second": ((rows, width), f32, VMEM), "stream": ((rows, width), f32, VMEM),
            "held_out": ((4 * rows, width), bf16, ANY), "active_out": ((4 * rows, hidden), bf16, ANY),
            "slope_out": ((4 * rows, hidden), bf16, ANY), **fetch_outputs(weights),
            **({} if cotangent is None else {"grad": ((rows, width), f32, VMEM)}),
        },
        {
            "held": VMEM((4 * rows, width), bf16), "active": VMEM((4 * rows, hidden), bf16), "slope": VMEM((4 * rows, hidden), bf16),
            "up": VMEM(w_up.shape, bf16), "down": VMEM(w_down.shape, bf16), **group_scratch(rows, width), "local": semaphores(5),
            **fetch_scratch(weights),
            **({} if cotangent is None else {"landed": VMEM(cotangent.shape, bf16), "swap": semaphores(4)}),
        },
        16 * rows * width * hidden,
        4 * rows * hidden,
    )


def ffn_backward(layer, grad, saved, gains, shifts, w_up, w_down, own_up, own_down, grads):
    middle = saved.middle
    rows, width = middle.shape
    hidden = w_up.shape[1]

    def body(r):
        held, active, slope, pushed, past = r.held, r.active, r.slope, r.pushed, r.past
        loads = [
            Loading(r.own_down.at[layer], r.w_down, r.down, r.local.at[0]),
            Loading(r.own_up.at[layer], r.w_up, r.up, r.local.at[1]),
            pltpu.make_async_copy(r.slope_in, slope, r.local.at[2]),
            pltpu.make_async_copy(r.active_in, active, r.local.at[3]),
            pltpu.make_async_copy(r.held_in, past, r.local.at[4]),
        ]
        for copy in loads:
            copy.start()
        greet(*GROUP, *(FETCH if grads else ()))
        jobs = pass_jobs(r, grads)
        new = [name for name in grads if grads[name][1] == 0]
        late = [name for name in grads if grads[name][1] == 2]
        r.ready()
        crossing = [name for name in grads if grads[name][1] == 1]
        every_of(jobs, crossing, "step_load", "step_loaded", "step_inner")
        every_of(jobs, late, "step_load")
        every_of(jobs, new, "step_spread")
        norms = {}

        def pull(row, values, part, grad):
            pulled, *sums = norm_pull(values[part, :], r.gains[layer, row : row + 1, :], grad)
            norms[row] = [old + new for old, new in zip(norms.get(row, (0.0, 0.0)), sums)]
            return pulled

        def prepare(start, size):
            part = pl.ds(start, size)
            held[part, :] = pull(3, r.second, part, r.grad[part, :]).astype(bf16)

        calls = []

        def work(start, size, sink):
            calls.append(start)
            if len(calls) == 1:
                every_of(jobs, crossing, "step_outer")
                every_of(jobs, late, "step_loaded", "step_share")
                every(loads, "wait")
            if len(calls) == 4:
                every_of(jobs, new, "step_fold")
                every_of(jobs, crossing, "step_join_outer")
            here = pl.ds(start, size)

            def step(columns):
                value = dot_nt(held[here, :], r.down[columns, :])
                pushed[here, columns] = (value * slope[here, columns].astype(f32)).astype(bf16)

            tiles(hidden, step)

            def step_up(columns):
                sink(start, columns, dot_nt(pushed[here, :], r.up[columns, :]))

            tiles(width, step_up)

        finish = exchange(rows, held, prepare, work, r.first, r.sums, r.send, r.receive)

        every_of(jobs, late, "step_relay")
        every_of(jobs, crossing, "step_join_inner")

        def step_down(columns):
            r.outcome[0, columns, :] = dot_tn(active[:, columns], held[...]).astype(bf16)

        tiles(hidden, step_down)
        out_down = pltpu.make_async_copy(r.outcome.at[0], r.grad_down, r.local.at[0])
        out_down.start()
        def step_up(columns):
            r.outcome[1, columns, :] = dot_tn(past[:, columns], pushed[...]).astype(bf16)

        tiles(width, step_up)
        out_up = pltpu.make_async_copy(r.outcome.at[1], r.grad_up, r.local.at[1])
        out_up.start()
        every_of(jobs, new, "step_add", "step_store")
        every_of(jobs, crossing, "step_relay")
        every_of(jobs, late, "step_mate")

        def done(start, size, total):
            part = pl.ds(start, size)
            r.grad_middle[part, :] = r.grad[part, :] + pull(2, r.middle, part, total)

        finish(done)
        every_of(jobs, crossing, "step_mate")
        for index, value in enumerate((*norms[2], *norms[3])):
            r.norms[index : index + 1, :] = value
        out_down.wait()
        out_up.wait()
        every_of(jobs, grads, "step_end")

    return run(
        body,
        5 + layer,
        {
            "grad": (grad, VMEM), "second": (saved.second, VMEM), "middle": (middle, VMEM), "gains": (gains, VMEM),
            "shifts": (shifts, VMEM), "held_in": (saved.held_out, ANY), "active_in": (saved.active_out, ANY),
            "slope_in": (saved.slope_out, ANY), "w_up": (w_up, ANY), "w_down": (w_down, ANY), "own_up": (own_up, ANY), "own_down": (own_down, ANY),
            **pass_inputs(grads),
        },
        {
            **pass_outputs(grads),
            "grad_middle": ((rows, width), f32, VMEM), "norms": ((4, width), f32, VMEM),
            "grad_up": (w_up.shape, bf16, ANY), "grad_down": (w_down.shape, bf16, ANY),
        },
        {
            "held": VMEM((4 * rows, width), bf16), "past": VMEM((4 * rows, width), bf16),
            "active": VMEM((4 * rows, hidden), bf16), "slope": VMEM((4 * rows, hidden), bf16),
            "pushed": VMEM((4 * rows, hidden), bf16), "up": VMEM(w_up.shape, bf16), "down": VMEM(w_down.shape, bf16),
            "outcome": VMEM((2, width, hidden), bf16), **group_scratch(rows, width), "local": semaphores(5),
            **pass_scratch(grads),
        },
        32 * rows * width * hidden,
    )


def places(rows):
    c, zl = lax.axis_index("c"), lax.axis_index("zl")

    def at(core, part):
        return pl.multiple_of((2 * core + part) * rows, 16)

    return at(c, zl), at(1 - c, zl), at(c, 1 - zl), at(1 - c, 1 - zl)


def gather(rows, held, prepare, arrived, send, receive):
    mate, near = flipped("c"), flipped("zl")
    own, others, along, across = places(rows)
    parts = cut_rows(rows)
    copies = []
    for index, (start, size) in enumerate(parts):
        prepare(start, size)
        part = pl.ds(pl.multiple_of(own + start, 16), size)
        copy = remote(held.at[part], held.at[part], send.at[1 + index], receive.at[1 + index], near)
        copy.start()
        copies.append(copy)
    here = pl.ds(own, rows)
    copies.append(remote(held.at[here], held.at[here], send.at[0], receive.at[0], mate))
    copies[-1].start()
    arrived(own, rows)
    copies[-1].wait_recv()
    arrived(others, rows)
    for index, (start, size) in enumerate(parts):
        copies[index].wait_recv()
        first = pl.multiple_of(along + start, 16)
        part = pl.ds(first, size)
        relay = remote(held.at[part], held.at[part], send.at[4 + index], receive.at[4 + index], mate)
        relay.start()
        copies.append(relay)
        arrived(first, size)
        relay.wait_recv()
        arrived(pl.multiple_of(across + start, 16), size)

    def finish():
        every(copies, "wait_send")

    return finish


def scatter(rows, before, project, first, sums, send, receive):
    mate, near = flipped("c"), flipped("zl")
    own, others, _, _ = places(rows)
    parts = cut_rows(rows)
    crossing = [
        remote(sums.at[2, pl.ds(start, size)], sums.at[3, pl.ds(start, size)], send.at[6 + index], receive.at[6 + index], mate)
        for index, (start, size) in enumerate(parts)
    ]
    final = [
        remote(sums.at[4, pl.ds(start, size)], sums.at[5, pl.ds(start, size)], send.at[8 + index], receive.at[8 + index], near)
        for index, (start, size) in enumerate(parts)
    ]
    for half, name in ((1, "high"), (0, "low")):
        before(name)
        base = pl.multiple_of((2 * half + 1 - lax.axis_index("zl")) * rows, 16)
        far = lax.axis_index("c") != half
        for index, (start, size) in enumerate(parts):

            def keep(columns, value, start=start, size=size):
                first[pl.ds(rows + start, size), columns] = value

            project(pl.multiple_of(base + start, 16), size, keep)

            @pl.when(far)
            def _(index=index, start=start, size=size):
                sums[2, pl.ds(start, size), :] = first[pl.ds(rows + start, size), :].astype(bf16)
                crossing[index].start()

        @pl.when(jnp.logical_not(far))
        def _():
            for index, (start, size) in enumerate(parts):
                crossing[index].wait_recv()
                part = pl.ds(start, size)
                sums[4, part, :] = (first[pl.ds(rows + start, size), :] + sums[3, part, :].astype(f32)).astype(bf16)
                final[index].start()

    before("rest")

    def keep_mate(columns, value):
        sums[0, :, columns] = value.astype(bf16)

    project(others, rows, keep_mate)
    back = remote(sums.at[0], sums.at[1], send.at[3], receive.at[3], mate)
    back.start()

    def keep_own(columns, value):
        first[pl.ds(0, rows), columns] = value

    project(own, rows, keep_own)

    def finish(done):
        back.wait_recv()
        for copy, (start, size) in zip(final, parts):
            copy.wait_recv()
            done(start, size, summed(first, sums, start, size))
        every([back] + crossing + final, "wait_send")

    return finish


def head_lanes(shape, half):
    lane = lax.broadcasted_iota(jnp.int32, shape, len(shape) - 1)
    return (lane < HEAD_DIM) if half == 0 else (lane >= HEAD_DIM)


def masked(scores, start, first_key):
    query = lax.broadcasted_iota(jnp.int32, scores.shape, 0) + start
    key = lax.broadcasted_iota(jnp.int32, scores.shape, 1) + first_key
    return jnp.where(key <= query, scores, -1e30)


def spans(rows, high):
    if not high:
        return ((0, 2 * rows, True),)
    free = 2 * rows // 128 * 128
    return ((0, free, False), (free, 4 * rows - free, True))


def attend_block(rows, start, high, qkv, attended, lse):
    width = attended.shape[1]
    here = pl.ds(start, rows)
    lane = lax.broadcasted_iota(jnp.int32, (rows, 128), 1)
    tops = jnp.zeros((rows, 128), f32)
    for pair in range(width // 128):
        columns = slice(pair * 128, pair * 128 + 128)
        query = qkv[here, columns] * bf16(HEAD_DIM ** (-0.5))
        results = []
        for half in range(2):
            only = jnp.where(head_lanes(query.shape, half), query, 0)
            scores = []
            for begin, size, mask in spans(rows, high):
                part = dot_nt(only, qkv[pl.ds(begin, size), width + pair * 128 : width + pair * 128 + 128])
                scores.append(masked(part, start, begin) if mask else part)
            top = functools.reduce(jnp.maximum, [jnp.max(part, axis=-1, keepdims=True) for part in scores])
            total, result = 0.0, 0.0
            for (begin, size, _), part in zip(spans(rows, high), scores):
                weights = jnp.exp(part - top)
                total = total + jnp.sum(weights, axis=-1, keepdims=True)
                values = qkv[pl.ds(begin, size), 2 * width + pair * 128 : 2 * width + pair * 128 + 128]
                result = result + dot_nn(weights.astype(bf16), values)
            results.append(result / total)
            tops = jnp.where(lane == 2 * pair + half, top + jnp.log(total), tops)
        attended[here, columns] = jnp.where(head_lanes((rows, 128), 0), results[0], results[1]).astype(bf16)
    lse[here, :] = tops


def attention_forward(layer, stream, gains, shifts, w_qkv, w_out, own_qkv, own_out, weights, groups=None):
    rows, model = stream.shape
    width = own_out.shape[1]
    first = groups is not None
    early = {"qkv": own_qkv, "out": own_out} if first else {}

    def body(r):
        held, qkv, attended, lse, weight = r.held, r.qkv, r.attended, r.lse, r.matrix
        w_qkv, w_out = (r.qkv_to, r.out_to) if first else (r.w_qkv, r.w_out)
        loads = [
            Loading(r.own_qkv.at[layer, index], w_qkv.at[index], weight.at[:, pl.ds(index * width, width)], r.local.at[index])
            for index in range(3)
        ]
        loads.append(Loading(r.own_out.at[layer], w_out, r.out, r.local.at[3]))
        if not first:
            every(loads, "start")
        r.greet(*GROUP, *(FETCH if weights else ()), *((("c", "zh"),) if first else ()))
        jobs = fetch_jobs(r, weights, layer)
        stream = r.stream
        r.ready()
        if first:
            swap = Swapping(r.stream, r.landed, r.swap)
            index = lax.broadcasted_iota(jnp.int32, r.sizes.shape, 1)
            size = jnp.sum(jnp.where(index == r.ids[...], r.sizes[...], 0), axis=1, keepdims=True)
            r.weight[...] = jnp.broadcast_to(1.0 / size.astype(f32), r.weight.shape)
            exchanged = remote(r.weight, r.other, r.swap.at[4], r.swap.at[5], flipped("c"))
            before = [
                Fetching(source.at[layer], target, send, receive)
                for source, target, send, receive in (
                    (r.own_qkv, r.qkv_to, r.qkv_send, r.qkv_receive), (r.own_out, r.out_to, r.out_send, r.out_receive)
                )
            ]
            before[0].step_inner()
            before[0].step_outer()
            before[0].step_sent()
            exchanged.start()
            before[0].step_share()
            exchanged.wait()
            r.scale[...] = jnp.where(holds(), r.weight[...], r.other[...])
            swap.start()
            before[1].step_inner()
            before[1].step_outer()
            before[0].step_relay()
            stream = r.stream_out
        own = places(rows)[0]

        def prepare(start, size):
            part = pl.ds(start, size)
            if first:
                swap.give(r.stream_out, r.stream, None, (0 if start == 0 else 1,))
            value = norm_rows(stream[part, :], r.gains[layer, 0:1, :], r.shifts[layer, 0:1, :])
            held[pl.ds(pl.multiple_of(own + start, 16), size), :] = value.astype(bf16)

        calls = []

        def arrived(start, size):
            calls.append(start)
            if len(calls) == 1:
                if first:
                    before[1].step_share()
                    before[0].step_got()
                    every(loads[:3], "start")
                    every(loads[:3], "wait")
                else:
                    every(jobs, "step_outer")
                    every(loads, "wait")
            if len(calls) == 2 and first:
                every(jobs, "step_outer")
                before[1].step_relay()
            here = pl.ds(start, size)

            def step(columns):
                qkv[here, columns] = dot_nn(held[here, :], weight[:, columns]).astype(bf16)

            tiles(3 * width, step)

        sent = gather(rows, held, prepare, arrived, r.send, r.receive)
        stores = [pltpu.make_async_copy(held, r.held_out, r.local.at[0]), pltpu.make_async_copy(qkv, r.qkv_out, r.local.at[1])]
        for copy in stores:
            copy.start()
        zl = lax.axis_index("zl")

        def attend(quarter, high):
            attend_block(rows, pl.multiple_of(quarter * rows, 16), high, qkv, attended, lse)

        every(jobs, "step_inner")

        def before_part(name):
            if name == "high":
                attend(3 - zl, True)
                if first:
                    before[1].step_end()
                    loads[3].start()
                    loads[3].wait()
            elif name == "low":
                attend(1 - zl, False)
                if first:
                    every(jobs[:1], "step_share")
            else:
                attend(2 + zl, True)
                every(jobs[1:] if first else jobs, "step_share")
                attend(zl, False)

        def term(start, size, sink):
            here = pl.ds(start, size)

            def step(columns):
                sink(columns, dot_nn(attended[here, :], r.out[:, columns]))

            tiles(model, step)

        finish = scatter(rows, before_part, term, r.first, r.sums, r.send, r.receive)
        late = [pltpu.make_async_copy(attended, r.attended_out, r.local.at[2]), pltpu.make_async_copy(lse, r.lse_out, r.local.at[3])]
        for copy in late:
            copy.start()
        every(jobs, "step_relay")

        def done(start, size, total):
            part = pl.ds(start, size)
            r.branch[part, :] = total
            r.middle[part, :] = stream[part, :] + norm_rows(total, r.gains[layer, 1:2, :], r.shifts[layer, 1:2, :])

        finish(done)
        sent()
        every(jobs, "step_end")
        if first:
            swap.end()
        for copy in stores + late:
            copy.wait()

    return plan(
        body,
        {
            "stream": (stream, VMEM), "gains": (gains, VMEM), "shifts": (shifts, VMEM), "own_qkv": (own_qkv, ANY), "own_out": (own_out, ANY),
            **fetch_inputs(weights), **({"ids": (groups[0], VMEM), "sizes": (groups[1], VMEM)} if first else {"w_qkv": (w_qkv, ANY), "w_out": (w_out, ANY)}),
        },
        {
            "branch": ((rows, model), f32, VMEM), "middle": ((rows, model), f32, VMEM),
            "held_out": ((4 * rows, model), bf16, ANY), "qkv_out": ((4 * rows, 3 * width), bf16, ANY),
            "attended_out": ((4 * rows, width), bf16, ANY), "lse_out": ((4 * rows, 128), f32, ANY), **fetch_outputs(weights),
            **fetch_outputs(early),
            **({"stream_out": (stream.shape, f32, VMEM), "scale": ((8, 128), f32, VMEM)} if first else {}),
        },
        {
            "held": VMEM((4 * rows, model), bf16), "qkv": VMEM((4 * rows, 3 * width), bf16), "attended": VMEM((4 * rows, width), bf16),
            "lse": VMEM((4 * rows, 128), f32), "matrix": VMEM((model, 3 * width), bf16), "out": VMEM((width, model), bf16),
            **group_scratch(rows, model), "local": semaphores(4), **fetch_scratch(weights),
            **fetch_scratch(early),
            **({"landed": VMEM(stream.shape, bf16), "weight": VMEM((8, 128), f32), "other": VMEM((8, 128), f32), "swap": semaphores(6)} if first else {}),
        },
        24 * rows * model * width,
        64 * rows * rows,
    )


def attend_block_back(rows, start, high, qkv, attended_grad, lse, inner, grad_query, grad_key, grad_value):
    width = attended_grad.shape[1]
    here = pl.ds(start, rows)
    scale = HEAD_DIM ** (-0.5)
    for pair in range(width // 128):
        columns = slice(pair * 128, pair * 128 + 128)
        query = qkv[here, columns] * bf16(scale)
        above = attended_grad[here, columns]
        queries = [jnp.where(head_lanes(query.shape, half), query, 0) for half in range(2)]
        grads = [jnp.where(head_lanes(query.shape, half), above, 0) for half in range(2)]
        result = 0.0
        for begin, size, mask in spans(rows, high):
            keys = pl.ds(begin, size)
            key = qkv[keys, width + pair * 128 : width + pair * 128 + 128]
            value = qkv[keys, 2 * width + pair * 128 : 2 * width + pair * 128 + 128]
            both_probs, both_scores = [], []
            for half in range(2):
                head = 2 * pair + half
                scores = dot_nt(queries[half], key)
                if mask:
                    scores = masked(scores, start, begin)
                probs = jnp.exp(scores - lse[here, head : head + 1])
                grad_probs = dot_nt(grads[half], value)
                grad_scores = (probs * (grad_probs - inner[here, head : head + 1])).astype(bf16)
                key_only = jnp.where(head_lanes(key.shape, half), key, 0)
                result = result + dot_nn(grad_scores, key_only)
                both_probs.append(probs.astype(bf16))
                both_scores.append(grad_scores)
            grad_key[keys, columns] += dot_tn(jnp.concatenate(both_scores), jnp.concatenate(queries))
            grad_value[keys, columns] += dot_tn(jnp.concatenate(both_probs), jnp.concatenate(grads))
        grad_query[here, columns] = (result * scale).astype(bf16)


def attention_backward(layer, grad, stream, saved, gains, shifts, w_qkv, w_out, own_qkv, own_out, grads, norms=None, mixed=None):
    rows, model = stream.shape
    width = w_out.shape[0]
    final = norms is not None
    shape = jax.ShapeDtypeStruct
    thirds = ("query_last", "key_last", "value_last")
    mine = {name: (shape(w_qkv.shape[1:], bf16), 0, 2) for name in thirds} if final else {}
    mine_out = {"out_last": (shape(w_out.shape, bf16), 0, 2)} if final else {}

    def body(r):
        held, past, qkv, attended, lse, inner, above = r.held, r.past, r.qkv, r.attended, r.lse, r.inner, r.above
        pushed, grad_key, grad_value, weight = r.pushed, r.grad_key, r.grad_value, r.weight
        loads = [
            Loading(r.own_out.at[layer], r.w_out, r.out, r.local.at[3]),
            pltpu.make_async_copy(r.attended_in, attended, r.local.at[4]),
            pltpu.make_async_copy(r.qkv_in, qkv, r.local.at[5]),
            pltpu.make_async_copy(r.lse_in, lse, r.local.at[6]),
            *[
                Loading(r.own_qkv.at[layer, index], r.w_qkv.at[index], weight.at[:, pl.ds(index * width, width)], r.local.at[index])
                for index in range(3)
            ],
            pltpu.make_async_copy(r.held_in, past, r.local.at[7]),
        ]
        for copy in loads:
            copy.start()
        greet(*GROUP, *(FETCH if grads else ()), *((("c", "zh"),) if final or mixed is not None else ()))
        ends = {"out_last": (r.outcome_out,)}
        if final:
            ends.update({name: (r.outcome.at[index], r.qkv_last_out.at[index]) for index, name in enumerate(thirds)})
        jobs = pass_jobs(r, {**grads, **mine, **mine_out}, ends)
        new = [name for name in grads if grads[name][1] == 0]
        crossing = [name for name in grads if grads[name][1] == 1]
        r.ready()
        swaps = []
        if mixed is not None:
            r.low[...] = r.mixed[...].astype(bf16)
            swaps.append(Swapping(r.low, r.landed, r.swap))
        every_of(jobs, crossing, "step_load")
        every_of(jobs, new[:1], "step_spread")
        older = crossing
        own = places(rows)[0]
        norms_of = {}

        def pull(row, values, part, grad):
            pulled, *sums = norm_pull(values[part, :], r.gains[layer, row : row + 1, :], grad)
            norms_of[row] = [old + new for old, new in zip(norms_of.get(row, (0.0, 0.0)), sums)]
            return pulled

        def prepare(start, size):
            part = pl.ds(start, size)
            value = pull(1, r.branch, part, r.grad[part, :])
            held[pl.ds(pl.multiple_of(own + start, 16), size), :] = value.astype(bf16)

        zl = lax.axis_index("zl")

        def back(quarter, high):
            attend_block_back(
                rows, pl.multiple_of(quarter * rows, 16), high, qkv, above, lse, inner, pushed, grad_key, grad_value
            )

        blocks = []

        def arrived(start, size):
            if not blocks:
                grad_key[...] = jnp.zeros_like(grad_key)
                grad_value[...] = jnp.zeros_like(grad_value)
                every(loads, "wait")
            here = pl.ds(start, size)
            value = dot_nt(held[here, :], r.out[...]).astype(bf16)
            above[here, :] = value
            product = value.astype(f32) * attended[here, :].astype(f32)
            lane = lax.broadcasted_iota(jnp.int32, (size, 128), 1)
            tile = jnp.zeros((size, 128), f32)
            for pair in range(width // 128):
                part = product[:, pair * 128 : pair * 128 + 128]
                for half in range(2):
                    one = jnp.sum(jnp.where(head_lanes(part.shape, half), part, 0.0), axis=-1, keepdims=True)
                    tile = jnp.where(lane == 2 * pair + half, one, tile)
            inner[here, :] = tile
            blocks.append(size)
            if len(blocks) == 2:
                back(2 + zl, True)
                every_of(jobs, new[1:], "step_spread")
                back(zl, False)

        sent = gather(rows, held, prepare, arrived, r.send, r.receive)
        every(swaps, "start")
        every_of(jobs, crossing, "step_loaded", "step_outer", "step_inner")

        def step_out(columns):
            r.outcome_out[:, columns] = dot_tn(attended[...], held[:, columns]).astype(bf16)

        outs = []
        if final:
            tiles(model, step_out)
            every_of(jobs, mine_out, "step_spread")
        every_of(jobs, new[:1], "step_fold")

        def step_qkv(columns):
            value = dot_tn(past[:, columns], pushed[...]).astype(bf16)
            for index in range(3):
                r.outcome[index, columns, :] = value[:, index * width : (index + 1) * width]

        def cast(quarter):
            part = pl.ds(pl.multiple_of(quarter * rows, 16), rows)
            pushed[part, pl.ds(width, width)] = grad_key[part, :].astype(bf16)
            pushed[part, pl.ds(2 * width, width)] = grad_value[part, :].astype(bf16)

        def before_part(name):
            if name == "high":
                back(3 - zl, True)
                cast(3 - zl)
            elif name == "low":
                every_of(jobs, new[1:], "step_fold")
                every_of(jobs, new[:1], "step_add", "step_outer", "step_inner")
                every_of(jobs, mine_out, "step_fold")
                back(1 - zl, False)
                cast(1 - zl)
            else:
                cast(2 + zl)
                cast(zl)
                if final:
                    every_of(jobs, older, "step_join")
                    tiles(model, step_qkv)
                    every_of(jobs, mine, "step_spread")
                    every_of(jobs, mine_out, "step_add")
                    every_of(jobs, new[1:], "step_add", "step_outer", "step_inner")
                    every_of(jobs, mine_out, "step_outer", "step_inner")

        def term(start, size, sink):
            here = pl.ds(start, size)

            def step(columns):
                sink(columns, dot_nt(pushed[here, :], weight[columns, :]))

            tiles(model, step)

        finish = scatter(rows, before_part, term, r.first, r.sums, r.send, r.receive)
        if final:
            every_of(jobs, mine, "step_fold")
            every_of(jobs, older, "step_relay")
            every_of(jobs, new[:1], "step_join")
        else:
            every_of(jobs, new[1:], "step_add")
            tiles(model, step_out)
            outs.append(pltpu.make_async_copy(r.outcome_out, r.grad_out, r.local.at[0]))
            outs[0].start()
            tiles(model, step_qkv)
            outs.append(pltpu.make_async_copy(r.outcome, r.grad_qkv, r.local.at[1]))
            outs[1].start()

        def done(start, size, total):
            part = pl.ds(start, size)
            target = r.home if final else r.grad_stream
            target[part, :] = r.grad[part, :] + pull(0, r.stream, part, total)

        finish(done)
        if not final:
            every_of(jobs, new[:1], "step_join")
            every_of(jobs, new, "step_store")
        for swap in swaps:
            swap.give(r.mixed_out, r.mixed)
            swap.end()
        rows_norms = (*norms_of[0], *norms_of[1])
        if final:
            r.low[...] = r.home[...].astype(bf16)
            swap = Swapping(r.low, r.landed, r.swap)
            for index, value in enumerate(rows_norms):
                r.norms[index : index + 1, :] = value
            for index in range(len(norms)):
                r.norms[pl.ds(4 + 4 * index, 4), :] = getattr(r, f"norms{index}")[...]

            def cube(index, wait):
                copy = remote(
                    r.norms, r.norms_land.at[index], r.swap.at[4 + index], r.swap.at[9 + index], flipped(CUBE[index])
                )
                if not wait:
                    copy.start()
                    return
                copy.wait()
                r.norms[...] = r.norms[...] + r.norms_land[index]

            cube(0, False)
            cube(0, True)
            cube(1, False)
            for name in mine:
                every_of(jobs, [name], "step_add", "step_outer", "step_inner")
            cube(1, True)
            cube(2, False)
            every_of(jobs, older, "step_mate")
            cube(2, True)
            cube(3, False)
            every_of(jobs, new[1:], "step_join")
            every_of(jobs, mine_out, "step_join")
            cube(3, True)
            cube(4, False)
            swap.start()
            every_of(jobs, new[:1], "step_relay")
            every_of(jobs, new[:1], "step_mate")
            for name in mine:
                every_of(jobs, [name], "step_join")
            every_of(jobs, new[1:], "step_relay")
            every_of(jobs, mine_out, "step_relay")
            every_of(jobs, mine, "step_relay")
            every_of(jobs, new[1:], "step_mate")
            every_of(jobs, mine_out, "step_mate")
            every_of(jobs, mine, "step_mate")
            cube(4, True)
            swap.give(r.grad_stream, r.home)
            swap.end()
        else:
            for index, value in enumerate(rows_norms):
                r.norms[index : index + 1, :] = value
        sent()
        every(outs, "wait")
        every_of(jobs, jobs, "step_end")

    return run(
        body,
        7 + layer,
        {
            "grad": (grad, VMEM), "branch": (saved.branch, VMEM), "stream": (stream, VMEM), "gains": (gains, VMEM),
            "shifts": (shifts, VMEM), "held_in": (saved.held_out, ANY), "qkv_in": (saved.qkv_out, ANY),
            "attended_in": (saved.attended_out, ANY), "lse_in": (saved.lse_out, ANY), "w_qkv": (w_qkv, ANY), "w_out": (w_out, ANY), "own_qkv": (own_qkv, ANY), "own_out": (own_out, ANY),
            **pass_inputs(grads), **({} if mixed is None else {"mixed": (mixed, VMEM)}), **({f"norms{index}": (value, VMEM) for index, value in enumerate(norms)} if final else {}),
        },
        {
            **pass_outputs({**grads, **mine_out}),
            **({"qkv_last_out": (w_qkv.shape, bf16, ANY)} if final else {}),
            **({} if mixed is None else {"mixed_out": (mixed.shape, f32, VMEM)}),
            "grad_stream": ((rows, model), f32, VMEM), "norms": ((16 if final else 4, model), f32, VMEM),
            **({} if final else {"grad_qkv": (w_qkv.shape, bf16, ANY), "grad_out": (w_out.shape, bf16, ANY)}),
        },
        {
            "held": VMEM((4 * rows, model), bf16), "past": VMEM((4 * rows, model), bf16), "qkv": VMEM((4 * rows, 3 * width), bf16),
            "attended": VMEM((4 * rows, width), bf16), "lse": VMEM((4 * rows, 128), f32), "inner": VMEM((4 * rows, 128), f32),
            "above": VMEM((4 * rows, width), bf16), "pushed": VMEM((4 * rows, 3 * width), bf16),
            "grad_key": VMEM((4 * rows, width), f32), "grad_value": VMEM((4 * rows, width), f32),
            "weight": VMEM((model, 3 * width), bf16), "out": VMEM(w_out.shape, bf16), "outcome": VMEM((3, model, width), bf16),
            "outcome_out": VMEM(w_out.shape, bf16), **group_scratch(rows, model), "local": semaphores(8),
            **pass_scratch({**grads, **mine, **mine_out}),
            **(
                {}
                if mixed is None
                else {"low": VMEM(mixed.shape, bf16), "landed": VMEM(mixed.shape, bf16), "swap": semaphores(4)}
            ),
            **(
                {
                    "home": VMEM((rows, model), f32), "low": VMEM((rows, model), bf16), "landed": VMEM((rows, model), bf16),
                    "norms_land": VMEM((len(CUBE), 16, model), f32), "swap": semaphores(14),
                }
                if final
                else {}
            ),
        },
        60 * rows * model * width,
        64 * rows * rows,
    )


def per_device(hidden_in, cotangent, group_ids, group_sizes, w_qkv, w_out, w_up, w_down, gains, shifts):
    groups = (group_ids.reshape(1, 1), group_sizes.reshape(1, -1))
    own_att, own_ffn = (w_qkv, w_out), (w_up, w_down)
    links = {"middle": "middle", "gains": "gains", "shifts": "shifts", "w_up": "up_to", "w_down": "down_to"}
    rows = jax.ShapeDtypeStruct(hidden_in.shape, f32)
    up, down = [jax.ShapeDtypeStruct(value.shape[1:], bf16) for value in own_ffn]
    att_zero, ffn_zero = run_both(
        1,
        attention_forward(0, hidden_in, gains, shifts, None, None, *own_att, {"up": w_up, "down": w_down}, groups),
        ffn_forward(0, rows, gains, shifts, up, down, *own_ffn, {"qkv": w_qkv, "out": w_out, "down": w_down}),
        links,
    )
    att_weights = [(att_zero.qkv_to, att_zero.out_to), (ffn_zero.qkv_to, ffn_zero.out_to)]
    links.pop("w_down")
    att_one, ffn_one = run_both(
        2,
        attention_forward(1, ffn_zero.stream, gains, shifts, *att_weights[1], *own_att, {"up": w_up}),
        ffn_forward(1, rows, gains, shifts, up, ffn_zero.down_to, *own_ffn, {}, cotangent, att_zero.scale),
        links,
        (("c", "zh"),),
    )
    ffn_weights = [(att_zero.up_to, att_zero.down_to), (att_one.up_to, ffn_zero.down_to)]
    ffn_zero.middle, ffn_one.middle = att_zero.middle, att_one.middle
    back_one = ffn_backward(1, ffn_one.grad, ffn_one, gains, shifts, *ffn_weights[1], *own_ffn, {})
    deep_one = attention_backward(
        1, back_one.grad_middle, ffn_zero.stream, att_one, gains, shifts, *att_weights[1], *own_att,
        {"up1": (back_one.grad_up, 0, 1), "down1": (back_one.grad_down, 0, 0)},
        mixed=ffn_one.stream,
    )
    back_zero = ffn_backward(
        0, deep_one.grad_stream, ffn_zero, gains, shifts, *ffn_weights[0], *own_ffn,
        {"up1": (deep_one.up1_out, 2, 2), "down1": (deep_one.down1_out, 1, 2), "qkv1": (deep_one.grad_qkv, 0, 0), "out1": (deep_one.grad_out, 0, 0)},
    )
    last = attention_backward(
        0, back_zero.grad_middle, att_zero.stream_out, att_zero, gains, shifts, *att_weights[0], *own_att,
        {
            "qkv1": (back_zero.qkv1_out, 1, 2), "out1": (back_zero.out1_out, 1, 2),
            "up0": (back_zero.grad_up, 0, 2), "down0": (back_zero.grad_down, 0, 2),
        },
        (back_zero.norms, deep_one.norms, back_one.norms),
    )
    grads = [
        jnp.stack(pair).astype(f32)
        for pair in (
            (last.qkv_last_out, last.qkv1_out),
            (last.out_last_out, last.out1_out),
            (last.up0_out, back_zero.up1_out),
            (last.down0_out, back_zero.down1_out),
        )
    ]
    sums = last.norms.reshape(2, 4, 2, -1)
    if lax.axis_size("gh") > 1:
        grads, sums = lax.psum((grads, sums), "gh")
    return (deep_one.mixed_out, last.grad_stream, *grads, sums[:, :, 0], sums[:, :, 1])


def solution(mesh):
    fine = jax.sharding.Mesh(mesh.devices.reshape(-1, 2, 2, 2, 2, 2), AXES)
    dp = ("gh", "gl", "p", "c")
    tensor = ("zh", "zl")
    rows = P((*dp, *tensor), None)
    weights = (
        P(None, None, None, tensor),
        P(None, tensor, None),
        P(None, None, tensor),
        P(None, tensor, None),
    )
    return jax.shard_map(
        per_device,
        mesh=fine,
        in_specs=(rows, rows, P(dp), P(), *weights, P(), P()),
        out_specs=(rows, rows, *weights, P(), P()),
        check_vma=False,
    )
```

```python
import functools
import types

import jax
import jax.numpy as jnp
from jax import lax
from jax.experimental import pallas as pl
from jax.experimental.pallas import tpu as pltpu
from jax.sharding import PartitionSpec as P

HEAD_DIM = 64
AXES = ("gh", "gl", "p", "c", "zh", "zl")
f32 = jnp.float32
bf16 = jnp.bfloat16
MESH = pl.DeviceIdType.MESH
VMEM, ANY = pltpu.VMEM, pl.ANY
eps_norm = 1e-05
TILE = 256


def centre(values):
    mean = jnp.mean(values, axis=-1, keepdims=True)
    centred = values - mean
    spread = jnp.mean(centred * centred, axis=-1, keepdims=True)
    rate = lax.rsqrt(spread + eps_norm)
    return centred * rate, rate


def norm_rows(values, gain, shift):
    return centre(values)[0] * gain + shift


def norm_pull(values, gain, grad):
    hat, rate = centre(values)
    scaled = grad * gain
    along = jnp.mean(scaled * hat, axis=-1, keepdims=True)
    level = jnp.mean(scaled, axis=-1, keepdims=True)
    return (
        rate * (scaled - level - hat * along),
        jnp.sum(grad * hat, axis=0, keepdims=True),
        jnp.sum(grad, axis=0, keepdims=True),
    )


def dot_nt(left, right):
    return lax.dot_general(left, right, (((1,), (1,)), ((), ())), preferred_element_type=f32)


def dot_tn(left, right):
    return lax.dot_general(left, right, (((0,), (0,)), ((), ())), preferred_element_type=f32)


def dot_nn(left, right):
    return jnp.dot(left, right, preferred_element_type=f32)


def cut_rows(rows):
    first = (rows // 2 + 15) // 16 * 16
    return ((0, first), (first, rows - first))


def flipped(*names):
    return {name: 1 - lax.axis_index(name) for name in names}


def greet(*others):
    barrier = pltpu.get_barrier_semaphore()
    for names in others:
        pl.semaphore_signal(barrier, inc=1, device_id=flipped(*names), device_id_type=MESH)
    pl.semaphore_wait(barrier, len(others))


GROUP = (("c",), ("zl",))
FETCH = (("zh",), ("p",), ("gl",))


def remote(source, target, send, receive, device):
    return pltpu.make_async_remote_copy(
        src_ref=source,
        dst_ref=target,
        send_sem=send,
        recv_sem=receive,
        device_id=device,
        device_id_type=MESH,
    )


def tiles(width, body):
    def step(index, carry):
        body(pl.ds(pl.multiple_of(index * TILE, TILE), TILE))
        return carry

    lax.fori_loop(0, width // TILE, step, 0)


def exchange(rows, held, prepare, work, first, sums, send, receive):
    mate, near = flipped("c"), flipped("zl")
    own = pl.ds(0, rows)
    parts = cut_rows(rows)
    along = []
    for index, (start, size) in enumerate(parts):
        prepare(start, size)
        place = pl.ds(2 * rows + 2 * start, size)
        copy = remote(held.at[pl.ds(start, size)], held.at[place], send.at[1 + index], receive.at[1 + index], near)
        copy.start()
        along.append(copy)
    copies = [remote(held.at[own], held.at[pl.ds(rows, rows)], send.at[0], receive.at[0], mate)]
    copies[0].start()

    def keep(row, columns, value):
        first[pl.ds(row, value.shape[0]), columns] = value

    work(0, rows, keep)
    copies[0].wait_recv()

    def keep_mate(row, columns, value):
        sums[0, pl.ds(row - rows, value.shape[0]), columns] = value.astype(bf16)

    work(rows, rows, keep_mate)
    back = remote(sums.at[0], sums.at[1], send.at[3], receive.at[3], mate)
    back.start()
    copies.append(back)
    final = []
    for index, (start, size) in enumerate(parts):
        place = 2 * rows + 2 * start
        along[index].wait_recv()
        relay = remote(
            held.at[pl.ds(place, size)], held.at[pl.ds(place + size, size)], send.at[4 + index], receive.at[4 + index], mate
        )
        relay.start()
        relay.wait_recv()

        def keep_far(row, columns, value, place=place, start=start, size=size):
            first[pl.ds(rows + start, size), columns] = value[:size]
            sums[2, pl.ds(start, size), columns] = value[size:].astype(bf16)

        work(place, 2 * size, keep_far)
        part = pl.ds(start, size)
        cross = remote(sums.at[2, part], sums.at[3, part], send.at[6 + index], receive.at[6 + index], mate)
        cross.start()
        cross.wait_recv()
        sums[4, part, :] = (first[pl.ds(rows + start, size), :] + sums[3, part, :].astype(f32)).astype(bf16)
        last = remote(sums.at[4, part], sums.at[5, part], send.at[8 + index], receive.at[8 + index], near)
        last.start()
        final.append(last)
        copies += [relay, cross]

    def finish(done):
        back.wait_recv()
        for copy, (start, size) in zip(final, parts):
            copy.wait_recv()
            done(start, size, summed(first, sums, start, size))
        every(copies + along + final, "wait_send")

    return finish


def summed(first, sums, start, size):
    part = pl.ds(start, size)
    return first[part, :] + sums[1, part, :].astype(f32) + sums[5, part, :].astype(f32)


def run(body, number, inputs, outputs, scratch, flops, transcendentals=0):
    copied = [name for name, (_, memory) in inputs.items() if memory is VMEM]
    own = {name: VMEM(inputs[name][0].shape, inputs[name][0].dtype) for name in copied}
    names = [*inputs, *outputs, *scratch, *(name + "_copy" for name in copied), "arrivals"]

    def kernel(*refs):
        found = dict(zip(names, refs))
        copies = [
            pltpu.make_async_copy(found[name], found[name + "_copy"], found["arrivals"].at[index])
            for index, name in enumerate(copied)
        ]
        every(copies, "start")
        found.update({name: found[name + "_copy"] for name in copied})
        body(types.SimpleNamespace(**found, ready=lambda: every(copies, "wait"), greet=greet))

    moved = sum(value.size * value.dtype.itemsize for value, _ in inputs.values())
    results = pl.pallas_call(
        kernel,
        out_shape=tuple(jax.ShapeDtypeStruct(shape, kind) for shape, kind, _ in outputs.values()),
        in_specs=[pl.BlockSpec(memory_space=ANY) for _ in inputs],
        out_specs=tuple(pl.BlockSpec(memory_space=memory) for _, _, memory in outputs.values()),
        scratch_shapes=[*scratch.values(), *own.values(), semaphores(len(copied))],
        compiler_params=pltpu.CompilerParams(collective_id=number, has_side_effects=True, vmem_limit_bytes=58 << 20),
        cost_estimate=pl.CostEstimate(flops=flops, bytes_accessed=moved, transcendentals=transcendentals),
    )(*[value for value, _ in inputs.values()])
    return types.SimpleNamespace(**dict(zip(outputs, results)))


def plan(body, inputs, outputs, scratch, flops, transcendentals=0):
    return types.SimpleNamespace(
        body=body, inputs=inputs, outputs=outputs, scratch=scratch, flops=flops, transcendentals=transcendentals
    )


def run_both(number, first, second, links, extra=()):
    def both(one, two):
        return {**{"a_" + name: value for name, value in one.items()}, **{"b_" + name: value for name, value in two.items()}}

    def parts(found):
        return [{name[2:]: value for name, value in found.items() if name[:2] == mark} for mark in ("a_", "b_")]

    def body(r):
        one, two = parts(vars(r))
        two.update({name: one[source] for name, source in links.items()})
        first.body(types.SimpleNamespace(**one, ready=r.ready, greet=lambda *others: greet(*others, *extra)))
        second.body(types.SimpleNamespace(**two, ready=lambda: None, greet=lambda *others: None))

    result = run(
        body,
        number,
        both(first.inputs, {name: value for name, value in second.inputs.items() if name not in links}),
        both(first.outputs, second.outputs),
        both(first.scratch, second.scratch),
        first.flops + second.flops,
        first.transcendentals + second.transcendentals,
    )
    return [types.SimpleNamespace(**part) for part in parts(vars(result))]


def semaphores(count):
    return pltpu.SemaphoreType.DMA((count,))


def group_scratch(rows, width):
    return {
        "first": VMEM((2 * rows, width), f32),
        "sums": VMEM((6, rows, width), bf16),
        "send": semaphores(10),
        "receive": semaphores(10),
    }


def pick(ref, rows):
    return ref.at[:, rows, :] if len(ref.shape) == 3 else ref.at[rows, :]


def part_shape(shape, parts):
    return (*shape[:-2], int(shape[-2] / parts), shape[-1])


def inner():
    return lax.axis_index("zl") != lax.axis_index("zh")


def holds():
    return lax.axis_index("c") == lax.axis_index("zh")


def fetch_jobs(refs, names, layer):
    return [
        Fetching(
            getattr(refs, name + "_from").at[layer], getattr(refs, name + "_to"), getattr(refs, name + "_send"),
            getattr(refs, name + "_receive"),
        )
        for name in names
    ]


def fetch_inputs(weights):
    return {name + "_from": (value, ANY) for name, value in weights.items()}


def fetch_outputs(weights):
    return {name + "_to": (value.shape[1:], bf16, ANY) for name, value in weights.items()}


def fetch_scratch(weights):
    result = {}
    for name in weights:
        result[name + "_send"] = semaphores(8)
        result[name + "_receive"] = semaphores(8)
    return result


class Loading:
    def __init__(self, own, fetched, target, semaphore):
        self.ways = [pltpu.make_async_copy(source, target, semaphore) for source in (own, fetched)]

    def start(self):
        pl.when(holds())(self.ways[0].start)
        pl.when(jnp.logical_not(holds()))(self.ways[1].start)

    def wait(self):
        pl.when(holds())(self.ways[0].wait)
        pl.when(jnp.logical_not(holds()))(self.ways[1].wait)


def every(jobs, step):
    for job in jobs:
        getattr(job, step)()


CUBE = ("c", "zl", "p", "gl", "zh")
ORDERS = (("p", "gl"), ("gl", "p"))


class Halves:
    def copy(self, slot, source, target, name):
        return remote(source, target, self.send.at[slot], self.receive.at[slot], flipped(name))

    def at(self, half, first, second=None):
        start = (4 * half + 2 * first) * self.size
        if second is None:
            return pl.ds(pl.multiple_of(start, 16), 2 * self.size)
        return pl.ds(pl.multiple_of(start + second * self.size, 16), self.size)


class Fetching(Halves):
    def __init__(self, source, target, send, receive):
        self.source, self.target, self.send, self.receive = source, target, send, receive
        self.size = source.shape[-2] // 8

    def own(self, half):
        return self.at(half, *[lax.axis_index(name) for name in ORDERS[half]])

    def quarter(self, half):
        return pick(self.target, self.own(half))

    def along(self, half):
        return self.copy(half, pick(self.source, self.own(half)), self.quarter(half), "zh")

    def direct(self, half, axis):
        rows = self.quarter(half)
        return self.copy(2 + 2 * half + axis, rows, rows, ORDERS[half][axis])

    def relay(self, half):
        first, second = ORDERS[half]
        rows = pick(self.target, self.at(half, lax.axis_index(first), 1 - lax.axis_index(second)))
        return self.copy(6 + half, rows, rows, first)

    def start_along(self, here):
        @pl.when(jnp.logical_and(holds(), here))
        def _():
            for half in range(2):
                self.along(half).start()

    def step_inner(self):
        self.start_along(inner())

    def step_outer(self):
        self.start_along(jnp.logical_not(inner()))

    def step_sent(self):
        @pl.when(holds())
        def _():
            for half in range(2):
                self.along(half).wait_send()

    def share_if(self, here):
        @pl.when(jnp.logical_and(jnp.logical_not(holds()), here))
        def _():
            for half in range(2):
                self.along(half).wait_recv()
                self.direct(half, 1).start()
                self.direct(half, 0).start()

    def step_share(self):
        self.share_if(True)

    def step_share_outer(self):
        self.share_if(jnp.logical_not(inner()))

    def step_share_inner(self):
        self.share_if(inner())

    def step_relay(self):
        @pl.when(jnp.logical_not(holds()))
        def _():
            for half in range(2):
                self.direct(half, 1).wait_recv()
                self.relay(half).start()

    def step_got(self):
        @pl.when(jnp.logical_not(holds()))
        def _():
            for half in range(2):
                self.direct(half, 0).wait()
                self.direct(half, 1).wait_send()
                self.relay(half).wait()

    def step_end(self):
        self.step_sent()
        self.step_got()


class Passing(Halves):
    def __init__(self, refs, name, first, last, source=None, out=None):
        self.first, self.last = first, last
        for field in ("in", "out", "land", "mine", "more", "sum", "cross", "send", "receive", "local"):
            setattr(self, field, getattr(refs, f"{name}_{field}", None))
        self.source = source if source is not None else getattr(refs, f"{name}_in", None)
        if out is not None:
            self.out = out
        self.size = self.sum.shape[-2] // 2

    def place_of(self, half):
        return [lax.axis_index(name) for name in ORDERS[half]]

    def spread(self, half):
        name = ORDERS[half][0]
        return self.copy(half, pick(self.source, self.at(half, 1 - lax.axis_index(name))), self.land.at[half], name)

    def keep(self, half):
        rows = self.at(half, lax.axis_index(ORDERS[half][0]))
        return pltpu.make_async_copy(pick(self.source, rows), self.mine.at[half], self.local.at[half])

    def second(self, index):
        return pl.ds(pl.multiple_of(index * self.size, 16), self.size)

    def fold(self, half):
        name = ORDERS[half][1]
        return self.copy(2 + half, pick(self.mine.at[half], self.second(1 - lax.axis_index(name))), self.more.at[half], name)

    def load(self):
        return pltpu.make_async_copy(self.source, self.sum, self.local.at[2])

    def store(self):
        return pltpu.make_async_copy(self.sum, self.out, self.local.at[2])

    def along(self):
        return self.copy(4, self.sum, self.cross, "zh")

    def own(self, half):
        return pick(self.sum, pl.ds(half * self.size, self.size))

    def place(self, half):
        return pltpu.make_async_copy(self.own(half), pick(self.out, self.at(half, *self.place_of(half))), self.local.at[half])

    def direct(self, half, axis):
        own = pick(self.out, self.at(half, *self.place_of(half)))
        return self.copy(5 + 2 * half + axis, self.own(half), own, ORDERS[half][axis])

    def relay(self, half):
        first, second = self.place_of(half)
        rows = pick(self.out, self.at(half, first, 1 - second))
        return self.copy(9 + half, rows, rows, ORDERS[half][0])

    def mate(self, half, index):
        first = self.place_of(half)[0]
        rows = pick(self.out, self.at(half, first if index == 0 else 1 - first))
        return self.copy(11 + 2 * half + index, rows, rows, "c")

    def step_spread(self):
        for half in range(2):
            self.spread(half).start()
            self.keep(half).start()

    def step_fold(self):
        for half in range(2):
            self.keep(half).wait()
            self.spread(half).wait_recv()
            self.mine[half] = (self.mine[half].astype(f32) + self.land[half].astype(f32)).astype(bf16)
            self.fold(half).start()

    def step_add(self):
        for half in range(2):
            self.fold(half).wait_recv()
            own = pick(self.mine.at[half], self.second(lax.axis_index(ORDERS[half][1])))
            self.own(half)[...] = (own[...].astype(f32) + self.more[half].astype(f32)).astype(bf16)

    def step_load(self):
        self.load().start()

    def step_loaded(self):
        self.load().wait()

    def step_inner(self):
        pl.when(jnp.logical_and(jnp.logical_not(holds()), inner()))(self.along().start)

    def step_outer(self):
        pl.when(jnp.logical_not(jnp.logical_or(holds(), inner())))(self.along().start)

    def join_if(self, here):
        @pl.when(jnp.logical_and(holds(), here))
        def _():
            self.along().wait_recv()
            self.sum[...] = (self.sum[...].astype(f32) + self.cross[...].astype(f32)).astype(bf16)
            if self.last == 2:
                for half in range(2):
                    self.direct(half, 1).start()
                    self.direct(half, 0).start()
                    self.place(half).start()

    def step_join_outer(self):
        self.join_if(jnp.logical_not(inner()))

    def step_join_inner(self):
        self.join_if(inner())

    def step_join(self):
        self.join_if(True)

    def step_share(self):
        @pl.when(holds())
        def _():
            for half in range(2):
                self.direct(half, 1).start()
                self.direct(half, 0).start()
                self.place(half).start()

    def step_relay(self):
        @pl.when(holds())
        def _():
            for half in range(2):
                self.direct(half, 1).wait_recv()
                self.relay(half).start()
                self.place(half).wait()
                self.mate(half, 0).start()

    def step_mate(self):
        @pl.when(holds())
        def _():
            for half in range(2):
                self.direct(half, 0).wait_recv()
                self.relay(half).wait_recv()
                self.mate(half, 1).start()

    def step_store(self):
        self.store().start()

    def step_end(self):
        if self.first == 0:
            for half in range(2):
                self.spread(half).wait_send()
                self.fold(half).wait_send()
        if self.last < 2:
            self.store().wait()

        @pl.when(holds())
        def _():
            if self.last == 2:
                for half in range(2):
                    self.direct(half, 0).wait_send()
                    self.direct(half, 1).wait_send()
                    self.relay(half).wait_send()
                    self.mate(half, 0).wait_send()
                    self.mate(half, 1).wait_send()

        @pl.when(jnp.logical_not(holds()))
        def _():
            if self.first <= 1 <= self.last:
                self.along().wait_send()
            if self.last == 2:
                for half in range(2):
                    self.mate(half, 0).wait_recv()
                    self.mate(half, 1).wait_recv()


def pass_shapes(grads):
    for name, (value, first, last) in grads.items():
        whole = value.shape if first == 0 else part_shape(value.shape, 1 / 4)
        yield name, whole, part_shape(whole, 4), first, last


def pass_jobs(refs, grads, ends=None):
    return {name: Passing(refs, name, first, last, *(ends or {}).get(name, ())) for name, (_, first, last) in grads.items()}


def pass_inputs(grads):
    return {name + "_in": (value, ANY) for name, (value, *_) in grads.items() if isinstance(value, jax.Array)}


def pass_outputs(grads):
    return {name + "_out": (whole if last == 2 else part, bf16, ANY) for name, whole, part, first, last in pass_shapes(grads)}


def pass_scratch(grads):
    result = {}
    for name, whole, part, first, last in pass_shapes(grads):
        if first == 0:
            result[name + "_land"] = VMEM((2, *part), bf16)
            result[name + "_mine"] = VMEM((2, *part), bf16)
            result[name + "_more"] = VMEM((2, *part_shape(whole, 8)), bf16)
        result[name + "_sum"] = VMEM(part, bf16)
        if first <= 1 <= last:
            result[name + "_cross"] = VMEM(part, bf16)
        result[name + "_send"] = semaphores(15)
        result[name + "_receive"] = semaphores(15)
        result[name + "_local"] = semaphores(3)
    return result


def every_of(jobs, names, *steps):
    for step in steps:
        for name in names:
            getattr(jobs[name], step)()


class Swapping:
    def __init__(self, source, landed, semaphores):
        self.source, self.landed = source, landed
        self.parts = cut_rows(source.shape[0])
        self.copies = [
            remote(
                source.at[pl.ds(start, size)], landed.at[pl.ds(start, size)], semaphores.at[index], semaphores.at[2 + index],
                flipped("c", "zh"),
            )
            for index, (start, size) in enumerate(self.parts)
        ]

    def start_if(self, here):
        @pl.when(here)
        def _():
            every(self.copies, "start")

    def start(self):
        self.start_if(jnp.logical_not(holds()))

    def step_inner(self):
        self.start_if(jnp.logical_and(jnp.logical_not(holds()), inner()))

    def step_outer(self):
        self.start_if(jnp.logical_not(jnp.logical_or(holds(), inner())))

    def give(self, target, own, scale=None, only=(0, 1)):
        factor = 1.0 if scale is None else scale
        for index in only:
            rows = pl.ds(*self.parts[index])

            @pl.when(holds())
            def _(rows=rows):
                target[rows, :] = own[rows, :].astype(f32) * factor

            @pl.when(jnp.logical_not(holds()))
            def _(index=index, rows=rows):
                self.copies[index].wait_recv()
                target[rows, :] = self.landed[rows, :].astype(f32) * factor

    def end(self):
        @pl.when(jnp.logical_not(holds()))
        def _():
            every(self.copies, "wait_send")


def gelu_and_slope(values):
    rate, cubic = 0.7978845608028654, 0.044715
    square = values * values
    bend = jnp.tanh(rate * values * (1.0 + cubic * square))
    half = 0.5 * (1.0 + bend)
    slope = half + 0.5 * values * (1.0 - bend * bend) * (rate * (1.0 + 3.0 * cubic * square))
    return values * half, slope


def ffn_forward(layer, middle, gains, shifts, w_up, w_down, own_up, own_down, weights, cotangent=None, scale=None):
    rows, width = middle.shape
    hidden = w_up.shape[1]

    def body(r):
        loads = [Loading(r.own_up.at[layer], r.w_up, r.up, r.local.at[0]), Loading(r.own_down.at[layer], r.w_down, r.down, r.local.at[1])]
        for copy in loads:
            copy.start()
        r.greet(*GROUP, *(FETCH if weights else ()), *(() if cotangent is None else (("c", "zh"),)))
        r.ready()
        jobs = fetch_jobs(r, weights, layer + 1)
        swaps = [] if cotangent is None else [Swapping(r.cotangent, r.landed, r.swap)]
        every(jobs + swaps, "step_inner")
        held, active, slope = r.held, r.active, r.slope

        def prepare(start, size):
            part = pl.ds(start, size)
            held[part, :] = norm_rows(r.middle[part, :], r.gains[layer, 2:3, :], r.shifts[layer, 2:3, :]).astype(bf16)

        calls = []

        def work(start, size, sink):
            calls.append(start)
            if len(calls) == 1:
                every(jobs + swaps, "step_outer")
                every(loads, "wait")
            if len(calls) == 3:
                every(jobs, "step_share_outer")
            if len(calls) == 4:
                every(jobs, "step_share_inner")
            here = pl.ds(start, size)

            def step(columns):
                upper = dot_nn(held[here, :], r.up[:, columns])
                value, bend = gelu_and_slope(upper)
                active[here, columns] = value.astype(bf16)
                slope[here, columns] = bend.astype(bf16)

            tiles(hidden, step)

            def step_down(columns):
                sink(start, columns, dot_nn(active[here, :], r.down[:, columns]))

            tiles(width, step_down)

        finish = exchange(rows, held, prepare, work, r.first, r.sums, r.send, r.receive)
        stores = [
            pltpu.make_async_copy(held, r.held_out, r.local.at[2]),
            pltpu.make_async_copy(active, r.active_out, r.local.at[3]),
            pltpu.make_async_copy(slope, r.slope_out, r.local.at[4]),
        ]
        for copy in stores:
            copy.start()
        every(jobs, "step_relay")

        def done(start, size, total):
            part = pl.ds(start, size)
            r.second[part, :] = total
            r.stream[part, :] = r.middle[part, :] + norm_rows(total, r.gains[layer, 3:4, :], r.shifts[layer, 3:4, :])

        finish(done)
        every(jobs, "step_end")
        for swap in swaps:
            swap.give(r.grad, r.cotangent, r.scale[0:1, 0:1])
            swap.end()
        for copy in stores:
            copy.wait()

    return plan(
        body,
        {
            "middle": (middle, VMEM), "gains": (gains, VMEM), "shifts": (shifts, VMEM), "w_up": (w_up, ANY), "w_down": (w_down, ANY), "own_up": (own_up, ANY), "own_down": (own_down, ANY),
            **fetch_inputs(weights), **({} if cotangent is None else {"cotangent": (cotangent, VMEM), "scale": (scale, VMEM)}),
        },
        {
            "second": ((rows, width), f32, VMEM), "stream": ((rows, width), f32, VMEM),
            "held_out": ((4 * rows, width), bf16, ANY), "active_out": ((4 * rows, hidden), bf16, ANY),
            "slope_out": ((4 * rows, hidden), bf16, ANY), **fetch_outputs(weights),
            **({} if cotangent is None else {"grad": ((rows, width), f32, VMEM)}),
        },
        {
            "held": VMEM((4 * rows, width), bf16), "active": VMEM((4 * rows, hidden), bf16), "slope": VMEM((4 * rows, hidden), bf16),
            "up": VMEM(w_up.shape, bf16), "down": VMEM(w_down.shape, bf16), **group_scratch(rows, width), "local": semaphores(5),
            **fetch_scratch(weights),
            **({} if cotangent is None else {"landed": VMEM(cotangent.shape, bf16), "swap": semaphores(4)}),
        },
        16 * rows * width * hidden,
        4 * rows * hidden,
    )


def ffn_backward(layer, grad, saved, gains, shifts, w_up, w_down, own_up, own_down, grads):
    middle = saved.middle
    rows, width = middle.shape
    hidden = w_up.shape[1]

    def body(r):
        held, active, slope, pushed, past = r.held, r.active, r.slope, r.pushed, r.past
        loads = [
            Loading(r.own_down.at[layer], r.w_down, r.down, r.local.at[0]),
            Loading(r.own_up.at[layer], r.w_up, r.up, r.local.at[1]),
            pltpu.make_async_copy(r.slope_in, slope, r.local.at[2]),
            pltpu.make_async_copy(r.active_in, active, r.local.at[3]),
            pltpu.make_async_copy(r.held_in, past, r.local.at[4]),
        ]
        for copy in loads:
            copy.start()
        greet(*GROUP, *(FETCH if grads else ()))
        jobs = pass_jobs(r, grads)
        new = [name for name in grads if grads[name][1] == 0]
        late = [name for name in grads if grads[name][1] == 2]
        r.ready()
        crossing = [name for name in grads if grads[name][1] == 1]
        every_of(jobs, crossing, "step_load", "step_loaded", "step_inner")
        every_of(jobs, late, "step_load")
        every_of(jobs, new, "step_spread")
        norms = {}

        def pull(row, values, part, grad):
            pulled, *sums = norm_pull(values[part, :], r.gains[layer, row : row + 1, :], grad)
            norms[row] = [old + new for old, new in zip(norms.get(row, (0.0, 0.0)), sums)]
            return pulled

        def prepare(start, size):
            part = pl.ds(start, size)
            held[part, :] = pull(3, r.second, part, r.grad[part, :]).astype(bf16)

        calls = []

        def work(start, size, sink):
            calls.append(start)
            if len(calls) == 1:
                every_of(jobs, crossing, "step_outer")
                every_of(jobs, late, "step_loaded", "step_share")
                every(loads, "wait")
            if len(calls) == 4:
                every_of(jobs, new, "step_fold")
                every_of(jobs, crossing, "step_join_outer")
            here = pl.ds(start, size)

            def step(columns):
                value = dot_nt(held[here, :], r.down[columns, :])
                pushed[here, columns] = (value * slope[here, columns].astype(f32)).astype(bf16)

            tiles(hidden, step)

            def step_up(columns):
                sink(start, columns, dot_nt(pushed[here, :], r.up[columns, :]))

            tiles(width, step_up)

        finish = exchange(rows, held, prepare, work, r.first, r.sums, r.send, r.receive)

        every_of(jobs, late, "step_relay")
        every_of(jobs, crossing, "step_join_inner")

        def step_down(columns):
            r.outcome[0, columns, :] = dot_tn(active[:, columns], held[...]).astype(bf16)

        tiles(hidden, step_down)
        out_down = pltpu.make_async_copy(r.outcome.at[0], r.grad_down, r.local.at[0])
        out_down.start()
        def step_up(columns):
            r.outcome[1, columns, :] = dot_tn(past[:, columns], pushed[...]).astype(bf16)

        tiles(width, step_up)
        out_up = pltpu.make_async_copy(r.outcome.at[1], r.grad_up, r.local.at[1])
        out_up.start()
        every_of(jobs, new, "step_add", "step_store")
        every_of(jobs, crossing, "step_relay")
        every_of(jobs, late, "step_mate")

        def done(start, size, total):
            part = pl.ds(start, size)
            r.grad_middle[part, :] = r.grad[part, :] + pull(2, r.middle, part, total)

        finish(done)
        every_of(jobs, crossing, "step_mate")
        for index, value in enumerate((*norms[2], *norms[3])):
            r.norms[index : index + 1, :] = value
        out_down.wait()
        out_up.wait()
        every_of(jobs, grads, "step_end")

    return run(
        body,
        5 + layer,
        {
            "grad": (grad, VMEM), "second": (saved.second, VMEM), "middle": (middle, VMEM), "gains": (gains, VMEM),
            "shifts": (shifts, VMEM), "held_in": (saved.held_out, ANY), "active_in": (saved.active_out, ANY),
            "slope_in": (saved.slope_out, ANY), "w_up": (w_up, ANY), "w_down": (w_down, ANY), "own_up": (own_up, ANY), "own_down": (own_down, ANY),
            **pass_inputs(grads),
        },
        {
            **pass_outputs(grads),
            "grad_middle": ((rows, width), f32, VMEM), "norms": ((4, width), f32, VMEM),
            "grad_up": (w_up.shape, bf16, ANY), "grad_down": (w_down.shape, bf16, ANY),
        },
        {
            "held": VMEM((4 * rows, width), bf16), "past": VMEM((4 * rows, width), bf16),
            "active": VMEM((4 * rows, hidden), bf16), "slope": VMEM((4 * rows, hidden), bf16),
            "pushed": VMEM((4 * rows, hidden), bf16), "up": VMEM(w_up.shape, bf16), "down": VMEM(w_down.shape, bf16),
            "outcome": VMEM((2, width, hidden), bf16), **group_scratch(rows, width), "local": semaphores(5),
            **pass_scratch(grads),
        },
        32 * rows * width * hidden,
    )


def places(rows):
    c, zl = lax.axis_index("c"), lax.axis_index("zl")

    def at(core, part):
        return pl.multiple_of((2 * core + part) * rows, 16)

    return at(c, zl), at(1 - c, zl), at(c, 1 - zl), at(1 - c, 1 - zl)


def gather(rows, held, prepare, arrived, send, receive):
    mate, near = flipped("c"), flipped("zl")
    own, others, along, across = places(rows)
    parts = cut_rows(rows)
    copies = []
    for index, (start, size) in enumerate(parts):
        prepare(start, size)
        part = pl.ds(pl.multiple_of(own + start, 16), size)
        copy = remote(held.at[part], held.at[part], send.at[1 + index], receive.at[1 + index], near)
        copy.start()
        copies.append(copy)
    here = pl.ds(own, rows)
    copies.append(remote(held.at[here], held.at[here], send.at[0], receive.at[0], mate))
    copies[-1].start()
    arrived(own, rows)
    copies[-1].wait_recv()
    arrived(others, rows)
    for index, (start, size) in enumerate(parts):
        copies[index].wait_recv()
        first = pl.multiple_of(along + start, 16)
        part = pl.ds(first, size)
        relay = remote(held.at[part], held.at[part], send.at[4 + index], receive.at[4 + index], mate)
        relay.start()
        copies.append(relay)
        arrived(first, size)
        relay.wait_recv()
        arrived(pl.multiple_of(across + start, 16), size)

    def finish():
        every(copies, "wait_send")

    return finish


def scatter(rows, before, project, first, sums, send, receive):
    mate, near = flipped("c"), flipped("zl")
    own, others, _, _ = places(rows)
    parts = cut_rows(rows)
    crossing = [
        remote(sums.at[2, pl.ds(start, size)], sums.at[3, pl.ds(start, size)], send.at[6 + index], receive.at[6 + index], mate)
        for index, (start, size) in enumerate(parts)
    ]
    final = [
        remote(sums.at[4, pl.ds(start, size)], sums.at[5, pl.ds(start, size)], send.at[8 + index], receive.at[8 + index], near)
        for index, (start, size) in enumerate(parts)
    ]
    for half, name in ((1, "high"), (0, "low")):
        before(name)
        base = pl.multiple_of((2 * half + 1 - lax.axis_index("zl")) * rows, 16)
        far = lax.axis_index("c") != half
        for index, (start, size) in enumerate(parts):

            def keep(columns, value, start=start, size=size):
                first[pl.ds(rows + start, size), columns] = value

            project(pl.multiple_of(base + start, 16), size, keep)

            @pl.when(far)
            def _(index=index, start=start, size=size):
                sums[2, pl.ds(start, size), :] = first[pl.ds(rows + start, size), :].astype(bf16)
                crossing[index].start()

        @pl.when(jnp.logical_not(far))
        def _():
            for index, (start, size) in enumerate(parts):
                crossing[index].wait_recv()
                part = pl.ds(start, size)
                sums[4, part, :] = (first[pl.ds(rows + start, size), :] + sums[3, part, :].astype(f32)).astype(bf16)
                final[index].start()

    before("rest")

    def keep_mate(columns, value):
        sums[0, :, columns] = value.astype(bf16)

    project(others, rows, keep_mate)
    back = remote(sums.at[0], sums.at[1], send.at[3], receive.at[3], mate)
    back.start()

    def keep_own(columns, value):
        first[pl.ds(0, rows), columns] = value

    project(own, rows, keep_own)

    def finish(done):
        back.wait_recv()
        for copy, (start, size) in zip(final, parts):
            copy.wait_recv()
            done(start, size, summed(first, sums, start, size))
        every([back] + crossing + final, "wait_send")

    return finish


def head_lanes(shape, half):
    lane = lax.broadcasted_iota(jnp.int32, shape, len(shape) - 1)
    return (lane < HEAD_DIM) if half == 0 else (lane >= HEAD_DIM)


def masked(scores, start, first_key):
    query = lax.broadcasted_iota(jnp.int32, scores.shape, 0) + start
    key = lax.broadcasted_iota(jnp.int32, scores.shape, 1) + first_key
    return jnp.where(key <= query, scores, -1e30)


def spans(rows, high):
    if not high:
        return ((0, 2 * rows, True),)
    free = 2 * rows // 128 * 128
    return ((0, free, False), (free, 4 * rows - free, True))


def attend_block(rows, start, high, qkv, attended, lse):
    width = attended.shape[1]
    here = pl.ds(start, rows)
    lane = lax.broadcasted_iota(jnp.int32, (rows, 128), 1)
    tops = jnp.zeros((rows, 128), f32)
    for pair in range(width // 128):
        columns = slice(pair * 128, pair * 128 + 128)
        query = qkv[here, columns] * bf16(HEAD_DIM ** (-0.5))
        results = []
        for half in range(2):
            only = jnp.where(head_lanes(query.shape, half), query, 0)
            scores = []
            for begin, size, mask in spans(rows, high):
                part = dot_nt(only, qkv[pl.ds(begin, size), width + pair * 128 : width + pair * 128 + 128])
                scores.append(masked(part, start, begin) if mask else part)
            top = functools.reduce(jnp.maximum, [jnp.max(part, axis=-1, keepdims=True) for part in scores])
            total, result = 0.0, 0.0
            for (begin, size, _), part in zip(spans(rows, high), scores):
                weights = jnp.exp(part - top)
                total = total + jnp.sum(weights, axis=-1, keepdims=True)
                values = qkv[pl.ds(begin, size), 2 * width + pair * 128 : 2 * width + pair * 128 + 128]
                result = result + dot_nn(weights.astype(bf16), values)
            results.append(result / total)
            tops = jnp.where(lane == 2 * pair + half, top + jnp.log(total), tops)
        attended[here, columns] = jnp.where(head_lanes((rows, 128), 0), results[0], results[1]).astype(bf16)
    lse[here, :] = tops


def attention_forward(layer, stream, gains, shifts, w_qkv, w_out, own_qkv, own_out, weights, groups=None):
    rows, model = stream.shape
    width = own_out.shape[1]
    first = groups is not None
    early = {"qkv": own_qkv, "out": own_out} if first else {}

    def body(r):
        held, qkv, attended, lse, weight = r.held, r.qkv, r.attended, r.lse, r.matrix
        w_qkv, w_out = (r.qkv_to, r.out_to) if first else (r.w_qkv, r.w_out)
        loads = [
            Loading(r.own_qkv.at[layer, index], w_qkv.at[index], weight.at[:, pl.ds(index * width, width)], r.local.at[index])
            for index in range(3)
        ]
        loads.append(Loading(r.own_out.at[layer], w_out, r.out, r.local.at[3]))
        if not first:
            every(loads, "start")
        r.greet(*GROUP, *(FETCH if weights else ()), *((("c", "zh"),) if first else ()))
        jobs = fetch_jobs(r, weights, layer)
        stream = r.stream
        r.ready()
        if first:
            swap = Swapping(r.stream, r.landed, r.swap)
            index = lax.broadcasted_iota(jnp.int32, r.sizes.shape, 1)
            size = jnp.sum(jnp.where(index == r.ids[...], r.sizes[...], 0), axis=1, keepdims=True)
            r.weight[...] = jnp.broadcast_to(1.0 / size.astype(f32), r.weight.shape)
            exchanged = remote(r.weight, r.other, r.swap.at[4], r.swap.at[5], flipped("c"))
            before = [
                Fetching(source.at[layer], target, send, receive)
                for source, target, send, receive in (
                    (r.own_qkv, r.qkv_to, r.qkv_send, r.qkv_receive), (r.own_out, r.out_to, r.out_send, r.out_receive)
                )
            ]
            before[0].step_inner()
            before[0].step_outer()
            before[0].step_sent()
            exchanged.start()
            before[0].step_share()
            exchanged.wait()
            r.scale[...] = jnp.where(holds(), r.weight[...], r.other[...])
            swap.start()
            before[1].step_inner()
            before[1].step_outer()
            before[0].step_relay()
            stream = r.stream_out
        own = places(rows)[0]

        def prepare(start, size):
            part = pl.ds(start, size)
            if first:
                swap.give(r.stream_out, r.stream, None, (0 if start == 0 else 1,))
            value = norm_rows(stream[part, :], r.gains[layer, 0:1, :], r.shifts[layer, 0:1, :])
            held[pl.ds(pl.multiple_of(own + start, 16), size), :] = value.astype(bf16)

        calls = []

        def arrived(start, size):
            calls.append(start)
            if len(calls) == 1:
                if first:
                    before[1].step_share()
                    before[0].step_got()
                    every(loads[:3], "start")
                    every(loads[:3], "wait")
                else:
                    every(jobs, "step_outer")
                    every(loads, "wait")
            if len(calls) == 2 and first:
                every(jobs, "step_outer")
                before[1].step_relay()
            here = pl.ds(start, size)

            def step(columns):
                qkv[here, columns] = dot_nn(held[here, :], weight[:, columns]).astype(bf16)

            tiles(3 * width, step)

        sent = gather(rows, held, prepare, arrived, r.send, r.receive)
        stores = [pltpu.make_async_copy(held, r.held_out, r.local.at[0]), pltpu.make_async_copy(qkv, r.qkv_out, r.local.at[1])]
        for copy in stores:
            copy.start()
        zl = lax.axis_index("zl")

        def attend(quarter, high):
            attend_block(rows, pl.multiple_of(quarter * rows, 16), high, qkv, attended, lse)

        every(jobs, "step_inner")

        def before_part(name):
            if name == "high":
                attend(3 - zl, True)
                if first:
                    before[1].step_end()
                    loads[3].start()
                    loads[3].wait()
            elif name == "low":
                attend(1 - zl, False)
                if first:
                    every(jobs[:1], "step_share")
            else:
                attend(2 + zl, True)
                every(jobs[1:] if first else jobs, "step_share")
                attend(zl, False)

        def term(start, size, sink):
            here = pl.ds(start, size)

            def step(columns):
                sink(columns, dot_nn(attended[here, :], r.out[:, columns]))

            tiles(model, step)

        finish = scatter(rows, before_part, term, r.first, r.sums, r.send, r.receive)
        late = [pltpu.make_async_copy(attended, r.attended_out, r.local.at[2]), pltpu.make_async_copy(lse, r.lse_out, r.local.at[3])]
        for copy in late:
            copy.start()
        every(jobs, "step_relay")

        def done(start, size, total):
            part = pl.ds(start, size)
            r.branch[part, :] = total
            r.middle[part, :] = stream[part, :] + norm_rows(total, r.gains[layer, 1:2, :], r.shifts[layer, 1:2, :])

        finish(done)
        sent()
        every(jobs, "step_end")
        if first:
            swap.end()
        for copy in stores + late:
            copy.wait()

    return plan(
        body,
        {
            "stream": (stream, VMEM), "gains": (gains, VMEM), "shifts": (shifts, VMEM), "own_qkv": (own_qkv, ANY), "own_out": (own_out, ANY),
            **fetch_inputs(weights), **({"ids": (groups[0], VMEM), "sizes": (groups[1], VMEM)} if first else {"w_qkv": (w_qkv, ANY), "w_out": (w_out, ANY)}),
        },
        {
            "branch": ((rows, model), f32, VMEM), "middle": ((rows, model), f32, VMEM),
            "held_out": ((4 * rows, model), bf16, ANY), "qkv_out": ((4 * rows, 3 * width), bf16, ANY),
            "attended_out": ((4 * rows, width), bf16, ANY), "lse_out": ((4 * rows, 128), f32, ANY), **fetch_outputs(weights),
            **fetch_outputs(early),
            **({"stream_out": (stream.shape, f32, VMEM), "scale": ((8, 128), f32, VMEM)} if first else {}),
        },
        {
            "held": VMEM((4 * rows, model), bf16), "qkv": VMEM((4 * rows, 3 * width), bf16), "attended": VMEM((4 * rows, width), bf16),
            "lse": VMEM((4 * rows, 128), f32), "matrix": VMEM((model, 3 * width), bf16), "out": VMEM((width, model), bf16),
            **group_scratch(rows, model), "local": semaphores(4), **fetch_scratch(weights),
            **fetch_scratch(early),
            **({"landed": VMEM(stream.shape, bf16), "weight": VMEM((8, 128), f32), "other": VMEM((8, 128), f32), "swap": semaphores(6)} if first else {}),
        },
        24 * rows * model * width,
        64 * rows * rows,
    )


def attend_block_back(rows, start, high, qkv, attended_grad, lse, inner, grad_query, grad_key, grad_value):
    width = attended_grad.shape[1]
    here = pl.ds(start, rows)
    scale = HEAD_DIM ** (-0.5)
    for pair in range(width // 128):
        columns = slice(pair * 128, pair * 128 + 128)
        query = qkv[here, columns] * bf16(scale)
        above = attended_grad[here, columns]
        queries = [jnp.where(head_lanes(query.shape, half), query, 0) for half in range(2)]
        grads = [jnp.where(head_lanes(query.shape, half), above, 0) for half in range(2)]
        result = 0.0
        for begin, size, mask in spans(rows, high):
            keys = pl.ds(begin, size)
            key = qkv[keys, width + pair * 128 : width + pair * 128 + 128]
            value = qkv[keys, 2 * width + pair * 128 : 2 * width + pair * 128 + 128]
            both_probs, both_scores = [], []
            for half in range(2):
                head = 2 * pair + half
                scores = dot_nt(queries[half], key)
                if mask:
                    scores = masked(scores, start, begin)
                probs = jnp.exp(scores - lse[here, head : head + 1])
                grad_probs = dot_nt(grads[half], value)
                grad_scores = (probs * (grad_probs - inner[here, head : head + 1])).astype(bf16)
                key_only = jnp.where(head_lanes(key.shape, half), key, 0)
                result = result + dot_nn(grad_scores, key_only)
                both_probs.append(probs.astype(bf16))
                both_scores.append(grad_scores)
            grad_key[keys, columns] += dot_tn(jnp.concatenate(both_scores), jnp.concatenate(queries))
            grad_value[keys, columns] += dot_tn(jnp.concatenate(both_probs), jnp.concatenate(grads))
        grad_query[here, columns] = (result * scale).astype(bf16)


def attention_backward(layer, grad, stream, saved, gains, shifts, w_qkv, w_out, own_qkv, own_out, grads, norms=None, mixed=None):
    rows, model = stream.shape
    width = w_out.shape[0]
    final = norms is not None
    shape = jax.ShapeDtypeStruct
    thirds = ("query_last", "key_last", "value_last")
    mine = {name: (shape(w_qkv.shape[1:], bf16), 0, 2) for name in thirds} if final else {}
    mine_out = {"out_last": (shape(w_out.shape, bf16), 0, 2)} if final else {}

    def body(r):
        held, past, qkv, attended, lse, inner, above = r.held, r.past, r.qkv, r.attended, r.lse, r.inner, r.above
        pushed, grad_key, grad_value, weight = r.pushed, r.grad_key, r.grad_value, r.weight
        loads = [
            Loading(r.own_out.at[layer], r.w_out, r.out, r.local.at[3]),
            pltpu.make_async_copy(r.attended_in, attended, r.local.at[4]),
            pltpu.make_async_copy(r.qkv_in, qkv, r.local.at[5]),
            pltpu.make_async_copy(r.lse_in, lse, r.local.at[6]),
            *[
                Loading(r.own_qkv.at[layer, index], r.w_qkv.at[index], weight.at[:, pl.ds(index * width, width)], r.local.at[index])
                for index in range(3)
            ],
            pltpu.make_async_copy(r.held_in, past, r.local.at[7]),
        ]
        for copy in loads:
            copy.start()
        greet(*GROUP, *(FETCH if grads else ()), *((("c", "zh"),) if final or mixed is not None else ()))
        ends = {"out_last": (r.outcome_out,)}
        if final:
            ends.update({name: (r.outcome.at[index], r.qkv_last_out.at[index]) for index, name in enumerate(thirds)})
        jobs = pass_jobs(r, {**grads, **mine, **mine_out}, ends)
        new = [name for name in grads if grads[name][1] == 0]
        crossing = [name for name in grads if grads[name][1] == 1]
        r.ready()
        swaps = []
        if mixed is not None:
            r.low[...] = r.mixed[...].astype(bf16)
            swaps.append(Swapping(r.low, r.landed, r.swap))
        every_of(jobs, crossing, "step_load")
        every_of(jobs, new[:1], "step_spread")
        older = crossing
        own = places(rows)[0]
        norms_of = {}

        def pull(row, values, part, grad):
            pulled, *sums = norm_pull(values[part, :], r.gains[layer, row : row + 1, :], grad)
            norms_of[row] = [old + new for old, new in zip(norms_of.get(row, (0.0, 0.0)), sums)]
            return pulled

        def prepare(start, size):
            part = pl.ds(start, size)
            value = pull(1, r.branch, part, r.grad[part, :])
            held[pl.ds(pl.multiple_of(own + start, 16), size), :] = value.astype(bf16)

        zl = lax.axis_index("zl")

        def back(quarter, high):
            attend_block_back(
                rows, pl.multiple_of(quarter * rows, 16), high, qkv, above, lse, inner, pushed, grad_key, grad_value
            )

        blocks = []

        def arrived(start, size):
            if not blocks:
                grad_key[...] = jnp.zeros_like(grad_key)
                grad_value[...] = jnp.zeros_like(grad_value)
                every(loads, "wait")
            here = pl.ds(start, size)
            value = dot_nt(held[here, :], r.out[...]).astype(bf16)
            above[here, :] = value
            product = value.astype(f32) * attended[here, :].astype(f32)
            lane = lax.broadcasted_iota(jnp.int32, (size, 128), 1)
            tile = jnp.zeros((size, 128), f32)
            for pair in range(width // 128):
                part = product[:, pair * 128 : pair * 128 + 128]
                for half in range(2):
                    one = jnp.sum(jnp.where(head_lanes(part.shape, half), part, 0.0), axis=-1, keepdims=True)
                    tile = jnp.where(lane == 2 * pair + half, one, tile)
            inner[here, :] = tile
            blocks.append(size)
            if len(blocks) == 2:
                back(2 + zl, True)
                every_of(jobs, new[1:], "step_spread")
                back(zl, False)

        sent = gather(rows, held, prepare, arrived, r.send, r.receive)
        every(swaps, "start")
        every_of(jobs, crossing, "step_loaded", "step_outer", "step_inner")

        def step_out(columns):
            r.outcome_out[:, columns] = dot_tn(attended[...], held[:, columns]).astype(bf16)

        outs = []
        if final:
            tiles(model, step_out)
            every_of(jobs, mine_out, "step_spread")
        every_of(jobs, new[:1], "step_fold")

        def step_qkv(columns):
            value = dot_tn(past[:, columns], pushed[...]).astype(bf16)
            for index in range(3):
                r.outcome[index, columns, :] = value[:, index * width : (index + 1) * width]

        def cast(quarter):
            part = pl.ds(pl.multiple_of(quarter * rows, 16), rows)
            pushed[part, pl.ds(width, width)] = grad_key[part, :].astype(bf16)
            pushed[part, pl.ds(2 * width, width)] = grad_value[part, :].astype(bf16)

        def before_part(name):
            if name == "high":
                back(3 - zl, True)
                cast(3 - zl)
            elif name == "low":
                every_of(jobs, new[1:], "step_fold")
                every_of(jobs, new[:1], "step_add", "step_outer", "step_inner")
                every_of(jobs, mine_out, "step_fold")
                back(1 - zl, False)
                cast(1 - zl)
            else:
                cast(2 + zl)
                cast(zl)
                if final:
                    every_of(jobs, older, "step_join")
                    tiles(model, step_qkv)
                    every_of(jobs, mine, "step_spread")
                    every_of(jobs, mine_out, "step_add")
                    every_of(jobs, new[1:], "step_add", "step_outer", "step_inner")
                    every_of(jobs, mine_out, "step_outer", "step_inner")

        def term(start, size, sink):
            here = pl.ds(start, size)

            def step(columns):
                sink(columns, dot_nt(pushed[here, :], weight[columns, :]))

            tiles(model, step)

        finish = scatter(rows, before_part, term, r.first, r.sums, r.send, r.receive)
        if final:
            every_of(jobs, mine, "step_fold")
            every_of(jobs, older, "step_relay")
            every_of(jobs, new[:1], "step_join")
        else:
            every_of(jobs, new[1:], "step_add")
            tiles(model, step_out)
            outs.append(pltpu.make_async_copy(r.outcome_out, r.grad_out, r.local.at[0]))
            outs[0].start()
            tiles(model, step_qkv)
            outs.append(pltpu.make_async_copy(r.outcome, r.grad_qkv, r.local.at[1]))
            outs[1].start()

        def done(start, size, total):
            part = pl.ds(start, size)
            target = r.home if final else r.grad_stream
            target[part, :] = r.grad[part, :] + pull(0, r.stream, part, total)

        finish(done)
        if not final:
            every_of(jobs, new[:1], "step_join")
            every_of(jobs, new, "step_store")
        for swap in swaps:
            swap.give(r.mixed_out, r.mixed)
            swap.end()
        rows_norms = (*norms_of[0], *norms_of[1])
        if final:
            r.low[...] = r.home[...].astype(bf16)
            swap = Swapping(r.low, r.landed, r.swap)
            for index, value in enumerate(rows_norms):
                r.norms[index : index + 1, :] = value
            for index in range(len(norms)):
                r.norms[pl.ds(4 + 4 * index, 4), :] = getattr(r, f"norms{index}")[...]

            def cube(index, wait):
                copy = remote(
                    r.norms, r.norms_land.at[index], r.swap.at[4 + index], r.swap.at[9 + index], flipped(CUBE[index])
                )
                if not wait:
                    copy.start()
                    return
                copy.wait()
                r.norms[...] = r.norms[...] + r.norms_land[index]

            cube(0, False)
            cube(0, True)
            cube(1, False)
            for name in mine:
                every_of(jobs, [name], "step_add", "step_outer", "step_inner")
            cube(1, True)
            cube(2, False)
            every_of(jobs, older, "step_mate")
            cube(2, True)
            cube(3, False)
            every_of(jobs, new[1:], "step_join")
            every_of(jobs, mine_out, "step_join")
            cube(3, True)
            cube(4, False)
            swap.start()
            every_of(jobs, new[:1], "step_relay")
            every_of(jobs, new[:1], "step_mate")
            for name in mine:
                every_of(jobs, [name], "step_join")
            every_of(jobs, new[1:], "step_relay")
            every_of(jobs, mine_out, "step_relay")
            every_of(jobs, mine, "step_relay")
            every_of(jobs, new[1:], "step_mate")
            every_of(jobs, mine_out, "step_mate")
            every_of(jobs, mine, "step_mate")
            cube(4, True)
            swap.give(r.grad_stream, r.home)
            swap.end()
        else:
            for index, value in enumerate(rows_norms):
                r.norms[index : index + 1, :] = value
        sent()
        every(outs, "wait")
        every_of(jobs, jobs, "step_end")

    return run(
        body,
        7 + layer,
        {
            "grad": (grad, VMEM), "branch": (saved.branch, VMEM), "stream": (stream, VMEM), "gains": (gains, VMEM),
            "shifts": (shifts, VMEM), "held_in": (saved.held_out, ANY), "qkv_in": (saved.qkv_out, ANY),
            "attended_in": (saved.attended_out, ANY), "lse_in": (saved.lse_out, ANY), "w_qkv": (w_qkv, ANY), "w_out": (w_out, ANY), "own_qkv": (own_qkv, ANY), "own_out": (own_out, ANY),
            **pass_inputs(grads), **({} if mixed is None else {"mixed": (mixed, VMEM)}), **({f"norms{index}": (value, VMEM) for index, value in enumerate(norms)} if final else {}),
        },
        {
            **pass_outputs({**grads, **mine_out}),
            **({"qkv_last_out": (w_qkv.shape, bf16, ANY)} if final else {}),
            **({} if mixed is None else {"mixed_out": (mixed.shape, f32, VMEM)}),
            "grad_stream": ((rows, model), f32, VMEM), "norms": ((16 if final else 4, model), f32, VMEM),
            **({} if final else {"grad_qkv": (w_qkv.shape, bf16, ANY), "grad_out": (w_out.shape, bf16, ANY)}),
        },
        {
            "held": VMEM((4 * rows, model), bf16), "past": VMEM((4 * rows, model), bf16), "qkv": VMEM((4 * rows, 3 * width), bf16),
            "attended": VMEM((4 * rows, width), bf16), "lse": VMEM((4 * rows, 128), f32), "inner": VMEM((4 * rows, 128), f32),
            "above": VMEM((4 * rows, width), bf16), "pushed": VMEM((4 * rows, 3 * width), bf16),
            "grad_key": VMEM((4 * rows, width), f32), "grad_value": VMEM((4 * rows, width), f32),
            "weight": VMEM((model, 3 * width), bf16), "out": VMEM(w_out.shape, bf16), "outcome": VMEM((3, model, width), bf16),
            "outcome_out": VMEM(w_out.shape, bf16), **group_scratch(rows, model), "local": semaphores(8),
            **pass_scratch({**grads, **mine, **mine_out}),
            **(
                {}
                if mixed is None
                else {"low": VMEM(mixed.shape, bf16), "landed": VMEM(mixed.shape, bf16), "swap": semaphores(4)}
            ),
            **(
                {
                    "home": VMEM((rows, model), f32), "low": VMEM((rows, model), bf16), "landed": VMEM((rows, model), bf16),
                    "norms_land": VMEM((len(CUBE), 16, model), f32), "swap": semaphores(14),
                }
                if final
                else {}
            ),
        },
        60 * rows * model * width,
        64 * rows * rows,
    )


def widened(*pairs):
    steps = 4

    def block(shape):
        return part_shape(shape, steps)

    def place(rank):
        return lambda step: (*[0] * (rank - 2), step, 0)

    def body(*refs):
        count = len(pairs)
        for index in range(count):
            for layer in range(2):
                refs[2 * count + index][layer] = refs[2 * index + layer][...].astype(f32)

    values = [value for pair in pairs for value in pair]
    return pl.pallas_call(
        body,
        grid=(steps,),
        out_shape=tuple(jax.ShapeDtypeStruct((2, *one.shape), f32) for one, _ in pairs),
        in_specs=[pl.BlockSpec(block(value.shape), place(value.ndim)) for value in values],
        out_specs=tuple(pl.BlockSpec((2, *block(one.shape)), place(one.ndim + 1)) for one, _ in pairs),
        compiler_params=pltpu.CompilerParams(vmem_limit_bytes=60 << 20),
    )(*values)


def per_device(hidden_in, cotangent, group_ids, group_sizes, w_qkv, w_out, w_up, w_down, gains, shifts):
    groups = (group_ids.reshape(1, 1), group_sizes.reshape(1, -1))
    own_att, own_ffn = (w_qkv, w_out), (w_up, w_down)
    links = {"middle": "middle", "gains": "gains", "shifts": "shifts", "w_up": "up_to", "w_down": "down_to"}
    rows = jax.ShapeDtypeStruct(hidden_in.shape, f32)
    up, down = [jax.ShapeDtypeStruct(value.shape[1:], bf16) for value in own_ffn]
    att_zero, ffn_zero = run_both(
        1,
        attention_forward(0, hidden_in, gains, shifts, None, None, *own_att, {"up": w_up, "down": w_down}, groups),
        ffn_forward(0, rows, gains, shifts, up, down, *own_ffn, {"qkv": w_qkv, "out": w_out, "down": w_down}),
        links,
    )
    att_weights = [(att_zero.qkv_to, att_zero.out_to), (ffn_zero.qkv_to, ffn_zero.out_to)]
    links.pop("w_down")
    att_one, ffn_one = run_both(
        2,
        attention_forward(1, ffn_zero.stream, gains, shifts, *att_weights[1], *own_att, {"up": w_up}),
        ffn_forward(1, rows, gains, shifts, up, ffn_zero.down_to, *own_ffn, {}, cotangent, att_zero.scale),
        links,
        (("c", "zh"),),
    )
    ffn_weights = [(att_zero.up_to, att_zero.down_to), (att_one.up_to, ffn_zero.down_to)]
    ffn_zero.middle, ffn_one.middle = att_zero.middle, att_one.middle
    back_one = ffn_backward(1, ffn_one.grad, ffn_one, gains, shifts, *ffn_weights[1], *own_ffn, {})
    deep_one = attention_backward(
        1, back_one.grad_middle, ffn_zero.stream, att_one, gains, shifts, *att_weights[1], *own_att,
        {"up1": (back_one.grad_up, 0, 1), "down1": (back_one.grad_down, 0, 0)},
        mixed=ffn_one.stream,
    )
    back_zero = ffn_backward(
        0, deep_one.grad_stream, ffn_zero, gains, shifts, *ffn_weights[0], *own_ffn,
        {"up1": (deep_one.up1_out, 2, 2), "down1": (deep_one.down1_out, 1, 2), "qkv1": (deep_one.grad_qkv, 0, 0), "out1": (deep_one.grad_out, 0, 0)},
    )
    last = attention_backward(
        0, back_zero.grad_middle, att_zero.stream_out, att_zero, gains, shifts, *att_weights[0], *own_att,
        {
            "qkv1": (back_zero.qkv1_out, 1, 2), "out1": (back_zero.out1_out, 1, 2),
            "up0": (back_zero.grad_up, 0, 2), "down0": (back_zero.grad_down, 0, 2),
        },
        (back_zero.norms, deep_one.norms, back_one.norms),
    )
    grads = widened(
        (last.qkv_last_out, last.qkv1_out),
        (last.out_last_out, last.out1_out),
        (last.up0_out, back_zero.up1_out),
        (last.down0_out, back_zero.down1_out),
    )
    sums = last.norms.reshape(2, 4, 2, -1)
    if lax.axis_size("gh") > 1:
        grads, sums = lax.psum((grads, sums), "gh")
    return (deep_one.mixed_out, last.grad_stream, *grads, sums[:, :, 0], sums[:, :, 1])


def solution(mesh):
    fine = jax.sharding.Mesh(mesh.devices.reshape(-1, 2, 2, 2, 2, 2), AXES)
    dp = ("gh", "gl", "p", "c")
    tensor = ("zh", "zl")
    rows = P((*dp, *tensor), None)
    weights = (
        P(None, None, None, tensor),
        P(None, tensor, None),
        P(None, None, tensor),
        P(None, tensor, None),
    )
    return jax.shard_map(
        per_device,
        mesh=fine,
        in_specs=(rows, rows, P(dp), P(), *weights, P(), P()),
        out_specs=(rows, rows, *weights, P(), P()),
        check_vma=False,
    )
```
